128 devices in a mesh: seq: 64 (over x, z, y_lo, core), head: 2 (over y_hi).
Axes of the slice: x: 4, y: 4 (y_hi: 2, y_lo: 2; y = y_hi * 2 + y_lo), z: 4, core: 2. Of those that a mesh axis runs over, the one named last changes fastest.
Arguments:
- dna_bases: int32 [1048576], P('seq'), may hold values from 0 to 3
- stem_weight: bfloat16 [256, 1536], replicated, may hold values from -1 to 1
- encoder_weight: bfloat16 [3, 1536, 1536], P(None, None, 'head'), may hold values from -0.09375 to 0.09375
- norm_gain: float32 [1536], replicated, may hold values from 0.25 to 1.75
- attention_weight: bfloat16 [3, 1536, 1536], P(None, None, 'head'), may hold values from -0.15625 to 0.15625
- logit_scale: float32 [8], P('head'), may hold values from 8 to 400
- out_weight: bfloat16 [1536, 1536], P('head'), may hold values from -1.25 to 1.25
- decoder_weight: bfloat16 [3, 1536, 1536], P(None, 'head'), may hold values from -0.09375 to 0.09375
- grad_out: bfloat16 [16384, 1536], P('seq'), may hold values from -6 to 6
Outputs:
- decoded: bfloat16 [16384, 1536], P('seq', 'head')
- bins_grad: bfloat16 [8192, 1536], P('seq', 'head')
The draws below stay inside these ranges and needn't reach their ends.
Inputs may be any that keep to these rules, and one draw needn't show every extreme that they name: `dna_bases`: each entry names one of four bases.
All inputs are finite; a program needn't handle non-finite values.
Results may differ from the reference program's by a relative error of at most 0.034.
The reference program's roundings to bfloat16 on the way (of `embedded`, `encoded`, `normed`, `exps`, `attended`, `block_out`, `decoder_in` and `slope_grad`) count: a program that leaves them out, or rounds other values in their place, can miss the bound.
Values may be sent and summed in bfloat16 or wider, within the bound.
No kernel may reach another device: no remote copies, remote signals or barrier semaphores. Data moves between devices by JAX's collectives and lax.ppermute only.
A program may use at most 192 MiB of HBM per device.

```python
import jax
import jax.numpy as jnp
from jax import lax

D = 1536
HEADS = 8
HEAD_DIM = 192
PATCH = 64
KERNEL = 3
BINS = 8192
POSITIONS = 16384
BASES = 1048576


def draw_logit_scale(key, part):
    key = jax.random.fold_in(key, 7)
    return jax.random.uniform(key, (HEADS,), jnp.float32, 8.0, 30.0)


def draw_stem_weight(key, part):
    key = jax.random.fold_in(key, 11)
    raw_values = jax.random.uniform(key, (PATCH, 4, D), jnp.float32, -1.0, 1.0) * (3.0 / PATCH) ** 0.5
    centred = raw_values - jnp.mean(raw_values, axis=1, keepdims=True)
    return jnp.clip(centred, -1.0, 1.0).reshape(4 * PATCH, D).astype(jnp.bfloat16)


def plant(values, rng, low, high):
    index_at = [jax.random.randint(jax.random.fold_in(rng, axis), (), 0, length) for axis, length in enumerate(values.shape)]
    widest = values.shape.index(max(values.shape))
    neighbour = index_at[:widest] + [(index_at[widest] + 1) % values.shape[widest]] + index_at[widest + 1:]
    return values.at[tuple(index_at)].set(low).at[tuple(neighbour)].set(high)


def steps_of(stream_key, shape, pieces, least, high):
    gain, own = 1.0, jax.random.fold_in(stream_key, 6)
    for position, shards_of in pieces:
        steps = jnp.exp(jax.random.uniform(jax.random.fold_in(own, position), (shards_of,), jnp.float32, least / len(pieces), high / len(pieces)))
        gain = gain * jnp.repeat(steps, shape[position] // shards_of).reshape([-1 if axis == position else 1 for axis in range(len(shape))])
    return gain


def noise(stream_key, extent, deviation, limit, shards=(), kind=jnp.bfloat16):
    gain = steps_of(stream_key, extent, shards, -0.22, 0.18) if shards else 1.0
    values = jax.random.normal(stream_key, extent, jnp.float32) * deviation * gain
    return jnp.minimum(jnp.maximum(values, -limit), limit).astype(kind)


def setup_inputs(seed: int = 0) -> dict:
    key_list = jax.random.split(jax.random.key(seed), 10)
    return {
        "dna_bases": plant(jax.random.randint(key_list[0], (BASES,), 0, 4), jax.random.fold_in(key_list[0], 1), 0, 3).astype(jnp.int32),
        "stem_weight": draw_stem_weight(jax.random.fold_in(key_list[9], 71), 0),
        "encoder_weight": noise(key_list[2], (KERNEL, D, D), (KERNEL * D) ** -0.5, 0.09375, ((2, 2),)),
        "norm_gain": jnp.clip(1.0 + 0.15 * jax.random.normal(key_list[3], (D,), jnp.float32), 0.25, 1.75),
        "attention_weight": noise(key_list[4], (3, D, HEADS * HEAD_DIM), D ** -0.5, 0.15625, ((2, 2),)),
        "logit_scale": draw_logit_scale(jax.random.fold_in(key_list[9], 71), 0),
        "out_weight": noise(key_list[6], (HEADS * HEAD_DIM, D), (max(1, HEADS * HEAD_DIM // 64)) ** -0.5, 1.25, ((0, 2),)),
        "decoder_weight": noise(key_list[7], (KERNEL, D, D), (KERNEL * D) ** -0.5, 0.09375, ((1, 2),)),
        "grad_out": noise(key_list[8], (POSITIONS, D), 1.0, 6.0, ((0, 64),)),
    }


def embed_bases(dna_bases, stem_weight):
    grouped = dna_bases.reshape(-1, PATCH)
    letters = jnp.arange(4, dtype=jnp.int32)
    onehot = (grouped[:, :, None] == letters).astype(jnp.bfloat16).reshape(grouped.shape[0], 4 * PATCH)
    return jnp.dot(onehot, stem_weight, preferred_element_type=jnp.float32).astype(jnp.bfloat16)

def conv_forward(padded, weight, rows_here):
    result = jnp.dot(padded[0:rows_here], weight[0], preferred_element_type=jnp.float32)
    for tap in range(1, KERNEL):
        result = result + jnp.dot(padded[tap:tap + rows_here], weight[tap], preferred_element_type=jnp.float32)
    return result

def conv_backward(padded, weight, rows_here):
    margin = KERNEL // 2
    result = None
    for tap in range(KERNEL):
        begin = 2 * margin - tap
        term = lax.dot_general(padded[begin:begin + rows_here], weight[tap], (((1,), (1,)), ((), ())), preferred_element_type=jnp.float32)
        result = term if result is None else result + term
    return result

def attend(queries, keys, values, logit_scale):
    keys_count = queries.shape[0]
    block_rows = min(keys_count, 1024)
    query_heads = queries.reshape(keys_count, HEADS, HEAD_DIM).transpose(1, 0, 2)
    key_heads = keys.reshape(keys_count, HEADS, HEAD_DIM).transpose(1, 0, 2)
    value_heads = values.reshape(keys_count, HEADS, HEAD_DIM).transpose(1, 0, 2)

    def one_head(packed):
        head_queries, head_keys, head_values, scale_head = packed
        key_inv = lax.rsqrt(lax.optimization_barrier(jnp.mean(jnp.square(head_keys.astype(jnp.float32)), axis=1)) + 1e-06)
        query_blocks = head_queries.reshape(-1, block_rows, HEAD_DIM)

        def one_block(block_queries):
            query_inv = lax.rsqrt(lax.optimization_barrier(jnp.mean(jnp.square(block_queries.astype(jnp.float32)), axis=1)) + 1e-06)
            raw_dot = jnp.dot(block_queries, head_keys.T, preferred_element_type=jnp.float32)
            scores = raw_dot * (scale_head / HEAD_DIM) * query_inv[:, None] * key_inv[None, :]
            row_max = lax.optimization_barrier(jnp.max(scores, axis=1, keepdims=True))
            exps = jnp.exp(scores - row_max)
            row_sum = lax.optimization_barrier(jnp.sum(exps, axis=1, keepdims=True))
            return jnp.dot(exps.astype(jnp.bfloat16), head_values, preferred_element_type=jnp.float32) / row_sum
        return lax.map(one_block, query_blocks).reshape(keys_count, HEAD_DIM)
    mixed_heads = lax.map(one_head, (query_heads, key_heads, value_heads, logit_scale))
    return mixed_heads.transpose(1, 0, 2).reshape(keys_count, HEADS * HEAD_DIM).astype(jnp.bfloat16)

def reference(dna_bases, stem_weight, encoder_weight, norm_gain, attention_weight, logit_scale, out_weight, decoder_weight, grad_out):
    margin = KERNEL // 2
    rows_here = POSITIONS
    embedded = embed_bases(dna_bases, stem_weight)
    padded = jnp.pad(embedded, ((margin, margin), (0, 0)))
    encoder_pre = conv_forward(padded, encoder_weight, rows_here)
    encoded = (embedded.astype(jnp.float32) + jax.nn.gelu(encoder_pre)).astype(jnp.bfloat16)
    binned = lax.optimization_barrier(jnp.mean(encoded.astype(jnp.float32).reshape(BINS, 2, D), axis=1))
    normed = (binned * lax.rsqrt(lax.optimization_barrier(jnp.mean(jnp.square(binned), axis=1, keepdims=True)) + 1e-06) * norm_gain).astype(jnp.bfloat16)
    queries = jnp.dot(normed, attention_weight[0], preferred_element_type=jnp.float32).astype(jnp.bfloat16)
    keys = jnp.dot(normed, attention_weight[1], preferred_element_type=jnp.float32).astype(jnp.bfloat16)
    values = jnp.dot(normed, attention_weight[2], preferred_element_type=jnp.float32).astype(jnp.bfloat16)
    attended = attend(queries, keys, values, logit_scale)
    projected = jnp.dot(attended, out_weight, preferred_element_type=jnp.float32)
    block_out = (binned + projected).astype(jnp.bfloat16)
    decoder_in = (jnp.repeat(block_out, 2, axis=0).astype(jnp.float32) + encoded.astype(jnp.float32)).astype(jnp.bfloat16)
    decoder_pad = jnp.pad(decoder_in, ((margin, margin), (0, 0)))
    decoder_pre = conv_forward(decoder_pad, decoder_weight, rows_here)
    decoded = (decoder_in.astype(jnp.float32) + jax.nn.gelu(decoder_pre)).astype(jnp.bfloat16)
    cotangent = grad_out.astype(jnp.float32)
    slope_grad = jax.vjp(jax.nn.gelu, decoder_pre)[1](cotangent)[0].astype(jnp.bfloat16)
    slope_pad = jnp.pad(slope_grad, ((margin, margin), (0, 0)))
    input_grad = cotangent + conv_backward(slope_pad, decoder_weight, rows_here)
    bins_grad = lax.optimization_barrier(jnp.sum(input_grad.reshape(BINS, 2, D), axis=1)).astype(jnp.bfloat16)
    return (decoded, bins_grad)
```

```python
import functools

import jax
import jax.numpy as jnp
from jax import lax
from jax.experimental import pallas as pl
from jax.experimental.pallas import tpu as pltpu
from jax.sharding import PartitionSpec as P

BF16 = jnp.bfloat16
F32 = jnp.float32
ROWS = 136
OWN = 128
TILE = 256
HEAD = 192
EPS = 1e-06
VMEM = 56 * 1024 * 1024


def params():
    return pltpu.CompilerParams(vmem_limit_bytes=VMEM)


def dot(a, b):
    return jnp.dot(a, b, preferred_element_type=F32)


def dot_t(a, b):
    return lax.dot_general(a, b, (((1,), (1,)), ((), ())), preferred_element_type=F32)


def cost(flops, nbytes):
    return pl.CostEstimate(flops=int(flops), bytes_accessed=int(nbytes), transcendentals=0)


def shape(dims, dtype):
    return jax.ShapeDtypeStruct(dims, dtype)


def whole(dims):
    return pl.BlockSpec(dims, lambda *_: (0,) * len(dims))


def above(rows):
    return pltpu.roll(rows, 1, 0)


def below(rows):
    return pltpu.roll(rows, ROWS - 1, 0)


def gelu_parts(x):
    inner = 0.7978845608028654 * (x + 0.044715 * (x * x * x))
    return inner, jnp.tanh(inner)


def conv_taps(rows, weight):
    first, mid, last = (dot(rows, weight(t)) for t in range(3))
    even = above(first[ROWS:]) + mid[:ROWS] + last[ROWS:]
    odd = first[:ROWS] + mid[ROWS:] + below(last[:ROWS])
    return even, odd


def encoder_kernel(ids, codes, stem, weight, encoded, squares, embedded):
    step = pl.program_id(0)

    @pl.when(step == 0)
    def _():
        patch = stem.shape[0] // 4
        row = lax.broadcasted_iota(jnp.int32, (2 * patch, 4 * patch), 0)
        col = lax.broadcasted_iota(jnp.int32, (2 * patch, 4 * patch), 1)
        code = codes[...]
        spread = [
            dot(code, (row == col // 4 + offset).astype(F32).astype(BF16))
            for offset in (0, patch)
        ]
        spread = jnp.concatenate(spread, axis=0)
        base = lax.broadcasted_iota(jnp.int32, spread.shape, 1) % 4 + 1
        onehot = (spread == base.astype(F32)).astype(F32).astype(BF16)
        embedded[...] = dot(onehot, stem[...]).astype(BF16)
        squares[...] = jnp.zeros_like(squares)

    even, odd = conv_taps(embedded[...], lambda t: weight[t])
    column = ids[0] * (3 * TILE) + step * TILE
    mine = embedded[:, pl.ds(pl.multiple_of(column, TILE), TILE)].astype(F32)
    pre = jnp.concatenate([even, odd], axis=0)
    _, tanh = gelu_parts(pre)
    out = (mine + 0.5 * pre * (1.0 + tanh)).astype(BF16)
    encoded[...] = out
    out = out.astype(F32)
    binned = (out[:ROWS] + out[ROWS:]) * 0.5
    squares[...] += jnp.broadcast_to(
        jnp.sum(binned * binned, axis=1, keepdims=True), squares.shape
    )


def encode(ids, codes, stem, weight):
    half = weight.shape[2]
    feats = stem.shape[1]
    return pl.pallas_call(
        encoder_kernel,
        grid_spec=pltpu.PrefetchScalarGridSpec(
            num_scalar_prefetch=1,
            grid=(half // TILE,),
            in_specs=[
                whole(codes.shape),
                whole(stem.shape),
                pl.BlockSpec((3, feats, TILE), lambda i, ids: (0, 0, i)),
            ],
            out_specs=[
                pl.BlockSpec((2 * ROWS, TILE), lambda i, ids: (0, i)),
                whole((ROWS, 128)),
            ],
            scratch_shapes=[pltpu.VMEM((2 * ROWS, feats), BF16)],
        ),
        out_shape=[shape((2 * ROWS, half), BF16), shape((ROWS, 128), F32)],
        compiler_params=params(),
        cost_estimate=cost(2 * 2 * ROWS * 3 * feats * half, weight.size * 2),
        name="encode",
    )(ids, codes, stem, weight)


def norm_kernel(ids, encoded, mine, theirs, gain, out):
    enc = encoded[...].astype(F32)
    binned = (enc[:ROWS] + enc[ROWS:]) * 0.5
    mean = (mine[:, 0:1] + theirs[:, 0:1]) * (1.0 / (2 * encoded.shape[1]))
    out[...] = (binned * lax.rsqrt(mean + EPS) * gain[...]).astype(BF16)


def normalize(ids, encoded, mine, theirs, gain):
    half = encoded.shape[1]
    return pl.pallas_call(
        norm_kernel,
        grid_spec=pltpu.PrefetchScalarGridSpec(
            num_scalar_prefetch=1,
            grid=(1,),
            in_specs=[
                whole(encoded.shape),
                whole(mine.shape),
                whole(theirs.shape),
                pl.BlockSpec((1, half), lambda i, ids: (0, ids[0])),
            ],
            out_specs=whole((ROWS, half)),
        ),
        out_shape=shape((ROWS, half), BF16),
        compiler_params=params(),
        cost_estimate=cost(8 * ROWS * half, encoded.size * 2),
        name="normalize",
    )(ids, encoded, mine, theirs, gain)


def project_kernel(ids, mine, theirs, weight, queries, keyvals):
    half = mine.shape[1]
    near = pl.ds(pl.multiple_of(ids[0] * half, half), half)
    far = pl.ds(pl.multiple_of((1 - ids[0]) * half, half), half)
    rows = []
    for kind in range(3):
        both = dot(mine[...], weight[kind, near, :]) + dot(theirs[...], weight[kind, far, :])
        both = both.astype(BF16).astype(F32)
        rows.append((both, pltpu.roll(both, 2 * HEAD - 64, 1)))
    low = lax.broadcasted_iota(jnp.int32, (ROWS, 128), 1) < 64
    for head in range(2):
        query, key, value = (
            (r[0][:, :128], r[0][:, 128:256]) if head == 0 else (r[1][:, 128:256], r[1][:, 256:384])
            for r in rows
        )
        queries[head, :, :128] = query[0].astype(BF16)
        queries[head, :, 128:] = jnp.where(low, query[1], 0.0).astype(BF16)
        keyvals[head, :, :128] = key[0][:OWN].astype(BF16)
        keyvals[head, :, 128:256] = value[0][:OWN].astype(BF16)
        tail = jnp.where(low, key[1], pltpu.roll(value[1], 64, 1))
        keyvals[head, :, 256:] = tail[:OWN].astype(BF16)


def project(ids, mine, theirs, weight):
    feats = weight.shape[1]
    return pl.pallas_call(
        project_kernel,
        grid_spec=pltpu.PrefetchScalarGridSpec(
            num_scalar_prefetch=1,
            grid=(2,),
            in_specs=[
                whole(mine.shape),
                whole(theirs.shape),
                pl.BlockSpec((3, feats, 2 * HEAD), lambda i, ids: (0, 0, i)),
            ],
            out_specs=[
                pl.BlockSpec((2, ROWS, 256), lambda i, ids: (i, 0, 0)),
                pl.BlockSpec((2, OWN, 384), lambda i, ids: (i, 0, 0)),
            ],
        ),
        out_shape=[shape((4, ROWS, 256), BF16), shape((4, OWN, 384), BF16)],
        compiler_params=params(),
        cost_estimate=cost(2 * ROWS * weight.size, weight.size * 2),
        name="project",
    )(ids, mine, theirs, weight)


def attend_kernel(scale, q0, q1, q2, q3, k0, k1, k2, k3, o0, o1, o2, o3, inverse):
    chunk = k0.shape[0]
    lane = lax.broadcasted_iota(jnp.int32, (8, 256), 1)
    ones = (lane < HEAD).astype(F32).astype(BF16)
    pieces = (k0, k1, k2, k3)

    def keys(ref):
        return jnp.concatenate([ref[:, :128], ref[:, 256:]], axis=1)

    @pl.when(pl.program_id(0) == 0)
    def _():
        for at, ref in enumerate(pieces):
            key = keys(ref).astype(F32)
            square = key * key
            high = square.astype(BF16)
            rest = (square - high.astype(F32)).astype(BF16)
            total = dot_t(ones, high) + dot_t(ones, rest)
            inverse[:, at * chunk : (at + 1) * chunk] = lax.rsqrt(total * (1.0 / HEAD) + EPS)

    for query_ref, out in ((q0, o0), (q1, o1), (q2, o2), (q3, o3)):
        query = query_ref[...]
        wide = query.astype(F32)
        own = lax.rsqrt(jnp.sum(wide * wide, axis=1, keepdims=True) * (1.0 / HEAD) + EPS)
        factor = own * (scale[0] * (1.0 / HEAD))
        scores = []
        peak = None
        for at, ref in enumerate(pieces):
            part = dot_t(query, keys(ref)) * factor
            part = part * inverse[0:1, at * chunk : (at + 1) * chunk]
            top = jnp.max(part, axis=1, keepdims=True)
            peak = top if peak is None else jnp.maximum(peak, top)
            scores.append(part)
        total, mixed = None, None
        for part, ref in zip(scores, pieces):
            exps = jnp.exp(part - peak)
            count = jnp.sum(exps, axis=1, keepdims=True)
            values = jnp.concatenate([ref[:, 128:256], ref[:, 256:]], axis=1)
            term = dot(exps.astype(BF16), values)
            total = count if total is None else total + count
            mixed = term if mixed is None else mixed + term
        mixed = mixed / total
        weight = peak + jnp.log(total)
        high = weight.astype(BF16).astype(F32)
        rest = weight - high
        mid = rest.astype(BF16).astype(F32)
        place = lax.broadcasted_iota(jnp.int32, mixed.shape, 1)
        mixed = jnp.where(place == 128, high, mixed)
        mixed = jnp.where(place == 129, mid, mixed)
        mixed = jnp.where(place == 130, rest - mid, mixed)
        out[...] = mixed.astype(BF16)


def attend(scale, queries, keyvals):
    rows = queries[0].shape[0]
    block = rows // 2
    keys = 4 * keyvals[0].shape[0]
    return pl.pallas_call(
        attend_kernel,
        grid=(2,),
        in_specs=[pl.BlockSpec(memory_space=pltpu.SMEM)]
        + [pl.BlockSpec((block, 256), lambda i: (i, 0))] * 4
        + [whole(keyvals[0].shape)] * 4,
        out_specs=[pl.BlockSpec((block, 256), lambda i: (i, 0))] * 4,
        out_shape=[shape((rows, 256), BF16)] * 4,
        scratch_shapes=[pltpu.VMEM((8, keys), F32)],
        compiler_params=params(),
        cost_estimate=cost(4 * 4 * rows * keys * 256, 4 * (rows + 512) * 1024),
        name="attend",
    )(scale, *queries, *keyvals)


def merge_kernel(a0, a1, a2, a3, out):
    parts = [ref[...].astype(F32) for ref in (a0, a1, a2, a3)]
    logs = [p[:, 128:129] + p[:, 129:130] + p[:, 130:131] for p in parts]
    peak = functools.reduce(jnp.maximum, logs)
    shares = [jnp.exp(log - peak) for log in logs]
    total = sum(shares)
    mixed = sum(p * (share / total) for p, share in zip(parts, shares))
    out[:, :128] = mixed[:, :128].astype(BF16)
    out[:, 128:] = pltpu.roll(mixed[:, 128:], 64, 1).astype(BF16)


def merge(parts):
    return pl.pallas_call(
        merge_kernel,
        out_shape=shape(parts[0].shape, BF16),
        compiler_params=params(),
        cost_estimate=cost(20 * parts[0].size, 10 * parts[0].size),
        name="merge",
    )(*parts)


def output_kernel(ids, a0, a1, a2, a3, weight, out):
    total = None
    for distance, ref in enumerate((a0, a1, a2, a3)):
        head = lax.rem(ids[1] + distance, 4)
        rows = weight[pl.ds(pl.multiple_of(head * HEAD, HEAD), HEAD), :]
        term = dot(ref[:, :HEAD], rows)
        total = term if total is None else total + term
    out[...] = total.astype(out.dtype)


def output(ids, parts, weight, mine, dtype):
    half = weight.shape[1] // 2
    return pl.pallas_call(
        output_kernel,
        grid_spec=pltpu.PrefetchScalarGridSpec(
            num_scalar_prefetch=1,
            grid=(half // TILE,),
            in_specs=[whole(parts[0].shape)] * 4
            + [
                pl.BlockSpec(
                    (weight.shape[0], TILE),
                    lambda i, ids: (0, 3 * (ids[0] if mine else 1 - ids[0]) + i),
                )
            ],
            out_specs=pl.BlockSpec((ROWS, TILE), lambda i, ids: (0, i)),
        ),
        out_shape=shape((ROWS, half), dtype),
        compiler_params=params(),
        cost_estimate=cost(2 * ROWS * weight.size // 2, weight.size),
        name="output",
    )(ids, *parts, weight)


def decode_send_kernel(ids, own, other, encoded, weight, inputs, out):
    @pl.when(pl.program_id(0) == 0)
    def _():
        enc = encoded[...].astype(F32)
        even, odd = enc[:ROWS], enc[ROWS:]
        binned = (even + odd) * 0.5
        block = (binned + (own[...] + other[...].astype(F32))).astype(BF16).astype(F32)
        row = lax.broadcasted_iota(jnp.int32, block.shape, 0)
        outside = ((ids[2] == 0) & (row == ROWS - 1)) | ((ids[2] == 63) & (row == OWN))
        even = jnp.where(outside, 0.0, block + even)
        odd = jnp.where(outside, 0.0, block + odd)
        inputs[...] = jnp.concatenate([even, odd], axis=0).astype(BF16)

    even, odd = conv_taps(inputs[...], lambda t: weight[t])
    out[...] = jnp.concatenate([even, odd], axis=0).astype(BF16)


def decode_send(ids, own, other, encoded, weight):
    half = weight.shape[1]
    return pl.pallas_call(
        decode_send_kernel,
        grid_spec=pltpu.PrefetchScalarGridSpec(
            num_scalar_prefetch=1,
            grid=(half // TILE,),
            in_specs=[
                whole(own.shape),
                whole(other.shape),
                whole(encoded.shape),
                pl.BlockSpec((3, half, TILE), lambda i, ids: (0, 0, 3 * (1 - ids[0]) + i)),
            ],
            out_specs=[
                whole((2 * ROWS, half)),
                pl.BlockSpec((2 * ROWS, TILE), lambda i, ids: (0, i)),
            ],
        ),
        out_shape=[shape((2 * ROWS, half), BF16)] * 2,
        compiler_params=params(),
        cost_estimate=cost(2 * 2 * ROWS * weight.size // 2, weight.size),
        name="decode_send",
    )(ids, own, other, encoded, weight)


def decode_own_kernel(ids, inputs, weight, out):
    even, odd = conv_taps(inputs[...], lambda t: weight[t])
    out[...] = jnp.concatenate([even, odd], axis=0)


def decode_own(ids, inputs, weight):
    half = weight.shape[1]
    return pl.pallas_call(
        decode_own_kernel,
        grid_spec=pltpu.PrefetchScalarGridSpec(
            num_scalar_prefetch=1,
            grid=(half // TILE,),
            in_specs=[
                whole(inputs.shape),
                pl.BlockSpec((3, half, TILE), lambda i, ids: (0, 0, 3 * ids[0] + i)),
            ],
            out_specs=pl.BlockSpec((2 * ROWS, TILE), lambda i, ids: (0, i)),
        ),
        out_shape=shape((2 * ROWS, half), F32),
        compiler_params=params(),
        cost_estimate=cost(2 * 2 * ROWS * weight.size // 2, weight.size),
        name="decode_own",
    )(ids, inputs, weight)


def slope_kernel(ids, own, other, inputs, grad, edges, decoded, slope, paired, wide):
    pre = own[...] + other[...].astype(F32)
    _, tanh = gelu_parts(pre)
    result = inputs[...].astype(F32) + 0.5 * pre * (1.0 + tanh)
    halves = (slice(0, 128), slice(128, TILE))
    for lanes in halves:
        wide[pl.ds(0, OWN, 2), :] = result[:OWN, lanes]
        wide[pl.ds(1, OWN, 2), :] = result[ROWS : ROWS + OWN, lanes]
        decoded[:, lanes] = wide[...].astype(BF16)
    slant = 0.5 * (1.0 + tanh) + (0.5 * 0.7978845608028654) * pre * (1.0 - tanh * tanh) * (
        1.0 + (3 * 0.044715) * (pre * pre)
    )
    evens, odds = [], []
    for lanes in halves:
        wide[...] = grad[:, lanes].astype(F32)
        evens.append(wide[pl.ds(0, OWN, 2), :])
        odds.append(wide[pl.ds(1, OWN, 2), :])
    even = jnp.concatenate(evens, axis=1)
    odd = jnp.concatenate(odds, axis=1)
    paired[...] = even + odd
    edge = edges[...].astype(F32)
    row = lax.broadcasted_iota(jnp.int32, (ROWS - OWN, even.shape[1]), 0)
    even_edge = jnp.where(row == 0, edge[1:2], 0.0)
    odd_edge = jnp.where(row == ROWS - OWN - 1, edge[0:1], 0.0)
    cotangent = jnp.concatenate([even, even_edge, odd, odd_edge], axis=0)
    slope[...] = (cotangent * slant).astype(BF16)


def slopes(ids, own, other, inputs, grad, edges):
    half = own.shape[1]

    def tile(rows):
        return pl.BlockSpec((rows, TILE), lambda i, ids: (0, i))

    def mine(rows):
        return pl.BlockSpec((rows, TILE), lambda i, ids: (0, 3 * ids[0] + i))

    return pl.pallas_call(
        slope_kernel,
        grid_spec=pltpu.PrefetchScalarGridSpec(
            num_scalar_prefetch=1,
            grid=(half // TILE,),
            in_specs=[tile(2 * ROWS)] * 3 + [mine(2 * OWN), mine(8)],
            out_specs=[tile(2 * OWN), tile(2 * ROWS), tile(OWN)],
            scratch_shapes=[pltpu.VMEM((2 * OWN, 128), F32)],
        ),
        out_shape=[
            shape((2 * OWN, half), BF16),
            shape((2 * ROWS, half), BF16),
            shape((OWN, half), F32),
        ],
        compiler_params=params(),
        cost_estimate=cost(30 * own.size, 14 * own.size),
        name="slopes",
    )(ids, own, other, inputs, grad, edges)


def backward_kernel(ids, slope, start, weight, out, level, lower, upper):
    step = pl.program_id(0)
    first, mid, last = (dot_t(slope[...], weight[t]) for t in range(3))
    flat = first[ROWS:] + mid[:ROWS] + mid[ROWS:] + last[:ROWS]

    @pl.when(step == 0)
    def _():
        level[...] = flat
        lower[...] = first[:ROWS]
        upper[...] = last[ROWS:]

    @pl.when(step > 0)
    def _():
        level[...] += flat
        lower[...] += first[:ROWS]
        upper[...] += last[ROWS:]

    @pl.when(step == pl.num_programs(0) - 1)
    def _():
        total = level[...] + below(lower[...]) + above(upper[...])
        out[...] = (start[...] + total[:OWN]).astype(out.dtype)


def backward(ids, slope, start, weight, mine, dtype):
    half = weight.shape[1]
    return pl.pallas_call(
        backward_kernel,
        grid_spec=pltpu.PrefetchScalarGridSpec(
            num_scalar_prefetch=1,
            grid=(half // TILE,),
            in_specs=[
                pl.BlockSpec((2 * ROWS, TILE), lambda i, ids: (0, i)),
                whole(start.shape),
                pl.BlockSpec(
                    (3, half, TILE),
                    lambda i, ids: (0, 0, 3 * (ids[0] if mine else 1 - ids[0]) + i),
                ),
            ],
            out_specs=whole((OWN, half)),
            scratch_shapes=[pltpu.VMEM((ROWS, half), F32)] * 3,
        ),
        out_shape=shape((OWN, half), dtype),
        compiler_params=params(),
        cost_estimate=cost(2 * 2 * ROWS * weight.size // 2, weight.size),
        name="backward",
    )(ids, slope, start, weight)


def place(at):
    return at // 16, at // 4 % 4, at // 2 % 2, at % 2


def moves(dx=0, dz=0, dy=0, dc=0):
    pairs = []
    for at in range(64):
        x, z, y, c = place(at)
        pairs.append((at, (x + dx) % 4 * 16 + (z + dz) % 4 * 4 + (y ^ dy) * 2 + (c ^ dc)))
    return pairs


def swap(value):
    return lax.ppermute(value, "head", [(0, 1), (1, 0)])


def send(value, **step):
    return lax.ppermute(value, "seq", moves(**step))


def per_device(
    dna_bases,
    stem_weight,
    encoder_weight,
    norm_gain,
    attention_weight,
    logit_scale,
    out_weight,
    decoder_weight,
    grad_out,
):
    at = lax.axis_index("seq")
    x = at // 16
    ids = jnp.stack([lax.axis_index("head"), x, at]).astype(jnp.int32)

    codes = (dna_bases + 1).astype(BF16).reshape(OWN, 128)
    forward = [(i, i + 1) for i in range(63)]
    backwards = [(i + 1, i) for i in range(63)]
    feats = grad_out.shape[1]
    last = jnp.concatenate([codes[-2:].reshape(1, 256), grad_out[-1:]], axis=1)
    first = jnp.concatenate([codes[:2].reshape(1, 256), grad_out[:1]], axis=1)
    before = lax.ppermute(last, "seq", forward)
    after = lax.ppermute(first, "seq", backwards)
    gap = jnp.zeros((ROWS - OWN - 4, 128), BF16)
    ring = jnp.concatenate(
        [codes, after[:, :256].reshape(2, 128), gap, before[:, :256].reshape(2, 128)], axis=0
    )
    edges = jnp.concatenate(
        [before[:, 256:], after[:, 256:], jnp.zeros((6, feats), BF16)], axis=0
    )

    encoded, squares = encode(ids, ring, stem_weight, encoder_weight)
    normed = normalize(ids, encoded, squares, swap(squares), norm_gain.reshape(1, feats))
    queries, keyvals = project(ids, normed, swap(normed), attention_weight)

    def pick(stack, distance):
        return lax.dynamic_index_in_dim(stack, (x + distance) % 4, 0, keepdims=False)

    def regroup(stack):
        return jnp.concatenate(
            [pick(stack, 0)] + [send(pick(stack, d), dx=d) for d in (1, 3, 2)], axis=0
        )

    keyvals = regroup(keyvals)
    queries = regroup(queries)
    turns = ({"dc": 1}, {"dy": 1}, {"dy": 1, "dc": 1})
    all_keys = [keyvals] + [send(keyvals, dz=d) for d in (1, 3, 2)]
    all_queries = [queries] + [send(queries, **turn) for turn in turns]
    scale = lax.dynamic_slice_in_dim(logit_scale, x, 1)
    parts = attend(scale, all_queries, all_keys)
    mixed = merge([parts[0]] + [send(part, **turn) for part, turn in zip(parts[1:], turns)])
    mixed = mixed.reshape(4, ROWS, 256)
    back = [send(mixed[i], dx=-d) for i, d in ((1, 1), (2, 3), (3, 2))]
    heads = [mixed[0], back[0], back[2], back[1]]

    sent = swap(output(ids, heads, out_weight, False, BF16))
    kept = output(ids, heads, out_weight, True, F32)
    inputs, sent = decode_send(ids, kept, sent, encoded, decoder_weight)
    sent = swap(sent)
    kept = decode_own(ids, inputs, decoder_weight)
    decoded, slope, paired = slopes(ids, kept, sent, inputs, grad_out, edges)
    sent = swap(slope)
    partial = backward(ids, slope, paired, decoder_weight, True, F32)
    bins_grad = backward(ids, sent, partial, decoder_weight, False, BF16)
    return decoded, bins_grad


def solution(mesh):
    in_specs = (
        P("seq"),
        P(),
        P(None, None, "head"),
        P(),
        P(None, None, "head"),
        P("head"),
        P("head", None),
        P(None, "head", None),
        P("seq", None),
    )
    out_specs = (P("seq", "head"), P("seq", "head"))
    return jax.shard_map(
        per_device, mesh=mesh, in_specs=in_specs, out_specs=out_specs, check_vma=False
    )
```

```python
import functools

import jax
import jax.numpy as jnp
from jax import lax
from jax.experimental import pallas as pl
from jax.experimental.pallas import tpu as pltpu
from jax.sharding import PartitionSpec as P

BF16 = jnp.bfloat16
F32 = jnp.float32
ROWS = 136
OWN = 128
TILE = 256
HEAD = 192
EPS = 1e-06
MIB = 1024 * 1024


def params(mib):
    return pltpu.CompilerParams(vmem_limit_bytes=mib * MIB)


def dot(a, b):
    return jnp.dot(a, b, preferred_element_type=F32)


def dot_t(a, b):
    return lax.dot_general(a, b, (((1,), (1,)), ((), ())), preferred_element_type=F32)


def cost(flops, nbytes):
    return pl.CostEstimate(flops=int(flops), bytes_accessed=int(nbytes), transcendentals=0)


def shape(dims, dtype):
    return jax.ShapeDtypeStruct(dims, dtype)


def whole(dims):
    return pl.BlockSpec(dims, lambda *_: (0,) * len(dims))


def above(rows):
    return pltpu.roll(rows, 1, 0)


def below(rows):
    return pltpu.roll(rows, ROWS - 1, 0)


def gelu_parts(x):
    inner = 0.7978845608028654 * (x + 0.044715 * (x * x * x))
    return inner, jnp.tanh(inner)


def conv_taps(rows, weight):
    first, mid, last = (dot(rows, weight(t)) for t in range(3))
    even = above(first[ROWS:]) + mid[:ROWS] + last[ROWS:]
    odd = first[:ROWS] + mid[ROWS:] + below(last[:ROWS])
    return even, odd


def encoder_kernel(ids, codes, stem, weight, encoded, squares, embedded):
    step = pl.program_id(0)

    @pl.when(step == 0)
    def _():
        patch = stem.shape[0] // 4
        row = lax.broadcasted_iota(jnp.int32, (2 * patch, 4 * patch), 0)
        col = lax.broadcasted_iota(jnp.int32, (2 * patch, 4 * patch), 1)
        code = codes[...]
        spread = [
            dot(code, (row == col // 4 + offset).astype(F32).astype(BF16))
            for offset in (0, patch)
        ]
        spread = jnp.concatenate(spread, axis=0)
        base = lax.broadcasted_iota(jnp.int32, spread.shape, 1) % 4 + 1
        onehot = (spread == base.astype(F32)).astype(F32).astype(BF16)
        embedded[...] = dot(onehot, stem[...]).astype(BF16)
        squares[...] = jnp.zeros_like(squares)

    even, odd = conv_taps(embedded[...], lambda t: weight[t])
    column = ids[0] * (3 * TILE) + step * TILE
    mine = embedded[:, pl.ds(pl.multiple_of(column, TILE), TILE)].astype(F32)
    pre = jnp.concatenate([even, odd], axis=0)
    _, tanh = gelu_parts(pre)
    out = (mine + 0.5 * pre * (1.0 + tanh)).astype(BF16)
    encoded[...] = out
    out = out.astype(F32)
    binned = (out[:ROWS] + out[ROWS:]) * 0.5
    squares[...] += jnp.broadcast_to(
        jnp.sum(binned * binned, axis=1, keepdims=True), squares.shape
    )


def encode(ids, codes, stem, weight):
    half = weight.shape[2]
    feats = stem.shape[1]
    return pl.pallas_call(
        encoder_kernel,
        grid_spec=pltpu.PrefetchScalarGridSpec(
            num_scalar_prefetch=1,
            grid=(half // TILE,),
            in_specs=[
                whole(codes.shape),
                whole(stem.shape),
                pl.BlockSpec((3, feats, TILE), lambda i, ids: (0, 0, i)),
            ],
            out_specs=[
                pl.BlockSpec((2 * ROWS, TILE), lambda i, ids: (0, i)),
                whole((ROWS, 128)),
            ],
            scratch_shapes=[pltpu.VMEM((2 * ROWS, feats), BF16)],
        ),
        out_shape=[shape((2 * ROWS, half), BF16), shape((ROWS, 128), F32)],
        compiler_params=params(16),
        cost_estimate=cost(2 * 2 * ROWS * 3 * feats * half, weight.size * 2),
        name="encode",
    )(ids, codes, stem, weight)


def norm_kernel(ids, encoded, mine, theirs, gain, out):
    enc = encoded[...].astype(F32)
    binned = (enc[:ROWS] + enc[ROWS:]) * 0.5
    mean = (mine[:, 0:1] + theirs[:, 0:1]) * (1.0 / (2 * encoded.shape[1]))
    out[...] = (binned * lax.rsqrt(mean + EPS) * gain[...]).astype(BF16)


def normalize(ids, encoded, mine, theirs, gain):
    half = encoded.shape[1]
    return pl.pallas_call(
        norm_kernel,
        grid_spec=pltpu.PrefetchScalarGridSpec(
            num_scalar_prefetch=1,
            grid=(1,),
            in_specs=[
                whole(encoded.shape),
                whole(mine.shape),
                whole(theirs.shape),
                pl.BlockSpec((1, half), lambda i, ids: (0, ids[0])),
            ],
            out_specs=whole((ROWS, half)),
        ),
        out_shape=shape((ROWS, half), BF16),
        compiler_params=params(4),
        cost_estimate=cost(8 * ROWS * half, encoded.size * 2),
        name="normalize",
    )(ids, encoded, mine, theirs, gain)


def project_kernel(ids, mine, theirs, weight, queries, keyvals):
    half = mine.shape[1]
    near = pl.ds(pl.multiple_of(ids[0] * half, half), half)
    far = pl.ds(pl.multiple_of((1 - ids[0]) * half, half), half)
    rows = []
    for kind in range(3):
        both = dot(mine[...], weight[kind, near, :]) + dot(theirs[...], weight[kind, far, :])
        both = both.astype(BF16).astype(F32)
        rows.append((both, pltpu.roll(both, 2 * HEAD - 64, 1)))
    low = lax.broadcasted_iota(jnp.int32, (ROWS, 128), 1) < 64
    for head in range(2):
        query, key, value = (
            (r[0][:, :128], r[0][:, 128:256]) if head == 0 else (r[1][:, 128:256], r[1][:, 256:384])
            for r in rows
        )
        queries[head, :, :128] = query[0].astype(BF16)
        queries[head, :, 128:] = jnp.where(low, query[1], 0.0).astype(BF16)
        keyvals[head, :, :128] = key[0][:OWN].astype(BF16)
        keyvals[head, :, 128:256] = value[0][:OWN].astype(BF16)
        tail = jnp.where(low, key[1], pltpu.roll(value[1], 64, 1))
        keyvals[head, :, 256:] = tail[:OWN].astype(BF16)


def project(ids, mine, theirs, weight):
    feats = weight.shape[1]
    return pl.pallas_call(
        project_kernel,
        grid_spec=pltpu.PrefetchScalarGridSpec(
            num_scalar_prefetch=1,
            grid=(2,),
            in_specs=[
                whole(mine.shape),
                whole(theirs.shape),
                pl.BlockSpec((3, feats, 2 * HEAD), lambda i, ids: (0, 0, i)),
            ],
            out_specs=[
                pl.BlockSpec((2, ROWS, 256), lambda i, ids: (i, 0, 0)),
                pl.BlockSpec((2, OWN, 384), lambda i, ids: (i, 0, 0)),
            ],
        ),
        out_shape=[shape((4, ROWS, 256), BF16), shape((4, OWN, 384), BF16)],
        compiler_params=params(12),
        cost_estimate=cost(2 * ROWS * weight.size, weight.size * 2),
        name="project",
    )(ids, mine, theirs, weight)


def attend_kernel(scale, q0, q1, q2, q3, k0, k1, k2, k3, o0, o1, o2, o3, inverse):
    chunk = k0.shape[0]
    lane = lax.broadcasted_iota(jnp.int32, (8, 256), 1)
    ones = (lane < HEAD).astype(F32).astype(BF16)
    pieces = (k0, k1, k2, k3)

    def keys(ref):
        return jnp.concatenate([ref[:, :128], ref[:, 256:]], axis=1)

    @pl.when(pl.program_id(0) == 0)
    def _():
        for at, ref in enumerate(pieces):
            key = keys(ref).astype(F32)
            square = key * key
            high = square.astype(BF16)
            rest = (square - high.astype(F32)).astype(BF16)
            total = dot_t(ones, high) + dot_t(ones, rest)
            inverse[:, at * chunk : (at + 1) * chunk] = lax.rsqrt(total * (1.0 / HEAD) + EPS)

    for query_ref, out in ((q0, o0), (q1, o1), (q2, o2), (q3, o3)):
        query = query_ref[...]
        wide = query.astype(F32)
        own = lax.rsqrt(jnp.sum(wide * wide, axis=1, keepdims=True) * (1.0 / HEAD) + EPS)
        factor = own * (scale[0] * (1.0 / HEAD))
        scores = []
        peak = None
        for at, ref in enumerate(pieces):
            part = dot_t(query, keys(ref)) * factor
            part = part * inverse[0:1, at * chunk : (at + 1) * chunk]
            top = jnp.max(part, axis=1, keepdims=True)
            peak = top if peak is None else jnp.maximum(peak, top)
            scores.append(part)
        total, mixed = None, None
        for part, ref in zip(scores, pieces):
            exps = jnp.exp(part - peak)
            count = jnp.sum(exps, axis=1, keepdims=True)
            values = jnp.concatenate([ref[:, 128:256], ref[:, 256:]], axis=1)
            term = dot(exps.astype(BF16), values)
            total = count if total is None else total + count
            mixed = term if mixed is None else mixed + term
        mixed = mixed / total
        weight = peak + jnp.log(total)
        high = weight.astype(BF16).astype(F32)
        rest = weight - high
        mid = rest.astype(BF16).astype(F32)
        place = lax.broadcasted_iota(jnp.int32, mixed.shape, 1)
        mixed = jnp.where(place == 128, high, mixed)
        mixed = jnp.where(place == 129, mid, mixed)
        mixed = jnp.where(place == 130, rest - mid, mixed)
        out[...] = mixed.astype(BF16)


def attend(scale, queries, keyvals):
    rows = queries[0].shape[0]
    block = rows // 2
    keys = 4 * keyvals[0].shape[0]
    return pl.pallas_call(
        attend_kernel,
        grid=(2,),
        in_specs=[pl.BlockSpec(memory_space=pltpu.SMEM)]
        + [pl.BlockSpec((block, 256), lambda i: (i, 0))] * 4
        + [whole(keyvals[0].shape)] * 4,
        out_specs=[pl.BlockSpec((block, 256), lambda i: (i, 0))] * 4,
        out_shape=[shape((rows, 256), BF16)] * 4,
        scratch_shapes=[pltpu.VMEM((8, keys), F32)],
        compiler_params=params(24),
        cost_estimate=cost(4 * 4 * rows * keys * 256, 4 * (rows + 512) * 1024),
        name="attend",
    )(scale, *queries, *keyvals)


def merge_kernel(a0, a1, a2, a3, out):
    parts = [ref[...].astype(F32) for ref in (a0, a1, a2, a3)]
    logs = [p[:, 128:129] + p[:, 129:130] + p[:, 130:131] for p in parts]
    peak = functools.reduce(jnp.maximum, logs)
    shares = [jnp.exp(log - peak) for log in logs]
    total = sum(shares)
    mixed = sum(p * (share / total) for p, share in zip(parts, shares))
    out[:, :128] = mixed[:, :128].astype(BF16)
    out[:, 128:] = pltpu.roll(mixed[:, 128:], 64, 1).astype(BF16)


def merge(parts):
    return pl.pallas_call(
        merge_kernel,
        out_shape=shape(parts[0].shape, BF16),
        compiler_params=params(8),
        cost_estimate=cost(20 * parts[0].size, 10 * parts[0].size),
        name="merge",
    )(*parts)


def output_kernel(ids, a0, a1, a2, a3, weight, out):
    total = None
    for distance, ref in enumerate((a0, a1, a2, a3)):
        head = lax.rem(ids[1] + distance, 4)
        rows = weight[pl.ds(pl.multiple_of(head * HEAD, HEAD), HEAD), :]
        term = dot(ref[:, :HEAD], rows)
        total = term if total is None else total + term
    out[...] = total.astype(out.dtype)


def output(ids, parts, weight, mine, dtype):
    half = weight.shape[1] // 2
    return pl.pallas_call(
        output_kernel,
        grid_spec=pltpu.PrefetchScalarGridSpec(
            num_scalar_prefetch=1,
            grid=(half // TILE,),
            in_specs=[whole(parts[0].shape)] * 4
            + [
                pl.BlockSpec(
                    (weight.shape[0], TILE),
                    lambda i, ids: (0, 3 * (ids[0] if mine else 1 - ids[0]) + i),
                )
            ],
            out_specs=pl.BlockSpec((ROWS, TILE), lambda i, ids: (0, i)),
        ),
        out_shape=shape((ROWS, half), dtype),
        compiler_params=params(6),
        cost_estimate=cost(2 * ROWS * weight.size // 2, weight.size),
        name="output",
    )(ids, *parts, weight)


def decode_send_kernel(ids, own, other, encoded, weight, inputs, out):
    @pl.when(pl.program_id(0) == 0)
    def _():
        enc = encoded[...].astype(F32)
        even, odd = enc[:ROWS], enc[ROWS:]
        binned = (even + odd) * 0.5
        block = (binned + (own[...] + other[...].astype(F32))).astype(BF16).astype(F32)
        row = lax.broadcasted_iota(jnp.int32, block.shape, 0)
        outside = ((ids[2] == 0) & (row == ROWS - 1)) | ((ids[2] == 63) & (row == OWN))
        even = jnp.where(outside, 0.0, block + even)
        odd = jnp.where(outside, 0.0, block + odd)
        inputs[...] = jnp.concatenate([even, odd], axis=0).astype(BF16)

    even, odd = conv_taps(inputs[...], lambda t: weight[t])
    out[...] = jnp.concatenate([even, odd], axis=0).astype(BF16)


def decode_send(ids, own, other, encoded, weight):
    half = weight.shape[1]
    return pl.pallas_call(
        decode_send_kernel,
        grid_spec=pltpu.PrefetchScalarGridSpec(
            num_scalar_prefetch=1,
            grid=(half // TILE,),
            in_specs=[
                whole(own.shape),
                whole(other.shape),
                whole(encoded.shape),
                pl.BlockSpec((3, half, TILE), lambda i, ids: (0, 0, 3 * (1 - ids[0]) + i)),
            ],
            out_specs=[
                whole((2 * ROWS, half)),
                pl.BlockSpec((2 * ROWS, TILE), lambda i, ids: (0, i)),
            ],
        ),
        out_shape=[shape((2 * ROWS, half), BF16)] * 2,
        compiler_params=params(8),
        cost_estimate=cost(2 * 2 * ROWS * weight.size // 2, weight.size),
        name="decode_send",
    )(ids, own, other, encoded, weight)


def decode_own_kernel(ids, inputs, weight, out):
    even, odd = conv_taps(inputs[...], lambda t: weight[t])
    out[...] = jnp.concatenate([even, odd], axis=0)


def decode_own(ids, inputs, weight):
    half = weight.shape[1]
    return pl.pallas_call(
        decode_own_kernel,
        grid_spec=pltpu.PrefetchScalarGridSpec(
            num_scalar_prefetch=1,
            grid=(half // TILE,),
            in_specs=[
                whole(inputs.shape),
                pl.BlockSpec((3, half, TILE), lambda i, ids: (0, 0, 3 * ids[0] + i)),
            ],
            out_specs=pl.BlockSpec((2 * ROWS, TILE), lambda i, ids: (0, i)),
        ),
        out_shape=shape((2 * ROWS, half), F32),
        compiler_params=params(8),
        cost_estimate=cost(2 * 2 * ROWS * weight.size // 2, weight.size),
        name="decode_own",
    )(ids, inputs, weight)


def slope_kernel(ids, own, other, inputs, grad, edges, decoded, slope, paired, wide):
    pre = own[...] + other[...].astype(F32)
    _, tanh = gelu_parts(pre)
    result = inputs[...].astype(F32) + 0.5 * pre * (1.0 + tanh)
    halves = (slice(0, 128), slice(128, TILE))
    for lanes in halves:
        wide[pl.ds(0, OWN, 2), :] = result[:OWN, lanes]
        wide[pl.ds(1, OWN, 2), :] = result[ROWS : ROWS + OWN, lanes]
        decoded[:, lanes] = wide[...].astype(BF16)
    slant = 0.5 * (1.0 + tanh) + (0.5 * 0.7978845608028654) * pre * (1.0 - tanh * tanh) * (
        1.0 + (3 * 0.044715) * (pre * pre)
    )
    evens, odds = [], []
    for lanes in halves:
        wide[...] = grad[:, lanes].astype(F32)
        evens.append(wide[pl.ds(0, OWN, 2), :])
        odds.append(wide[pl.ds(1, OWN, 2), :])
    even = jnp.concatenate(evens, axis=1)
    odd = jnp.concatenate(odds, axis=1)
    paired[...] = even + odd
    edge = edges[...].astype(F32)
    row = lax.broadcasted_iota(jnp.int32, (ROWS - OWN, even.shape[1]), 0)
    even_edge = jnp.where(row == 0, edge[1:2], 0.0)
    odd_edge = jnp.where(row == ROWS - OWN - 1, edge[0:1], 0.0)
    cotangent = jnp.concatenate([even, even_edge, odd, odd_edge], axis=0)
    slope[...] = (cotangent * slant).astype(BF16)


def slopes(ids, own, other, inputs, grad, edges):
    half = own.shape[1]

    def tile(rows):
        return pl.BlockSpec((rows, TILE), lambda i, ids: (0, i))

    def mine(rows):
        return pl.BlockSpec((rows, TILE), lambda i, ids: (0, 3 * ids[0] + i))

    return pl.pallas_call(
        slope_kernel,
        grid_spec=pltpu.PrefetchScalarGridSpec(
            num_scalar_prefetch=1,
            grid=(half // TILE,),
            in_specs=[tile(2 * ROWS)] * 3 + [mine(2 * OWN), mine(8)],
            out_specs=[tile(2 * OWN), tile(2 * ROWS), tile(OWN)],
            scratch_shapes=[pltpu.VMEM((2 * OWN, 128), F32)],
        ),
        out_shape=[
            shape((2 * OWN, half), BF16),
            shape((2 * ROWS, half), BF16),
            shape((OWN, half), F32),
        ],
        compiler_params=params(6),
        cost_estimate=cost(30 * own.size, 14 * own.size),
        name="slopes",
    )(ids, own, other, inputs, grad, edges)


def backward_kernel(ids, slope, start, weight, out, level, lower, upper):
    step = pl.program_id(0)
    first, mid, last = (dot_t(slope[...], weight[t]) for t in range(3))
    flat = first[ROWS:] + mid[:ROWS] + mid[ROWS:] + last[:ROWS]

    @pl.when(step == 0)
    def _():
        level[...] = flat
        lower[...] = first[:ROWS]
        upper[...] = last[ROWS:]

    @pl.when(step > 0)
    def _():
        level[...] += flat
        lower[...] += first[:ROWS]
        upper[...] += last[ROWS:]

    @pl.when(step == pl.num_programs(0) - 1)
    def _():
        total = level[...] + below(lower[...]) + above(upper[...])
        out[...] = (start[...] + total[:OWN]).astype(out.dtype)


def backward(ids, slope, start, weight, mine, dtype):
    half = weight.shape[1]
    return pl.pallas_call(
        backward_kernel,
        grid_spec=pltpu.PrefetchScalarGridSpec(
            num_scalar_prefetch=1,
            grid=(half // TILE,),
            in_specs=[
                pl.BlockSpec((2 * ROWS, TILE), lambda i, ids: (0, i)),
                whole(start.shape),
                pl.BlockSpec(
                    (3, half, TILE),
                    lambda i, ids: (0, 0, 3 * (ids[0] if mine else 1 - ids[0]) + i),
                ),
            ],
            out_specs=whole((OWN, half)),
            scratch_shapes=[pltpu.VMEM((ROWS, half), F32)] * 3,
        ),
        out_shape=shape((OWN, half), dtype),
        compiler_params=params(10),
        cost_estimate=cost(2 * 2 * ROWS * weight.size // 2, weight.size),
        name="backward",
    )(ids, slope, start, weight)


def place(at):
    return at // 16, at // 4 % 4, at // 2 % 2, at % 2


def moves(dx=0, dz=0, dy=0, dc=0):
    pairs = []
    for at in range(64):
        x, z, y, c = place(at)
        pairs.append((at, (x + dx) % 4 * 16 + (z + dz) % 4 * 4 + (y ^ dy) * 2 + (c ^ dc)))
    return pairs


def swap(value):
    return lax.ppermute(value, "head", [(0, 1), (1, 0)])


def send(value, **step):
    return lax.ppermute(value, "seq", moves(**step))


def per_device(
    dna_bases,
    stem_weight,
    encoder_weight,
    norm_gain,
    attention_weight,
    logit_scale,
    out_weight,
    decoder_weight,
    grad_out,
):
    at = lax.axis_index("seq")
    x = at // 16
    ids = jnp.stack([lax.axis_index("head"), x, at]).astype(jnp.int32)

    codes = (dna_bases + 1).astype(BF16).reshape(OWN, 128)
    forward = [(i, i + 1) for i in range(63)]
    backwards = [(i + 1, i) for i in range(63)]
    feats = grad_out.shape[1]
    last = jnp.concatenate([codes[-2:].reshape(1, 256), grad_out[-1:]], axis=1)
    first = jnp.concatenate([codes[:2].reshape(1, 256), grad_out[:1]], axis=1)
    before = lax.ppermute(last, "seq", forward)
    after = lax.ppermute(first, "seq", backwards)
    gap = jnp.zeros((ROWS - OWN - 4, 128), BF16)
    ring = jnp.concatenate(
        [codes, after[:, :256].reshape(2, 128), gap, before[:, :256].reshape(2, 128)], axis=0
    )
    edges = jnp.concatenate(
        [before[:, 256:], after[:, 256:], jnp.zeros((6, feats), BF16)], axis=0
    )

    encoded, squares = encode(ids, ring, stem_weight, encoder_weight)
    normed = normalize(ids, encoded, squares, swap(squares), norm_gain.reshape(1, feats))
    queries, keyvals = project(ids, normed, swap(normed), attention_weight)

    def pick(stack, distance):
        return lax.dynamic_index_in_dim(stack, (x + distance) % 4, 0, keepdims=False)

    def regroup(stack):
        return jnp.concatenate(
            [pick(stack, 0)] + [send(pick(stack, d), dx=d) for d in (1, 3, 2)], axis=0
        )

    keyvals = regroup(keyvals)
    queries = regroup(queries)
    turns = ({"dc": 1}, {"dy": 1}, {"dy": 1, "dc": 1})
    all_keys = [keyvals] + [send(keyvals, dz=d) for d in (1, 3, 2)]
    all_queries = [queries] + [send(queries, **turn) for turn in turns]
    scale = lax.dynamic_slice_in_dim(logit_scale, x, 1)
    parts = attend(scale, all_queries, all_keys)
    mixed = merge([parts[0]] + [send(part, **turn) for part, turn in zip(parts[1:], turns)])
    mixed = mixed.reshape(4, ROWS, 256)
    back = [send(mixed[i], dx=-d) for i, d in ((1, 1), (2, 3), (3, 2))]
    heads = [mixed[0], back[0], back[2], back[1]]

    sent = swap(output(ids, heads, out_weight, False, BF16))
    kept = output(ids, heads, out_weight, True, F32)
    inputs, sent = decode_send(ids, kept, sent, encoded, decoder_weight)
    sent = swap(sent)
    kept = decode_own(ids, inputs, decoder_weight)
    decoded, slope, paired = slopes(ids, kept, sent, inputs, grad_out, edges)
    sent = swap(slope)
    partial = backward(ids, slope, paired, decoder_weight, True, F32)
    bins_grad = backward(ids, sent, partial, decoder_weight, False, BF16)
    return decoded, bins_grad


def solution(mesh):
    in_specs = (
        P("seq"),
        P(),
        P(None, None, "head"),
        P(),
        P(None, None, "head"),
        P("head"),
        P("head", None),
        P(None, "head", None),
        P("seq", None),
    )
    out_specs = (P("seq", "head"), P("seq", "head"))
    return jax.shard_map(
        per_device, mesh=mesh, in_specs=in_specs, out_specs=out_specs, check_vma=False
    )
```

```python
import functools

import jax
import jax.numpy as jnp
from jax import lax
from jax.experimental import pallas as pl
from jax.experimental.pallas import tpu as pltpu
from jax.sharding import PartitionSpec as P

BF16 = jnp.bfloat16
F32 = jnp.float32
ROWS = 136
OWN = 128
TILE = 256
HEAD = 192
EPS = 1e-06
MIB = 1024 * 1024


def params(mib):
    return pltpu.CompilerParams(vmem_limit_bytes=mib * MIB)


def dot(a, b):
    return jnp.dot(a, b, preferred_element_type=F32)


def dot_t(a, b):
    return lax.dot_general(a, b, (((1,), (1,)), ((), ())), preferred_element_type=F32)


def cost(flops, nbytes):
    return pl.CostEstimate(flops=int(flops), bytes_accessed=int(nbytes), transcendentals=0)


def shape(dims, dtype):
    return jax.ShapeDtypeStruct(dims, dtype)


VM = pl.BlockSpec(memory_space=pltpu.VMEM)
SM = pl.BlockSpec(memory_space=pltpu.SMEM)
HBM = pl.BlockSpec(memory_space=pltpu.HBM)


def above(rows):
    return pltpu.roll(rows, 1, 0)


def below(rows):
    return pltpu.roll(rows, ROWS - 1, 0)


def lanes(at, size):
    return pl.ds(pl.multiple_of(at, size), size)


def tiles(count, body):
    lax.fori_loop(0, count, lambda i, carry: (body(i), carry)[1], 0)


def gelu_tanh(x):
    return jnp.tanh(0.7978845608028654 * (x + 0.044715 * (x * x * x)))


def conv_taps(rows, weight):
    first, mid, last = (dot(rows, weight(t)) for t in range(3))
    even = above(first[ROWS:]) + mid[:ROWS] + last[ROWS:]
    odd = first[:ROWS] + mid[ROWS:] + below(last[:ROWS])
    return jnp.concatenate([even, odd], axis=0)


def prepare_kernel(bases, grad, weight, codes, last, first, loaded, sem):
    copy = pltpu.make_async_copy(weight, loaded, sem)
    copy.start()
    code = (bases[...] + 1).astype(F32)
    codes[...] = code.astype(BF16)
    feats = grad.shape[1]
    last[:, :feats] = grad[2 * OWN - 16 :, :].astype(F32)[8:].astype(BF16)
    last[:, feats:] = code[OWN - 8 :].astype(BF16)
    first[:, :feats] = grad[:16, :].astype(F32)[:8].astype(BF16)
    first[:, feats:] = code[:8].astype(BF16)
    copy.wait()


def prepare(bases, grad, weight):
    width = grad.shape[1] + 128
    return pl.pallas_call(
        prepare_kernel,
        in_specs=[VM, VM, HBM],
        out_specs=[VM] * 4,
        out_shape=[
            shape((OWN, 128), BF16),
            shape((8, width), BF16),
            shape((8, width), BF16),
            pltpu.VMEM(weight.shape, BF16),
        ],
        scratch_shapes=[pltpu.SemaphoreType.DMA(())],
        compiler_params=params(8),
        cost_estimate=cost(10**6, weight.size * 2),
        name="prepare",
    )(bases, grad, pltpu.with_memory_space_constraint(weight, pltpu.HBM))


def encode_kernel(ids, codes, before, after, stem, weight, ahead, encoded, loaded, embedded, sem):
    copy = pltpu.make_async_copy(ahead, loaded, sem)
    copy.start()
    patch = stem.shape[0] // 4
    feats = stem.shape[1]
    half = weight.shape[2]
    row = lax.broadcasted_iota(jnp.int32, (2 * patch, 4 * patch), 0)
    col = lax.broadcasted_iota(jnp.int32, (2 * patch, 4 * patch), 1)
    place = lax.broadcasted_iota(jnp.int32, (ROWS - OWN, 128), 0)
    halo = jnp.where(place >= 6, before[:, feats:].astype(F32), 0.0)
    halo = jnp.where(place < 2, after[:, feats:].astype(F32), halo)
    code = jnp.concatenate([codes[...].astype(F32), halo], axis=0).astype(BF16)
    spread = [
        dot(code, (row == col // 4 + offset).astype(F32).astype(BF16)) for offset in (0, patch)
    ]
    spread = jnp.concatenate(spread, axis=0)
    base = lax.broadcasted_iota(jnp.int32, spread.shape, 1) % 4 + 1
    onehot = (spread == base.astype(F32)).astype(F32).astype(BF16)

    def embed(i):
        at = lanes(i * TILE, TILE)
        embedded[:, at] = dot(onehot, stem[:, at]).astype(BF16)

    tiles(feats // TILE, embed)

    def convolve(i):
        at = lanes(i * TILE, TILE)
        pre = conv_taps(embedded[...], lambda t: weight[t, :, at])
        mine = embedded[:, lanes(ids[0] * half + i * TILE, TILE)].astype(F32)
        encoded[:, at] = (mine + 0.5 * pre * (1.0 + gelu_tanh(pre))).astype(BF16)

    tiles(half // TILE, convolve)
    copy.wait()


def encode(ids, codes, before, after, stem, weight, ahead):
    half = weight.shape[2]
    feats = stem.shape[1]
    return pl.pallas_call(
        encode_kernel,
        in_specs=[SM, VM, VM, VM, VM, VM, HBM],
        out_specs=[VM, VM],
        out_shape=[shape((2 * ROWS, half), BF16), pltpu.VMEM(ahead.shape, BF16)],
        scratch_shapes=[pltpu.VMEM((2 * ROWS, feats), BF16), pltpu.SemaphoreType.DMA(())],
        compiler_params=params(12),
        cost_estimate=cost(2 * 2 * ROWS * 3 * feats * half, weight.size * 4),
        name="encode",
    )(ids, codes, before, after, stem, weight, pltpu.with_memory_space_constraint(ahead, pltpu.HBM))


def project_kernel(ids, mine, theirs, gain, weight, queries, keyvals):
    half = mine.shape[1]
    near = lanes(ids[0] * half, half)
    far = lanes((1 - ids[0]) * half, half)

    def pairs(ref):
        enc = ref[...].astype(F32)
        return (enc[:ROWS] + enc[ROWS:]) * 0.5

    binned = pairs(mine), pairs(theirs)
    total = sum(jnp.sum(part * part, axis=1, keepdims=True) for part in binned)
    inverse = lax.rsqrt(total * (1.0 / (2 * half)) + EPS)
    here = (binned[0] * inverse * gain[:, near]).astype(BF16)
    there = (binned[1] * inverse * gain[:, far]).astype(BF16)
    low = lax.broadcasted_iota(jnp.int32, (ROWS, 128), 1) < 64
    for pair in range(2):
        at = slice(pair * 2 * HEAD, (pair + 1) * 2 * HEAD)
        rows = []
        for kind in range(3):
            both = dot(here, weight[kind, near, at]) + dot(there, weight[kind, far, at])
            both = both.astype(BF16).astype(F32)
            rows.append((both, pltpu.roll(both, 2 * HEAD - 64, 1)))
        for side in range(2):
            head = 2 * pair + side
            query, key, value = (
                (r[0][:, :128], r[0][:, 128:256]) if side == 0 else (r[1][:, 128:256], r[1][:, 256:384])
                for r in rows
            )
            queries[head, :, :128] = query[0].astype(BF16)
            queries[head, :, 128:] = jnp.where(low, query[1], 0.0).astype(BF16)
            keyvals[head, :, :128] = key[0][:OWN].astype(BF16)
            keyvals[head, :, 128:256] = value[0][:OWN].astype(BF16)
            tail = jnp.where(low, key[1], pltpu.roll(value[1], 64, 1))
            keyvals[head, :, 256:] = tail[:OWN].astype(BF16)


def project(ids, mine, theirs, gain, weight):
    return pl.pallas_call(
        project_kernel,
        in_specs=[SM, VM, VM, VM, VM],
        out_specs=[VM, VM],
        out_shape=[shape((4, ROWS, 256), BF16), shape((4, OWN, 384), BF16)],
        compiler_params=params(12),
        cost_estimate=cost(2 * ROWS * weight.size, weight.size * 2),
        name="project",
    )(ids, mine, theirs, gain, weight)


BLOCK = 2 * ROWS


def attend_kernel(count, resumed, final, scale, *refs):
    queries, refs = refs[:2], refs[2:]
    pieces, refs = refs[:count], refs[count:]
    if resumed:
        (old_mixed, old_stats), refs = refs[:2], refs[2:]
    outs, inverse = refs[:2], refs[2]
    chunk = pieces[0].shape[0]
    lane = lax.broadcasted_iota(jnp.int32, (8, 256), 1)
    ones = (lane < HEAD).astype(F32).astype(BF16)

    def keys(ref):
        return jnp.concatenate([ref[:, :128], ref[:, 256:]], axis=1)

    for at, ref in enumerate(pieces):
        key = keys(ref).astype(F32)
        square = key * key
        high = square.astype(BF16)
        rest = (square - high.astype(F32)).astype(BF16)
        total = dot_t(ones, high) + dot_t(ones, rest)
        inverse[:, at * chunk : (at + 1) * chunk] = lax.rsqrt(total * (1.0 / HEAD) + EPS)

    def block(i):
        for side, query_ref in enumerate(queries):
            span = query_ref.shape[0]
            rows = lanes(i * BLOCK, BLOCK)
            state = lanes(side * span + i * BLOCK, BLOCK)
            query = query_ref[rows, :]
            wide = query.astype(F32)
            own = lax.rsqrt(jnp.sum(wide * wide, axis=1, keepdims=True) * (1.0 / HEAD) + EPS)
            factor = own * (scale[0] * (1.0 / HEAD))
            scores = []
            peak = old_stats[state, 0:1] if resumed else None
            before = peak
            for at, ref in enumerate(pieces):
                part = dot_t(query, keys(ref)) * factor
                part = part * inverse[0:1, at * chunk : (at + 1) * chunk]
                top = jnp.max(part, axis=1, keepdims=True)
                peak = top if peak is None else jnp.maximum(peak, top)
                scores.append(part)
            total, mixed = None, None
            if resumed:
                shrink = jnp.exp(before - peak)
                total = old_stats[state, 64:65] * shrink
                mixed = old_mixed[state, :] * shrink
            for part, ref in zip(scores, pieces):
                exps = jnp.exp(part - peak)
                sums = jnp.sum(exps, axis=1, keepdims=True)
                values = jnp.concatenate([ref[:, 128:256], ref[:, 256:]], axis=1)
                term = dot(exps.astype(BF16), values)
                total = sums if total is None else total + sums
                mixed = term if mixed is None else mixed + term
            if not final:
                outs[0][state, :] = mixed
                half = lax.broadcasted_iota(jnp.int32, (BLOCK, 128), 1) < 64
                outs[1][state, :] = jnp.where(half, peak, total)
                continue
            mixed = mixed / total
            weight = peak + jnp.log(total)
            high = weight.astype(BF16).astype(F32)
            rest = weight - high
            mid = rest.astype(BF16).astype(F32)
            place = lax.broadcasted_iota(jnp.int32, mixed.shape, 1)
            mixed = jnp.where(place == 128, high, mixed)
            mixed = jnp.where(place == 129, mid, mixed)
            mixed = jnp.where(place == 130, rest - mid, mixed)
            outs[side][rows, :] = mixed.astype(BF16)

    tiles(queries[0].shape[0] // BLOCK, block)


def attend(scale, queries, pieces, state, final):
    rows = queries[0].shape[0]
    keys = len(pieces) * pieces[0].shape[0]
    if final:
        outs = [shape((rows, 256), BF16)] * 2
    else:
        outs = [shape((2 * rows, 256), F32), shape((2 * rows, 128), F32)]
    return pl.pallas_call(
        functools.partial(attend_kernel, len(pieces), bool(state), final),
        in_specs=[SM] + [VM] * (2 + len(pieces) + len(state)),
        out_specs=[VM] * 2,
        out_shape=outs,
        scratch_shapes=[pltpu.VMEM((8, keys), F32)],
        compiler_params=params(20),
        cost_estimate=cost(4 * 2 * rows * keys * 256, 8 * rows * 1024),
        name="attend",
    )(scale, *queries, *pieces, *state)


def merge_kernel(a0, a1, out):
    parts = [ref[...].astype(F32) for ref in (a0, a1)]
    logs = [p[:, 128:129] + p[:, 129:130] + p[:, 130:131] for p in parts]
    peak = functools.reduce(jnp.maximum, logs)
    shares = [jnp.exp(log - peak) for log in logs]
    total = sum(shares)
    mixed = sum(p * (share / total) for p, share in zip(parts, shares))
    mixed = jnp.concatenate([mixed[:, :128], pltpu.roll(mixed[:, 128:], 64, 1)], axis=1)
    for block in range(4):
        out[block] = mixed[block * ROWS : (block + 1) * ROWS].astype(BF16)


def merge(parts):
    return pl.pallas_call(
        merge_kernel,
        in_specs=[VM] * 2,
        out_specs=VM,
        out_shape=shape((4, ROWS, 256), BF16),
        compiler_params=params(8),
        cost_estimate=cost(20 * parts[0].size, 10 * parts[0].size),
        name="merge",
    )(*parts)


def output_kernel(mine, ids, heads, weight, out):
    half = out.shape[1]
    side = ids[0] if mine else 1 - ids[0]

    def tile(i):
        at = lanes(side * half + i * TILE, TILE)
        total = None
        for head in range(4):
            rows = weight[head * HEAD : (head + 1) * HEAD, at]
            term = dot(heads[head, :, :HEAD], rows)
            total = term if total is None else total + term
        out[:, lanes(i * TILE, TILE)] = total.astype(out.dtype)

    tiles(half // TILE, tile)


def output(ids, heads, weight, mine, dtype):
    half = weight.shape[1] // 2
    return pl.pallas_call(
        functools.partial(output_kernel, mine),
        in_specs=[SM, VM, VM],
        out_specs=VM,
        out_shape=shape((ROWS, half), dtype),
        compiler_params=params(6),
        cost_estimate=cost(2 * ROWS * weight.size // 2, weight.size),
        name="output",
    )(ids, heads, weight)


def decode_send_kernel(ids, own, other, encoded, weight, inputs, out):
    half = out.shape[1]

    def mix(i):
        at = lanes(i * TILE, TILE)
        enc = encoded[:, at].astype(F32)
        even, odd = enc[:ROWS], enc[ROWS:]
        binned = (even + odd) * 0.5
        block = (binned + (own[:, at] + other[:, at].astype(F32))).astype(BF16).astype(F32)
        row = lax.broadcasted_iota(jnp.int32, block.shape, 0)
        outside = ((ids[2] == 0) & (row == ROWS - 1)) | ((ids[2] == 63) & (row == OWN))
        even = jnp.where(outside, 0.0, block + even)
        odd = jnp.where(outside, 0.0, block + odd)
        inputs[:, at] = jnp.concatenate([even, odd], axis=0).astype(BF16)

    tiles(half // TILE, mix)

    def tile(i):
        at = lanes((1 - ids[0]) * half + i * TILE, TILE)
        out[:, lanes(i * TILE, TILE)] = conv_taps(inputs[...], lambda t: weight[t, :, at]).astype(BF16)

    tiles(half // TILE, tile)


def decode_send(ids, own, other, encoded, weight):
    half = weight.shape[1]
    return pl.pallas_call(
        decode_send_kernel,
        in_specs=[SM] + [VM] * 4,
        out_specs=[VM] * 2,
        out_shape=[shape((2 * ROWS, half), BF16)] * 2,
        compiler_params=params(8),
        cost_estimate=cost(2 * 2 * ROWS * weight.size // 2, weight.size),
        name="decode_send",
    )(ids, own, other, encoded, weight)


def decode_own_kernel(ids, inputs, weight, out):
    half = out.shape[1]

    def tile(i):
        at = lanes(ids[0] * half + i * TILE, TILE)
        out[:, lanes(i * TILE, TILE)] = conv_taps(inputs[...], lambda t: weight[t, :, at])

    tiles(half // TILE, tile)


def decode_own(ids, inputs, weight):
    half = weight.shape[1]
    return pl.pallas_call(
        decode_own_kernel,
        in_specs=[SM, VM, VM],
        out_specs=VM,
        out_shape=shape((2 * ROWS, half), F32),
        compiler_params=params(8),
        cost_estimate=cost(2 * 2 * ROWS * weight.size // 2, weight.size),
        name="decode_own",
    )(ids, inputs, weight)


def slope_kernel(ids, own, other, inputs, grad, before, after, decoded, slope, paired, wide):
    half = own.shape[1]

    def tile(i):
        at = lanes(i * 128, 128)
        column = lanes(ids[0] * half + i * 128, 128)
        pre = own[:, at] + other[:, at].astype(F32)
        tanh = gelu_tanh(pre)
        result = inputs[:, at].astype(F32) + 0.5 * pre * (1.0 + tanh)
        wide[0, pl.ds(0, OWN, 2), :] = result[:OWN]
        wide[0, pl.ds(1, OWN, 2), :] = result[ROWS : ROWS + OWN]
        decoded[:, at] = wide[0].astype(BF16)
        slant = 0.5 * (1.0 + tanh) + (0.5 * 0.7978845608028654) * pre * (1.0 - tanh * tanh) * (
            1.0 + (3 * 0.044715) * (pre * pre)
        )
        wide[1] = grad[:, column].astype(F32)
        even = wide[1, pl.ds(0, OWN, 2), :]
        odd = wide[1, pl.ds(1, OWN, 2), :]
        paired[:, at] = even + odd
        row = lax.broadcasted_iota(jnp.int32, (ROWS - OWN, 128), 0)
        even_edge = jnp.where(row == 0, after[:, column].astype(F32), 0.0)
        odd_edge = jnp.where(row == ROWS - OWN - 1, before[:, column].astype(F32), 0.0)
        cotangent = jnp.concatenate([even, even_edge, odd, odd_edge], axis=0)
        slope[:, at] = (cotangent * slant).astype(BF16)

    tiles(half // 128, tile)


def slopes(ids, own, other, inputs, grad, before, after):
    half = own.shape[1]
    return pl.pallas_call(
        slope_kernel,
        in_specs=[SM] + [VM] * 6,
        out_specs=[VM] * 3,
        out_shape=[
            shape((2 * OWN, half), BF16),
            shape((2 * ROWS, half), BF16),
            shape((OWN, half), F32),
        ],
        scratch_shapes=[pltpu.VMEM((2, 2 * OWN, 128), F32)],
        compiler_params=params(6),
        cost_estimate=cost(30 * own.size, 14 * own.size),
        name="slopes",
    )(ids, own, other, inputs, grad, before, after)


def backward_kernel(mine, ids, slope, start, weight, out, level, lower, upper):
    half = slope.shape[1]
    side = ids[0] if mine else 1 - ids[0]
    level[...] = jnp.zeros_like(level)
    lower[...] = jnp.zeros_like(lower)
    upper[...] = jnp.zeros_like(upper)

    def tile(i):
        at = lanes(side * half + i * TILE, TILE)
        part = slope[:, lanes(i * TILE, TILE)]
        first, mid, last = (dot_t(part, weight[t, :, at]) for t in range(3))
        level[...] += first[ROWS:] + mid[:ROWS] + mid[ROWS:] + last[:ROWS]
        lower[...] += first[:ROWS]
        upper[...] += last[ROWS:]

    tiles(half // TILE, tile)
    total = level[...] + below(lower[...]) + above(upper[...])
    out[...] = (start[...] + total[:OWN]).astype(out.dtype)


def backward(ids, slope, start, weight, mine, dtype):
    half = weight.shape[1]
    return pl.pallas_call(
        functools.partial(backward_kernel, mine),
        in_specs=[SM] + [VM] * 3,
        out_specs=VM,
        out_shape=shape((OWN, half), dtype),
        scratch_shapes=[pltpu.VMEM((ROWS, half), F32)] * 3,
        compiler_params=params(10),
        cost_estimate=cost(2 * 2 * ROWS * weight.size // 2, weight.size),
        name="backward",
    )(ids, slope, start, weight)


def place(at):
    return at // 16, at // 4 % 4, at // 2 % 2, at % 2


def moves(dx=0, dz=0, dy=0, dc=0):
    pairs = []
    for at in range(64):
        x, z, y, c = place(at)
        pairs.append((at, (x + dx) % 4 * 16 + (z + dz) % 4 * 4 + (y ^ dy) * 2 + (c ^ dc)))
    return pairs


def swap(value):
    return lax.ppermute(value, "head", [(0, 1), (1, 0)])


def send(value, **step):
    return lax.ppermute(value, "seq", moves(**step))


def regroup(value):
    groups = [[x * 16 + rest for x in range(4)] for rest in range(16)]
    return lax.all_to_all(value, "seq", 0, 0, axis_index_groups=groups, tiled=True)


def per_device(
    dna_bases,
    stem_weight,
    encoder_weight,
    norm_gain,
    attention_weight,
    logit_scale,
    out_weight,
    decoder_weight,
    grad_out,
):
    at = lax.axis_index("seq")
    x = at // 16
    ids = jnp.stack([lax.axis_index("head"), x, at]).astype(jnp.int32)
    feats = grad_out.shape[1]

    codes, last, first, encoder_weight = prepare(
        dna_bases.reshape(OWN, 128), grad_out, encoder_weight
    )
    before = lax.ppermute(last, "seq", [(i, i + 1) for i in range(63)])
    after = lax.ppermute(first, "seq", [(i + 1, i) for i in range(63)])
    encoded, attention_weight = encode(
        ids, codes, before, after, stem_weight, encoder_weight, attention_weight
    )
    gain = norm_gain.reshape(1, feats)
    queries, keyvals = project(ids, encoded, swap(encoded), gain, attention_weight)

    keyvals = regroup(keyvals).reshape(4 * OWN, 384)
    queries = regroup(queries).reshape(4 * ROWS, 256)
    near = [send(keyvals, dz=1), send(keyvals, dz=3)]
    far = send(keyvals, dz=2)
    near[0], near[1], queries = lax.optimization_barrier((near[0], near[1], queries))
    queries = [queries, send(queries, dy=1)]
    pieces = [keyvals, send(keyvals, dc=1)]
    pieces += near + [send(piece, dc=1) for piece in near]
    scale = lax.dynamic_slice_in_dim(logit_scale, x, 1)
    state = attend(scale, queries, pieces, (), False)
    far, *state = lax.optimization_barrier((far, *state))
    own, other = attend(scale, queries, [far, send(far, dc=1)], state, True)
    heads = regroup(merge([own, send(other, dy=1)]))

    sent = swap(output(ids, heads, out_weight, False, BF16))
    kept = output(ids, heads, out_weight, True, F32)
    inputs, sent = decode_send(ids, kept, sent, encoded, decoder_weight)
    sent = swap(sent)
    kept = decode_own(ids, inputs, decoder_weight)
    decoded, slope, paired = slopes(ids, kept, sent, inputs, grad_out, before, after)
    sent = swap(slope)
    partial = backward(ids, slope, paired, decoder_weight, True, F32)
    bins_grad = backward(ids, sent, partial, decoder_weight, False, BF16)
    return decoded, bins_grad


def solution(mesh):
    in_specs = (
        P("seq"),
        P(),
        P(None, None, "head"),
        P(),
        P(None, None, "head"),
        P("head"),
        P("head", None),
        P(None, "head", None),
        P("seq", None),
    )
    out_specs = (P("seq", "head"), P("seq", "head"))
    return jax.shard_map(
        per_device, mesh=mesh, in_specs=in_specs, out_specs=out_specs, check_vma=False
    )
```

```python
import functools

import jax
import jax.numpy as jnp
from jax import lax
from jax.experimental import pallas as pl
from jax.experimental.pallas import tpu as pltpu
from jax.sharding import PartitionSpec as P

BF16 = jnp.bfloat16
F32 = jnp.float32
ROWS = 136
OWN = 128
TILE = 256
HEAD = 192
EPS = 1e-06
MIB = 1024 * 1024


def params(mib):
    return pltpu.CompilerParams(vmem_limit_bytes=mib * MIB)


def dot(a, b):
    return jnp.dot(a, b, preferred_element_type=F32)


def dot_t(a, b):
    return lax.dot_general(a, b, (((1,), (1,)), ((), ())), preferred_element_type=F32)


def cost(flops, nbytes):
    return pl.CostEstimate(flops=int(flops), bytes_accessed=int(nbytes), transcendentals=0)


def shape(dims, dtype):
    return jax.ShapeDtypeStruct(dims, dtype)


VM = pl.BlockSpec(memory_space=pltpu.VMEM)
SM = pl.BlockSpec(memory_space=pltpu.SMEM)
HBM = pl.BlockSpec(memory_space=pltpu.HBM)


def above(rows):
    return pltpu.roll(rows, 1, 0)


def below(rows):
    return pltpu.roll(rows, ROWS - 1, 0)


def lanes(at, size):
    return pl.ds(pl.multiple_of(at, size), size)


def tiles(count, body):
    lax.fori_loop(0, count, lambda i, carry: (body(i), carry)[1], 0)


def gelu_tanh(x):
    return jnp.tanh(0.7978845608028654 * (x + 0.044715 * (x * x * x)))


def conv_taps(rows, weight):
    first, mid, last = (dot(rows, weight(t)) for t in range(3))
    even = above(first[ROWS:]) + mid[:ROWS] + last[ROWS:]
    odd = first[:ROWS] + mid[ROWS:] + below(last[:ROWS])
    return jnp.concatenate([even, odd], axis=0)


def prepare_kernel(bases, grad, codes, last, first, code, head, tail, sems):
    rows = grad.shape[0]
    copies = [
        pltpu.make_async_copy(bases, code, sems.at[0]),
        pltpu.make_async_copy(grad.at[pl.ds(0, 16)], head, sems.at[1]),
        pltpu.make_async_copy(grad.at[pl.ds(rows - 16, 16)], tail, sems.at[2]),
    ]
    for copy in copies:
        copy.start()
    for copy in copies:
        copy.wait()
    feats = grad.shape[1]
    letters = (code[...] + 1).astype(F32)
    codes[...] = letters.astype(BF16)
    last[:, :feats] = tail[...].astype(F32)[8:].astype(BF16)
    last[:, feats:] = letters[OWN - 8 :].astype(BF16)
    first[:, :feats] = head[...].astype(F32)[:8].astype(BF16)
    first[:, feats:] = letters[:8].astype(BF16)


def far_memory(value):
    return pltpu.with_memory_space_constraint(value, pltpu.HBM)


def prepare(bases, grad):
    feats = grad.shape[1]
    return pl.pallas_call(
        prepare_kernel,
        in_specs=[HBM, HBM],
        out_specs=[VM] * 3,
        out_shape=[
            shape((OWN, 128), BF16),
            shape((8, feats + 128), BF16),
            shape((8, feats + 128), BF16),
        ],
        scratch_shapes=[
            pltpu.VMEM(bases.shape, jnp.int32),
            pltpu.VMEM((16, feats), BF16),
            pltpu.VMEM((16, feats), BF16),
            pltpu.SemaphoreType.DMA((3,)),
        ],
        compiler_params=params(4),
        cost_estimate=cost(10**5, 10**5),
        name="prepare",
    )(far_memory(bases), far_memory(grad))


def encode_kernel(
    ids, codes, before, after, stems, weights, ahead, encoded, loaded, stem, weight, embedded, sems
):
    patch = stem.shape[0] // 4
    feats = stem.shape[1]
    half = weight.shape[2]
    count = half // TILE
    first = pltpu.make_async_copy(stems, stem, sems.at[count])
    copies = [
        pltpu.make_async_copy(
            weights.at[:, :, pl.ds(i * TILE, TILE)],
            weight.at[:, :, pl.ds(i * TILE, TILE)],
            sems.at[i],
        )
        for i in range(count)
    ]
    later = pltpu.make_async_copy(ahead, loaded, sems.at[count + 1])
    for copy in [first] + copies + [later]:
        copy.start()
    row = lax.broadcasted_iota(jnp.int32, (2 * patch, 4 * patch), 0)
    col = lax.broadcasted_iota(jnp.int32, (2 * patch, 4 * patch), 1)
    place = lax.broadcasted_iota(jnp.int32, (ROWS - OWN, 128), 0)
    halo = jnp.where(place >= 6, before[:, feats:].astype(F32), 0.0)
    halo = jnp.where(place < 2, after[:, feats:].astype(F32), halo)
    code = jnp.concatenate([codes[...].astype(F32), halo], axis=0).astype(BF16)
    spread = [
        dot(code, (row == col // 4 + offset).astype(F32).astype(BF16)) for offset in (0, patch)
    ]
    spread = jnp.concatenate(spread, axis=0)
    base = lax.broadcasted_iota(jnp.int32, spread.shape, 1) % 4 + 1
    onehot = (spread == base.astype(F32)).astype(F32).astype(BF16)

    first.wait()

    def embed(i):
        at = lanes(i * TILE, TILE)
        embedded[:, at] = dot(onehot, stem[:, at]).astype(BF16)

    tiles(feats // TILE, embed)

    for i in range(count):
        copies[i].wait()
        at = slice(i * TILE, (i + 1) * TILE)
        pre = conv_taps(embedded[...], lambda t: weight[t, :, at])
        mine = embedded[:, lanes(ids[0] * half + i * TILE, TILE)].astype(F32)
        encoded[:, at] = (mine + 0.5 * pre * (1.0 + gelu_tanh(pre))).astype(BF16)

    later.wait()


def encode(ids, codes, before, after, stem, weight, ahead):
    half = weight.shape[2]
    feats = stem.shape[1]
    return pl.pallas_call(
        encode_kernel,
        in_specs=[SM, VM, VM, VM, HBM, HBM, HBM],
        out_specs=[VM, VM],
        out_shape=[shape((2 * ROWS, half), BF16), pltpu.VMEM(ahead.shape, BF16)],
        scratch_shapes=[
            pltpu.VMEM(stem.shape, BF16),
            pltpu.VMEM(weight.shape, BF16),
            pltpu.VMEM((2 * ROWS, feats), BF16),
            pltpu.SemaphoreType.DMA((half // TILE + 2,)),
        ],
        compiler_params=params(20),
        cost_estimate=cost(2 * 2 * ROWS * 3 * feats * half, weight.size * 4),
        name="encode",
    )(ids, codes, before, after, far_memory(stem), far_memory(weight), far_memory(ahead))


def project_kernel(ids, mine, theirs, gain, weight, *refs):
    queries, keyvals, packed = refs[:4], refs[4:8], refs[8]
    half = mine.shape[1]
    near = lanes(ids[0] * half, half)
    far = lanes((1 - ids[0]) * half, half)

    def pairs(ref):
        enc = ref[...].astype(F32)
        return (enc[:ROWS] + enc[ROWS:]) * 0.5

    binned = pairs(mine), pairs(theirs)
    total = sum(jnp.sum(part * part, axis=1, keepdims=True) for part in binned)
    inverse = lax.rsqrt(total * (1.0 / (2 * half)) + EPS)
    here = (binned[0] * inverse * gain[:, near]).astype(BF16)
    there = (binned[1] * inverse * gain[:, far]).astype(BF16)
    low = lax.broadcasted_iota(jnp.int32, (ROWS, 128), 1) < 64
    for pair in range(2):
        at = slice(pair * 2 * HEAD, (pair + 1) * 2 * HEAD)
        rows = []
        for kind in range(3):
            both = dot(here, weight[kind, near, at]) + dot(there, weight[kind, far, at])
            both = both.astype(BF16).astype(F32)
            rows.append((both, pltpu.roll(both, 2 * HEAD - 64, 1)))
        for side in range(2):
            head = 2 * pair + side
            query, key, value = (
                (r[0][:, :128], r[0][:, 128:256]) if side == 0 else (r[1][:, 128:256], r[1][:, 256:384])
                for r in rows
            )
            packed[head, :, :128] = key[0].astype(BF16)
            packed[head, :, 128:256] = value[0].astype(BF16)
            tail = jnp.where(low, key[1], pltpu.roll(value[1], 64, 1))
            packed[head, :, 256:384] = tail.astype(BF16)
            packed[head, :, 384:512] = query[0].astype(BF16)
            packed[head, :, 512:] = jnp.where(low, query[1], 0.0).astype(BF16)
    for distance in range(4):
        head = lax.rem(ids[1] + distance, 4)
        keyvals[distance][...] = packed[head, :OWN, :384]
        queries[distance][...] = packed[head, :, 384:]


def project(ids, mine, theirs, gain, weight):
    return pl.pallas_call(
        project_kernel,
        in_specs=[SM, VM, VM, VM, VM],
        out_specs=[VM] * 8,
        out_shape=[shape((ROWS, 256), BF16)] * 4 + [shape((OWN, 384), BF16)] * 4,
        scratch_shapes=[pltpu.VMEM((4, ROWS, 640), BF16)],
        compiler_params=params(12),
        cost_estimate=cost(2 * ROWS * weight.size, weight.size * 2),
        name="project",
    )(ids, mine, theirs, gain, weight)


BLOCK = 2 * ROWS
LOG2E = 1.4426950408889634


def attend_kernel(count, again, scale, queries, *refs):
    pieces, refs = refs[:count], refs[count:]
    if again:
        inverse, out = refs
    else:
        out, inverse = refs
    chunk = pieces[0].shape[0]

    def keys(ref):
        return jnp.concatenate([ref[:, :128], ref[:, 256:]], axis=1)

    if not again:
        lane = lax.broadcasted_iota(jnp.int32, (8, 256), 1)
        ones = (lane < HEAD).astype(F32).astype(BF16)
        for at, ref in enumerate(pieces):
            key = keys(ref).astype(F32)
            square = key * key
            high = square.astype(BF16)
            rest = (square - high.astype(F32)).astype(BF16)
            total = dot_t(ones, high) + dot_t(ones, rest)
            inverse[:, at * chunk : (at + 1) * chunk] = lax.rsqrt(total * (1.0 / HEAD) + EPS)

    def block(i):
        rows = lanes(i * BLOCK, BLOCK)
        query = queries[rows, :]
        wide = query.astype(F32)
        own = lax.rsqrt(jnp.sum(wide * wide, axis=1, keepdims=True) * (1.0 / HEAD) + EPS)
        factor = own * (scale[0] * (LOG2E / HEAD))
        scores = []
        peak = None
        for at, ref in enumerate(pieces):
            part = dot_t(query, keys(ref)) * inverse[0:1, at * chunk : (at + 1) * chunk]
            top = jnp.max(part, axis=1, keepdims=True)
            peak = top if peak is None else jnp.maximum(peak, top)
            scores.append(part)
        total, mixed = None, None
        for part, ref in zip(scores, pieces):
            exps = jnp.exp2((part - peak) * factor)
            sums = jnp.sum(exps, axis=1, keepdims=True)
            values = jnp.concatenate([ref[:, 128:256], ref[:, 256:]], axis=1)
            term = dot(exps.astype(BF16), values)
            total = sums if total is None else total + sums
            mixed = term if mixed is None else mixed + term
        mixed = mixed / total
        weight = peak * factor + jnp.log(total) * LOG2E
        high = weight.astype(BF16).astype(F32)
        rest = weight - high
        mid = rest.astype(BF16).astype(F32)
        place = lax.broadcasted_iota(jnp.int32, mixed.shape, 1)
        mixed = jnp.where(place == 128, high, mixed)
        mixed = jnp.where(place == 129, mid, mixed)
        mixed = jnp.where(place == 130, rest - mid, mixed)
        out[rows, :] = mixed.astype(BF16)

    tiles(queries.shape[0] // BLOCK, block)


def attend(scale, queries, pieces, inverse=None):
    again = inverse is not None
    rows = queries.shape[0]
    keys = len(pieces) * pieces[0].shape[0]
    outs = [shape((rows, 256), BF16)] + ([] if again else [shape((8, keys), F32)])
    return pl.pallas_call(
        functools.partial(attend_kernel, len(pieces), again),
        in_specs=[SM] + [VM] * (1 + len(pieces) + again),
        out_specs=[VM] * len(outs),
        out_shape=outs,
        compiler_params=params(24),
        cost_estimate=cost(4 * rows * keys * 256, 8 * rows * 1024),
        name="attend",
    )(scale, queries, *pieces, *([inverse] if again else []))


def merge_kernel(a0, a1, *outs):
    parts = [ref[...].astype(F32) for ref in (a0, a1)]
    logs = [p[:, 128:129] + p[:, 129:130] + p[:, 130:131] for p in parts]
    peak = functools.reduce(jnp.maximum, logs)
    shares = [jnp.exp2(log - peak) for log in logs]
    total = sum(shares)
    mixed = sum(p * (share / total) for p, share in zip(parts, shares))
    mixed = jnp.concatenate([mixed[:, :128], pltpu.roll(mixed[:, 128:], 64, 1)], axis=1)
    for block in range(4):
        outs[block][...] = mixed[block * ROWS : (block + 1) * ROWS].astype(BF16)


def merge(parts):
    return pl.pallas_call(
        merge_kernel,
        in_specs=[VM] * 2,
        out_specs=[VM] * 4,
        out_shape=[shape((ROWS, 256), BF16)] * 4,
        compiler_params=params(8),
        cost_estimate=cost(20 * parts[0].size, 10 * parts[0].size),
        name="merge",
    )(*parts)


def output_kernel(mine, ids, a0, a1, a2, a3, weight, out):
    half = out.shape[1]
    side = ids[0] if mine else 1 - ids[0]

    def tile(i):
        at = lanes(side * half + i * TILE, TILE)
        total = None
        for distance, ref in enumerate((a0, a1, a2, a3)):
            head = lax.rem(ids[1] + distance, 4)
            rows = weight[pl.ds(pl.multiple_of(head * HEAD, HEAD), HEAD), at]
            term = dot(ref[:, :HEAD], rows)
            total = term if total is None else total + term
        out[:, lanes(i * TILE, TILE)] = total.astype(out.dtype)

    tiles(half // TILE, tile)


def output(ids, heads, weight, mine, dtype):
    half = weight.shape[1] // 2
    return pl.pallas_call(
        functools.partial(output_kernel, mine),
        in_specs=[SM] + [VM] * 5,
        out_specs=VM,
        out_shape=shape((ROWS, half), dtype),
        compiler_params=params(6),
        cost_estimate=cost(2 * ROWS * weight.size // 2, weight.size),
        name="output",
    )(ids, *heads, weight)


def decode_send_kernel(ids, own, other, encoded, weight, inputs, out):
    half = out.shape[1]

    def mix(i):
        at = lanes(i * TILE, TILE)
        enc = encoded[:, at].astype(F32)
        even, odd = enc[:ROWS], enc[ROWS:]
        binned = (even + odd) * 0.5
        block = (binned + (own[:, at] + other[:, at].astype(F32))).astype(BF16).astype(F32)
        row = lax.broadcasted_iota(jnp.int32, block.shape, 0)
        outside = ((ids[2] == 0) & (row == ROWS - 1)) | ((ids[2] == 63) & (row == OWN))
        even = jnp.where(outside, 0.0, block + even)
        odd = jnp.where(outside, 0.0, block + odd)
        inputs[:, at] = jnp.concatenate([even, odd], axis=0).astype(BF16)

    tiles(half // TILE, mix)

    def tile(i):
        at = lanes((1 - ids[0]) * half + i * TILE, TILE)
        out[:, lanes(i * TILE, TILE)] = conv_taps(inputs[...], lambda t: weight[t, :, at]).astype(BF16)

    tiles(half // TILE, tile)


def decode_send(ids, own, other, encoded, weight):
    half = weight.shape[1]
    return pl.pallas_call(
        decode_send_kernel,
        in_specs=[SM] + [VM] * 4,
        out_specs=[VM] * 2,
        out_shape=[shape((2 * ROWS, half), BF16)] * 2,
        compiler_params=params(8),
        cost_estimate=cost(2 * 2 * ROWS * weight.size // 2, weight.size),
        name="decode_send",
    )(ids, own, other, encoded, weight)


def decode_own_kernel(ids, inputs, weight, out):
    half = out.shape[1]

    def tile(i):
        at = lanes(ids[0] * half + i * TILE, TILE)
        out[:, lanes(i * TILE, TILE)] = conv_taps(inputs[...], lambda t: weight[t, :, at])

    tiles(half // TILE, tile)


def decode_own(ids, inputs, weight):
    half = weight.shape[1]
    return pl.pallas_call(
        decode_own_kernel,
        in_specs=[SM, VM, VM],
        out_specs=VM,
        out_shape=shape((2 * ROWS, half), F32),
        compiler_params=params(8),
        cost_estimate=cost(2 * 2 * ROWS * weight.size // 2, weight.size),
        name="decode_own",
    )(ids, inputs, weight)


def slope_kernel(ids, own, other, inputs, grad, before, after, decoded, slope, paired, wide):
    half = own.shape[1]

    def tile(i):
        at = lanes(i * 128, 128)
        column = lanes(ids[0] * half + i * 128, 128)
        pre = own[:, at] + other[:, at].astype(F32)
        tanh = gelu_tanh(pre)
        result = inputs[:, at].astype(F32) + 0.5 * pre * (1.0 + tanh)
        wide[0, pl.ds(0, OWN, 2), :] = result[:OWN]
        wide[0, pl.ds(1, OWN, 2), :] = result[ROWS : ROWS + OWN]
        decoded[:, at] = wide[0].astype(BF16)
        slant = 0.5 * (1.0 + tanh) + (0.5 * 0.7978845608028654) * pre * (1.0 - tanh * tanh) * (
            1.0 + (3 * 0.044715) * (pre * pre)
        )
        wide[1] = grad[:, column].astype(F32)
        even = wide[1, pl.ds(0, OWN, 2), :]
        odd = wide[1, pl.ds(1, OWN, 2), :]
        paired[:, at] = even + odd
        row = lax.broadcasted_iota(jnp.int32, (ROWS - OWN, 128), 0)
        even_edge = jnp.where(row == 0, after[:, column].astype(F32), 0.0)
        odd_edge = jnp.where(row == ROWS - OWN - 1, before[:, column].astype(F32), 0.0)
        cotangent = jnp.concatenate([even, even_edge, odd, odd_edge], axis=0)
        slope[:, at] = (cotangent * slant).astype(BF16)

    tiles(half // 128, tile)


def slopes(ids, own, other, inputs, grad, before, after):
    half = own.shape[1]
    return pl.pallas_call(
        slope_kernel,
        in_specs=[SM] + [VM] * 6,
        out_specs=[VM] * 3,
        out_shape=[
            shape((2 * OWN, half), BF16),
            shape((2 * ROWS, half), BF16),
            shape((OWN, half), F32),
        ],
        scratch_shapes=[pltpu.VMEM((2, 2 * OWN, 128), F32)],
        compiler_params=params(6),
        cost_estimate=cost(30 * own.size, 14 * own.size),
        name="slopes",
    )(ids, own, other, inputs, grad, before, after)


def backward_kernel(mine, ids, slope, start, weight, out, level, lower, upper):
    half = slope.shape[1]
    side = ids[0] if mine else 1 - ids[0]
    level[...] = jnp.zeros_like(level)
    lower[...] = jnp.zeros_like(lower)
    upper[...] = jnp.zeros_like(upper)

    def tile(i):
        at = lanes(side * half + i * TILE, TILE)
        part = slope[:, lanes(i * TILE, TILE)]
        first, mid, last = (dot_t(part, weight[t, :, at]) for t in range(3))
        level[...] += first[ROWS:] + mid[:ROWS] + mid[ROWS:] + last[:ROWS]
        lower[...] += first[:ROWS]
        upper[...] += last[ROWS:]

    tiles(half // TILE, tile)
    total = level[...] + below(lower[...]) + above(upper[...])
    out[...] = (start[...] + total[:OWN]).astype(out.dtype)


def backward(ids, slope, start, weight, mine, dtype):
    half = weight.shape[1]
    return pl.pallas_call(
        functools.partial(backward_kernel, mine),
        in_specs=[SM] + [VM] * 3,
        out_specs=VM,
        out_shape=shape((OWN, half), dtype),
        scratch_shapes=[pltpu.VMEM((ROWS, half), F32)] * 3,
        compiler_params=params(10),
        cost_estimate=cost(2 * 2 * ROWS * weight.size // 2, weight.size),
        name="backward",
    )(ids, slope, start, weight)


def place(at):
    return at // 16, at // 4 % 4, at // 2 % 2, at % 2


def moves(dx=0, dz=0, dy=0, dc=0):
    pairs = []
    for at in range(64):
        x, z, y, c = place(at)
        pairs.append((at, (x + dx) % 4 * 16 + (z + dz) % 4 * 4 + (y ^ dy) * 2 + (c ^ dc)))
    return pairs


def swap(value):
    return lax.ppermute(value, "head", [(0, 1), (1, 0)])


def send(value, **step):
    return lax.ppermute(value, "seq", moves(**step))


def per_device(
    dna_bases,
    stem_weight,
    encoder_weight,
    norm_gain,
    attention_weight,
    logit_scale,
    out_weight,
    decoder_weight,
    grad_out,
):
    at = lax.axis_index("seq")
    x = at // 16
    ids = jnp.stack([lax.axis_index("head"), x, at]).astype(jnp.int32)
    feats = grad_out.shape[1]

    codes, last, first = prepare(dna_bases.reshape(OWN, 128), grad_out)
    before = lax.ppermute(last, "seq", [(i, i + 1) for i in range(63)])
    after = lax.ppermute(first, "seq", [(i + 1, i) for i in range(63)])
    encoded, attention_weight = encode(
        ids, codes, before, after, stem_weight, encoder_weight, attention_weight
    )
    gain = norm_gain.reshape(1, feats)
    made = project(ids, encoded, swap(encoded), gain, attention_weight)
    queries, keyvals = made[:4], made[4:]

    def regroup(blocks):
        got = [blocks[0]] + [send(blocks[d], dx=d) for d in (1, 3, 2)]
        return jnp.concatenate(lax.optimization_barrier(got), axis=0)

    keyvals = regroup(keyvals)
    keyvals, *queries = lax.optimization_barrier((keyvals, *queries))
    pieces = [send(keyvals, dz=d) for d in (1, 3, 2)]
    queries = regroup(queries)
    others = send(queries, dy=1)
    pieces[0], pieces[1], others = lax.optimization_barrier((pieces[0], pieces[1], others))
    pieces = [keyvals] + pieces
    pieces += [send(piece, dc=1) for piece in pieces]
    scale = lax.dynamic_slice_in_dim(logit_scale, x, 1)
    other, inverse = attend(scale, others, pieces)
    other = send(other, dy=1)
    own = attend(scale, queries, pieces, inverse)[0]
    mixed = merge([own, other])
    heads = [mixed[0], send(mixed[1], dx=-1), send(mixed[3], dx=-2), send(mixed[2], dx=-3)]

    sent = swap(output(ids, heads, out_weight, False, BF16))
    kept = output(ids, heads, out_weight, True, F32)
    inputs, sent = decode_send(ids, kept, sent, encoded, decoder_weight)
    sent = swap(sent)
    kept = decode_own(ids, inputs, decoder_weight)
    decoded, slope, paired = slopes(ids, kept, sent, inputs, grad_out, before, after)
    sent = swap(slope)
    partial = backward(ids, slope, paired, decoder_weight, True, F32)
    bins_grad = backward(ids, sent, partial, decoder_weight, False, BF16)
    return decoded, bins_grad


def solution(mesh):
    in_specs = (
        P("seq"),
        P(),
        P(None, None, "head"),
        P(),
        P(None, None, "head"),
        P("head"),
        P("head", None),
        P(None, "head", None),
        P("seq", None),
    )
    out_specs = (P("seq", "head"), P("seq", "head"))
    return jax.shard_map(
        per_device, mesh=mesh, in_specs=in_specs, out_specs=out_specs, check_vma=False
    )
```

```python
import functools

import jax
import jax.numpy as jnp
from jax import lax
from jax.experimental import pallas as pl
from jax.experimental.pallas import tpu as pltpu
from jax.sharding import PartitionSpec as P

BF16 = jnp.bfloat16
F32 = jnp.float32
ROWS = 136
OWN = 128
TILE = 256
HEAD = 192
EPS = 1e-06
MIB = 1024 * 1024


def params(mib):
    return pltpu.CompilerParams(vmem_limit_bytes=mib * MIB)


def dot(a, b):
    return jnp.dot(a, b, preferred_element_type=F32)


def dot_t(a, b):
    return lax.dot_general(a, b, (((1,), (1,)), ((), ())), preferred_element_type=F32)


def cost(flops, nbytes):
    return pl.CostEstimate(flops=int(flops), bytes_accessed=int(nbytes), transcendentals=0)


def shape(dims, dtype):
    return jax.ShapeDtypeStruct(dims, dtype)


VM = pl.BlockSpec(memory_space=pltpu.VMEM)
SM = pl.BlockSpec(memory_space=pltpu.SMEM)
HBM = pl.BlockSpec(memory_space=pltpu.HBM)


def above(rows):
    return pltpu.roll(rows, 1, 0)


def below(rows):
    return pltpu.roll(rows, ROWS - 1, 0)


def lanes(at, size):
    return pl.ds(pl.multiple_of(at, size), size)


def tiles(count, body):
    lax.fori_loop(0, count, lambda i, carry: (body(i), carry)[1], 0)


def gelu_tanh(x):
    return jnp.tanh(0.7978845608028654 * (x + 0.044715 * (x * x * x)))


def conv_taps(rows, weight):
    first, mid, last = (dot(rows, weight(t)) for t in range(3))
    even = above(first[ROWS:]) + mid[:ROWS] + last[ROWS:]
    odd = first[:ROWS] + mid[ROWS:] + below(last[:ROWS])
    return jnp.concatenate([even, odd], axis=0)


def prepare_kernel(bases, grad, codes, last, first, code, head, tail, sems):
    rows = grad.shape[0]
    copies = [
        pltpu.make_async_copy(bases, code, sems.at[0]),
        pltpu.make_async_copy(grad.at[pl.ds(0, 16)], head, sems.at[1]),
        pltpu.make_async_copy(grad.at[pl.ds(rows - 16, 16)], tail, sems.at[2]),
    ]
    for copy in copies:
        copy.start()
    for copy in copies:
        copy.wait()
    feats = grad.shape[1]
    letters = (code[...] + 1).astype(F32)
    codes[...] = letters.astype(BF16)
    last[:, :feats] = tail[...].astype(F32)[8:].astype(BF16)
    last[:, feats:] = letters[OWN - 8 :].astype(BF16)
    first[:, :feats] = head[...].astype(F32)[:8].astype(BF16)
    first[:, feats:] = letters[:8].astype(BF16)


def near_memory(value):
    return pltpu.with_memory_space_constraint(value, pltpu.VMEM)


def far_memory(value):
    return pltpu.with_memory_space_constraint(value, pltpu.HBM)


def prepare(bases, grad):
    feats = grad.shape[1]
    return pl.pallas_call(
        prepare_kernel,
        in_specs=[HBM, HBM],
        out_specs=[VM] * 3,
        out_shape=[
            shape((OWN, 128), BF16),
            shape((8, feats + 128), BF16),
            shape((8, feats + 128), BF16),
        ],
        scratch_shapes=[
            pltpu.VMEM(bases.shape, jnp.int32),
            pltpu.VMEM((16, feats), BF16),
            pltpu.VMEM((16, feats), BF16),
            pltpu.SemaphoreType.DMA((3,)),
        ],
        compiler_params=params(4),
        cost_estimate=cost(10**5, 10**5),
        name="prepare",
    )(far_memory(bases), far_memory(grad))


def encode_kernel(
    ids, codes, before, after, stems, weights, ahead, encoded, loaded, stem, weight, embedded, sems
):
    patch = stem.shape[0] // 4
    feats = stem.shape[1]
    half = weight.shape[2]
    count = half // TILE
    first = pltpu.make_async_copy(stems, stem, sems.at[count])
    copies = [
        pltpu.make_async_copy(
            weights.at[:, :, pl.ds(i * TILE, TILE)],
            weight.at[:, :, pl.ds(i * TILE, TILE)],
            sems.at[i],
        )
        for i in range(count)
    ]
    later = pltpu.make_async_copy(ahead, loaded, sems.at[count + 1])
    for copy in [first] + copies + [later]:
        copy.start()
    row = lax.broadcasted_iota(jnp.int32, (2 * patch, 4 * patch), 0)
    col = lax.broadcasted_iota(jnp.int32, (2 * patch, 4 * patch), 1)
    place = lax.broadcasted_iota(jnp.int32, (ROWS - OWN, 128), 0)
    halo = jnp.where(place >= 6, before[:, feats:].astype(F32), 0.0)
    halo = jnp.where(place < 2, after[:, feats:].astype(F32), halo)
    code = jnp.concatenate([codes[...].astype(F32), halo], axis=0).astype(BF16)
    spread = [
        dot(code, (row == col // 4 + offset).astype(F32).astype(BF16)) for offset in (0, patch)
    ]
    spread = jnp.concatenate(spread, axis=0)
    base = lax.broadcasted_iota(jnp.int32, spread.shape, 1) % 4 + 1
    onehot = (spread == base.astype(F32)).astype(F32).astype(BF16)

    first.wait()

    def embed(i):
        at = lanes(i * TILE, TILE)
        embedded[:, at] = dot(onehot, stem[:, at]).astype(BF16)

    tiles(feats // TILE, embed)

    for i in range(count):
        copies[i].wait()
        at = slice(i * TILE, (i + 1) * TILE)
        pre = conv_taps(embedded[...], lambda t: weight[t, :, at])
        mine = embedded[:, lanes(ids[0] * half + i * TILE, TILE)].astype(F32)
        encoded[:, at] = (mine + 0.5 * pre * (1.0 + gelu_tanh(pre))).astype(BF16)

    later.wait()


def encode(ids, codes, before, after, stem, weight, ahead):
    half = weight.shape[2]
    feats = stem.shape[1]
    return pl.pallas_call(
        encode_kernel,
        in_specs=[SM, VM, VM, VM, HBM, HBM, HBM],
        out_specs=[VM, VM],
        out_shape=[shape((2 * ROWS, half), BF16), pltpu.VMEM(ahead.shape, BF16)],
        scratch_shapes=[
            pltpu.VMEM(stem.shape, BF16),
            pltpu.VMEM(weight.shape, BF16),
            pltpu.VMEM((2 * ROWS, feats), BF16),
            pltpu.SemaphoreType.DMA((half // TILE + 2,)),
        ],
        compiler_params=params(20),
        cost_estimate=cost(2 * 2 * ROWS * 3 * feats * half, weight.size * 4),
        name="encode",
    )(ids, codes, before, after, far_memory(stem), far_memory(weight), far_memory(ahead))


def project_kernel(ids, mine, theirs, gain, weight, *refs):
    queries, keyvals, packed = refs[:4], refs[4:8], refs[8]
    half = mine.shape[1]
    near = lanes(ids[0] * half, half)
    far = lanes((1 - ids[0]) * half, half)

    def pairs(ref):
        enc = ref[...].astype(F32)
        return (enc[:ROWS] + enc[ROWS:]) * 0.5

    binned = pairs(mine), pairs(theirs)
    total = sum(jnp.sum(part * part, axis=1, keepdims=True) for part in binned)
    inverse = lax.rsqrt(total * (1.0 / (2 * half)) + EPS)
    here = (binned[0] * inverse * gain[:, near]).astype(BF16)
    there = (binned[1] * inverse * gain[:, far]).astype(BF16)
    low = lax.broadcasted_iota(jnp.int32, (ROWS, 128), 1) < 64
    for pair in range(2):
        at = slice(pair * 2 * HEAD, (pair + 1) * 2 * HEAD)
        rows = []
        for kind in range(3):
            both = dot(here, weight[kind, near, at]) + dot(there, weight[kind, far, at])
            both = both.astype(BF16).astype(F32)
            rows.append((both, pltpu.roll(both, 2 * HEAD - 64, 1)))
        for side in range(2):
            head = 2 * pair + side
            query, key, value = (
                (r[0][:, :128], r[0][:, 128:256]) if side == 0 else (r[1][:, 128:256], r[1][:, 256:384])
                for r in rows
            )
            packed[head, :, :128] = key[0].astype(BF16)
            packed[head, :, 128:256] = value[0].astype(BF16)
            tail = jnp.where(low, key[1], pltpu.roll(value[1], 64, 1))
            packed[head, :, 256:384] = tail.astype(BF16)
            packed[head, :, 384:512] = query[0].astype(BF16)
            packed[head, :, 512:] = jnp.where(low, query[1], 0.0).astype(BF16)
    for distance in range(4):
        head = lax.rem(ids[1] + distance, 4)
        keyvals[distance][...] = packed[head, :OWN, :384]
        queries[distance][...] = packed[head, :, 384:]


def project(ids, mine, theirs, gain, weight):
    return pl.pallas_call(
        project_kernel,
        in_specs=[SM, VM, VM, VM, VM],
        out_specs=[VM] * 8,
        out_shape=[shape((ROWS, 256), BF16)] * 4 + [shape((OWN, 384), BF16)] * 4,
        scratch_shapes=[pltpu.VMEM((4, ROWS, 640), BF16)],
        compiler_params=params(12),
        cost_estimate=cost(2 * ROWS * weight.size, weight.size * 2),
        name="project",
    )(ids, mine, theirs, gain, weight)


BLOCK = 2 * ROWS
LOG2E = 1.4426950408889634


def attend_kernel(count, known, resumed, final, ids, scale, queries, *refs):
    pieces, refs = refs[:count], refs[count:]
    inverses, refs = refs[:known], refs[known:]
    if resumed:
        (old_mixed, old_stats), refs = refs[:2], refs[2:]
    sizes = [ref.shape[0] for ref in pieces]
    starts = [sum(sizes[:i]) for i in range(count)]

    def keys(ref):
        return jnp.concatenate([ref[:, :128], ref[:, 256:]], axis=1)

    if not known:
        outs, inverse = refs[:-1], refs[-1]
        lane = lax.broadcasted_iota(jnp.int32, (8, 256), 1)
        ones = (lane < HEAD).astype(F32).astype(BF16)
        for at, size, ref in zip(starts, sizes, pieces):
            key = keys(ref).astype(F32)
            square = key * key
            high = square.astype(BF16)
            rest = (square - high.astype(F32)).astype(BF16)
            total = dot_t(ones, high) + dot_t(ones, rest)
            inverse[:, at : at + size] = lax.rsqrt(total * (1.0 / HEAD) + EPS)
        inverses = (inverse,)
    else:
        outs = refs

    def inverse_of(at, size):
        for ref in inverses:
            if at < ref.shape[1]:
                return ref[0:1, at : at + size]
            at -= ref.shape[1]

    groups, room = [], 0
    for triple in zip(starts, sizes, pieces):
        if room < triple[1]:
            groups.append([])
            room = 2048
        groups[-1].append(triple)
        room -= triple[1]

    def unit(query, factor, group):
        scores, peak = [], None
        for at, size, ref in group:
            part = dot_t(query, keys(ref)) * inverse_of(at, size)
            top = jnp.max(part, axis=1, keepdims=True)
            peak = top if peak is None else jnp.maximum(peak, top)
            scores.append(part)
        total, mixed = None, None
        for part, (_, _, ref) in zip(scores, group):
            exps = jnp.exp2((part - peak) * factor)
            sums = jnp.sum(exps, axis=1, keepdims=True)
            values = jnp.concatenate([ref[:, 128:256], ref[:, 256:]], axis=1)
            term = dot(exps.astype(BF16), values)
            total = sums if total is None else total + sums
            mixed = term if mixed is None else mixed + term
        return peak, total, mixed

    for begin in range(0, queries.shape[0], BLOCK):
        rows = slice(begin, begin + BLOCK)
        query = queries[rows, :]
        wide = query.astype(F32)
        own = lax.rsqrt(jnp.sum(wide * wide, axis=1, keepdims=True) * (1.0 / HEAD) + EPS)
        factor = own * (scale[ids[1]] * (LOG2E / HEAD))
        states = [unit(query, factor, group) for group in groups]
        if resumed:
            states.append((old_stats[rows, 0:1], old_stats[rows, 64:65], old_mixed[rows, :]))
        peak = functools.reduce(jnp.maximum, [state[0] for state in states])
        if len(states) > 1:
            shrink = [jnp.exp2((state[0] - peak) * factor) for state in states]
            total = sum(state[1] * part for state, part in zip(states, shrink))
            mixed = sum(state[2] * part for state, part in zip(states, shrink))
        else:
            _, total, mixed = states[0]
        if not final:
            outs[0][rows, :] = mixed
            half = lax.broadcasted_iota(jnp.int32, (BLOCK, 128), 1) < 64
            outs[1][rows, :] = jnp.where(half, peak, total)
            continue
        mixed = mixed / total
        weight = peak * factor + jnp.log(total) * LOG2E
        high = weight.astype(BF16).astype(F32)
        rest = weight - high
        mid = rest.astype(BF16).astype(F32)
        place = lax.broadcasted_iota(jnp.int32, mixed.shape, 1)
        mixed = jnp.where(place == 128, high, mixed)
        mixed = jnp.where(place == 129, mid, mixed)
        mixed = jnp.where(place == 130, rest - mid, mixed)
        outs[0][rows, :] = mixed.astype(BF16)


def attend(ids, scale, queries, pieces, inverses=(), state=(), final=True):
    rows = queries.shape[0]
    keys = sum(piece.shape[0] for piece in pieces)
    if final:
        outs = [shape((rows, 256), BF16)]
    else:
        outs = [shape((rows, 256), F32), shape((rows, 128), F32)]
    if not inverses:
        outs.append(shape((8, keys), F32))
    return pl.pallas_call(
        functools.partial(attend_kernel, len(pieces), len(inverses), bool(state), final),
        in_specs=[SM, SM] + [VM] * (1 + len(pieces) + len(inverses) + len(state)),
        out_specs=[VM] * len(outs),
        out_shape=outs,
        compiler_params=params(28),
        cost_estimate=cost(4 * rows * keys * 256, 8 * rows * 1024),
        name="attend",
    )(ids, scale, near_memory(queries), *pieces, *inverses, *state)


def merge_kernel(a0, a1, *outs):
    parts = [ref[...].astype(F32) for ref in (a0, a1)]
    logs = [p[:, 128:129] + p[:, 129:130] + p[:, 130:131] for p in parts]
    peak = functools.reduce(jnp.maximum, logs)
    shares = [jnp.exp2(log - peak) for log in logs]
    total = sum(shares)
    mixed = sum(p * (share / total) for p, share in zip(parts, shares))
    mixed = jnp.concatenate([mixed[:, :128], pltpu.roll(mixed[:, 128:], 64, 1)], axis=1)
    for block in range(4):
        outs[block][...] = mixed[block * ROWS : (block + 1) * ROWS].astype(BF16)


def merge(parts):
    return pl.pallas_call(
        merge_kernel,
        in_specs=[VM] * 2,
        out_specs=[VM] * 4,
        out_shape=[shape((ROWS, 256), BF16)] * 4,
        compiler_params=params(8),
        cost_estimate=cost(20 * parts[0].size, 10 * parts[0].size),
        name="merge",
    )(*parts)


def output_kernel(mine, ids, a0, a1, a2, a3, weight, out):
    half = out.shape[1]
    side = ids[0] if mine else 1 - ids[0]

    def tile(i):
        at = lanes(side * half + i * TILE, TILE)
        total = None
        for distance, ref in enumerate((a0, a1, a2, a3)):
            head = lax.rem(ids[1] + distance, 4)
            rows = weight[pl.ds(pl.multiple_of(head * HEAD, HEAD), HEAD), at]
            term = dot(ref[:, :HEAD], rows)
            total = term if total is None else total + term
        out[:, lanes(i * TILE, TILE)] = total.astype(out.dtype)

    tiles(half // TILE, tile)


def output(ids, heads, weight, mine, dtype):
    half = weight.shape[1] // 2
    return pl.pallas_call(
        functools.partial(output_kernel, mine),
        in_specs=[SM] + [VM] * 5,
        out_specs=VM,
        out_shape=shape((ROWS, half), dtype),
        compiler_params=params(6),
        cost_estimate=cost(2 * ROWS * weight.size // 2, weight.size),
        name="output",
    )(ids, *heads, weight)


def decode_send_kernel(ids, own, other, encoded, weight, inputs, out):
    half = out.shape[1]

    def mix(i):
        at = lanes(i * TILE, TILE)
        enc = encoded[:, at].astype(F32)
        even, odd = enc[:ROWS], enc[ROWS:]
        binned = (even + odd) * 0.5
        block = (binned + (own[:, at] + other[:, at].astype(F32))).astype(BF16).astype(F32)
        row = lax.broadcasted_iota(jnp.int32, block.shape, 0)
        outside = ((ids[2] == 0) & (row == ROWS - 1)) | ((ids[2] == 63) & (row == OWN))
        even = jnp.where(outside, 0.0, block + even)
        odd = jnp.where(outside, 0.0, block + odd)
        inputs[:, at] = jnp.concatenate([even, odd], axis=0).astype(BF16)

    tiles(half // TILE, mix)

    def tile(i):
        at = lanes((1 - ids[0]) * half + i * TILE, TILE)
        out[:, lanes(i * TILE, TILE)] = conv_taps(inputs[...], lambda t: weight[t, :, at]).astype(BF16)

    tiles(half // TILE, tile)


def decode_send(ids, own, other, encoded, weight):
    half = weight.shape[1]
    return pl.pallas_call(
        decode_send_kernel,
        in_specs=[SM] + [VM] * 4,
        out_specs=[VM] * 2,
        out_shape=[shape((2 * ROWS, half), BF16)] * 2,
        compiler_params=params(8),
        cost_estimate=cost(2 * 2 * ROWS * weight.size // 2, weight.size),
        name="decode_send",
    )(ids, own, other, encoded, weight)


def decode_own_kernel(ids, inputs, weight, out):
    half = out.shape[1]

    def tile(i):
        at = lanes(ids[0] * half + i * TILE, TILE)
        out[:, lanes(i * TILE, TILE)] = conv_taps(inputs[...], lambda t: weight[t, :, at])

    tiles(half // TILE, tile)


def decode_own(ids, inputs, weight):
    half = weight.shape[1]
    return pl.pallas_call(
        decode_own_kernel,
        in_specs=[SM, VM, VM],
        out_specs=VM,
        out_shape=shape((2 * ROWS, half), F32),
        compiler_params=params(8),
        cost_estimate=cost(2 * 2 * ROWS * weight.size // 2, weight.size),
        name="decode_own",
    )(ids, inputs, weight)


def slope_kernel(ids, own, other, inputs, grad, before, after, decoded, slope, paired, wide):
    half = own.shape[1]

    def tile(i):
        at = lanes(i * 128, 128)
        column = lanes(ids[0] * half + i * 128, 128)
        pre = own[:, at] + other[:, at].astype(F32)
        tanh = gelu_tanh(pre)
        result = inputs[:, at].astype(F32) + 0.5 * pre * (1.0 + tanh)
        wide[0, pl.ds(0, OWN, 2), :] = result[:OWN]
        wide[0, pl.ds(1, OWN, 2), :] = result[ROWS : ROWS + OWN]
        decoded[:, at] = wide[0].astype(BF16)
        slant = 0.5 * (1.0 + tanh) + (0.5 * 0.7978845608028654) * pre * (1.0 - tanh * tanh) * (
            1.0 + (3 * 0.044715) * (pre * pre)
        )
        wide[1] = grad[:, column].astype(F32)
        even = wide[1, pl.ds(0, OWN, 2), :]
        odd = wide[1, pl.ds(1, OWN, 2), :]
        paired[:, at] = even + odd
        row = lax.broadcasted_iota(jnp.int32, (ROWS - OWN, 128), 0)
        even_edge = jnp.where(row == 0, after[:, column].astype(F32), 0.0)
        odd_edge = jnp.where(row == ROWS - OWN - 1, before[:, column].astype(F32), 0.0)
        cotangent = jnp.concatenate([even, even_edge, odd, odd_edge], axis=0)
        slope[:, at] = (cotangent * slant).astype(BF16)

    tiles(half // 128, tile)


def slopes(ids, own, other, inputs, grad, before, after):
    half = own.shape[1]
    return pl.pallas_call(
        slope_kernel,
        in_specs=[SM] + [VM] * 6,
        out_specs=[VM] * 3,
        out_shape=[
            shape((2 * OWN, half), BF16),
            shape((2 * ROWS, half), BF16),
            shape((OWN, half), F32),
        ],
        scratch_shapes=[pltpu.VMEM((2, 2 * OWN, 128), F32)],
        compiler_params=params(6),
        cost_estimate=cost(30 * own.size, 14 * own.size),
        name="slopes",
    )(ids, own, other, inputs, grad, before, after)


def backward_kernel(mine, ids, slope, start, weight, out, level, lower, upper):
    half = slope.shape[1]
    side = ids[0] if mine else 1 - ids[0]
    level[...] = jnp.zeros_like(level)
    lower[...] = jnp.zeros_like(lower)
    upper[...] = jnp.zeros_like(upper)

    def tile(i):
        at = lanes(side * half + i * TILE, TILE)
        part = slope[:, lanes(i * TILE, TILE)]
        first, mid, last = (dot_t(part, weight[t, :, at]) for t in range(3))
        level[...] += first[ROWS:] + mid[:ROWS] + mid[ROWS:] + last[:ROWS]
        lower[...] += first[:ROWS]
        upper[...] += last[ROWS:]

    tiles(half // TILE, tile)
    total = level[...] + below(lower[...]) + above(upper[...])
    out[...] = (start[...] + total[:OWN]).astype(out.dtype)


def backward(ids, slope, start, weight, mine, dtype):
    half = weight.shape[1]
    return pl.pallas_call(
        functools.partial(backward_kernel, mine),
        in_specs=[SM] + [VM] * 3,
        out_specs=VM,
        out_shape=shape((OWN, half), dtype),
        scratch_shapes=[pltpu.VMEM((ROWS, half), F32)] * 3,
        compiler_params=params(10),
        cost_estimate=cost(2 * 2 * ROWS * weight.size // 2, weight.size),
        name="backward",
    )(ids, slope, start, weight)


def place(at):
    return at // 16, at // 4 % 4, at // 2 % 2, at % 2


def moves(dx=0, dz=0, dy=0, dc=0):
    pairs = []
    for at in range(64):
        x, z, y, c = place(at)
        pairs.append((at, (x + dx) % 4 * 16 + (z + dz) % 4 * 4 + (y ^ dy) * 2 + (c ^ dc)))
    return pairs


def swap(value):
    return lax.ppermute(value, "head", [(0, 1), (1, 0)])


def send(value, **step):
    return lax.ppermute(value, "seq", moves(**step))


def per_device(
    dna_bases,
    stem_weight,
    encoder_weight,
    norm_gain,
    attention_weight,
    logit_scale,
    out_weight,
    decoder_weight,
    grad_out,
):
    at = lax.axis_index("seq")
    x = at // 16
    ids = jnp.stack([lax.axis_index("head"), x, at]).astype(jnp.int32)
    feats = grad_out.shape[1]

    codes, last, first = prepare(dna_bases.reshape(OWN, 128), grad_out)
    before = lax.ppermute(last, "seq", [(i, i + 1) for i in range(63)])
    after = lax.ppermute(first, "seq", [(i + 1, i) for i in range(63)])
    encoded, attention_weight = encode(
        ids, codes, before, after, stem_weight, encoder_weight, attention_weight
    )
    gain = norm_gain.reshape(1, feats)
    made = project(ids, encoded, swap(encoded), gain, attention_weight)
    queries, keyvals = made[:4], made[4:]

    def regroup(blocks):
        got = [blocks[0]] + [send(blocks[d], dx=d) for d in (1, 3, 2)]
        return jnp.concatenate(lax.optimization_barrier(got), axis=0)

    keyvals = regroup(keyvals)
    keyvals, *queries = lax.optimization_barrier((keyvals, *queries))
    near = [send(keyvals, dz=1), send(keyvals, dz=3)]
    queries = regroup(queries)
    others = send(queries, dy=1)
    near[0], near[1], others = lax.optimization_barrier((near[0], near[1], others))
    half = keyvals.shape[0] // 2
    far = [send(near[0][:half], dz=1), send(near[1][half:], dz=3)]
    pieces = [keyvals] + near
    pieces += [send(piece, dc=1) for piece in pieces]
    *state, inverse = attend(ids, logit_scale, others, pieces, final=False)
    *far, state[0], state[1] = lax.optimization_barrier((*far, *state))
    far = jnp.concatenate(far, axis=0)
    late = [far, send(far, dc=1)]
    other, later = attend(ids, logit_scale, others, late, state=state)
    other = send(other, dy=1)
    own = attend(ids, logit_scale, queries, pieces + late, inverses=[inverse, later])[0]
    mixed = merge([own, other])
    heads = [mixed[0], send(mixed[1], dx=-1), send(mixed[3], dx=-2), send(mixed[2], dx=-3)]

    sent = swap(output(ids, heads, out_weight, False, BF16))
    kept = output(ids, heads, out_weight, True, F32)
    inputs, sent = decode_send(ids, kept, sent, encoded, decoder_weight)
    sent = swap(sent)
    kept = decode_own(ids, inputs, decoder_weight)
    decoded, slope, paired = slopes(ids, kept, sent, inputs, grad_out, before, after)
    sent = swap(slope)
    partial = backward(ids, slope, paired, decoder_weight, True, F32)
    bins_grad = backward(ids, sent, partial, decoder_weight, False, BF16)
    return decoded, bins_grad


def solution(mesh):
    in_specs = (
        P("seq"),
        P(),
        P(None, None, "head"),
        P(),
        P(None, None, "head"),
        P("head"),
        P("head", None),
        P(None, "head", None),
        P("seq", None),
    )
    out_specs = (P("seq", "head"), P("seq", "head"))
    return jax.shard_map(
        per_device, mesh=mesh, in_specs=in_specs, out_specs=out_specs, check_vma=False
    )
```

```python
import functools

import jax
import jax.numpy as jnp
from jax import lax
from jax.experimental import pallas as pl
from jax.experimental.pallas import tpu as pltpu
from jax.sharding import PartitionSpec as P

BF16 = jnp.bfloat16
F32 = jnp.float32
ROWS = 136
OWN = 128
TILE = 256
HEAD = 192
EPS = 1e-06
MIB = 1024 * 1024


def params(mib):
    return pltpu.CompilerParams(vmem_limit_bytes=mib * MIB)


def dot(a, b):
    return jnp.dot(a, b, preferred_element_type=F32)


def dot_t(a, b):
    return lax.dot_general(a, b, (((1,), (1,)), ((), ())), preferred_element_type=F32)


def cost(flops, nbytes):
    return pl.CostEstimate(flops=int(flops), bytes_accessed=int(nbytes), transcendentals=0)


def shape(dims, dtype):
    return jax.ShapeDtypeStruct(dims, dtype)


VM = pl.BlockSpec(memory_space=pltpu.VMEM)
SM = pl.BlockSpec(memory_space=pltpu.SMEM)
HBM = pl.BlockSpec(memory_space=pltpu.HBM)


def above(rows, span):
    parts = [pltpu.roll(rows[i : i + span], 1, 0) for i in range(0, rows.shape[0], span)]
    return jnp.concatenate(parts, axis=0)


def below(rows, span):
    parts = [pltpu.roll(rows[i : i + span], span - 1, 0) for i in range(0, rows.shape[0], span)]
    return jnp.concatenate(parts, axis=0)


def lanes(at, size):
    return pl.ds(pl.multiple_of(at, size), size)


def tiles(count, body):
    lax.fori_loop(0, count, lambda i, carry: (body(i), carry)[1], 0)


def gelu_tanh(x):
    return jnp.tanh(0.7978845608028654 * (x + 0.044715 * (x * x * x)))


def conv_taps(rows, weight, span):
    half = rows.shape[0] // 2
    first, mid, last = (dot(rows, weight(t)) for t in range(3))
    even = above(first[half:], span) + mid[:half] + last[half:]
    odd = first[:half] + mid[half:] + below(last[:half], span)
    return jnp.concatenate([even, odd], axis=0)


def prepare_kernel(bases, grad, codes, last, first, code, head, tail, sems):
    rows = grad.shape[0]
    copies = [
        pltpu.make_async_copy(bases, code, sems.at[0]),
        pltpu.make_async_copy(grad.at[pl.ds(0, 16)], head, sems.at[1]),
        pltpu.make_async_copy(grad.at[pl.ds(rows - 16, 16)], tail, sems.at[2]),
    ]
    for copy in copies:
        copy.start()
    for copy in copies:
        copy.wait()
    feats = grad.shape[1]
    letters = (code[...] + 1).astype(F32)
    codes[...] = letters.astype(BF16)
    last[:, :feats] = tail[...].astype(F32)[8:].astype(BF16)
    last[:, feats:] = letters[OWN - 8 :].astype(BF16)
    first[:, :feats] = head[...].astype(F32)[:8].astype(BF16)
    first[:, feats:] = letters[:8].astype(BF16)


def near_memory(value):
    return pltpu.with_memory_space_constraint(value, pltpu.VMEM)


def far_memory(value):
    return pltpu.with_memory_space_constraint(value, pltpu.HBM)


def prepare(bases, grad):
    feats = grad.shape[1]
    return pl.pallas_call(
        prepare_kernel,
        in_specs=[HBM, HBM],
        out_specs=[VM] * 3,
        out_shape=[
            shape((OWN, 128), BF16),
            shape((8, feats + 128), BF16),
            shape((8, feats + 128), BF16),
        ],
        scratch_shapes=[
            pltpu.VMEM(bases.shape, jnp.int32),
            pltpu.VMEM((16, feats), BF16),
            pltpu.VMEM((16, feats), BF16),
            pltpu.SemaphoreType.DMA((3,)),
        ],
        compiler_params=params(4),
        cost_estimate=cost(10**5, 10**5),
        name="prepare",
    )(far_memory(bases), far_memory(grad))


def encode_body(side, code, stems, weights, encoded, stem, weight, embedded, sems, span):
    patch = stem.shape[0] // 4
    feats = stem.shape[1]
    half = weight.shape[2]
    count = half // TILE
    first = pltpu.make_async_copy(stems, stem, sems.at[count])
    copies = [
        pltpu.make_async_copy(
            weights.at[:, :, pl.ds(i * TILE, TILE)],
            weight.at[:, :, pl.ds(i * TILE, TILE)],
            sems.at[i],
        )
        for i in range(count)
    ]
    for copy in [first] + copies:
        copy.start()
    row = lax.broadcasted_iota(jnp.int32, (2 * patch, 4 * patch), 0)
    col = lax.broadcasted_iota(jnp.int32, (2 * patch, 4 * patch), 1)
    spread = [
        dot(code, (row == col // 4 + offset).astype(F32).astype(BF16)) for offset in (0, patch)
    ]
    spread = jnp.concatenate(spread, axis=0)
    base = lax.broadcasted_iota(jnp.int32, spread.shape, 1) % 4 + 1
    onehot = (spread == base.astype(F32)).astype(F32).astype(BF16)
    first.wait()

    def embed(i):
        at = lanes(i * TILE, TILE)
        embedded[:, at] = dot(onehot, stem[:, at]).astype(BF16)

    tiles(feats // TILE, embed)
    for i in range(count):
        copies[i].wait()
        at = slice(i * TILE, (i + 1) * TILE)
        pre = conv_taps(embedded[...], lambda t: weight[t, :, at], span)
        mine = embedded[:, lanes(side * half + i * TILE, TILE)].astype(F32)
        encoded[:, at] = (mine + 0.5 * pre * (1.0 + gelu_tanh(pre))).astype(BF16)


def encode_kernel(ids, codes, stems, weights, encoded, *scratch):
    encode_body(ids[0], codes[...], stems, weights, encoded, *scratch, OWN)


def encode_edges_kernel(
    ids, codes, before, after, stems, weights, ahead, encoded, loaded, stem, weight, embedded, sems
):
    later = pltpu.make_async_copy(ahead, loaded, sems.at[sems.shape[0] - 1])
    later.start()
    feats = stem.shape[1]
    place = lax.broadcasted_iota(jnp.int32, (8, 128), 0)
    code = codes[...].astype(F32)
    low = jnp.where(place >= 6, before[:, feats:].astype(F32), 0.0)
    low = jnp.where(place == 0, code[:8], low)
    high = jnp.where(place < 2, after[:, feats:].astype(F32), 0.0)
    high = jnp.where(place == 7, code[OWN - 8 :], high)
    code = jnp.concatenate([low, high], axis=0).astype(BF16)
    encode_body(ids[0], code, stems, weights, encoded, stem, weight, embedded, sems, 8)
    later.wait()


def encode_scratch(rows, stem, weight):
    return [
        pltpu.VMEM(stem.shape, BF16),
        pltpu.VMEM(weight.shape, BF16),
        pltpu.VMEM((rows, stem.shape[1]), BF16),
        pltpu.SemaphoreType.DMA((weight.shape[2] // TILE + 2,)),
    ]


def encode(ids, codes, stem, weight):
    half = weight.shape[2]
    return pl.pallas_call(
        encode_kernel,
        in_specs=[SM, VM, HBM, HBM],
        out_specs=VM,
        out_shape=shape((2 * OWN, half), BF16),
        scratch_shapes=encode_scratch(2 * OWN, stem, weight),
        compiler_params=params(20),
        cost_estimate=cost(4 * OWN * weight.size, weight.size * 4),
        name="encode",
    )(ids, codes, far_memory(stem), far_memory(weight))


def encode_edges(ids, codes, before, after, stem, weight, ahead):
    half = weight.shape[2]
    return pl.pallas_call(
        encode_edges_kernel,
        in_specs=[SM, VM, VM, VM, HBM, HBM, HBM],
        out_specs=[VM, VM],
        out_shape=[shape((32, half), BF16), pltpu.VMEM(ahead.shape, BF16)],
        scratch_shapes=encode_scratch(32, stem, weight),
        compiler_params=params(14),
        cost_estimate=cost(4 * OWN * weight.size, weight.size * 4),
        name="encode_edges",
    )(ids, codes, before, after, far_memory(stem), far_memory(weight), far_memory(ahead))


def joined(main, edges):
    main, edges = main[...].astype(F32), edges[...].astype(F32)
    even, odd = main[:OWN], main[OWN:]
    even_low, even_high, odd_low, odd_high = (edges[i : i + 8] for i in range(0, 32, 8))
    place = lax.broadcasted_iota(jnp.int32, even_low.shape, 0)
    return jnp.concatenate(
        [
            jnp.where(place == 0, even_low, even[:8]),
            even[8:],
            jnp.where(place < 4, even_high, even_low),
            odd[: OWN - 8],
            jnp.where(place == 7, odd_high, odd[OWN - 8 :]),
            jnp.where(place < 4, odd_high, odd_low),
        ],
        axis=0,
    )


def unpacked(both):
    both = both.astype(BF16).astype(F32)
    turned = pltpu.roll(both, 2 * HEAD - 64, 1)
    return (both[:, :128], both[:, 128:256]), (turned[:, 128:256], turned[:, 256:384])


def project_keys_kernel(
    ids, mine, mine_edges, theirs, their_edges, gain, weight, encoded, normed, k0, k1, k2, k3, packed
):
    half = mine.shape[1]
    near = lanes(ids[0] * half, half)
    far = lanes((1 - ids[0]) * half, half)
    ring = joined(mine, mine_edges)
    encoded[...] = ring.astype(BF16)
    other = joined(theirs, their_edges)
    binned = [(part[:ROWS] + part[ROWS:]) * 0.5 for part in (ring, other)]
    total = sum(jnp.sum(part * part, axis=1, keepdims=True) for part in binned)
    inverse = lax.rsqrt(total * (1.0 / (2 * half)) + EPS)
    here = (binned[0] * inverse * gain[:, near]).astype(BF16)
    there = (binned[1] * inverse * gain[:, far]).astype(BF16)
    normed[0] = here
    normed[1] = there
    low = lax.broadcasted_iota(jnp.int32, (ROWS, 128), 1) < 64
    for pair in range(2):
        at = slice(pair * 2 * HEAD, (pair + 1) * 2 * HEAD)
        keys, values = (
            unpacked(dot(here, weight[kind, near, at]) + dot(there, weight[kind, far, at]))
            for kind in (1, 2)
        )
        for side in range(2):
            head = 2 * pair + side
            key, value = keys[side], values[side]
            packed[head, :, :128] = key[0].astype(BF16)
            packed[head, :, 128:256] = value[0].astype(BF16)
            tail = jnp.where(low, key[1], pltpu.roll(value[1], 64, 1))
            packed[head, :, 256:] = tail.astype(BF16)
    for distance, out in enumerate((k0, k1, k2, k3)):
        out[...] = packed[lax.rem(ids[1] + distance, 4), :OWN, :]


def project_keys(ids, mine, mine_edges, theirs, their_edges, gain, weight):
    half = mine.shape[1]
    return pl.pallas_call(
        project_keys_kernel,
        in_specs=[SM] + [VM] * 6,
        out_specs=[VM] * 6,
        out_shape=[shape((2 * ROWS, half), BF16), shape((2, ROWS, half), BF16)]
        + [shape((OWN, 384), BF16)] * 4,
        scratch_shapes=[pltpu.VMEM((4, ROWS, 384), BF16)],
        compiler_params=params(12),
        cost_estimate=cost(2 * ROWS * weight.size * 2 // 3, weight.size * 2),
        name="project_keys",
    )(ids, mine, mine_edges, theirs, their_edges, gain, weight)


def project_queries_kernel(ids, normed, weight, q0, q1, q2, q3, packed):
    half = normed.shape[2]
    near = lanes(ids[0] * half, half)
    far = lanes((1 - ids[0]) * half, half)
    low = lax.broadcasted_iota(jnp.int32, (ROWS, 128), 1) < 64
    for pair in range(2):
        at = slice(pair * 2 * HEAD, (pair + 1) * 2 * HEAD)
        both = dot(normed[0], weight[0, near, at]) + dot(normed[1], weight[0, far, at])
        for side, query in enumerate(unpacked(both)):
            packed[2 * pair + side, :, :128] = query[0].astype(BF16)
            packed[2 * pair + side, :, 128:] = jnp.where(low, query[1], 0.0).astype(BF16)
    for distance, out in enumerate((q0, q1, q2, q3)):
        out[...] = packed[lax.rem(ids[1] + distance, 4)]


def project_queries(ids, normed, weight):
    return pl.pallas_call(
        project_queries_kernel,
        in_specs=[SM, VM, VM],
        out_specs=[VM] * 4,
        out_shape=[shape((ROWS, 256), BF16)] * 4,
        scratch_shapes=[pltpu.VMEM((4, ROWS, 256), BF16)],
        compiler_params=params(10),
        cost_estimate=cost(2 * ROWS * weight.size // 3, weight.size),
        name="project_queries",
    )(ids, normed, near_memory(weight))


BLOCK = 2 * ROWS
LOG2E = 1.4426950408889634


def attend_kernel(count, known, resumed, final, ids, scale, queries, *refs):
    pieces, refs = refs[:count], refs[count:]
    inverses, refs = refs[:known], refs[known:]
    if resumed:
        (old_mixed, old_stats), refs = refs[:2], refs[2:]
    sizes = [ref.shape[0] for ref in pieces]
    starts = [sum(sizes[:i]) for i in range(count)]

    def keys(ref):
        return jnp.concatenate([ref[:, :128], ref[:, 256:]], axis=1)

    if not known:
        outs, inverse = refs[:-1], refs[-1]
        lane = lax.broadcasted_iota(jnp.int32, (8, 256), 1)
        ones = (lane < HEAD).astype(F32).astype(BF16)
        for at, size, ref in zip(starts, sizes, pieces):
            key = keys(ref).astype(F32)
            square = key * key
            high = square.astype(BF16)
            rest = (square - high.astype(F32)).astype(BF16)
            total = dot_t(ones, high) + dot_t(ones, rest)
            inverse[:, at : at + size] = lax.rsqrt(total * (1.0 / HEAD) + EPS)
        inverses = (inverse,)
    else:
        outs = refs

    def inverse_of(at, size):
        for ref in inverses:
            if at < ref.shape[1]:
                return ref[0:1, at : at + size]
            at -= ref.shape[1]

    groups, room = [], 0
    for triple in zip(starts, sizes, pieces):
        if room < triple[1]:
            groups.append([])
            room = 2048
        groups[-1].append(triple)
        room -= triple[1]

    def unit(query, factor, group):
        scores, peak = [], None
        for at, size, ref in group:
            part = dot_t(query, keys(ref)) * inverse_of(at, size)
            top = jnp.max(part, axis=1, keepdims=True)
            peak = top if peak is None else jnp.maximum(peak, top)
            scores.append(part)
        total, mixed = None, None
        for part, (_, _, ref) in zip(scores, group):
            exps = jnp.exp2((part - peak) * factor)
            sums = jnp.sum(exps, axis=1, keepdims=True)
            values = jnp.concatenate([ref[:, 128:256], ref[:, 256:]], axis=1)
            term = dot(exps.astype(BF16), values)
            total = sums if total is None else total + sums
            mixed = term if mixed is None else mixed + term
        return peak, total, mixed

    for begin in range(0, queries.shape[0], BLOCK):
        rows = slice(begin, begin + BLOCK)
        query = queries[rows, :]
        wide = query.astype(F32)
        own = lax.rsqrt(jnp.sum(wide * wide, axis=1, keepdims=True) * (1.0 / HEAD) + EPS)
        factor = own * (scale[ids[1]] * (LOG2E / HEAD))
        states = [unit(query, factor, group) for group in groups]
        if resumed:
            states.append((old_stats[rows, 0:1], old_stats[rows, 64:65], old_mixed[rows, :]))
        peak = functools.reduce(jnp.maximum, [state[0] for state in states])
        if len(states) > 1:
            shrink = [jnp.exp2((state[0] - peak) * factor) for state in states]
            total = sum(state[1] * part for state, part in zip(states, shrink))
            mixed = sum(state[2] * part for state, part in zip(states, shrink))
        else:
            _, total, mixed = states[0]
        if not final:
            outs[0][rows, :] = mixed
            half = lax.broadcasted_iota(jnp.int32, (BLOCK, 128), 1) < 64
            outs[1][rows, :] = jnp.where(half, peak, total)
            continue
        mixed = mixed / total
        weight = peak * factor + jnp.log(total) * LOG2E
        high = weight.astype(BF16).astype(F32)
        rest = weight - high
        mid = rest.astype(BF16).astype(F32)
        place = lax.broadcasted_iota(jnp.int32, mixed.shape, 1)
        mixed = jnp.where(place == 128, high, mixed)
        mixed = jnp.where(place == 129, mid, mixed)
        mixed = jnp.where(place == 130, rest - mid, mixed)
        outs[0][rows, :] = mixed.astype(BF16)


def attend(ids, scale, queries, pieces, inverses=(), state=(), final=True):
    rows = queries.shape[0]
    keys = sum(piece.shape[0] for piece in pieces)
    if final:
        outs = [shape((rows, 256), BF16)]
    else:
        outs = [shape((rows, 256), F32), shape((rows, 128), F32)]
    if not inverses:
        outs.append(shape((8, keys), F32))
    return pl.pallas_call(
        functools.partial(attend_kernel, len(pieces), len(inverses), bool(state), final),
        in_specs=[SM, SM] + [VM] * (1 + len(pieces) + len(inverses) + len(state)),
        out_specs=[VM] * len(outs),
        out_shape=outs,
        compiler_params=params(28),
        cost_estimate=cost(4 * rows * keys * 256, 8 * rows * 1024),
        name="attend",
    )(ids, scale, near_memory(queries), *pieces, *inverses, *state)


def merge_kernel(a0, a1, *outs):
    parts = [ref[...].astype(F32) for ref in (a0, a1)]
    logs = [p[:, 128:129] + p[:, 129:130] + p[:, 130:131] for p in parts]
    peak = functools.reduce(jnp.maximum, logs)
    shares = [jnp.exp2(log - peak) for log in logs]
    total = sum(shares)
    mixed = sum(p * (share / total) for p, share in zip(parts, shares))
    mixed = jnp.concatenate([mixed[:, :128], pltpu.roll(mixed[:, 128:], 64, 1)], axis=1)
    for block in range(4):
        outs[block][...] = mixed[block * ROWS : (block + 1) * ROWS].astype(BF16)


def merge(parts):
    return pl.pallas_call(
        merge_kernel,
        in_specs=[VM] * 2,
        out_specs=[VM] * 4,
        out_shape=[shape((ROWS, 256), BF16)] * 4,
        compiler_params=params(8),
        cost_estimate=cost(20 * parts[0].size, 10 * parts[0].size),
        name="merge",
    )(*parts)


def output_kernel(mine, ids, a0, a1, a2, a3, weight, out):
    half = out.shape[1]
    side = ids[0] if mine else 1 - ids[0]

    def tile(i):
        at = lanes(side * half + i * TILE, TILE)
        total = None
        for distance, ref in enumerate((a0, a1, a2, a3)):
            head = lax.rem(ids[1] + distance, 4)
            rows = weight[pl.ds(pl.multiple_of(head * HEAD, HEAD), HEAD), at]
            term = dot(ref[:, :HEAD], rows)
            total = term if total is None else total + term
        out[:, lanes(i * TILE, TILE)] = total.astype(out.dtype)

    tiles(half // TILE, tile)


def output(ids, heads, weight, mine, dtype):
    half = weight.shape[1] // 2
    return pl.pallas_call(
        functools.partial(output_kernel, mine),
        in_specs=[SM] + [VM] * 5,
        out_specs=VM,
        out_shape=shape((ROWS, half), dtype),
        compiler_params=params(6),
        cost_estimate=cost(2 * ROWS * weight.size // 2, weight.size),
        name="output",
    )(ids, *heads, weight)


def decode_first_kernel(ids, own, other, encoded, weight, inputs, out):
    half = weight.shape[1]

    def mix(i):
        at = lanes(i * TILE, TILE)
        enc = encoded[:, at].astype(F32)
        even, odd = enc[:ROWS], enc[ROWS:]
        binned = (even + odd) * 0.5
        block = (binned + (own[:, at] + other[:, at].astype(F32))).astype(BF16).astype(F32)
        row = lax.broadcasted_iota(jnp.int32, block.shape, 0)
        outside = ((ids[2] == 0) & (row == ROWS - 1)) | ((ids[2] == 63) & (row == OWN))
        even = jnp.where(outside, 0.0, block + even)
        odd = jnp.where(outside, 0.0, block + odd)
        inputs[:, at] = jnp.concatenate([even, odd], axis=0).astype(BF16)

    tiles(half // TILE, mix)
    decode_tiles(inputs, weight, out, (1 - ids[0]) * half)


def decode_tiles(inputs, weight, out, begin):
    def tile(i):
        at = lanes(begin + i * TILE, TILE)
        result = conv_taps(inputs[...], lambda t: weight[t, :, at], ROWS)
        out[:, lanes(i * TILE, TILE)] = result.astype(out.dtype)

    tiles(out.shape[1] // TILE, tile)


def decode_first(ids, own, other, encoded, weight, width):
    half = weight.shape[1]
    return pl.pallas_call(
        decode_first_kernel,
        in_specs=[SM] + [VM] * 4,
        out_specs=[VM] * 2,
        out_shape=[shape((2 * ROWS, half), BF16), shape((2 * ROWS, width), BF16)],
        compiler_params=params(8),
        cost_estimate=cost(2 * 2 * ROWS * 3 * half * width, weight.size),
        name="decode_first",
    )(ids, own, other, encoded, weight)


def decode_kernel(mine, first, ids, inputs, weight, out):
    side = ids[0] if mine else 1 - ids[0]
    decode_tiles(inputs, weight, out, side * weight.shape[1] + first)


def decode(ids, inputs, weight, mine, first, width, dtype):
    half = weight.shape[1]
    return pl.pallas_call(
        functools.partial(decode_kernel, mine, first),
        in_specs=[SM, VM, VM],
        out_specs=VM,
        out_shape=shape((2 * ROWS, width), dtype),
        compiler_params=params(8),
        cost_estimate=cost(2 * 2 * ROWS * 3 * half * width, weight.size),
        name="decode",
    )(ids, inputs, weight)


def slope_kernel(first, ids, own, other, inputs, grad, before, after, *refs):
    done, (decoded, slope, paired, wide) = refs[:-4], refs[-4:]
    half = own.shape[1]
    begin = 0
    if done:
        begin = first
        decoded[:, :first] = done[0][...]

    def tile(i):
        at = lanes(i * 128, 128)
        target = lanes(begin + i * 128, 128)
        source = lanes(first + i * 128, 128)
        column = lanes(ids[0] * half + first + i * 128, 128)
        pre = own[:, source] + other[:, at].astype(F32)
        tanh = gelu_tanh(pre)
        result = inputs[:, source].astype(F32) + 0.5 * pre * (1.0 + tanh)
        wide[0, pl.ds(0, OWN, 2), :] = result[:OWN]
        wide[0, pl.ds(1, OWN, 2), :] = result[ROWS : ROWS + OWN]
        decoded[:, target] = wide[0].astype(BF16)
        slant = 0.5 * (1.0 + tanh) + (0.5 * 0.7978845608028654) * pre * (1.0 - tanh * tanh) * (
            1.0 + (3 * 0.044715) * (pre * pre)
        )
        wide[1] = grad[:, column].astype(F32)
        even = wide[1, pl.ds(0, OWN, 2), :]
        odd = wide[1, pl.ds(1, OWN, 2), :]
        paired[:, at] = even + odd
        row = lax.broadcasted_iota(jnp.int32, (ROWS - OWN, 128), 0)
        even_edge = jnp.where(row == 0, after[:, column].astype(F32), 0.0)
        odd_edge = jnp.where(row == ROWS - OWN - 1, before[:, column].astype(F32), 0.0)
        cotangent = jnp.concatenate([even, even_edge, odd, odd_edge], axis=0)
        slope[:, at] = (cotangent * slant).astype(BF16)

    tiles(other.shape[1] // 128, tile)


def slopes(ids, own, other, inputs, grad, before, after, first, done=()):
    width = other.shape[1]
    return pl.pallas_call(
        functools.partial(slope_kernel, first),
        in_specs=[SM] + [VM] * (6 + len(done)),
        out_specs=[VM] * 3,
        out_shape=[
            shape((2 * OWN, width + (first if done else 0)), BF16),
            shape((2 * ROWS, width), BF16),
            shape((OWN, width), F32),
        ],
        scratch_shapes=[pltpu.VMEM((2, 2 * OWN, 128), F32)],
        compiler_params=params(6),
        cost_estimate=cost(30 * other.size, 14 * other.size),
        name="slopes",
    )(ids, own, other, inputs, grad, before, after, *done)


def backward_kernel(mine, firsts, count, ids, *refs):
    slopes_in, starts, (weight, out, level, lower, upper) = (
        refs[: len(firsts)],
        refs[len(firsts) : len(firsts) + count],
        refs[len(firsts) + count :],
    )
    half = weight.shape[1]
    side = ids[0] if mine else 1 - ids[0]
    level[...] = jnp.zeros_like(level)
    lower[...] = jnp.zeros_like(lower)
    upper[...] = jnp.zeros_like(upper)

    for begin, slope in zip(firsts, slopes_in):

        def tile(i):
            at = lanes(side * half + begin + i * TILE, TILE)
            part = slope[:, lanes(i * TILE, TILE)]
            first, mid, last = (dot_t(part, weight[t, :, at]) for t in range(3))
            level[...] += first[ROWS:] + mid[:ROWS] + mid[ROWS:] + last[:ROWS]
            lower[...] += first[:ROWS]
            upper[...] += last[ROWS:]

        tiles(slope.shape[1] // TILE, tile)
    total = level[...] + below(lower[...], ROWS) + above(upper[...], ROWS)
    base = jnp.concatenate([start[...] for start in starts], axis=1)
    out[...] = (base + total[:OWN]).astype(out.dtype)


def backward(ids, parts, starts, weight, mine, dtype):
    half = weight.shape[1]
    size = sum(part.size for _, part in parts)
    return pl.pallas_call(
        functools.partial(backward_kernel, mine, [first for first, _ in parts], len(starts)),
        in_specs=[SM] + [VM] * (len(parts) + len(starts) + 1),
        out_specs=VM,
        out_shape=shape((OWN, half), dtype),
        scratch_shapes=[pltpu.VMEM((ROWS, half), F32)] * 3,
        compiler_params=params(10),
        cost_estimate=cost(2 * 3 * half * size, 6 * size),
        name="backward",
    )(ids, *[part for _, part in parts], *starts, weight)


def place(at):
    return at // 16, at // 4 % 4, at // 2 % 2, at % 2


def moves(dx=0, dz=0, dy=0, dc=0):
    pairs = []
    for at in range(64):
        x, z, y, c = place(at)
        pairs.append((at, (x + dx) % 4 * 16 + (z + dz) % 4 * 4 + (y ^ dy) * 2 + (c ^ dc)))
    return pairs


def swap(value):
    return lax.ppermute(value, "head", [(0, 1), (1, 0)])


def send(value, **step):
    return lax.ppermute(value, "seq", moves(**step))


def per_device(
    dna_bases,
    stem_weight,
    encoder_weight,
    norm_gain,
    attention_weight,
    logit_scale,
    out_weight,
    decoder_weight,
    grad_out,
):
    at = lax.axis_index("seq")
    x = at // 16
    ids = jnp.stack([lax.axis_index("head"), x, at]).astype(jnp.int32)
    feats = grad_out.shape[1]

    codes, last, first = prepare(dna_bases.reshape(OWN, 128), grad_out)
    before = lax.ppermute(last, "seq", [(i, i + 1) for i in range(63)])
    after = lax.ppermute(first, "seq", [(i + 1, i) for i in range(63)])
    encoded = encode(ids, codes, stem_weight, encoder_weight)
    theirs = swap(encoded)
    edges, attention_weight = encode_edges(
        ids, codes, before, after, stem_weight, encoder_weight, attention_weight
    )
    gain = norm_gain.reshape(1, feats)
    encoded, normed, *keyvals = project_keys(
        ids, encoded, edges, theirs, swap(edges), gain, attention_weight
    )
    queries = project_queries(ids, normed, attention_weight)

    def regroup(blocks):
        got = [blocks[0]] + [send(blocks[d], dx=d) for d in (1, 3, 2)]
        return jnp.concatenate(lax.optimization_barrier(got), axis=0)

    keyvals = regroup(keyvals)
    keyvals, *queries = lax.optimization_barrier((keyvals, *queries))
    near = [send(keyvals, dz=1), send(keyvals, dz=3)]
    queries = regroup(queries)
    others = send(queries, dy=1)
    near[0], near[1], others = lax.optimization_barrier((near[0], near[1], others))
    half = keyvals.shape[0] // 2
    far = [send(near[0][:half], dz=1), send(near[1][half:], dz=3)]
    pieces = [keyvals] + near
    pieces += [send(piece, dc=1) for piece in pieces]
    *state, inverse = attend(ids, logit_scale, others, pieces, final=False)
    *far, state[0], state[1] = lax.optimization_barrier((*far, *state))
    far = jnp.concatenate(far, axis=0)
    late = [far, send(far, dc=1)]
    other, later = attend(ids, logit_scale, others, late, state=state)
    other = send(other, dy=1)
    own = attend(ids, logit_scale, queries, pieces + late, inverses=[inverse, later])[0]
    mixed = merge([own, other])
    heads = [mixed[0], send(mixed[1], dx=-1), send(mixed[3], dx=-2), send(mixed[2], dx=-3)]

    sent = swap(output(ids, heads, out_weight, False, BF16))
    kept = output(ids, heads, out_weight, True, F32)
    half = decoder_weight.shape[1]
    split = half - TILE
    inputs, early = decode_first(ids, kept, sent, encoded, decoder_weight, split)
    early = swap(early)
    late = decode(ids, inputs, decoder_weight, False, split, TILE, BF16)
    late, inputs = lax.optimization_barrier((late, inputs))
    late = swap(late)
    kept = decode(ids, inputs, decoder_weight, True, 0, half, F32)
    decoded, early, paired = slopes(ids, kept, early, inputs, grad_out, before, after, 0)
    early_back = swap(early)
    decoded, late, rest = slopes(
        ids, kept, late, inputs, grad_out, before, after, split, (decoded,)
    )
    late_back = swap(late)
    total = backward(
        ids, [(0, early), (split, late)], [paired, rest], decoder_weight, True, F32
    )
    total = backward(ids, [(0, early_back)], [total], decoder_weight, False, F32)
    bins_grad = backward(ids, [(split, late_back)], [total], decoder_weight, False, BF16)
    return decoded, bins_grad


def solution(mesh):
    in_specs = (
        P("seq"),
        P(),
        P(None, None, "head"),
        P(),
        P(None, None, "head"),
        P("head"),
        P("head", None),
        P(None, "head", None),
        P("seq", None),
    )
    out_specs = (P("seq", "head"), P("seq", "head"))
    return jax.shard_map(
        per_device, mesh=mesh, in_specs=in_specs, out_specs=out_specs, check_vma=False
    )
```

```python
import functools

import jax
import jax.numpy as jnp
from jax import lax
from jax.experimental import pallas as pl
from jax.experimental.pallas import tpu as pltpu
from jax.sharding import PartitionSpec as P

BF16 = jnp.bfloat16
F32 = jnp.float32
ROWS = 136
OWN = 128
TILE = 256
HEAD = 192
EPS = 1e-06
MIB = 1024 * 1024


def params(mib):
    return pltpu.CompilerParams(vmem_limit_bytes=mib * MIB)


def dot(a, b):
    return jnp.dot(a, b, preferred_element_type=F32)


def dot_t(a, b):
    return lax.dot_general(a, b, (((1,), (1,)), ((), ())), preferred_element_type=F32)


def cost(flops, nbytes):
    return pl.CostEstimate(flops=int(flops), bytes_accessed=int(nbytes), transcendentals=0)


def shape(dims, dtype):
    return jax.ShapeDtypeStruct(dims, dtype)


VM = pl.BlockSpec(memory_space=pltpu.VMEM)
SM = pl.BlockSpec(memory_space=pltpu.SMEM)
HBM = pl.BlockSpec(memory_space=pltpu.HBM)


def above(rows, span):
    parts = [pltpu.roll(rows[i : i + span], 1, 0) for i in range(0, rows.shape[0], span)]
    return jnp.concatenate(parts, axis=0)


def below(rows, span):
    parts = [pltpu.roll(rows[i : i + span], span - 1, 0) for i in range(0, rows.shape[0], span)]
    return jnp.concatenate(parts, axis=0)


def lanes(at, size):
    return pl.ds(pl.multiple_of(at, size), size)


def tiles(count, body):
    lax.fori_loop(0, count, lambda i, carry: (body(i), carry)[1], 0)


def gelu_tanh(x):
    return jnp.tanh(0.7978845608028654 * (x + 0.044715 * (x * x * x)))


def conv_taps(rows, weight, span):
    half = rows.shape[0] // 2
    first, mid, last = (dot(rows, weight(t)) for t in range(3))
    even = above(first[half:], span) + mid[:half] + last[half:]
    odd = first[:half] + mid[half:] + below(last[:half], span)
    return jnp.concatenate([even, odd], axis=0)


def prepare_kernel(bases, grad, codes, last, first, code, head, tail, sems):
    rows = grad.shape[0]
    copies = [
        pltpu.make_async_copy(bases, code, sems.at[0]),
        pltpu.make_async_copy(grad.at[pl.ds(0, 16)], head, sems.at[1]),
        pltpu.make_async_copy(grad.at[pl.ds(rows - 16, 16)], tail, sems.at[2]),
    ]
    for copy in copies:
        copy.start()
    for copy in copies:
        copy.wait()
    feats = grad.shape[1]
    letters = (code[...] + 1).astype(F32)
    codes[...] = letters.astype(BF16)
    last[:, :feats] = tail[...].astype(F32)[8:].astype(BF16)
    last[:, feats:] = letters[OWN - 8 :].astype(BF16)
    first[:, :feats] = head[...].astype(F32)[:8].astype(BF16)
    first[:, feats:] = letters[:8].astype(BF16)


def near_memory(value):
    return pltpu.with_memory_space_constraint(value, pltpu.VMEM)


def far_memory(value):
    return pltpu.with_memory_space_constraint(value, pltpu.HBM)


def prepare(bases, grad):
    feats = grad.shape[1]
    return pl.pallas_call(
        prepare_kernel,
        in_specs=[HBM, HBM],
        out_specs=[VM] * 3,
        out_shape=[
            shape((OWN, 128), BF16),
            shape((8, feats + 128), BF16),
            shape((8, feats + 128), BF16),
        ],
        scratch_shapes=[
            pltpu.VMEM(bases.shape, jnp.int32),
            pltpu.VMEM((16, feats), BF16),
            pltpu.VMEM((16, feats), BF16),
            pltpu.SemaphoreType.DMA((3,)),
        ],
        compiler_params=params(4),
        cost_estimate=cost(10**5, 10**5),
        name="prepare",
    )(far_memory(bases), far_memory(grad))


def load_kernel(*refs):
    count = len(refs) // 2
    sources, targets, sems = refs[:count], refs[count : 2 * count], refs[-1]
    copies = [
        pltpu.make_async_copy(source, target, sems.at[i])
        for i, (source, target) in enumerate(zip(sources, targets))
    ]
    for copy in copies:
        copy.start()
    for copy in copies:
        copy.wait()


def load(*values):
    return pl.pallas_call(
        load_kernel,
        in_specs=[HBM] * len(values),
        out_specs=[VM] * len(values),
        out_shape=[pltpu.VMEM(value.shape, value.dtype) for value in values],
        scratch_shapes=[pltpu.SemaphoreType.DMA((len(values),))],
        compiler_params=params(2),
        cost_estimate=cost(10**5, sum(value.size for value in values) * 2),
        name="load",
    )(*[far_memory(value) for value in values])


def encode_kernel(ids, codes, before, after, stem, weight, ahead, encoded, loaded, embedded, sem):
    copy = pltpu.make_async_copy(ahead, loaded, sem)
    copy.start()
    patch = stem.shape[0] // 4
    feats = stem.shape[1]
    half = weight.shape[2]
    row = lax.broadcasted_iota(jnp.int32, (2 * patch, 4 * patch), 0)
    col = lax.broadcasted_iota(jnp.int32, (2 * patch, 4 * patch), 1)
    place = lax.broadcasted_iota(jnp.int32, (ROWS - OWN, 128), 0)
    halo = jnp.where(place >= 6, before[:, feats:].astype(F32), 0.0)
    halo = jnp.where(place < 2, after[:, feats:].astype(F32), halo)
    code = jnp.concatenate([codes[...].astype(F32), halo], axis=0).astype(BF16)
    spread = [
        dot(code, (row == col // 4 + offset).astype(F32).astype(BF16)) for offset in (0, patch)
    ]
    spread = jnp.concatenate(spread, axis=0)
    base = lax.broadcasted_iota(jnp.int32, spread.shape, 1) % 4 + 1
    onehot = (spread == base.astype(F32)).astype(F32).astype(BF16)

    def embed(i):
        at = lanes(i * TILE, TILE)
        embedded[:, at] = dot(onehot, stem[:, at]).astype(BF16)

    tiles(feats // TILE, embed)

    def convolve(i):
        at = lanes(i * TILE, TILE)
        pre = conv_taps(embedded[...], lambda t: weight[t, :, at], ROWS)
        mine = embedded[:, lanes(ids[0] * half + i * TILE, TILE)].astype(F32)
        encoded[:, at] = (mine + 0.5 * pre * (1.0 + gelu_tanh(pre))).astype(BF16)

    tiles(half // TILE, convolve)
    copy.wait()


def encode(ids, codes, before, after, stem, weight, ahead):
    half = weight.shape[2]
    feats = stem.shape[1]
    return pl.pallas_call(
        encode_kernel,
        in_specs=[SM] + [VM] * 5 + [HBM],
        out_specs=[VM, VM],
        out_shape=[shape((2 * ROWS, half), BF16), pltpu.VMEM(ahead.shape, BF16)],
        scratch_shapes=[pltpu.VMEM((2 * ROWS, feats), BF16), pltpu.SemaphoreType.DMA(())],
        compiler_params=params(12),
        cost_estimate=cost(2 * 2 * ROWS * 3 * feats * half, weight.size * 4),
        name="encode",
    )(ids, codes, before, after, near_memory(stem), near_memory(weight), far_memory(ahead))


def unpacked(both):
    both = both.astype(BF16).astype(F32)
    turned = pltpu.roll(both, 2 * HEAD - 64, 1)
    return (both[:, :128], both[:, 128:256]), (turned[:, 128:256], turned[:, 256:384])


def project_keys_kernel(
    ids, mine, theirs, gain, weight, normed, k0, k1, k2, k3, packed
):
    half = mine.shape[1]
    near = lanes(ids[0] * half, half)
    far = lanes((1 - ids[0]) * half, half)
    rings = [ref[...].astype(F32) for ref in (mine, theirs)]
    binned = [(ring[:ROWS] + ring[ROWS:]) * 0.5 for ring in rings]
    total = sum(jnp.sum(part * part, axis=1, keepdims=True) for part in binned)
    inverse = lax.rsqrt(total * (1.0 / (2 * half)) + EPS)
    here = (binned[0] * inverse * gain[:, near]).astype(BF16)
    there = (binned[1] * inverse * gain[:, far]).astype(BF16)
    normed[0] = here
    normed[1] = there
    low = lax.broadcasted_iota(jnp.int32, (ROWS, 128), 1) < 64
    for pair in range(2):
        at = slice(pair * 2 * HEAD, (pair + 1) * 2 * HEAD)
        keys, values = (
            unpacked(dot(here, weight[kind, near, at]) + dot(there, weight[kind, far, at]))
            for kind in (1, 2)
        )
        for side in range(2):
            head = 2 * pair + side
            key, value = keys[side], values[side]
            packed[head, :, :128] = key[0].astype(BF16)
            packed[head, :, 128:256] = value[0].astype(BF16)
            tail = jnp.where(low, key[1], pltpu.roll(value[1], 64, 1))
            packed[head, :, 256:] = tail.astype(BF16)
    for distance, out in enumerate((k0, k1, k2, k3)):
        out[...] = packed[lax.rem(ids[1] + distance, 4), :OWN, :]


def project_keys(ids, mine, theirs, gain, weight):
    half = mine.shape[1]
    return pl.pallas_call(
        project_keys_kernel,
        in_specs=[SM] + [VM] * 4,
        out_specs=[VM] * 5,
        out_shape=[shape((2, ROWS, half), BF16)] + [shape((OWN, 384), BF16)] * 4,
        scratch_shapes=[pltpu.VMEM((4, ROWS, 384), BF16)],
        compiler_params=params(12),
        cost_estimate=cost(2 * ROWS * weight.size * 2 // 3, weight.size * 2),
        name="project_keys",
    )(ids, mine, theirs, gain, weight)


def project_queries_kernel(ids, normed, weight, q0, q1, q2, q3, packed):
    half = normed.shape[2]
    near = lanes(ids[0] * half, half)
    far = lanes((1 - ids[0]) * half, half)
    low = lax.broadcasted_iota(jnp.int32, (ROWS, 128), 1) < 64
    for pair in range(2):
        at = slice(pair * 2 * HEAD, (pair + 1) * 2 * HEAD)
        both = dot(normed[0], weight[0, near, at]) + dot(normed[1], weight[0, far, at])
        for side, query in enumerate(unpacked(both)):
            packed[2 * pair + side, :, :128] = query[0].astype(BF16)
            packed[2 * pair + side, :, 128:] = jnp.where(low, query[1], 0.0).astype(BF16)
    for distance, out in enumerate((q0, q1, q2, q3)):
        out[...] = packed[lax.rem(ids[1] + distance, 4)]


def project_queries(ids, normed, weight):
    return pl.pallas_call(
        project_queries_kernel,
        in_specs=[SM, VM, VM],
        out_specs=[VM] * 4,
        out_shape=[shape((ROWS, 256), BF16)] * 4,
        scratch_shapes=[pltpu.VMEM((4, ROWS, 256), BF16)],
        compiler_params=params(10),
        cost_estimate=cost(2 * ROWS * weight.size // 3, weight.size),
        name="project_queries",
    )(ids, normed, near_memory(weight))


BLOCK = 2 * ROWS
LOG2E = 1.4426950408889634


def attend_kernel(count, known, resumed, final, ids, scale, queries, *refs):
    pieces, refs = refs[:count], refs[count:]
    inverses, refs = refs[:known], refs[known:]
    if resumed:
        (old_mixed, old_stats), refs = refs[:2], refs[2:]
    sizes = [ref.shape[0] for ref in pieces]
    starts = [sum(sizes[:i]) for i in range(count)]

    def keys(ref):
        return jnp.concatenate([ref[:, :128], ref[:, 256:]], axis=1)

    if not known:
        outs, inverse = refs[:-1], refs[-1]
        lane = lax.broadcasted_iota(jnp.int32, (8, 256), 1)
        ones = (lane < HEAD).astype(F32).astype(BF16)
        for at, size, ref in zip(starts, sizes, pieces):
            key = keys(ref).astype(F32)
            square = key * key
            high = square.astype(BF16)
            rest = (square - high.astype(F32)).astype(BF16)
            total = dot_t(ones, high) + dot_t(ones, rest)
            inverse[:, at : at + size] = lax.rsqrt(total * (1.0 / HEAD) + EPS)
        inverses = (inverse,)
    else:
        outs = refs

    def inverse_of(at, size):
        for ref in inverses:
            if at < ref.shape[1]:
                return ref[0:1, at : at + size]
            at -= ref.shape[1]

    limit = min(1024, starts[-1])
    groups, room = [], 0
    for triple in zip(starts, sizes, pieces):
        if room < triple[1]:
            groups.append([])
            room = limit
        groups[-1].append(triple)
        room -= triple[1]

    def unit(query, factor, group):
        scores, peak = [], None
        for at, size, ref in group:
            part = dot_t(query, keys(ref)) * inverse_of(at, size)
            top = jnp.max(part, axis=1, keepdims=True)
            peak = top if peak is None else jnp.maximum(peak, top)
            scores.append(part)
        total, mixed = None, None
        for part, (_, _, ref) in zip(scores, group):
            exps = jnp.exp2((part - peak) * factor)
            sums = jnp.sum(exps, axis=1, keepdims=True)
            values = jnp.concatenate([ref[:, 128:256], ref[:, 256:]], axis=1)
            term = dot(exps.astype(BF16), values)
            total = sums if total is None else total + sums
            mixed = term if mixed is None else mixed + term
        return peak, total, mixed

    for begin in range(0, queries.shape[0], BLOCK):
        rows = slice(begin, begin + BLOCK)
        query = queries[rows, :]
        wide = query.astype(F32)
        own = lax.rsqrt(jnp.sum(wide * wide, axis=1, keepdims=True) * (1.0 / HEAD) + EPS)
        factor = own * (scale[ids[1]] * (LOG2E / HEAD))
        states = [unit(query, factor, group) for group in groups]
        if resumed:
            states.append((old_stats[rows, 0:1], old_stats[rows, 64:65], old_mixed[rows, :]))
        peak = functools.reduce(jnp.maximum, [state[0] for state in states])
        if len(states) > 1:
            shrink = [jnp.exp2((state[0] - peak) * factor) for state in states]
            total = sum(state[1] * part for state, part in zip(states, shrink))
            mixed = sum(state[2] * part for state, part in zip(states, shrink))
        else:
            _, total, mixed = states[0]
        if not final:
            outs[0][rows, :] = mixed
            half = lax.broadcasted_iota(jnp.int32, (BLOCK, 128), 1) < 64
            outs[1][rows, :] = jnp.where(half, peak, total)
            continue
        mixed = mixed / total
        weight = peak * factor + jnp.log(total) * LOG2E
        high = weight.astype(BF16).astype(F32)
        rest = weight - high
        mid = rest.astype(BF16).astype(F32)
        place = lax.broadcasted_iota(jnp.int32, mixed.shape, 1)
        mixed = jnp.where(place == 128, high, mixed)
        mixed = jnp.where(place == 129, mid, mixed)
        mixed = jnp.where(place == 130, rest - mid, mixed)
        outs[0][rows, :] = mixed.astype(BF16)


def attend(ids, scale, queries, pieces, inverses=(), state=(), final=True):
    rows = queries.shape[0]
    keys = sum(piece.shape[0] for piece in pieces)
    if final:
        outs = [shape((rows, 256), BF16)]
    else:
        outs = [shape((rows, 256), F32), shape((rows, 128), F32)]
    if not inverses:
        outs.append(shape((8, keys), F32))
    return pl.pallas_call(
        functools.partial(attend_kernel, len(pieces), len(inverses), bool(state), final),
        in_specs=[SM, SM] + [VM] * (1 + len(pieces) + len(inverses) + len(state)),
        out_specs=[VM] * len(outs),
        out_shape=outs,
        compiler_params=params(28),
        cost_estimate=cost(4 * rows * keys * 256, 8 * rows * 1024),
        name="attend",
    )(ids, scale, near_memory(queries), *pieces, *inverses, *state)


def merge_kernel(a0, a1, *outs):
    parts = [ref[...].astype(F32) for ref in (a0, a1)]
    logs = [p[:, 128:129] + p[:, 129:130] + p[:, 130:131] for p in parts]
    peak = functools.reduce(jnp.maximum, logs)
    shares = [jnp.exp2(log - peak) for log in logs]
    total = sum(shares)
    mixed = sum(p * (share / total) for p, share in zip(parts, shares))
    mixed = jnp.concatenate([mixed[:, :128], pltpu.roll(mixed[:, 128:], 64, 1)], axis=1)
    for block in range(4):
        outs[block][...] = mixed[block * ROWS : (block + 1) * ROWS].astype(BF16)


def merge(parts):
    return pl.pallas_call(
        merge_kernel,
        in_specs=[VM] * 2,
        out_specs=[VM] * 4,
        out_shape=[shape((ROWS, 256), BF16)] * 4,
        compiler_params=params(8),
        cost_estimate=cost(20 * parts[0].size, 10 * parts[0].size),
        name="merge",
    )(*parts)


def output_kernel(mine, ids, a0, a1, a2, a3, weight, out):
    half = out.shape[1]
    side = ids[0] if mine else 1 - ids[0]

    def tile(i):
        at = lanes(side * half + i * TILE, TILE)
        total = None
        for distance, ref in enumerate((a0, a1, a2, a3)):
            head = lax.rem(ids[1] + distance, 4)
            rows = weight[pl.ds(pl.multiple_of(head * HEAD, HEAD), HEAD), at]
            term = dot(ref[:, :HEAD], rows)
            total = term if total is None else total + term
        out[:, lanes(i * TILE, TILE)] = total.astype(out.dtype)

    tiles(half // TILE, tile)


def output(ids, heads, weight, mine, dtype):
    half = weight.shape[1] // 2
    return pl.pallas_call(
        functools.partial(output_kernel, mine),
        in_specs=[SM] + [VM] * 5,
        out_specs=VM,
        out_shape=shape((ROWS, half), dtype),
        compiler_params=params(6),
        cost_estimate=cost(2 * ROWS * weight.size // 2, weight.size),
        name="output",
    )(ids, *heads, weight)


def decode_first_kernel(ids, own, other, encoded, weight, inputs, out):
    half = weight.shape[1]

    def mix(i):
        at = lanes(i * TILE, TILE)
        enc = encoded[:, at].astype(F32)
        even, odd = enc[:ROWS], enc[ROWS:]
        binned = (even + odd) * 0.5
        block = (binned + (own[:, at] + other[:, at].astype(F32))).astype(BF16).astype(F32)
        row = lax.broadcasted_iota(jnp.int32, block.shape, 0)
        outside = ((ids[2] == 0) & (row == ROWS - 1)) | ((ids[2] == 63) & (row == OWN))
        even = jnp.where(outside, 0.0, block + even)
        odd = jnp.where(outside, 0.0, block + odd)
        inputs[:, at] = jnp.concatenate([even, odd], axis=0).astype(BF16)

    tiles(half // TILE, mix)
    decode_tiles(inputs, weight, out, (1 - ids[0]) * half)


def decode_tiles(inputs, weight, out, begin):
    def tile(i):
        at = lanes(begin + i * TILE, TILE)
        result = conv_taps(inputs[...], lambda t: weight[t, :, at], ROWS)
        out[:, lanes(i * TILE, TILE)] = result.astype(out.dtype)

    tiles(out.shape[1] // TILE, tile)


def decode_first(ids, own, other, encoded, weight, width):
    half = weight.shape[1]
    return pl.pallas_call(
        decode_first_kernel,
        in_specs=[SM] + [VM] * 4,
        out_specs=[VM] * 2,
        out_shape=[shape((2 * ROWS, half), BF16), shape((2 * ROWS, width), BF16)],
        compiler_params=params(8),
        cost_estimate=cost(10**6, 10**4),
        name="decode_first",
    )(ids, own, other, encoded, weight)


def decode_kernel(mine, first, ids, inputs, weight, out):
    side = ids[0] if mine else 1 - ids[0]
    decode_tiles(inputs, weight, out, side * weight.shape[1] + first)


def decode(ids, inputs, weight, mine, first, width, dtype):
    half = weight.shape[1]
    return pl.pallas_call(
        functools.partial(decode_kernel, mine, first),
        in_specs=[SM, VM, VM],
        out_specs=VM,
        out_shape=shape((2 * ROWS, width), dtype),
        compiler_params=params(8),
        cost_estimate=cost(10**6, 10**4),
        name="decode",
    )(ids, inputs, weight)


def slope_kernel(first, ids, own, other, inputs, grad, before, after, *refs):
    done, (decoded, slope, paired, wide) = refs[:-4], refs[-4:]
    half = own.shape[1]
    begin = 0
    if done:
        begin = first
        decoded[:, :first] = done[0][...]

    def tile(i):
        at = lanes(i * 128, 128)
        target = lanes(begin + i * 128, 128)
        source = lanes(first + i * 128, 128)
        column = lanes(ids[0] * half + first + i * 128, 128)
        pre = own[:, source] + other[:, at].astype(F32)
        tanh = gelu_tanh(pre)
        result = inputs[:, source].astype(F32) + 0.5 * pre * (1.0 + tanh)
        wide[0, pl.ds(0, OWN, 2), :] = result[:OWN]
        wide[0, pl.ds(1, OWN, 2), :] = result[ROWS : ROWS + OWN]
        decoded[:, target] = wide[0].astype(BF16)
        slant = 0.5 * (1.0 + tanh) + (0.5 * 0.7978845608028654) * pre * (1.0 - tanh * tanh) * (
            1.0 + (3 * 0.044715) * (pre * pre)
        )
        wide[1] = grad[:, column].astype(F32)
        even = wide[1, pl.ds(0, OWN, 2), :]
        odd = wide[1, pl.ds(1, OWN, 2), :]
        paired[:, at] = even + odd
        row = lax.broadcasted_iota(jnp.int32, (ROWS - OWN, 128), 0)
        even_edge = jnp.where(row == 0, after[:, column].astype(F32), 0.0)
        odd_edge = jnp.where(row == ROWS - OWN - 1, before[:, column].astype(F32), 0.0)
        cotangent = jnp.concatenate([even, even_edge, odd, odd_edge], axis=0)
        slope[:, at] = (cotangent * slant).astype(BF16)

    tiles(other.shape[1] // 128, tile)


def slopes(ids, own, other, inputs, grad, before, after, first, done=()):
    width = other.shape[1]
    return pl.pallas_call(
        functools.partial(slope_kernel, first),
        in_specs=[SM] + [VM] * (6 + len(done)),
        out_specs=[VM] * 3,
        out_shape=[
            shape((2 * OWN, width + (first if done else 0)), BF16),
            shape((2 * ROWS, width), BF16),
            shape((OWN, width), F32),
        ],
        scratch_shapes=[pltpu.VMEM((2, 2 * OWN, 128), F32)],
        compiler_params=params(6),
        cost_estimate=cost(100 * 30 * 1000 * other.size, 14 * other.size),
        name="slopes",
    )(ids, own, other, inputs, grad, before, after, *done)


def backward_kernel(mine, firsts, count, ids, *refs):
    slopes_in, starts, (weight, out, level, lower, upper) = (
        refs[: len(firsts)],
        refs[len(firsts) : len(firsts) + count],
        refs[len(firsts) + count :],
    )
    half = weight.shape[1]
    side = ids[0] if mine else 1 - ids[0]
    level[...] = jnp.zeros_like(level)
    lower[...] = jnp.zeros_like(lower)
    upper[...] = jnp.zeros_like(upper)

    for begin, slope in zip(firsts, slopes_in):

        def tile(i):
            at = lanes(side * half + begin + i * TILE, TILE)
            part = slope[:, lanes(i * TILE, TILE)]
            first, mid, last = (dot_t(part, weight[t, :, at]) for t in range(3))
            level[...] += first[ROWS:] + mid[:ROWS] + mid[ROWS:] + last[:ROWS]
            lower[...] += first[:ROWS]
            upper[...] += last[ROWS:]

        tiles(slope.shape[1] // TILE, tile)
    total = level[...] + below(lower[...], ROWS) + above(upper[...], ROWS)
    base = jnp.concatenate([start[...] for start in starts], axis=1)
    out[...] = (base + total[:OWN]).astype(out.dtype)


def backward(ids, parts, starts, weight, mine, dtype):
    half = weight.shape[1]
    size = sum(part.size for _, part in parts)
    return pl.pallas_call(
        functools.partial(backward_kernel, mine, [first for first, _ in parts], len(starts)),
        in_specs=[SM] + [VM] * (len(parts) + len(starts) + 1),
        out_specs=VM,
        out_shape=shape((OWN, half), dtype),
        scratch_shapes=[pltpu.VMEM((ROWS, half), F32)] * 3,
        compiler_params=params(10),
        cost_estimate=cost(100 * 2 * 3 * half * size, 6 * size),
        name="backward",
    )(ids, *[part for _, part in parts], *starts, weight)


def place(at):
    return at // 16, at // 4 % 4, at // 2 % 2, at % 2


def moves(dx=0, dz=0, dy=0, dc=0):
    pairs = []
    for at in range(64):
        x, z, y, c = place(at)
        pairs.append((at, (x + dx) % 4 * 16 + (z + dz) % 4 * 4 + (y ^ dy) * 2 + (c ^ dc)))
    return pairs


def swap(value):
    return lax.ppermute(value, "head", [(0, 1), (1, 0)])


def send(value, **step):
    return lax.ppermute(value, "seq", moves(**step))


def per_device(
    dna_bases,
    stem_weight,
    encoder_weight,
    norm_gain,
    attention_weight,
    logit_scale,
    out_weight,
    decoder_weight,
    grad_out,
):
    at = lax.axis_index("seq")
    x = at // 16
    ids = jnp.stack([lax.axis_index("head"), x, at]).astype(jnp.int32)
    feats = grad_out.shape[1]

    codes, last, first = prepare(dna_bases.reshape(OWN, 128), grad_out)
    before = lax.ppermute(last, "seq", [(i, i + 1) for i in range(63)])
    after = lax.ppermute(first, "seq", [(i + 1, i) for i in range(63)])
    stem_weight, encoder_weight = load(stem_weight, encoder_weight)
    encoded, attention_weight = encode(
        ids, codes, before, after, stem_weight, encoder_weight, attention_weight
    )
    gain = norm_gain.reshape(1, feats)
    normed, *keyvals = project_keys(ids, encoded, swap(encoded), gain, attention_weight)

    def spread(blocks):
        return [send(blocks[d], dx=d) for d in (1, 3, 2)]

    def stacked(blocks):
        return jnp.concatenate(lax.optimization_barrier(blocks), axis=0)

    got = spread(keyvals)
    got[0], normed = lax.optimization_barrier((got[0], normed))
    queries = project_queries(ids, normed, attention_weight)
    others = spread(queries)
    keyvals = stacked([keyvals[0]] + got)
    near = [send(keyvals, dz=1), send(keyvals, dz=3)]
    queries = stacked([queries[0]] + others)
    others = send(queries, dy=1)
    near[0], near[1], others = lax.optimization_barrier((near[0], near[1], others))
    half = keyvals.shape[0] // 2
    far = [send(near[0][:half], dz=1), send(near[1][half:], dz=3)]
    pieces = [keyvals] + near
    pieces += [send(piece, dc=1) for piece in pieces]
    *state, inverse = attend(ids, logit_scale, others, pieces, final=False)
    *far, state[0], state[1] = lax.optimization_barrier((*far, *state))
    far = jnp.concatenate(far, axis=0)
    late = [far, send(far, dc=1)]
    other, later = attend(ids, logit_scale, others, late, state=state)
    other = send(other, dy=1)
    own = attend(ids, logit_scale, queries, pieces + late, inverses=[inverse, later])[0]
    mixed = merge([own, other])
    heads = [mixed[0], send(mixed[1], dx=-1), send(mixed[3], dx=-2), send(mixed[2], dx=-3)]

    sent = swap(output(ids, heads, out_weight, False, BF16))
    kept = output(ids, heads, out_weight, True, F32)
    half = decoder_weight.shape[1]
    split = 2 * TILE
    inputs, early = decode_first(ids, kept, sent, encoded, decoder_weight, split)
    early = swap(early)
    late = decode(ids, inputs, decoder_weight, False, split, half - split, BF16)
    late, inputs = lax.optimization_barrier((late, inputs))
    late = swap(late)
    kept = decode(ids, inputs, decoder_weight, True, 0, half, F32)
    decoded, early, paired = slopes(ids, kept, early, inputs, grad_out, before, after, 0)
    early_back = swap(early)
    decoded, late, rest = slopes(
        ids, kept, late, inputs, grad_out, before, after, split, (decoded,)
    )
    late_back = swap(late)
    total = backward(
        ids, [(0, early), (split, late)], [paired, rest], decoder_weight, True, F32
    )
    total = backward(ids, [(0, early_back)], [total], decoder_weight, False, F32)
    bins_grad = backward(ids, [(split, late_back)], [total], decoder_weight, False, BF16)
    return decoded, bins_grad


def solution(mesh):
    in_specs = (
        P("seq"),
        P(),
        P(None, None, "head"),
        P(),
        P(None, None, "head"),
        P("head"),
        P("head", None),
        P(None, "head", None),
        P("seq", None),
    )
    out_specs = (P("seq", "head"), P("seq", "head"))
    return jax.shard_map(
        per_device, mesh=mesh, in_specs=in_specs, out_specs=out_specs, check_vma=False
    )
```

```python
import functools

import jax
import jax.numpy as jnp
from jax import lax
from jax.experimental import pallas as pl
from jax.experimental.pallas import tpu as pltpu
from jax.sharding import PartitionSpec as P

BF16 = jnp.bfloat16
F32 = jnp.float32
ROWS = 136
OWN = 128
TILE = 256
HEAD = 192
EPS = 1e-06
MIB = 1024 * 1024


def params(mib):
    return pltpu.CompilerParams(vmem_limit_bytes=mib * MIB)


def dot(a, b):
    return jnp.dot(a, b, preferred_element_type=F32)


def dot_t(a, b):
    return lax.dot_general(a, b, (((1,), (1,)), ((), ())), preferred_element_type=F32)


def cost(flops, nbytes):
    return pl.CostEstimate(flops=int(flops), bytes_accessed=int(nbytes), transcendentals=0)


def shape(dims, dtype):
    return jax.ShapeDtypeStruct(dims, dtype)


VM = pl.BlockSpec(memory_space=pltpu.VMEM)
SM = pl.BlockSpec(memory_space=pltpu.SMEM)
HBM = pl.BlockSpec(memory_space=pltpu.HBM)


def above(rows, span):
    parts = [pltpu.roll(rows[i : i + span], 1, 0) for i in range(0, rows.shape[0], span)]
    return jnp.concatenate(parts, axis=0)


def below(rows, span):
    parts = [pltpu.roll(rows[i : i + span], span - 1, 0) for i in range(0, rows.shape[0], span)]
    return jnp.concatenate(parts, axis=0)


def lanes(at, size):
    return pl.ds(pl.multiple_of(at, size), size)


def tiles(count, body):
    lax.fori_loop(0, count, lambda i, carry: (body(i), carry)[1], 0)


def gelu_tanh(x):
    return jnp.tanh(0.7978845608028654 * (x + 0.044715 * (x * x * x)))


def conv_taps(rows, weight, span):
    half = rows.shape[0] // 2
    first, mid, last = (dot(rows, weight(t)) for t in range(3))
    even = above(first[half:], span) + mid[:half] + last[half:]
    odd = first[:half] + mid[half:] + below(last[:half], span)
    return jnp.concatenate([even, odd], axis=0)


def prepare_kernel(ids, bases, grad, codes, near, far, code, head, tail, sems):
    rows = grad.shape[0]
    copies = [
        pltpu.make_async_copy(bases, code, sems.at[0]),
        pltpu.make_async_copy(grad.at[pl.ds(0, 16)], head, sems.at[1]),
        pltpu.make_async_copy(grad.at[pl.ds(rows - 16, 16)], tail, sems.at[2]),
    ]
    for copy in copies:
        copy.start()
    for copy in copies:
        copy.wait()
    feats = grad.shape[1]
    letters = (code[...] + 1).astype(F32)
    codes[...] = letters.astype(BF16)
    odd = lax.rem(ids[2], 2) == 1
    last = jnp.concatenate([tail[...].astype(F32)[8:], letters[OWN - 8 :]], axis=1)
    first = jnp.concatenate([head[...].astype(F32)[:8], letters[:8]], axis=1)
    near[...] = jnp.where(odd, first, last).astype(BF16)
    far[...] = jnp.where(odd, last, first).astype(BF16)


def near_memory(value):
    return pltpu.with_memory_space_constraint(value, pltpu.VMEM)


def far_memory(value):
    return pltpu.with_memory_space_constraint(value, pltpu.HBM)


def prepare(ids, bases, grad):
    feats = grad.shape[1]
    return pl.pallas_call(
        prepare_kernel,
        in_specs=[SM, HBM, HBM],
        out_specs=[VM] * 3,
        out_shape=[
            shape((OWN, 128), BF16),
            shape((8, feats + 128), BF16),
            shape((8, feats + 128), BF16),
        ],
        scratch_shapes=[
            pltpu.VMEM(bases.shape, jnp.int32),
            pltpu.VMEM((16, feats), BF16),
            pltpu.VMEM((16, feats), BF16),
            pltpu.SemaphoreType.DMA((3,)),
        ],
        compiler_params=params(4),
        cost_estimate=cost(10**5, 10**5),
        name="prepare",
    )(ids, far_memory(bases), far_memory(grad))


def load_kernel(*refs):
    count = len(refs) // 2
    sources, targets, sems = refs[:count], refs[count : 2 * count], refs[-1]
    copies = [
        pltpu.make_async_copy(source, target, sems.at[i])
        for i, (source, target) in enumerate(zip(sources, targets))
    ]
    for copy in copies:
        copy.start()
    for copy in copies:
        copy.wait()


def load(*values):
    return pl.pallas_call(
        load_kernel,
        in_specs=[HBM] * len(values),
        out_specs=[VM] * len(values),
        out_shape=[pltpu.VMEM(value.shape, value.dtype) for value in values],
        scratch_shapes=[pltpu.SemaphoreType.DMA((len(values),))],
        compiler_params=params(2),
        cost_estimate=cost(10**5, sum(value.size for value in values) * 2),
        name="load",
    )(*[far_memory(value) for value in values])


def encode_kernel(ids, codes, before, after, stem, weight, ahead, encoded, loaded, embedded, sem):
    copy = pltpu.make_async_copy(ahead, loaded, sem)
    copy.start()
    patch = stem.shape[0] // 4
    feats = stem.shape[1]
    half = weight.shape[2]
    row = lax.broadcasted_iota(jnp.int32, (2 * patch, 4 * patch), 0)
    col = lax.broadcasted_iota(jnp.int32, (2 * patch, 4 * patch), 1)
    place = lax.broadcasted_iota(jnp.int32, (ROWS - OWN, 128), 0)
    halo = jnp.where(place >= 6, before[:, feats:].astype(F32), 0.0)
    halo = jnp.where(place < 2, after[:, feats:].astype(F32), halo)
    code = jnp.concatenate([codes[...].astype(F32), halo], axis=0).astype(BF16)
    spread = [
        dot(code, (row == col // 4 + offset).astype(F32).astype(BF16)) for offset in (0, patch)
    ]
    spread = jnp.concatenate(spread, axis=0)
    base = lax.broadcasted_iota(jnp.int32, spread.shape, 1) % 4 + 1
    onehot = (spread == base.astype(F32)).astype(F32).astype(BF16)

    def embed(i):
        at = lanes(i * TILE, TILE)
        embedded[:, at] = dot(onehot, stem[:, at]).astype(BF16)

    tiles(feats // TILE, embed)

    def convolve(i):
        at = lanes(i * TILE, TILE)
        pre = conv_taps(embedded[...], lambda t: weight[t, :, at], ROWS)
        mine = embedded[:, lanes(ids[0] * half + i * TILE, TILE)].astype(F32)
        encoded[:, at] = (mine + 0.5 * pre * (1.0 + gelu_tanh(pre))).astype(BF16)

    tiles(half // TILE, convolve)
    copy.wait()


def encode(ids, codes, before, after, stem, weight, ahead):
    half = weight.shape[2]
    feats = stem.shape[1]
    return pl.pallas_call(
        encode_kernel,
        in_specs=[SM] + [VM] * 5 + [HBM],
        out_specs=[VM, VM],
        out_shape=[shape((2 * ROWS, half), BF16), pltpu.VMEM(ahead.shape, BF16)],
        scratch_shapes=[pltpu.VMEM((2 * ROWS, feats), BF16), pltpu.SemaphoreType.DMA(())],
        compiler_params=params(12),
        cost_estimate=cost(2 * 2 * ROWS * 3 * feats * half, weight.size * 4),
        name="encode",
    )(ids, codes, before, after, near_memory(stem), near_memory(weight), far_memory(ahead))


def unpacked(both):
    both = both.astype(BF16).astype(F32)
    turned = pltpu.roll(both, 2 * HEAD - 64, 1)
    return (both[:, :128], both[:, 128:256]), (turned[:, 128:256], turned[:, 256:384])


def project_keys_kernel(
    ids, mine, theirs, gain, weight, normed, k0, k1, k2, k3, packed
):
    half = mine.shape[1]
    near = lanes(ids[0] * half, half)
    far = lanes((1 - ids[0]) * half, half)
    rings = [ref[...].astype(F32) for ref in (mine, theirs)]
    binned = [(ring[:ROWS] + ring[ROWS:]) * 0.5 for ring in rings]
    total = sum(jnp.sum(part * part, axis=1, keepdims=True) for part in binned)
    inverse = lax.rsqrt(total * (1.0 / (2 * half)) + EPS)
    here = (binned[0] * inverse * gain[:, near]).astype(BF16)
    there = (binned[1] * inverse * gain[:, far]).astype(BF16)
    normed[0] = here
    normed[1] = there
    low = lax.broadcasted_iota(jnp.int32, (ROWS, 128), 1) < 64
    for pair in range(2):
        at = slice(pair * 2 * HEAD, (pair + 1) * 2 * HEAD)
        keys, values = (
            unpacked(dot(here, weight[kind, near, at]) + dot(there, weight[kind, far, at]))
            for kind in (1, 2)
        )
        for side in range(2):
            head = 2 * pair + side
            key, value = keys[side], values[side]
            packed[head, :, :128] = key[0].astype(BF16)
            packed[head, :, 128:256] = value[0].astype(BF16)
            tail = jnp.where(low, key[1], pltpu.roll(value[1], 64, 1))
            packed[head, :, 256:] = tail.astype(BF16)
    for distance, out in enumerate((k0, k1, k2, k3)):
        out[...] = packed[lax.rem(ids[1] + distance, 4), :OWN, :]


def project_keys(ids, mine, theirs, gain, weight):
    half = mine.shape[1]
    return pl.pallas_call(
        project_keys_kernel,
        in_specs=[SM] + [VM] * 4,
        out_specs=[VM] * 5,
        out_shape=[shape((2, ROWS, half), BF16)] + [shape((OWN, 384), BF16)] * 4,
        scratch_shapes=[pltpu.VMEM((4, ROWS, 384), BF16)],
        compiler_params=params(12),
        cost_estimate=cost(2 * ROWS * weight.size * 2 // 3, weight.size * 2),
        name="project_keys",
    )(ids, mine, theirs, gain, weight)


def project_queries_kernel(ids, normed, weight, q0, q1, q2, q3, packed):
    half = normed.shape[2]
    near = lanes(ids[0] * half, half)
    far = lanes((1 - ids[0]) * half, half)
    low = lax.broadcasted_iota(jnp.int32, (ROWS, 128), 1) < 64
    for pair in range(2):
        at = slice(pair * 2 * HEAD, (pair + 1) * 2 * HEAD)
        both = dot(normed[0], weight[0, near, at]) + dot(normed[1], weight[0, far, at])
        for side, query in enumerate(unpacked(both)):
            packed[2 * pair + side, :, :128] = query[0].astype(BF16)
            packed[2 * pair + side, :, 128:] = jnp.where(low, query[1], 0.0).astype(BF16)
    for distance, out in enumerate((q0, q1, q2, q3)):
        out[...] = packed[lax.rem(ids[1] + distance, 4)]


def project_queries(ids, normed, weight):
    return pl.pallas_call(
        project_queries_kernel,
        in_specs=[SM, VM, VM],
        out_specs=[VM] * 4,
        out_shape=[shape((ROWS, 256), BF16)] * 4,
        scratch_shapes=[pltpu.VMEM((4, ROWS, 256), BF16)],
        compiler_params=params(10),
        cost_estimate=cost(2 * ROWS * weight.size // 3, weight.size),
        name="project_queries",
    )(ids, normed, near_memory(weight))


BLOCK = 2 * ROWS
LOG2E = 1.4426950408889634


def attend_kernel(count, known, resumed, final, ids, scale, queries, *refs):
    pieces, refs = refs[:count], refs[count:]
    inverses, refs = refs[:known], refs[known:]
    if resumed:
        (old_mixed, old_stats), refs = refs[:2], refs[2:]
    sizes = [ref.shape[0] for ref in pieces]
    starts = [sum(sizes[:i]) for i in range(count)]

    def keys(ref):
        return jnp.concatenate([ref[:, :128], ref[:, 256:]], axis=1)

    total_known = sum(ref.shape[1] for ref in inverses)
    if total_known < sum(sizes):
        outs, inverse = refs[:-1], refs[-1]
        lane = lax.broadcasted_iota(jnp.int32, (8, 256), 1)
        ones = (lane < HEAD).astype(F32).astype(BF16)
        for at, size, ref in zip(starts, sizes, pieces):
            if at < total_known:
                continue
            key = keys(ref).astype(F32)
            square = key * key
            high = square.astype(BF16)
            rest = (square - high.astype(F32)).astype(BF16)
            total = dot_t(ones, high) + dot_t(ones, rest)
            at -= total_known
            inverse[:, at : at + size] = lax.rsqrt(total * (1.0 / HEAD) + EPS)
        inverses = (*inverses, inverse)
    else:
        outs = refs

    def inverse_of(at, size):
        for ref in inverses:
            if at < ref.shape[1]:
                return ref[0:1, at : at + size]
            at -= ref.shape[1]

    limit = 1024
    groups, room = [], 0
    for triple in zip(starts, sizes, pieces):
        if room < triple[1]:
            groups.append([])
            room = limit
        groups[-1].append(triple)
        room -= triple[1]

    def unit(query, factor, group):
        scores, peak = [], None
        for at, size, ref in group:
            part = dot_t(query, keys(ref)) * inverse_of(at, size)
            top = jnp.max(part, axis=1, keepdims=True)
            peak = top if peak is None else jnp.maximum(peak, top)
            scores.append(part)
        total, mixed = None, None
        for part, (_, _, ref) in zip(scores, group):
            exps = jnp.exp2((part - peak) * factor)
            sums = jnp.sum(exps, axis=1, keepdims=True)
            values = jnp.concatenate([ref[:, 128:256], ref[:, 256:]], axis=1)
            term = dot(exps.astype(BF16), values)
            total = sums if total is None else total + sums
            mixed = term if mixed is None else mixed + term
        return peak, total, mixed

    for begin in range(0, queries.shape[0], BLOCK):
        rows = slice(begin, begin + BLOCK)
        query = queries[rows, :]
        wide = query.astype(F32)
        own = lax.rsqrt(jnp.sum(wide * wide, axis=1, keepdims=True) * (1.0 / HEAD) + EPS)
        factor = own * (scale[ids[1]] * (LOG2E / HEAD))
        states = [unit(query, factor, group) for group in groups]
        if resumed:
            states.append((old_stats[rows, 0:1], old_stats[rows, 64:65], old_mixed[rows, :]))
        peak = functools.reduce(jnp.maximum, [state[0] for state in states])
        if len(states) > 1:
            shrink = [jnp.exp2((state[0] - peak) * factor) for state in states]
            total = sum(state[1] * part for state, part in zip(states, shrink))
            mixed = sum(state[2] * part for state, part in zip(states, shrink))
        else:
            _, total, mixed = states[0]
        if not final:
            outs[0][rows, :] = mixed
            half = lax.broadcasted_iota(jnp.int32, (BLOCK, 128), 1) < 64
            outs[1][rows, :] = jnp.where(half, peak, total)
            continue
        mixed = mixed / total
        weight = peak * factor + jnp.log(total) * LOG2E
        high = weight.astype(BF16).astype(F32)
        rest = weight - high
        mid = rest.astype(BF16).astype(F32)
        place = lax.broadcasted_iota(jnp.int32, mixed.shape, 1)
        mixed = jnp.where(place == 128, high, mixed)
        mixed = jnp.where(place == 129, mid, mixed)
        mixed = jnp.where(place == 130, rest - mid, mixed)
        outs[0][rows, :] = mixed.astype(BF16)


def attend(ids, scale, queries, pieces, inverses=(), state=(), final=True):
    rows = queries.shape[0]
    keys = sum(piece.shape[0] for piece in pieces)
    if final:
        outs = [shape((rows, 256), BF16)]
    else:
        outs = [shape((rows, 256), F32), shape((rows, 128), F32)]
    known = sum(inverse.shape[1] for inverse in inverses)
    if known < keys:
        outs.append(shape((8, keys - known), F32))
    return pl.pallas_call(
        functools.partial(attend_kernel, len(pieces), len(inverses), bool(state), final),
        in_specs=[SM, SM] + [VM] * (1 + len(pieces) + len(inverses) + len(state)),
        out_specs=[VM] * len(outs),
        out_shape=outs,
        compiler_params=params(28),
        cost_estimate=cost(4 * rows * keys * 256, 8 * rows * 1024),
        name="attend",
    )(ids, scale, near_memory(queries), *pieces, *inverses, *state)


def merge_kernel(a0, a1, *outs):
    parts = [ref[...].astype(F32) for ref in (a0, a1)]
    logs = [p[:, 128:129] + p[:, 129:130] + p[:, 130:131] for p in parts]
    peak = functools.reduce(jnp.maximum, logs)
    shares = [jnp.exp2(log - peak) for log in logs]
    total = sum(shares)
    mixed = sum(p * (share / total) for p, share in zip(parts, shares))
    mixed = jnp.concatenate([mixed[:, :128], pltpu.roll(mixed[:, 128:], 64, 1)], axis=1)
    for block in range(4):
        outs[block][...] = mixed[block * ROWS : (block + 1) * ROWS].astype(BF16)


def merge(parts):
    return pl.pallas_call(
        merge_kernel,
        in_specs=[VM] * 2,
        out_specs=[VM] * 4,
        out_shape=[shape((ROWS, 256), BF16)] * 4,
        compiler_params=params(8),
        cost_estimate=cost(20 * parts[0].size, 10 * parts[0].size),
        name="merge",
    )(*parts)


def output_kernel(mine, ids, a0, a1, a2, a3, weight, out):
    half = out.shape[1]
    side = ids[0] if mine else 1 - ids[0]

    def tile(i):
        at = lanes(side * half + i * TILE, TILE)
        total = None
        for distance, ref in enumerate((a0, a1, a2, a3)):
            head = lax.rem(ids[1] + distance, 4)
            rows = weight[pl.ds(pl.multiple_of(head * HEAD, HEAD), HEAD), at]
            term = dot(ref[:, :HEAD], rows)
            total = term if total is None else total + term
        out[:, lanes(i * TILE, TILE)] = total.astype(out.dtype)

    tiles(half // TILE, tile)


def output(ids, heads, weight, mine, dtype):
    half = weight.shape[1] // 2
    return pl.pallas_call(
        functools.partial(output_kernel, mine),
        in_specs=[SM] + [VM] * 5,
        out_specs=VM,
        out_shape=shape((ROWS, half), dtype),
        compiler_params=params(6),
        cost_estimate=cost(2 * ROWS * weight.size // 2, weight.size),
        name="output",
    )(ids, *heads, weight)


def decode_first_kernel(ids, own, other, encoded, weight, inputs, out):
    half = weight.shape[1]

    def mix(i):
        at = lanes(i * TILE, TILE)
        enc = encoded[:, at].astype(F32)
        even, odd = enc[:ROWS], enc[ROWS:]
        binned = (even + odd) * 0.5
        block = (binned + (own[:, at] + other[:, at].astype(F32))).astype(BF16).astype(F32)
        row = lax.broadcasted_iota(jnp.int32, block.shape, 0)
        outside = ((ids[2] == 0) & (row == ROWS - 1)) | ((ids[2] == 63) & (row == OWN))
        even = jnp.where(outside, 0.0, block + even)
        odd = jnp.where(outside, 0.0, block + odd)
        inputs[:, at] = jnp.concatenate([even, odd], axis=0).astype(BF16)

    tiles(half // TILE, mix)
    decode_tiles(inputs, weight, out, (1 - ids[0]) * half)


def decode_tiles(inputs, weight, out, begin):
    def tile(i):
        at = lanes(begin + i * TILE, TILE)
        result = conv_taps(inputs[...], lambda t: weight[t, :, at], ROWS)
        out[:, lanes(i * TILE, TILE)] = result.astype(out.dtype)

    tiles(out.shape[1] // TILE, tile)


def decode_first(ids, own, other, encoded, weight, width):
    half = weight.shape[1]
    return pl.pallas_call(
        decode_first_kernel,
        in_specs=[SM] + [VM] * 4,
        out_specs=[VM] * 2,
        out_shape=[shape((2 * ROWS, half), BF16), shape((2 * ROWS, width), BF16)],
        compiler_params=params(8),
        cost_estimate=cost(10**6, 10**4),
        name="decode_first",
    )(ids, own, other, encoded, weight)


def decode_kernel(mine, first, ids, inputs, weight, out):
    side = ids[0] if mine else 1 - ids[0]
    decode_tiles(inputs, weight, out, side * weight.shape[1] + first)


def decode(ids, inputs, weight, mine, first, width, dtype):
    half = weight.shape[1]
    return pl.pallas_call(
        functools.partial(decode_kernel, mine, first),
        in_specs=[SM, VM, VM],
        out_specs=VM,
        out_shape=shape((2 * ROWS, width), dtype),
        compiler_params=params(8),
        cost_estimate=cost(10**6, 10**4),
        name="decode",
    )(ids, inputs, weight)


def slope_kernel(first, ids, own, other, inputs, grad, before, after, *refs):
    done, (decoded, slope, paired, wide) = refs[:-4], refs[-4:]
    half = own.shape[1]
    begin = 0
    if done:
        begin = first
        decoded[:, :first] = done[0][...]

    def tile(i):
        at = lanes(i * 128, 128)
        target = lanes(begin + i * 128, 128)
        source = lanes(first + i * 128, 128)
        column = lanes(ids[0] * half + first + i * 128, 128)
        pre = own[:, source] + other[:, at].astype(F32)
        tanh = gelu_tanh(pre)
        result = inputs[:, source].astype(F32) + 0.5 * pre * (1.0 + tanh)
        wide[0, pl.ds(0, OWN, 2), :] = result[:OWN]
        wide[0, pl.ds(1, OWN, 2), :] = result[ROWS : ROWS + OWN]
        decoded[:, target] = wide[0].astype(BF16)
        slant = 0.5 * (1.0 + tanh) + (0.5 * 0.7978845608028654) * pre * (1.0 - tanh * tanh) * (
            1.0 + (3 * 0.044715) * (pre * pre)
        )
        wide[1] = grad[:, column].astype(F32)
        even = wide[1, pl.ds(0, OWN, 2), :]
        odd = wide[1, pl.ds(1, OWN, 2), :]
        paired[:, at] = even + odd
        row = lax.broadcasted_iota(jnp.int32, (ROWS - OWN, 128), 0)
        even_edge = jnp.where(row == 0, after[:, column].astype(F32), 0.0)
        odd_edge = jnp.where(row == ROWS - OWN - 1, before[:, column].astype(F32), 0.0)
        cotangent = jnp.concatenate([even, even_edge, odd, odd_edge], axis=0)
        slope[:, at] = (cotangent * slant).astype(BF16)

    tiles(other.shape[1] // 128, tile)


def slopes(ids, own, other, inputs, grad, before, after, first, done=()):
    width = other.shape[1]
    return pl.pallas_call(
        functools.partial(slope_kernel, first),
        in_specs=[SM] + [VM] * (6 + len(done)),
        out_specs=[VM] * 3,
        out_shape=[
            shape((2 * OWN, width + (first if done else 0)), BF16),
            shape((2 * ROWS, width), BF16),
            shape((OWN, width), F32),
        ],
        scratch_shapes=[pltpu.VMEM((2, 2 * OWN, 128), F32)],
        compiler_params=params(6),
        cost_estimate=cost(100 * 30 * 1000 * other.size, 14 * other.size),
        name="slopes",
    )(ids, own, other, inputs, grad, before, after, *done)


def backward_kernel(mine, firsts, count, ids, *refs):
    slopes_in, starts, (weight, out, level, lower, upper) = (
        refs[: len(firsts)],
        refs[len(firsts) : len(firsts) + count],
        refs[len(firsts) + count :],
    )
    half = weight.shape[1]
    side = ids[0] if mine else 1 - ids[0]
    level[...] = jnp.zeros_like(level)
    lower[...] = jnp.zeros_like(lower)
    upper[...] = jnp.zeros_like(upper)

    for begin, slope in zip(firsts, slopes_in):

        def tile(i):
            at = lanes(side * half + begin + i * TILE, TILE)
            part = slope[:, lanes(i * TILE, TILE)]
            first, mid, last = (dot_t(part, weight[t, :, at]) for t in range(3))
            level[...] += first[ROWS:] + mid[:ROWS] + mid[ROWS:] + last[:ROWS]
            lower[...] += first[:ROWS]
            upper[...] += last[ROWS:]

        tiles(slope.shape[1] // TILE, tile)
    total = level[...] + below(lower[...], ROWS) + above(upper[...], ROWS)
    base = jnp.concatenate([start[...] for start in starts], axis=1)
    out[...] = (base + total[:OWN]).astype(out.dtype)


def backward(ids, parts, starts, weight, mine, dtype):
    half = weight.shape[1]
    size = sum(part.size for _, part in parts)
    return pl.pallas_call(
        functools.partial(backward_kernel, mine, [first for first, _ in parts], len(starts)),
        in_specs=[SM] + [VM] * (len(parts) + len(starts) + 1),
        out_specs=VM,
        out_shape=shape((OWN, half), dtype),
        scratch_shapes=[pltpu.VMEM((ROWS, half), F32)] * 3,
        compiler_params=params(10),
        cost_estimate=cost(100 * 2 * 3 * half * size, 6 * size),
        name="backward",
    )(ids, *[part for _, part in parts], *starts, weight)


def place(at):
    return at // 16, at // 4 % 4, at // 2 % 2, at % 2


def moves(dx=0, dz=0, dy=0, dc=0):
    pairs = []
    for at in range(64):
        x, z, y, c = place(at)
        pairs.append((at, (x + dx) % 4 * 16 + (z + dz) % 4 * 4 + (y ^ dy) * 2 + (c ^ dc)))
    return pairs


def swap(value):
    return lax.ppermute(value, "head", [(0, 1), (1, 0)])


def send(value, **step):
    return lax.ppermute(value, "seq", moves(**step))


def per_device(
    dna_bases,
    stem_weight,
    encoder_weight,
    norm_gain,
    attention_weight,
    logit_scale,
    out_weight,
    decoder_weight,
    grad_out,
):
    at = lax.axis_index("seq")
    x = at // 16
    ids = jnp.stack([lax.axis_index("head"), x, at]).astype(jnp.int32)
    feats = grad_out.shape[1]

    codes, near, far = prepare(ids, dna_bases.reshape(OWN, 128), grad_out)
    near = send(near, dc=1)
    pairs = [(i, i + 1) for i in range(1, 63, 2)]
    far = lax.ppermute(far, "seq", pairs + [(b, a) for a, b in pairs])
    odd = at % 2 == 1
    before = jnp.where(odd, near, far)
    after = jnp.where(odd, far, near)
    stem_weight, encoder_weight = load(stem_weight, encoder_weight)
    encoded, attention_weight = encode(
        ids, codes, before, after, stem_weight, encoder_weight, attention_weight
    )
    gain = norm_gain.reshape(1, feats)
    normed, *keyvals = project_keys(ids, encoded, swap(encoded), gain, attention_weight)

    def spread(blocks):
        return [send(blocks[d], dx=d) for d in (1, 3, 2)]

    def stacked(blocks):
        return jnp.concatenate(lax.optimization_barrier(blocks), axis=0)

    keyvals = stacked([keyvals[0]] + spread(keyvals))
    near = [send(keyvals, dz=1), send(keyvals, dz=3)]
    beside, normed = lax.optimization_barrier((send(keyvals, dc=1), normed))
    queries = project_queries(ids, normed, attention_weight)
    *near, got1, got3, got2 = lax.optimization_barrier((*near, *spread(queries)))
    queries = jnp.concatenate([queries[0], got1, got3, got2], axis=0)
    others = send(queries, dy=1)
    half = keyvals.shape[0] // 2
    far = [send(near[0][:half], dz=1), send(near[1][half:], dz=3)]
    across = [send(piece, dc=1) for piece in near]
    *far, across[0], across[1], others = lax.optimization_barrier((*far, *across, others))
    far = jnp.concatenate(far, axis=0)
    pieces = [keyvals, beside] + near + across + [far, send(far, dc=1)]
    other, inverse = attend(ids, logit_scale, others, pieces)
    other = send(other, dy=1)
    own = attend(ids, logit_scale, queries, pieces, inverses=[inverse])[0]
    mixed = merge([own, other])
    heads = [mixed[0], send(mixed[1], dx=-1), send(mixed[3], dx=-2), send(mixed[2], dx=-3)]

    sent = swap(output(ids, heads, out_weight, False, BF16))
    kept = output(ids, heads, out_weight, True, F32)
    half = decoder_weight.shape[1]
    split = 2 * TILE
    inputs, early = decode_first(ids, kept, sent, encoded, decoder_weight, split)
    early = swap(early)
    late = decode(ids, inputs, decoder_weight, False, split, half - split, BF16)
    late, inputs = lax.optimization_barrier((late, inputs))
    late = swap(late)
    kept = decode(ids, inputs, decoder_weight, True, 0, half, F32)
    decoded, early, paired = slopes(ids, kept, early, inputs, grad_out, before, after, 0)
    early_back = swap(early)
    decoded, late, rest = slopes(
        ids, kept, late, inputs, grad_out, before, after, split, (decoded,)
    )
    late_back = swap(late)
    total = backward(
        ids, [(0, early), (split, late)], [paired, rest], decoder_weight, True, F32
    )
    total = backward(ids, [(0, early_back)], [total], decoder_weight, False, F32)
    bins_grad = backward(ids, [(split, late_back)], [total], decoder_weight, False, BF16)
    return decoded, bins_grad


def solution(mesh):
    in_specs = (
        P("seq"),
        P(),
        P(None, None, "head"),
        P(),
        P(None, None, "head"),
        P("head"),
        P("head", None),
        P(None, "head", None),
        P("seq", None),
    )
    out_specs = (P("seq", "head"), P("seq", "head"))
    return jax.shard_map(
        per_device, mesh=mesh, in_specs=in_specs, out_specs=out_specs, check_vma=False
    )
```

```python
import functools

import jax
import jax.numpy as jnp
from jax import lax
from jax.experimental import pallas as pl
from jax.experimental.pallas import tpu as pltpu
from jax.sharding import PartitionSpec as P

BF16 = jnp.bfloat16
F32 = jnp.float32
ROWS = 136
OWN = 128
TILE = 256
HEAD = 192
EPS = 1e-06
MIB = 1024 * 1024


def params(mib):
    return pltpu.CompilerParams(vmem_limit_bytes=mib * MIB)


def dot(a, b):
    return jnp.dot(a, b, preferred_element_type=F32)


def dot_t(a, b):
    return lax.dot_general(a, b, (((1,), (1,)), ((), ())), preferred_element_type=F32)


def cost(flops, nbytes):
    return pl.CostEstimate(flops=int(flops), bytes_accessed=int(nbytes), transcendentals=0)


def shape(dims, dtype):
    return jax.ShapeDtypeStruct(dims, dtype)


VM = pl.BlockSpec(memory_space=pltpu.VMEM)
SM = pl.BlockSpec(memory_space=pltpu.SMEM)
HBM = pl.BlockSpec(memory_space=pltpu.HBM)


def above(rows, span):
    parts = [pltpu.roll(rows[i : i + span], 1, 0) for i in range(0, rows.shape[0], span)]
    return jnp.concatenate(parts, axis=0)


def below(rows, span):
    parts = [pltpu.roll(rows[i : i + span], span - 1, 0) for i in range(0, rows.shape[0], span)]
    return jnp.concatenate(parts, axis=0)


def lanes(at, size):
    return pl.ds(pl.multiple_of(at, size), size)


def tiles(count, body):
    lax.fori_loop(0, count, lambda i, carry: (body(i), carry)[1], 0)


def gelu_tanh(x):
    return jnp.tanh(0.7978845608028654 * (x + 0.044715 * (x * x * x)))


def conv_taps(rows, weight, span):
    half = rows.shape[0] // 2
    first, mid, last = (dot(rows, weight(t)) for t in range(3))
    even = above(first[half:], span) + mid[:half] + last[half:]
    odd = first[:half] + mid[half:] + below(last[:half], span)
    return jnp.concatenate([even, odd], axis=0)


def sides(ids, near, far):
    odd = lax.rem(ids[2], 2) == 1
    return jnp.where(odd, near, far), jnp.where(odd, far, near)


def prepare_kernel(ids, bases, grad, codes, near, far, code, head, tail, sems):
    rows = grad.shape[0]
    copies = [
        pltpu.make_async_copy(bases, code, sems.at[0]),
        pltpu.make_async_copy(grad.at[pl.ds(0, 16)], head, sems.at[1]),
        pltpu.make_async_copy(grad.at[pl.ds(rows - 16, 16)], tail, sems.at[2]),
    ]
    for copy in copies:
        copy.start()
    for copy in copies:
        copy.wait()
    feats = grad.shape[1]
    letters = (code[...] + 1).astype(F32)
    codes[...] = letters.astype(BF16)
    odd = lax.rem(ids[2], 2) == 1
    last = jnp.concatenate([tail[...].astype(F32)[8:], letters[OWN - 8 :]], axis=1)
    first = jnp.concatenate([head[...].astype(F32)[:8], letters[:8]], axis=1)
    near[...] = jnp.where(odd, first, last).astype(BF16)
    far[...] = jnp.where(odd, last, first).astype(BF16)


def near_memory(value):
    return pltpu.with_memory_space_constraint(value, pltpu.VMEM)


def far_memory(value):
    return pltpu.with_memory_space_constraint(value, pltpu.HBM)


def prepare(ids, bases, grad):
    feats = grad.shape[1]
    return pl.pallas_call(
        prepare_kernel,
        in_specs=[SM, HBM, HBM],
        out_specs=[VM] * 3,
        out_shape=[
            shape((OWN, 128), BF16),
            shape((8, feats + 128), BF16),
            shape((8, feats + 128), BF16),
        ],
        scratch_shapes=[
            pltpu.VMEM(bases.shape, jnp.int32),
            pltpu.VMEM((16, feats), BF16),
            pltpu.VMEM((16, feats), BF16),
            pltpu.SemaphoreType.DMA((3,)),
        ],
        compiler_params=params(4),
        cost_estimate=cost(10**5, 10**5),
        name="prepare",
    )(ids, far_memory(bases), far_memory(grad))


def embed_letters(code, stem, embedded):
    patch = stem.shape[0] // 4
    row = lax.broadcasted_iota(jnp.int32, (2 * patch, 4 * patch), 0)
    col = lax.broadcasted_iota(jnp.int32, (2 * patch, 4 * patch), 1)
    spread = [
        dot(code, (row == col // 4 + offset).astype(F32).astype(BF16)) for offset in (0, patch)
    ]
    spread = jnp.concatenate(spread, axis=0)
    base = lax.broadcasted_iota(jnp.int32, spread.shape, 1) % 4 + 1
    onehot = (spread == base.astype(F32)).astype(F32).astype(BF16)

    def embed(i):
        at = lanes(i * TILE, TILE)
        embedded[:, at] = dot(onehot, stem[:, at]).astype(BF16)

    tiles(stem.shape[1] // TILE, embed)


def activate(side, pre, embedded, encoded):
    half = encoded.shape[1]

    def tile(i):
        at = lanes(i * TILE, TILE)
        mine = embedded[:, lanes(side * half + i * TILE, TILE)].astype(F32)
        value = pre[:, at]
        encoded[:, at] = (mine + 0.5 * value * (1.0 + gelu_tanh(value))).astype(BF16)

    tiles(half // TILE, tile)


def convolve_tap(tap, weight, embedded, pre, span):
    rows = embedded.shape[0] // 2

    def tile(i):
        at = lanes(i * TILE, TILE)
        part = dot(embedded[...], weight[tap, :, at])
        if tap == 1:
            pre[:, at] = part
        elif tap == 0:
            pre[:, at] += jnp.concatenate([above(part[rows:], span), part[:rows]], axis=0)
        else:
            pre[:, at] += jnp.concatenate([part[rows:], below(part[:rows], span)], axis=0)

    tiles(pre.shape[1] // TILE, tile)


def encode_kernel(ids, codes, stems, weights, encoded, stem, weight, embedded, pre, sems):
    copies = [pltpu.make_async_copy(stems, stem, sems.at[3])]
    copies += [
        pltpu.make_async_copy(weights.at[tap], weight.at[tap], sems.at[tap]) for tap in (1, 0, 2)
    ]
    for copy in copies:
        copy.start()
    copies[0].wait()
    embed_letters(codes[...], stem, embedded)
    for tap, copy in zip((1, 0, 2), copies[1:]):
        copy.wait()
        convolve_tap(tap, weight, embedded, pre, OWN)
    activate(ids[0], pre, embedded, encoded)


def encode(ids, codes, stem, weight):
    half = weight.shape[2]
    feats = stem.shape[1]
    return pl.pallas_call(
        encode_kernel,
        in_specs=[SM, VM, HBM, HBM],
        out_specs=[VM] * 3,
        out_shape=[
            shape((2 * OWN, half), BF16),
            pltpu.VMEM(stem.shape, BF16),
            pltpu.VMEM(weight.shape, BF16),
        ],
        scratch_shapes=[
            pltpu.VMEM((2 * OWN, feats), BF16),
            pltpu.VMEM((2 * OWN, half), F32),
            pltpu.SemaphoreType.DMA((4,)),
        ],
        compiler_params=params(10),
        cost_estimate=cost(4 * OWN * weight.size, weight.size * 4),
        name="encode",
    )(ids, codes, far_memory(stem), far_memory(weight))


def encode_edges_kernel(
    ids, codes, near, far, stem, weight, ahead, encoded, loaded, embedded, pre, sem
):
    copy = pltpu.make_async_copy(ahead, loaded, sem)
    copy.start()
    feats = stem.shape[1]
    place = lax.broadcasted_iota(jnp.int32, (8, 128), 0)
    code = codes[...].astype(F32)
    before, after = sides(ids, near[:, feats:].astype(F32), far[:, feats:].astype(F32))
    low = jnp.where(place >= 6, before, 0.0)
    low = jnp.where(place == 0, code[:8], low)
    high = jnp.where(place < 2, after, 0.0)
    high = jnp.where(place == 7, code[OWN - 8 :], high)
    embed_letters(jnp.concatenate([low, high], axis=0).astype(BF16), stem, embedded)
    for tap in (1, 0, 2):
        convolve_tap(tap, weight, embedded, pre, 8)
    activate(ids[0], pre, embedded, encoded)
    copy.wait()


def encode_edges(ids, codes, near, far, stem, weight, ahead):
    half = weight.shape[2]
    feats = stem.shape[1]
    return pl.pallas_call(
        encode_edges_kernel,
        in_specs=[SM] + [VM] * 5 + [HBM],
        out_specs=[VM, VM],
        out_shape=[shape((32, half), BF16), pltpu.VMEM(ahead.shape, BF16)],
        scratch_shapes=[
            pltpu.VMEM((32, feats), BF16),
            pltpu.VMEM((32, half), F32),
            pltpu.SemaphoreType.DMA(()),
        ],
        compiler_params=params(6),
        cost_estimate=cost(4 * OWN * weight.size, weight.size * 4),
        name="encode_edges",
    )(ids, codes, near, far, near_memory(stem), near_memory(weight), far_memory(ahead))


def joined(main, edges):
    main, edges = main[...].astype(F32), edges[...].astype(F32)
    even, odd = main[:OWN], main[OWN:]
    even_low, even_high, odd_low, odd_high = (edges[i : i + 8] for i in range(0, 32, 8))
    place = lax.broadcasted_iota(jnp.int32, even_low.shape, 0)
    return jnp.concatenate(
        [
            jnp.where(place == 0, even_low, even[:8]),
            even[8:],
            jnp.where(place < 4, even_high, even_low),
            odd[: OWN - 8],
            jnp.where(place == 7, odd_high, odd[OWN - 8 :]),
            jnp.where(place < 4, odd_high, odd_low),
        ],
        axis=0,
    )


def unpacked(both):
    both = both.astype(BF16).astype(F32)
    turned = pltpu.roll(both, 2 * HEAD - 64, 1)
    return (both[:, :128], both[:, 128:256]), (turned[:, 128:256], turned[:, 256:384])


def project_keys_kernel(
    ids, mine, mine_edges, theirs, their_edges, gain, weight, encoded, normed, k0, k1, k2, k3, packed
):
    half = mine.shape[1]
    near = lanes(ids[0] * half, half)
    far = lanes((1 - ids[0]) * half, half)
    rings = joined(mine, mine_edges), joined(theirs, their_edges)
    encoded[...] = rings[0].astype(BF16)
    binned = [(ring[:ROWS] + ring[ROWS:]) * 0.5 for ring in rings]
    total = sum(jnp.sum(part * part, axis=1, keepdims=True) for part in binned)
    inverse = lax.rsqrt(total * (1.0 / (2 * half)) + EPS)
    here = (binned[0] * inverse * gain[:, near]).astype(BF16)
    there = (binned[1] * inverse * gain[:, far]).astype(BF16)
    normed[0] = here
    normed[1] = there
    low = lax.broadcasted_iota(jnp.int32, (ROWS, 128), 1) < 64
    for pair in range(2):
        at = slice(pair * 2 * HEAD, (pair + 1) * 2 * HEAD)
        keys, values = (
            unpacked(dot(here, weight[kind, near, at]) + dot(there, weight[kind, far, at]))
            for kind in (1, 2)
        )
        for side in range(2):
            head = 2 * pair + side
            key, value = keys[side], values[side]
            packed[head, :, :128] = key[0].astype(BF16)
            packed[head, :, 128:256] = value[0].astype(BF16)
            tail = jnp.where(low, key[1], pltpu.roll(value[1], 64, 1))
            packed[head, :, 256:] = tail.astype(BF16)
    for distance, out in enumerate((k0, k1, k2, k3)):
        out[...] = packed[lax.rem(ids[1] + distance, 4), :OWN, :]


def project_keys(ids, mine, mine_edges, theirs, their_edges, gain, weight):
    half = mine.shape[1]
    return pl.pallas_call(
        project_keys_kernel,
        in_specs=[SM] + [VM] * 6,
        out_specs=[VM] * 6,
        out_shape=[shape((2 * ROWS, half), BF16), shape((2, ROWS, half), BF16)]
        + [shape((OWN, 384), BF16)] * 4,
        scratch_shapes=[pltpu.VMEM((4, ROWS, 384), BF16)],
        compiler_params=params(12),
        cost_estimate=cost(2 * ROWS * weight.size * 2 // 3, weight.size * 2),
        name="project_keys",
    )(ids, mine, mine_edges, theirs, their_edges, gain, weight)


def project_queries_kernel(ids, normed, weight, q0, q1, q2, q3, packed):
    half = normed.shape[2]
    near = lanes(ids[0] * half, half)
    far = lanes((1 - ids[0]) * half, half)
    low = lax.broadcasted_iota(jnp.int32, (ROWS, 128), 1) < 64
    for pair in range(2):
        at = slice(pair * 2 * HEAD, (pair + 1) * 2 * HEAD)
        both = dot(normed[0], weight[0, near, at]) + dot(normed[1], weight[0, far, at])
        for side, query in enumerate(unpacked(both)):
            packed[2 * pair + side, :, :128] = query[0].astype(BF16)
            packed[2 * pair + side, :, 128:] = jnp.where(low, query[1], 0.0).astype(BF16)
    for distance, out in enumerate((q0, q1, q2, q3)):
        out[...] = packed[lax.rem(ids[1] + distance, 4)]


def project_queries(ids, normed, weight):
    return pl.pallas_call(
        project_queries_kernel,
        in_specs=[SM, VM, VM],
        out_specs=[VM] * 4,
        out_shape=[shape((ROWS, 256), BF16)] * 4,
        scratch_shapes=[pltpu.VMEM((4, ROWS, 256), BF16)],
        compiler_params=params(10),
        cost_estimate=cost(2 * ROWS * weight.size // 3, weight.size),
        name="project_queries",
    )(ids, normed, near_memory(weight))


BLOCK = 2 * ROWS
LOG2E = 1.4426950408889634


def attend_kernel(count, known, resumed, final, ids, scale, queries, *refs):
    pieces, refs = refs[:count], refs[count:]
    inverses, refs = refs[:known], refs[known:]
    if resumed:
        (old_mixed, old_stats), refs = refs[:2], refs[2:]
    sizes = [ref.shape[0] for ref in pieces]
    starts = [sum(sizes[:i]) for i in range(count)]

    def keys(ref):
        return jnp.concatenate([ref[:, :128], ref[:, 256:]], axis=1)

    total_known = sum(ref.shape[1] for ref in inverses)
    if total_known < sum(sizes):
        outs, inverse = refs[:-1], refs[-1]
        lane = lax.broadcasted_iota(jnp.int32, (8, 256), 1)
        ones = (lane < HEAD).astype(F32).astype(BF16)
        for at, size, ref in zip(starts, sizes, pieces):
            if at < total_known:
                continue
            key = keys(ref).astype(F32)
            square = key * key
            high = square.astype(BF16)
            rest = (square - high.astype(F32)).astype(BF16)
            total = dot_t(ones, high) + dot_t(ones, rest)
            at -= total_known
            inverse[:, at : at + size] = lax.rsqrt(total * (1.0 / HEAD) + EPS)
        inverses = (*inverses, inverse)
    else:
        outs = refs

    def inverse_of(at, size):
        for ref in inverses:
            if at < ref.shape[1]:
                return ref[0:1, at : at + size]
            at -= ref.shape[1]

    limit = 1024
    groups, room = [], 0
    for triple in zip(starts, sizes, pieces):
        if room < triple[1]:
            groups.append([])
            room = limit
        groups[-1].append(triple)
        room -= triple[1]

    def unit(query, factor, group):
        scores, peak = [], None
        for at, size, ref in group:
            part = dot_t(query, keys(ref)) * inverse_of(at, size)
            top = jnp.max(part, axis=1, keepdims=True)
            peak = top if peak is None else jnp.maximum(peak, top)
            scores.append(part)
        total, mixed = None, None
        for part, (_, _, ref) in zip(scores, group):
            exps = jnp.exp2((part - peak) * factor)
            sums = jnp.sum(exps, axis=1, keepdims=True)
            values = jnp.concatenate([ref[:, 128:256], ref[:, 256:]], axis=1)
            term = dot(exps.astype(BF16), values)
            total = sums if total is None else total + sums
            mixed = term if mixed is None else mixed + term
        return peak, total, mixed

    for begin in range(0, queries.shape[0], BLOCK):
        rows = slice(begin, begin + BLOCK)
        query = queries[rows, :]
        wide = query.astype(F32)
        own = lax.rsqrt(jnp.sum(wide * wide, axis=1, keepdims=True) * (1.0 / HEAD) + EPS)
        factor = own * (scale[ids[1]] * (LOG2E / HEAD))
        states = [unit(query, factor, group) for group in groups]
        if resumed:
            states.append((old_stats[rows, 0:1], old_stats[rows, 64:65], old_mixed[rows, :]))
        peak = functools.reduce(jnp.maximum, [state[0] for state in states])
        if len(states) > 1:
            shrink = [jnp.exp2((state[0] - peak) * factor) for state in states]
            total = sum(state[1] * part for state, part in zip(states, shrink))
            mixed = sum(state[2] * part for state, part in zip(states, shrink))
        else:
            _, total, mixed = states[0]
        if not final:
            outs[0][rows, :] = mixed
            half = lax.broadcasted_iota(jnp.int32, (BLOCK, 128), 1) < 64
            outs[1][rows, :] = jnp.where(half, peak, total)
            continue
        mixed = mixed / total
        weight = peak * factor + jnp.log(total) * LOG2E
        high = weight.astype(BF16).astype(F32)
        rest = weight - high
        mid = rest.astype(BF16).astype(F32)
        place = lax.broadcasted_iota(jnp.int32, mixed.shape, 1)
        mixed = jnp.where(place == 128, high, mixed)
        mixed = jnp.where(place == 129, mid, mixed)
        mixed = jnp.where(place == 130, rest - mid, mixed)
        outs[0][rows, :] = mixed.astype(BF16)


def attend(ids, scale, queries, pieces, inverses=(), state=(), final=True):
    rows = queries.shape[0]
    keys = sum(piece.shape[0] for piece in pieces)
    if final:
        outs = [shape((rows, 256), BF16)]
    else:
        outs = [shape((rows, 256), F32), shape((rows, 128), F32)]
    known = sum(inverse.shape[1] for inverse in inverses)
    if known < keys:
        outs.append(shape((8, keys - known), F32))
    return pl.pallas_call(
        functools.partial(attend_kernel, len(pieces), len(inverses), bool(state), final),
        in_specs=[SM, SM] + [VM] * (1 + len(pieces) + len(inverses) + len(state)),
        out_specs=[VM] * len(outs),
        out_shape=outs,
        compiler_params=params(28),
        cost_estimate=cost(4 * rows * keys * 256, 8 * rows * 1024),
        name="attend",
    )(ids, scale, near_memory(queries), *pieces, *inverses, *state)


def merge_kernel(a0, a1, *outs):
    parts = [ref[...].astype(F32) for ref in (a0, a1)]
    logs = [p[:, 128:129] + p[:, 129:130] + p[:, 130:131] for p in parts]
    peak = functools.reduce(jnp.maximum, logs)
    shares = [jnp.exp2(log - peak) for log in logs]
    total = sum(shares)
    mixed = sum(p * (share / total) for p, share in zip(parts, shares))
    mixed = jnp.concatenate([mixed[:, :128], pltpu.roll(mixed[:, 128:], 64, 1)], axis=1)
    for block in range(4):
        outs[block][...] = mixed[block * ROWS : (block + 1) * ROWS].astype(BF16)


def merge(parts):
    return pl.pallas_call(
        merge_kernel,
        in_specs=[VM] * 2,
        out_specs=[VM] * 4,
        out_shape=[shape((ROWS, 256), BF16)] * 4,
        compiler_params=params(8),
        cost_estimate=cost(20 * parts[0].size, 10 * parts[0].size),
        name="merge",
    )(*parts)


def output_kernel(mine, ids, a0, a1, a2, a3, weight, out):
    half = out.shape[1]
    side = ids[0] if mine else 1 - ids[0]

    def tile(i):
        at = lanes(side * half + i * TILE, TILE)
        total = None
        for distance, ref in enumerate((a0, a1, a2, a3)):
            head = lax.rem(ids[1] + distance, 4)
            rows = weight[pl.ds(pl.multiple_of(head * HEAD, HEAD), HEAD), at]
            term = dot(ref[:, :HEAD], rows)
            total = term if total is None else total + term
        out[:, lanes(i * TILE, TILE)] = total.astype(out.dtype)

    tiles(half // TILE, tile)


def output(ids, heads, weight, mine, dtype):
    half = weight.shape[1] // 2
    return pl.pallas_call(
        functools.partial(output_kernel, mine),
        in_specs=[SM] + [VM] * 5,
        out_specs=VM,
        out_shape=shape((ROWS, half), dtype),
        compiler_params=params(6),
        cost_estimate=cost(2 * ROWS * weight.size // 2, weight.size),
        name="output",
    )(ids, *heads, weight)


def decode_first_kernel(ids, own, other, encoded, weight, inputs, out):
    half = weight.shape[1]

    def mix(i):
        at = lanes(i * TILE, TILE)
        enc = encoded[:, at].astype(F32)
        even, odd = enc[:ROWS], enc[ROWS:]
        binned = (even + odd) * 0.5
        block = (binned + (own[:, at] + other[:, at].astype(F32))).astype(BF16).astype(F32)
        row = lax.broadcasted_iota(jnp.int32, block.shape, 0)
        outside = ((ids[2] == 0) & (row == ROWS - 1)) | ((ids[2] == 63) & (row == OWN))
        even = jnp.where(outside, 0.0, block + even)
        odd = jnp.where(outside, 0.0, block + odd)
        inputs[:, at] = jnp.concatenate([even, odd], axis=0).astype(BF16)

    tiles(half // TILE, mix)
    decode_tiles(inputs, weight, out, (1 - ids[0]) * half)


def decode_tiles(inputs, weight, out, begin):
    def tile(i):
        at = lanes(begin + i * TILE, TILE)
        result = conv_taps(inputs[...], lambda t: weight[t, :, at], ROWS)
        out[:, lanes(i * TILE, TILE)] = result.astype(out.dtype)

    tiles(out.shape[1] // TILE, tile)


def decode_first(ids, own, other, encoded, weight, width):
    half = weight.shape[1]
    return pl.pallas_call(
        decode_first_kernel,
        in_specs=[SM] + [VM] * 4,
        out_specs=[VM] * 2,
        out_shape=[shape((2 * ROWS, half), BF16), shape((2 * ROWS, width), BF16)],
        compiler_params=params(8),
        cost_estimate=cost(10**6, 10**4),
        name="decode_first",
    )(ids, own, other, encoded, weight)


def decode_kernel(mine, first, ids, inputs, weight, out):
    side = ids[0] if mine else 1 - ids[0]
    decode_tiles(inputs, weight, out, side * weight.shape[1] + first)


def decode(ids, inputs, weight, mine, first, width, dtype):
    half = weight.shape[1]
    return pl.pallas_call(
        functools.partial(decode_kernel, mine, first),
        in_specs=[SM, VM, VM],
        out_specs=VM,
        out_shape=shape((2 * ROWS, width), dtype),
        compiler_params=params(8),
        cost_estimate=cost(10**6, 10**4),
        name="decode",
    )(ids, inputs, weight)


def slope_kernel(first, ids, own, other, inputs, grad, near, far, *refs):
    done, (decoded, slope, paired, wide) = refs[:-4], refs[-4:]
    half = own.shape[1]
    begin = 0
    if done:
        begin = first
        decoded[:, :first] = done[0][...]

    def tile(i):
        at = lanes(i * 128, 128)
        target = lanes(begin + i * 128, 128)
        source = lanes(first + i * 128, 128)
        column = lanes(ids[0] * half + first + i * 128, 128)
        pre = own[:, source] + other[:, at].astype(F32)
        tanh = gelu_tanh(pre)
        result = inputs[:, source].astype(F32) + 0.5 * pre * (1.0 + tanh)
        wide[0, pl.ds(0, OWN, 2), :] = result[:OWN]
        wide[0, pl.ds(1, OWN, 2), :] = result[ROWS : ROWS + OWN]
        decoded[:, target] = wide[0].astype(BF16)
        slant = 0.5 * (1.0 + tanh) + (0.5 * 0.7978845608028654) * pre * (1.0 - tanh * tanh) * (
            1.0 + (3 * 0.044715) * (pre * pre)
        )
        wide[1] = grad[:, column].astype(F32)
        even = wide[1, pl.ds(0, OWN, 2), :]
        odd = wide[1, pl.ds(1, OWN, 2), :]
        paired[:, at] = even + odd
        row = lax.broadcasted_iota(jnp.int32, (ROWS - OWN, 128), 0)
        before, after = sides(ids, near[:, column].astype(F32), far[:, column].astype(F32))
        even_edge = jnp.where(row == 0, after, 0.0)
        odd_edge = jnp.where(row == ROWS - OWN - 1, before, 0.0)
        cotangent = jnp.concatenate([even, even_edge, odd, odd_edge], axis=0)
        slope[:, at] = (cotangent * slant).astype(BF16)

    tiles(other.shape[1] // 128, tile)


def slopes(ids, own, other, inputs, grad, near, far, first, done=()):
    width = other.shape[1]
    return pl.pallas_call(
        functools.partial(slope_kernel, first),
        in_specs=[SM] + [VM] * (6 + len(done)),
        out_specs=[VM] * 3,
        out_shape=[
            shape((2 * OWN, width + (first if done else 0)), BF16),
            shape((2 * ROWS, width), BF16),
            shape((OWN, width), F32),
        ],
        scratch_shapes=[pltpu.VMEM((2, 2 * OWN, 128), F32)],
        compiler_params=params(6),
        cost_estimate=cost(100 * 30 * 1000 * other.size, 14 * other.size),
        name="slopes",
    )(ids, own, other, inputs, grad, near, far, *done)


def backward_kernel(mine, firsts, count, ids, *refs):
    slopes_in, starts, (weight, out, level, lower, upper) = (
        refs[: len(firsts)],
        refs[len(firsts) : len(firsts) + count],
        refs[len(firsts) + count :],
    )
    half = weight.shape[1]
    side = ids[0] if mine else 1 - ids[0]
    level[...] = jnp.zeros_like(level)
    lower[...] = jnp.zeros_like(lower)
    upper[...] = jnp.zeros_like(upper)

    for begin, slope in zip(firsts, slopes_in):

        def tile(i):
            at = lanes(side * half + begin + i * TILE, TILE)
            part = slope[:, lanes(i * TILE, TILE)]
            first, mid, last = (dot_t(part, weight[t, :, at]) for t in range(3))
            level[...] += first[ROWS:] + mid[:ROWS] + mid[ROWS:] + last[:ROWS]
            lower[...] += first[:ROWS]
            upper[...] += last[ROWS:]

        tiles(slope.shape[1] // TILE, tile)
    total = level[...] + below(lower[...], ROWS) + above(upper[...], ROWS)
    base = jnp.concatenate([start[...] for start in starts], axis=1)
    out[...] = (base + total[:OWN]).astype(out.dtype)


def backward(ids, parts, starts, weight, mine, dtype):
    half = weight.shape[1]
    size = sum(part.size for _, part in parts)
    return pl.pallas_call(
        functools.partial(backward_kernel, mine, [first for first, _ in parts], len(starts)),
        in_specs=[SM] + [VM] * (len(parts) + len(starts) + 1),
        out_specs=VM,
        out_shape=shape((OWN, half), dtype),
        scratch_shapes=[pltpu.VMEM((ROWS, half), F32)] * 3,
        compiler_params=params(10),
        cost_estimate=cost(100 * 2 * 3 * half * size, 6 * size),
        name="backward",
    )(ids, *[part for _, part in parts], *starts, weight)


def place(at):
    return at // 16, at // 4 % 4, at // 2 % 2, at % 2


def moves(dx=0, dz=0, dy=0, dc=0):
    pairs = []
    for at in range(64):
        x, z, y, c = place(at)
        pairs.append((at, (x + dx) % 4 * 16 + (z + dz) % 4 * 4 + (y ^ dy) * 2 + (c ^ dc)))
    return pairs


def swap(value):
    return lax.ppermute(value, "head", [(0, 1), (1, 0)])


def send(value, **step):
    return lax.ppermute(value, "seq", moves(**step))


def per_device(
    dna_bases,
    stem_weight,
    encoder_weight,
    norm_gain,
    attention_weight,
    logit_scale,
    out_weight,
    decoder_weight,
    grad_out,
):
    at = lax.axis_index("seq")
    x = at // 16
    ids = jnp.stack([lax.axis_index("head"), x, at]).astype(jnp.int32)
    feats = grad_out.shape[1]

    codes, near, far = prepare(ids, dna_bases.reshape(OWN, 128), grad_out)
    near = send(near, dc=1)
    pairs = [(i, i + 1) for i in range(1, 63, 2)]
    far = lax.ppermute(far, "seq", pairs + [(b, a) for a, b in pairs])
    halo = near, far
    encoded, stem_weight, encoder_weight = encode(ids, codes, stem_weight, encoder_weight)
    theirs = swap(encoded)
    edges, attention_weight = encode_edges(
        ids, codes, *halo, stem_weight, encoder_weight, attention_weight
    )
    gain = norm_gain.reshape(1, feats)
    encoded, normed, *keyvals = project_keys(
        ids, encoded, edges, theirs, swap(edges), gain, attention_weight
    )

    def spread(blocks):
        return [send(blocks[d], dx=d) for d in (1, 3, 2)]

    def stacked(blocks):
        return jnp.concatenate(lax.optimization_barrier(blocks), axis=0)

    keyvals = stacked([keyvals[0]] + spread(keyvals))
    ring = [send(keyvals, dz=d) for d in (1, 3, 2)]
    beside, normed = lax.optimization_barrier((send(keyvals, dc=1), normed))
    queries = project_queries(ids, normed, attention_weight)
    ring[0], ring[1], *got = lax.optimization_barrier((ring[0], ring[1], *spread(queries)))
    queries = jnp.concatenate([queries[0]] + got, axis=0)
    others = send(queries, dy=1)
    ring[2], others = lax.optimization_barrier((ring[2], others))
    pieces = [keyvals, beside] + ring + [send(piece, dc=1) for piece in ring]
    other, inverse = attend(ids, logit_scale, others, pieces)
    other = send(other, dy=1)
    own = attend(ids, logit_scale, queries, pieces, inverses=[inverse])[0]
    mixed = merge([own, other])
    heads = [mixed[0], send(mixed[1], dx=-1), send(mixed[3], dx=-2), send(mixed[2], dx=-3)]

    sent = swap(output(ids, heads, out_weight, False, BF16))
    kept = output(ids, heads, out_weight, True, F32)
    half = decoder_weight.shape[1]
    split = TILE
    inputs, early = decode_first(ids, kept, sent, encoded, decoder_weight, split)
    early = swap(early)
    late = decode(ids, inputs, decoder_weight, False, split, half - split, BF16)
    late, inputs = lax.optimization_barrier((late, inputs))
    late = swap(late)
    kept = decode(ids, inputs, decoder_weight, True, 0, half, F32)
    decoded, early, paired = slopes(ids, kept, early, inputs, grad_out, *halo, 0)
    early_back = swap(early)
    decoded, late, rest = slopes(
        ids, kept, late, inputs, grad_out, *halo, split, (decoded,)
    )
    late_back = swap(late)
    total = backward(
        ids, [(0, early), (split, late)], [paired, rest], decoder_weight, True, F32
    )
    total = backward(ids, [(0, early_back)], [total], decoder_weight, False, F32)
    bins_grad = backward(ids, [(split, late_back)], [total], decoder_weight, False, BF16)
    return decoded, bins_grad


def solution(mesh):
    in_specs = (
        P("seq"),
        P(),
        P(None, None, "head"),
        P(),
        P(None, None, "head"),
        P("head"),
        P("head", None),
        P(None, "head", None),
        P("seq", None),
    )
    out_specs = (P("seq", "head"), P("seq", "head"))
    return jax.shard_map(
        per_device, mesh=mesh, in_specs=in_specs, out_specs=out_specs, check_vma=False
    )
```

```python
import functools

import jax
import jax.numpy as jnp
from jax import lax
from jax.experimental import pallas as pl
from jax.experimental.pallas import tpu as pltpu
from jax.sharding import PartitionSpec as P

BF16 = jnp.bfloat16
F32 = jnp.float32
ROWS = 136
OWN = 128
TILE = 256
HEAD = 192
EPS = 1e-06
MIB = 1024 * 1024


def params(mib):
    return pltpu.CompilerParams(vmem_limit_bytes=mib * MIB)


def dot(a, b):
    return jnp.dot(a, b, preferred_element_type=F32)


def dot_t(a, b):
    return lax.dot_general(a, b, (((1,), (1,)), ((), ())), preferred_element_type=F32)


def cost(flops, nbytes):
    return pl.CostEstimate(flops=int(flops), bytes_accessed=int(nbytes), transcendentals=0)


def shape(dims, dtype):
    return jax.ShapeDtypeStruct(dims, dtype)


VM = pl.BlockSpec(memory_space=pltpu.VMEM)
SM = pl.BlockSpec(memory_space=pltpu.SMEM)
HBM = pl.BlockSpec(memory_space=pltpu.HBM)


def above(rows, span):
    parts = [pltpu.roll(rows[i : i + span], 1, 0) for i in range(0, rows.shape[0], span)]
    return jnp.concatenate(parts, axis=0)


def below(rows, span):
    parts = [pltpu.roll(rows[i : i + span], span - 1, 0) for i in range(0, rows.shape[0], span)]
    return jnp.concatenate(parts, axis=0)


def lanes(at, size):
    return pl.ds(pl.multiple_of(at, size), size)


def tiles(count, body):
    lax.fori_loop(0, count, lambda i, carry: (body(i), carry)[1], 0)


def gelu_tanh(x):
    return jnp.tanh(0.7978845608028654 * (x + 0.044715 * (x * x * x)))


def conv_taps(rows, weight, span):
    half = rows.shape[0] // 2
    first, mid, last = (dot(rows, weight(t)) for t in range(3))
    even = above(first[half:], span) + mid[:half] + last[half:]
    odd = first[:half] + mid[half:] + below(last[:half], span)
    return jnp.concatenate([even, odd], axis=0)


def sides(ids, near, far):
    odd = lax.rem(ids[2], 2) == 1
    return jnp.where(odd, near, far), jnp.where(odd, far, near)


def prepare_kernel(ids, bases, grad, codes, near, far, code, head, tail, sems):
    rows = grad.shape[0]
    copies = [
        pltpu.make_async_copy(bases, code, sems.at[0]),
        pltpu.make_async_copy(grad.at[pl.ds(0, 16)], head, sems.at[1]),
        pltpu.make_async_copy(grad.at[pl.ds(rows - 16, 16)], tail, sems.at[2]),
    ]
    for copy in copies:
        copy.start()
    for copy in copies:
        copy.wait()
    feats = grad.shape[1]
    letters = (code[...] + 1).astype(F32)
    codes[...] = letters.astype(BF16)
    odd = lax.rem(ids[2], 2) == 1
    last = jnp.concatenate([tail[...].astype(F32)[8:], letters[OWN - 8 :]], axis=1)
    first = jnp.concatenate([head[...].astype(F32)[:8], letters[:8]], axis=1)
    near[...] = jnp.where(odd, first, last).astype(BF16)
    far[...] = jnp.where(odd, last, first).astype(BF16)


def near_memory(value):
    return pltpu.with_memory_space_constraint(value, pltpu.VMEM)


def far_memory(value):
    return pltpu.with_memory_space_constraint(value, pltpu.HBM)


def prepare(ids, bases, grad):
    feats = grad.shape[1]
    return pl.pallas_call(
        prepare_kernel,
        in_specs=[SM, HBM, HBM],
        out_specs=[VM] * 3,
        out_shape=[
            shape((OWN, 128), BF16),
            shape((8, feats + 128), BF16),
            shape((8, feats + 128), BF16),
        ],
        scratch_shapes=[
            pltpu.VMEM(bases.shape, jnp.int32),
            pltpu.VMEM((16, feats), BF16),
            pltpu.VMEM((16, feats), BF16),
            pltpu.SemaphoreType.DMA((3,)),
        ],
        compiler_params=params(4),
        cost_estimate=cost(10**5, 10**5),
        name="prepare",
    )(ids, far_memory(bases), far_memory(grad))


def embed_letters(code, stem, embedded):
    patch = stem.shape[0] // 4
    row = lax.broadcasted_iota(jnp.int32, (2 * patch, 4 * patch), 0)
    col = lax.broadcasted_iota(jnp.int32, (2 * patch, 4 * patch), 1)
    spread = [
        dot(code, (row == col // 4 + offset).astype(F32).astype(BF16)) for offset in (0, patch)
    ]
    spread = jnp.concatenate(spread, axis=0)
    base = lax.broadcasted_iota(jnp.int32, spread.shape, 1) % 4 + 1
    onehot = (spread == base.astype(F32)).astype(F32).astype(BF16)

    def embed(i):
        at = lanes(i * TILE, TILE)
        embedded[:, at] = dot(onehot, stem[:, at]).astype(BF16)

    tiles(stem.shape[1] // TILE, embed)


def load_kernel(codes, stems, weights, embedded, stem, weight, sems):
    copies = [
        pltpu.make_async_copy(stems, stem, sems.at[0]),
        pltpu.make_async_copy(weights, weight, sems.at[1]),
    ]
    for copy in copies:
        copy.start()
    copies[0].wait()
    embed_letters(codes[...], stem, embedded)
    copies[1].wait()


def load(codes, stem, weight):
    return pl.pallas_call(
        load_kernel,
        in_specs=[VM, HBM, HBM],
        out_specs=[VM] * 3,
        out_shape=[
            pltpu.VMEM((2 * OWN, stem.shape[1]), BF16),
            pltpu.VMEM(stem.shape, BF16),
            pltpu.VMEM(weight.shape, BF16),
        ],
        scratch_shapes=[pltpu.SemaphoreType.DMA((2,))],
        compiler_params=params(4),
        cost_estimate=cost(10**5, weight.size * 2),
        name="load",
    )(codes, far_memory(stem), far_memory(weight))


def ring_order(rows):
    half = ROWS - OWN
    return (
        jnp.concatenate([rows[:OWN], rows[2 * OWN : 2 * OWN + half]], axis=0),
        jnp.concatenate([rows[OWN : 2 * OWN], rows[2 * OWN + half :]], axis=0),
    )


def encode_kernel(ids, near, far, rows, stem, weight, ahead, encoded, loaded, embedded, halo, sem):
    copy = pltpu.make_async_copy(ahead, loaded, sem)
    copy.start()
    feats = stem.shape[1]
    half = weight.shape[2]
    place = lax.broadcasted_iota(jnp.int32, (ROWS - OWN, 128), 0)
    before, after = sides(ids, near[:, feats:].astype(F32), far[:, feats:].astype(F32))
    code = jnp.where(place >= 6, before, 0.0)
    code = jnp.where(place < 2, after, code)
    embed_letters(code.astype(BF16), stem, halo)
    embedded[: 2 * OWN, :] = rows[...]
    embedded[2 * OWN :, :] = halo[...]

    def convolve(i):
        at = lanes(i * TILE, TILE)
        parts = [dot(embedded[...], weight[tap, :, at]) for tap in range(3)]
        (first_even, first_odd), (even, odd), (last_even, last_odd) = map(ring_order, parts)
        even = above(first_odd, ROWS) + even + last_odd
        odd = first_even + odd + below(last_even, ROWS)
        pre = jnp.concatenate([even, odd], axis=0)
        mine = embedded[:, lanes(ids[0] * half + i * TILE, TILE)].astype(F32)
        mine = jnp.concatenate(ring_order(mine), axis=0)
        encoded[:, at] = (mine + 0.5 * pre * (1.0 + gelu_tanh(pre))).astype(BF16)

    tiles(half // TILE, convolve)
    copy.wait()


def encode(ids, near, far, rows, stem, weight, ahead):
    half = weight.shape[2]
    feats = stem.shape[1]
    return pl.pallas_call(
        encode_kernel,
        in_specs=[SM] + [VM] * 5 + [HBM],
        out_specs=[VM, VM],
        out_shape=[shape((2 * ROWS, half), BF16), pltpu.VMEM(ahead.shape, BF16)],
        scratch_shapes=[
            pltpu.VMEM((2 * ROWS, feats), BF16),
            pltpu.VMEM((2 * (ROWS - OWN), feats), BF16),
            pltpu.SemaphoreType.DMA(()),
        ],
        compiler_params=params(12),
        cost_estimate=cost(4 * OWN * weight.size, weight.size * 4),
        name="encode",
    )(
        ids,
        near,
        far,
        near_memory(rows),
        near_memory(stem),
        near_memory(weight),
        far_memory(ahead),
    )


def unpacked(both):
    both = both.astype(BF16).astype(F32)
    turned = pltpu.roll(both, 2 * HEAD - 64, 1)
    return (both[:, :128], both[:, 128:256]), (turned[:, 128:256], turned[:, 256:384])


def project_keys_kernel(
    ids, mine, theirs, gain, weight, normed, k0, k1, k2, k3, packed
):
    half = mine.shape[1]
    near = lanes(ids[0] * half, half)
    far = lanes((1 - ids[0]) * half, half)
    rings = [ref[...].astype(F32) for ref in (mine, theirs)]
    binned = [(ring[:ROWS] + ring[ROWS:]) * 0.5 for ring in rings]
    total = sum(jnp.sum(part * part, axis=1, keepdims=True) for part in binned)
    inverse = lax.rsqrt(total * (1.0 / (2 * half)) + EPS)
    here = (binned[0] * inverse * gain[:, near]).astype(BF16)
    there = (binned[1] * inverse * gain[:, far]).astype(BF16)
    normed[0] = here
    normed[1] = there
    low = lax.broadcasted_iota(jnp.int32, (ROWS, 128), 1) < 64
    for pair in range(2):
        at = slice(pair * 2 * HEAD, (pair + 1) * 2 * HEAD)
        keys, values = (
            unpacked(dot(here, weight[kind, near, at]) + dot(there, weight[kind, far, at]))
            for kind in (1, 2)
        )
        for side in range(2):
            head = 2 * pair + side
            key, value = keys[side], values[side]
            packed[head, :, :128] = key[0].astype(BF16)
            packed[head, :, 128:256] = value[0].astype(BF16)
            tail = jnp.where(low, key[1], pltpu.roll(value[1], 64, 1))
            packed[head, :, 256:] = tail.astype(BF16)
    for distance, out in enumerate((k0, k1, k2, k3)):
        out[...] = packed[lax.rem(ids[1] + distance, 4), :OWN, :]


def project_keys(ids, mine, theirs, gain, weight):
    half = mine.shape[1]
    return pl.pallas_call(
        project_keys_kernel,
        in_specs=[SM] + [VM] * 4,
        out_specs=[VM] * 5,
        out_shape=[shape((2, ROWS, half), BF16)] + [shape((OWN, 384), BF16)] * 4,
        scratch_shapes=[pltpu.VMEM((4, ROWS, 384), BF16)],
        compiler_params=params(12),
        cost_estimate=cost(2 * ROWS * weight.size * 2 // 3, weight.size * 2),
        name="project_keys",
    )(ids, mine, theirs, gain, weight)


def project_queries_kernel(ids, normed, weight, q0, q1, q2, q3, packed):
    half = normed.shape[2]
    near = lanes(ids[0] * half, half)
    far = lanes((1 - ids[0]) * half, half)
    low = lax.broadcasted_iota(jnp.int32, (ROWS, 128), 1) < 64
    for pair in range(2):
        at = slice(pair * 2 * HEAD, (pair + 1) * 2 * HEAD)
        both = dot(normed[0], weight[0, near, at]) + dot(normed[1], weight[0, far, at])
        for side, query in enumerate(unpacked(both)):
            packed[2 * pair + side, :, :128] = query[0].astype(BF16)
            packed[2 * pair + side, :, 128:] = jnp.where(low, query[1], 0.0).astype(BF16)
    for distance, out in enumerate((q0, q1, q2, q3)):
        out[...] = packed[lax.rem(ids[1] + distance, 4)]


def project_queries(ids, normed, weight):
    return pl.pallas_call(
        project_queries_kernel,
        in_specs=[SM, VM, VM],
        out_specs=[VM] * 4,
        out_shape=[shape((ROWS, 256), BF16)] * 4,
        scratch_shapes=[pltpu.VMEM((4, ROWS, 256), BF16)],
        compiler_params=params(10),
        cost_estimate=cost(2 * ROWS * weight.size // 3, weight.size),
        name="project_queries",
    )(ids, normed, near_memory(weight))


BLOCK = 2 * ROWS
LOG2E = 1.4426950408889634


def attend_kernel(count, known, resumed, final, ids, scale, queries, *refs):
    pieces, refs = refs[:count], refs[count:]
    inverses, refs = refs[:known], refs[known:]
    if resumed:
        (old_mixed, old_stats), refs = refs[:2], refs[2:]
    sizes = [ref.shape[0] for ref in pieces]
    starts = [sum(sizes[:i]) for i in range(count)]

    def keys(ref):
        return jnp.concatenate([ref[:, :128], ref[:, 256:]], axis=1)

    total_known = sum(ref.shape[1] for ref in inverses)
    if total_known < sum(sizes):
        outs, inverse = refs[:-1], refs[-1]
        lane = lax.broadcasted_iota(jnp.int32, (8, 256), 1)
        ones = (lane < HEAD).astype(F32).astype(BF16)
        for at, size, ref in zip(starts, sizes, pieces):
            if at < total_known:
                continue
            key = keys(ref).astype(F32)
            square = key * key
            high = square.astype(BF16)
            rest = (square - high.astype(F32)).astype(BF16)
            total = dot_t(ones, high) + dot_t(ones, rest)
            at -= total_known
            inverse[:, at : at + size] = lax.rsqrt(total * (1.0 / HEAD) + EPS)
        inverses = (*inverses, inverse)
    else:
        outs = refs

    def inverse_of(at, size):
        for ref in inverses:
            if at < ref.shape[1]:
                return ref[0:1, at : at + size]
            at -= ref.shape[1]

    limit = 1024
    groups, room = [], 0
    for triple in zip(starts, sizes, pieces):
        if room < triple[1]:
            groups.append([])
            room = limit
        groups[-1].append(triple)
        room -= triple[1]

    def unit(query, factor, group):
        scores, peak = [], None
        for at, size, ref in group:
            part = dot_t(query, keys(ref)) * inverse_of(at, size)
            top = jnp.max(part, axis=1, keepdims=True)
            peak = top if peak is None else jnp.maximum(peak, top)
            scores.append(part)
        total, mixed = None, None
        for part, (_, _, ref) in zip(scores, group):
            exps = jnp.exp2((part - peak) * factor)
            sums = jnp.sum(exps, axis=1, keepdims=True)
            values = jnp.concatenate([ref[:, 128:256], ref[:, 256:]], axis=1)
            term = dot(exps.astype(BF16), values)
            total = sums if total is None else total + sums
            mixed = term if mixed is None else mixed + term
        return peak, total, mixed

    for begin in range(0, queries.shape[0], BLOCK):
        rows = slice(begin, begin + BLOCK)
        query = queries[rows, :]
        wide = query.astype(F32)
        own = lax.rsqrt(jnp.sum(wide * wide, axis=1, keepdims=True) * (1.0 / HEAD) + EPS)
        factor = own * (scale[ids[1]] * (LOG2E / HEAD))
        states = [unit(query, factor, group) for group in groups]
        if resumed:
            states.append((old_stats[rows, 0:1], old_stats[rows, 64:65], old_mixed[rows, :]))
        peak = functools.reduce(jnp.maximum, [state[0] for state in states])
        if len(states) > 1:
            shrink = [jnp.exp2((state[0] - peak) * factor) for state in states]
            total = sum(state[1] * part for state, part in zip(states, shrink))
            mixed = sum(state[2] * part for state, part in zip(states, shrink))
        else:
            _, total, mixed = states[0]
        if not final:
            outs[0][rows, :] = mixed
            half = lax.broadcasted_iota(jnp.int32, (BLOCK, 128), 1) < 64
            outs[1][rows, :] = jnp.where(half, peak, total)
            continue
        mixed = mixed / total
        weight = peak * factor + jnp.log(total) * LOG2E
        high = weight.astype(BF16).astype(F32)
        rest = weight - high
        mid = rest.astype(BF16).astype(F32)
        place = lax.broadcasted_iota(jnp.int32, mixed.shape, 1)
        mixed = jnp.where(place == 128, high, mixed)
        mixed = jnp.where(place == 129, mid, mixed)
        mixed = jnp.where(place == 130, rest - mid, mixed)
        outs[0][rows, :] = mixed.astype(BF16)


def attend(ids, scale, queries, pieces, inverses=(), state=(), final=True):
    rows = queries.shape[0]
    keys = sum(piece.shape[0] for piece in pieces)
    if final:
        outs = [shape((rows, 256), BF16)]
    else:
        outs = [shape((rows, 256), F32), shape((rows, 128), F32)]
    known = sum(inverse.shape[1] for inverse in inverses)
    if known < keys:
        outs.append(shape((8, keys - known), F32))
    return pl.pallas_call(
        functools.partial(attend_kernel, len(pieces), len(inverses), bool(state), final),
        in_specs=[SM, SM] + [VM] * (1 + len(pieces) + len(inverses) + len(state)),
        out_specs=[VM] * len(outs),
        out_shape=outs,
        compiler_params=params(28),
        cost_estimate=cost(4 * rows * keys * 256, 8 * rows * 1024),
        name="attend",
    )(ids, scale, near_memory(queries), *pieces, *inverses, *state)


def merge_kernel(a0, a1, *outs):
    parts = [ref[...].astype(F32) for ref in (a0, a1)]
    logs = [p[:, 128:129] + p[:, 129:130] + p[:, 130:131] for p in parts]
    peak = functools.reduce(jnp.maximum, logs)
    shares = [jnp.exp2(log - peak) for log in logs]
    total = sum(shares)
    mixed = sum(p * (share / total) for p, share in zip(parts, shares))
    mixed = jnp.concatenate([mixed[:, :128], pltpu.roll(mixed[:, 128:], 64, 1)], axis=1)
    for block in range(4):
        outs[block][...] = mixed[block * ROWS : (block + 1) * ROWS].astype(BF16)


def merge(parts):
    return pl.pallas_call(
        merge_kernel,
        in_specs=[VM] * 2,
        out_specs=[VM] * 4,
        out_shape=[shape((ROWS, 256), BF16)] * 4,
        compiler_params=params(8),
        cost_estimate=cost(20 * parts[0].size, 10 * parts[0].size),
        name="merge",
    )(*parts)


def output_kernel(mine, ids, a0, a1, a2, a3, weight, out):
    half = out.shape[1]
    side = ids[0] if mine else 1 - ids[0]

    def tile(i):
        at = lanes(side * half + i * TILE, TILE)
        total = None
        for distance, ref in enumerate((a0, a1, a2, a3)):
            head = lax.rem(ids[1] + distance, 4)
            rows = weight[pl.ds(pl.multiple_of(head * HEAD, HEAD), HEAD), at]
            term = dot(ref[:, :HEAD], rows)
            total = term if total is None else total + term
        out[:, lanes(i * TILE, TILE)] = total.astype(out.dtype)

    tiles(half // TILE, tile)


def output(ids, heads, weight, mine, dtype):
    half = weight.shape[1] // 2
    return pl.pallas_call(
        functools.partial(output_kernel, mine),
        in_specs=[SM] + [VM] * 5,
        out_specs=VM,
        out_shape=shape((ROWS, half), dtype),
        compiler_params=params(6),
        cost_estimate=cost(2 * ROWS * weight.size // 2, weight.size),
        name="output",
    )(ids, *heads, weight)


def decode_first_kernel(ids, own, other, encoded, weight, inputs, out):
    half = weight.shape[1]

    def mix(i):
        at = lanes(i * TILE, TILE)
        enc = encoded[:, at].astype(F32)
        even, odd = enc[:ROWS], enc[ROWS:]
        binned = (even + odd) * 0.5
        block = (binned + (own[:, at] + other[:, at].astype(F32))).astype(BF16).astype(F32)
        row = lax.broadcasted_iota(jnp.int32, block.shape, 0)
        outside = ((ids[2] == 0) & (row == ROWS - 1)) | ((ids[2] == 63) & (row == OWN))
        even = jnp.where(outside, 0.0, block + even)
        odd = jnp.where(outside, 0.0, block + odd)
        inputs[:, at] = jnp.concatenate([even, odd], axis=0).astype(BF16)

    tiles(half // TILE, mix)
    decode_tiles(inputs, weight, out, (1 - ids[0]) * half)


def decode_tiles(inputs, weight, out, begin):
    def tile(i):
        at = lanes(begin + i * TILE, TILE)
        result = conv_taps(inputs[...], lambda t: weight[t, :, at], ROWS)
        out[:, lanes(i * TILE, TILE)] = result.astype(out.dtype)

    tiles(out.shape[1] // TILE, tile)


def decode_first(ids, own, other, encoded, weight, width):
    half = weight.shape[1]
    return pl.pallas_call(
        decode_first_kernel,
        in_specs=[SM] + [VM] * 4,
        out_specs=[VM] * 2,
        out_shape=[shape((2 * ROWS, half), BF16), shape((2 * ROWS, width), BF16)],
        compiler_params=params(8),
        cost_estimate=cost(10**6, 10**4),
        name="decode_first",
    )(ids, own, other, encoded, weight)


def decode_kernel(mine, first, ids, inputs, weight, out):
    side = ids[0] if mine else 1 - ids[0]
    decode_tiles(inputs, weight, out, side * weight.shape[1] + first)


def decode(ids, inputs, weight, mine, first, width, dtype):
    half = weight.shape[1]
    return pl.pallas_call(
        functools.partial(decode_kernel, mine, first),
        in_specs=[SM, VM, VM],
        out_specs=VM,
        out_shape=shape((2 * ROWS, width), dtype),
        compiler_params=params(8),
        cost_estimate=cost(10**6, 10**4),
        name="decode",
    )(ids, inputs, weight)


def slope_kernel(first, ids, own, other, inputs, grad, near, far, *refs):
    done, (decoded, slope, paired, wide) = refs[:-4], refs[-4:]
    half = own.shape[1]
    begin = 0
    if done:
        begin = first
        decoded[:, :first] = done[0][...]

    def tile(i):
        at = lanes(i * 128, 128)
        target = lanes(begin + i * 128, 128)
        source = lanes(first + i * 128, 128)
        column = lanes(ids[0] * half + first + i * 128, 128)
        pre = own[:, source] + other[:, at].astype(F32)
        tanh = gelu_tanh(pre)
        result = inputs[:, source].astype(F32) + 0.5 * pre * (1.0 + tanh)
        wide[0, pl.ds(0, OWN, 2), :] = result[:OWN]
        wide[0, pl.ds(1, OWN, 2), :] = result[ROWS : ROWS + OWN]
        decoded[:, target] = wide[0].astype(BF16)
        slant = 0.5 * (1.0 + tanh) + (0.5 * 0.7978845608028654) * pre * (1.0 - tanh * tanh) * (
            1.0 + (3 * 0.044715) * (pre * pre)
        )
        wide[1] = grad[:, column].astype(F32)
        even = wide[1, pl.ds(0, OWN, 2), :]
        odd = wide[1, pl.ds(1, OWN, 2), :]
        paired[:, at] = even + odd
        row = lax.broadcasted_iota(jnp.int32, (ROWS - OWN, 128), 0)
        before, after = sides(ids, near[:, column].astype(F32), far[:, column].astype(F32))
        even_edge = jnp.where(row == 0, after, 0.0)
        odd_edge = jnp.where(row == ROWS - OWN - 1, before, 0.0)
        cotangent = jnp.concatenate([even, even_edge, odd, odd_edge], axis=0)
        slope[:, at] = (cotangent * slant).astype(BF16)

    tiles(other.shape[1] // 128, tile)


def slopes(ids, own, other, inputs, grad, near, far, first, done=()):
    width = other.shape[1]
    return pl.pallas_call(
        functools.partial(slope_kernel, first),
        in_specs=[SM] + [VM] * (6 + len(done)),
        out_specs=[VM] * 3,
        out_shape=[
            shape((2 * OWN, width + (first if done else 0)), BF16),
            shape((2 * ROWS, width), BF16),
            shape((OWN, width), F32),
        ],
        scratch_shapes=[pltpu.VMEM((2, 2 * OWN, 128), F32)],
        compiler_params=params(6),
        cost_estimate=cost(100 * 30 * 1000 * other.size, 14 * other.size),
        name="slopes",
    )(ids, own, other, inputs, grad, near, far, *done)


def backward_kernel(mine, firsts, count, ids, *refs):
    slopes_in, starts, (weight, out, level, lower, upper) = (
        refs[: len(firsts)],
        refs[len(firsts) : len(firsts) + count],
        refs[len(firsts) + count :],
    )
    half = weight.shape[1]
    side = ids[0] if mine else 1 - ids[0]
    level[...] = jnp.zeros_like(level)
    lower[...] = jnp.zeros_like(lower)
    upper[...] = jnp.zeros_like(upper)

    for begin, slope in zip(firsts, slopes_in):

        def tile(i):
            at = lanes(side * half + begin + i * TILE, TILE)
            part = slope[:, lanes(i * TILE, TILE)]
            first, mid, last = (dot_t(part, weight[t, :, at]) for t in range(3))
            level[...] += first[ROWS:] + mid[:ROWS] + mid[ROWS:] + last[:ROWS]
            lower[...] += first[:ROWS]
            upper[...] += last[ROWS:]

        tiles(slope.shape[1] // TILE, tile)
    total = level[...] + below(lower[...], ROWS) + above(upper[...], ROWS)
    base = jnp.concatenate([start[...] for start in starts], axis=1)
    out[...] = (base + total[:OWN]).astype(out.dtype)


def backward(ids, parts, starts, weight, mine, dtype):
    half = weight.shape[1]
    size = sum(part.size for _, part in parts)
    return pl.pallas_call(
        functools.partial(backward_kernel, mine, [first for first, _ in parts], len(starts)),
        in_specs=[SM] + [VM] * (len(parts) + len(starts) + 1),
        out_specs=VM,
        out_shape=shape((OWN, half), dtype),
        scratch_shapes=[pltpu.VMEM((ROWS, half), F32)] * 3,
        compiler_params=params(10),
        cost_estimate=cost(100 * 2 * 3 * half * size, 6 * size),
        name="backward",
    )(ids, *[part for _, part in parts], *starts, weight)


def place(at):
    return at // 16, at // 4 % 4, at // 2 % 2, at % 2


def moves(dx=0, dz=0, dy=0, dc=0):
    pairs = []
    for at in range(64):
        x, z, y, c = place(at)
        pairs.append((at, (x + dx) % 4 * 16 + (z + dz) % 4 * 4 + (y ^ dy) * 2 + (c ^ dc)))
    return pairs


def swap(value):
    return lax.ppermute(value, "head", [(0, 1), (1, 0)])


def send(value, **step):
    return lax.ppermute(value, "seq", moves(**step))


def per_device(
    dna_bases,
    stem_weight,
    encoder_weight,
    norm_gain,
    attention_weight,
    logit_scale,
    out_weight,
    decoder_weight,
    grad_out,
):
    at = lax.axis_index("seq")
    x = at // 16
    ids = jnp.stack([lax.axis_index("head"), x, at]).astype(jnp.int32)
    feats = grad_out.shape[1]

    codes, near, far = prepare(ids, dna_bases.reshape(OWN, 128), grad_out)
    near = send(near, dc=1)
    pairs = [(i, i + 1) for i in range(1, 63, 2)]
    far = lax.ppermute(far, "seq", pairs + [(b, a) for a, b in pairs])
    halo = near, far
    rows, stem_weight, encoder_weight = load(codes, stem_weight, encoder_weight)
    encoded, attention_weight = encode(
        ids, *halo, rows, stem_weight, encoder_weight, attention_weight
    )
    gain = norm_gain.reshape(1, feats)
    normed, *keyvals = project_keys(ids, encoded, swap(encoded), gain, attention_weight)

    def spread(blocks):
        return [send(blocks[d], dx=d) for d in (1, 3, 2)]

    def stacked(blocks):
        return jnp.concatenate(lax.optimization_barrier(blocks), axis=0)

    got = spread(keyvals)
    keyvals = stacked([keyvals[0]] + got)
    near = [send(keyvals, dz=1), send(keyvals, dz=3)]
    queries = project_queries(ids, normed, attention_weight)
    *near, got = lax.optimization_barrier((*near, spread(queries)))
    queries = jnp.concatenate([queries[0]] + got, axis=0)
    others = send(queries, dy=1)
    half = keyvals.shape[0] // 2
    far = [send(near[0][:half], dz=1), send(near[1][half:], dz=3)]
    across = [send(piece, dc=1) for piece in (keyvals, *near)]
    *far, across, others = lax.optimization_barrier((*far, across, others))
    far = jnp.concatenate(far, axis=0)
    pieces = [keyvals] + near + across + [far, send(far, dc=1)]
    other, inverse = attend(ids, logit_scale, others, pieces)
    other = send(other, dy=1)
    own = attend(ids, logit_scale, queries, pieces, inverses=[inverse])[0]
    mixed = merge([own, other])
    heads = [mixed[0], send(mixed[1], dx=-1), send(mixed[3], dx=-2), send(mixed[2], dx=-3)]

    sent = swap(output(ids, heads, out_weight, False, BF16))
    kept = output(ids, heads, out_weight, True, F32)
    half = decoder_weight.shape[1]
    split = TILE
    inputs, early = decode_first(ids, kept, sent, encoded, decoder_weight, split)
    early = swap(early)
    late = decode(ids, inputs, decoder_weight, False, split, half - split, BF16)
    late, inputs = lax.optimization_barrier((late, inputs))
    late = swap(late)
    kept = decode(ids, inputs, decoder_weight, True, 0, half, F32)
    decoded, early, paired = slopes(ids, kept, early, inputs, grad_out, *halo, 0)
    early_back = swap(early)
    decoded, late, rest = slopes(
        ids, kept, late, inputs, grad_out, *halo, split, (decoded,)
    )
    late_back = swap(late)
    total = backward(
        ids, [(0, early), (split, late)], [paired, rest], decoder_weight, True, F32
    )
    total = backward(ids, [(0, early_back)], [total], decoder_weight, False, F32)
    bins_grad = backward(ids, [(split, late_back)], [total], decoder_weight, False, BF16)
    return decoded, bins_grad


def solution(mesh):
    in_specs = (
        P("seq"),
        P(),
        P(None, None, "head"),
        P(),
        P(None, None, "head"),
        P("head"),
        P("head", None),
        P(None, "head", None),
        P("seq", None),
    )
    out_specs = (P("seq", "head"), P("seq", "head"))
    return jax.shard_map(
        per_device, mesh=mesh, in_specs=in_specs, out_specs=out_specs, check_vma=False
    )
```

```python
import functools

import jax
import jax.numpy as jnp
from jax import lax
from jax.experimental import pallas as pl
from jax.experimental.pallas import tpu as pltpu
from jax.sharding import PartitionSpec as P

BF16 = jnp.bfloat16
F32 = jnp.float32
ROWS = 136
OWN = 128
TILE = 256
HEAD = 192
EPS = 1e-06
MIB = 1024 * 1024


def params(mib):
    return pltpu.CompilerParams(vmem_limit_bytes=mib * MIB)


def dot(a, b):
    return jnp.dot(a, b, preferred_element_type=F32)


def dot_t(a, b):
    return lax.dot_general(a, b, (((1,), (1,)), ((), ())), preferred_element_type=F32)


def cost(flops, nbytes):
    return pl.CostEstimate(flops=int(flops), bytes_accessed=int(nbytes), transcendentals=0)


def shape(dims, dtype):
    return jax.ShapeDtypeStruct(dims, dtype)


VM = pl.BlockSpec(memory_space=pltpu.VMEM)
SM = pl.BlockSpec(memory_space=pltpu.SMEM)
HBM = pl.BlockSpec(memory_space=pltpu.HBM)


def above(rows, span):
    parts = [pltpu.roll(rows[i : i + span], 1, 0) for i in range(0, rows.shape[0], span)]
    return jnp.concatenate(parts, axis=0)


def below(rows, span):
    parts = [pltpu.roll(rows[i : i + span], span - 1, 0) for i in range(0, rows.shape[0], span)]
    return jnp.concatenate(parts, axis=0)


def lanes(at, size):
    return pl.ds(pl.multiple_of(at, size), size)


def tiles(count, body):
    lax.fori_loop(0, count, lambda i, carry: (body(i), carry)[1], 0)


def gelu_tanh(x):
    return jnp.tanh(0.7978845608028654 * (x + 0.044715 * (x * x * x)))


def conv_taps(rows, weight, span):
    half = rows.shape[0] // 2
    first, mid, last = (dot(rows, weight(t)) for t in range(3))
    even = above(first[half:], span) + mid[:half] + last[half:]
    odd = first[:half] + mid[half:] + below(last[:half], span)
    return jnp.concatenate([even, odd], axis=0)


def sides(ids, near, far):
    odd = lax.rem(ids[2], 2) == 1
    return jnp.where(odd, near, far), jnp.where(odd, far, near)


def prepare_kernel(ids, bases, grad, codes, near, far, code, head, tail, sems):
    rows = grad.shape[0]
    copies = [
        pltpu.make_async_copy(bases, code, sems.at[0]),
        pltpu.make_async_copy(grad.at[pl.ds(0, 16)], head, sems.at[1]),
        pltpu.make_async_copy(grad.at[pl.ds(rows - 16, 16)], tail, sems.at[2]),
    ]
    for copy in copies:
        copy.start()
    for copy in copies:
        copy.wait()
    feats = grad.shape[1]
    letters = (code[...] + 1).astype(F32)
    codes[...] = letters.astype(BF16)
    odd = lax.rem(ids[2], 2) == 1
    last = jnp.concatenate([tail[...].astype(F32)[8:], letters[OWN - 8 :]], axis=1)
    first = jnp.concatenate([head[...].astype(F32)[:8], letters[:8]], axis=1)
    near[...] = jnp.where(odd, first, last).astype(BF16)
    far[...] = jnp.where(odd, last, first).astype(BF16)


def near_memory(value):
    return pltpu.with_memory_space_constraint(value, pltpu.VMEM)


def far_memory(value):
    return pltpu.with_memory_space_constraint(value, pltpu.HBM)


def prepare(ids, bases, grad):
    feats = grad.shape[1]
    return pl.pallas_call(
        prepare_kernel,
        in_specs=[SM, HBM, HBM],
        out_specs=[VM] * 3,
        out_shape=[
            shape((OWN, 128), BF16),
            shape((8, feats + 128), BF16),
            shape((8, feats + 128), BF16),
        ],
        scratch_shapes=[
            pltpu.VMEM(bases.shape, jnp.int32),
            pltpu.VMEM((16, feats), BF16),
            pltpu.VMEM((16, feats), BF16),
            pltpu.SemaphoreType.DMA((3,)),
        ],
        compiler_params=params(4),
        cost_estimate=cost(10**5, 10**5),
        name="prepare",
    )(ids, far_memory(bases), far_memory(grad))


def embed_letters(code, stem, embedded):
    patch = stem.shape[0] // 4
    row = lax.broadcasted_iota(jnp.int32, (2 * patch, 4 * patch), 0)
    col = lax.broadcasted_iota(jnp.int32, (2 * patch, 4 * patch), 1)
    spread = [
        dot(code, (row == col // 4 + offset).astype(F32).astype(BF16)) for offset in (0, patch)
    ]
    spread = jnp.concatenate(spread, axis=0)
    base = lax.broadcasted_iota(jnp.int32, spread.shape, 1) % 4 + 1
    onehot = (spread == base.astype(F32)).astype(F32).astype(BF16)

    def embed(i):
        at = lanes(i * TILE, TILE)
        embedded[:, at] = dot(onehot, stem[:, at]).astype(BF16)

    tiles(stem.shape[1] // TILE, embed)


def load_kernel(codes, stems, weights, embedded, stem, weight, sems):
    copies = [
        pltpu.make_async_copy(stems, stem, sems.at[0]),
        pltpu.make_async_copy(weights, weight, sems.at[1]),
    ]
    for copy in copies:
        copy.start()
    copies[0].wait()
    embed_letters(codes[...], stem, embedded)
    copies[1].wait()


def load(codes, stem, weight):
    return pl.pallas_call(
        load_kernel,
        in_specs=[VM, HBM, HBM],
        out_specs=[VM] * 3,
        out_shape=[
            pltpu.VMEM((2 * OWN, stem.shape[1]), BF16),
            pltpu.VMEM(stem.shape, BF16),
            pltpu.VMEM(weight.shape, BF16),
        ],
        scratch_shapes=[pltpu.SemaphoreType.DMA((2,))],
        compiler_params=params(4),
        cost_estimate=cost(10**5, weight.size * 2),
        name="load",
    )(codes, far_memory(stem), far_memory(weight))


def ring_order(rows):
    half = ROWS - OWN
    return (
        jnp.concatenate([rows[:OWN], rows[2 * OWN : 2 * OWN + half]], axis=0),
        jnp.concatenate([rows[OWN : 2 * OWN], rows[2 * OWN + half :]], axis=0),
    )


def encode_kernel(ids, near, far, rows, stem, weight, ahead, encoded, loaded, embedded, halo, sem):
    copy = pltpu.make_async_copy(ahead, loaded, sem)
    copy.start()
    feats = stem.shape[1]
    half = weight.shape[2]
    place = lax.broadcasted_iota(jnp.int32, (ROWS - OWN, 128), 0)
    before, after = sides(ids, near[:, feats:].astype(F32), far[:, feats:].astype(F32))
    code = jnp.where(place >= 6, before, 0.0)
    code = jnp.where(place < 2, after, code)
    embed_letters(code.astype(BF16), stem, halo)
    embedded[: 2 * OWN, :] = rows[...]
    embedded[2 * OWN :, :] = halo[...]

    def convolve(i):
        at = lanes(i * TILE, TILE)
        parts = [dot(embedded[...], weight[tap, :, at]) for tap in range(3)]
        (first_even, first_odd), (even, odd), (last_even, last_odd) = map(ring_order, parts)
        even = above(first_odd, ROWS) + even + last_odd
        odd = first_even + odd + below(last_even, ROWS)
        pre = jnp.concatenate([even, odd], axis=0)
        mine = embedded[:, lanes(ids[0] * half + i * TILE, TILE)].astype(F32)
        mine = jnp.concatenate(ring_order(mine), axis=0)
        encoded[:, at] = (mine + 0.5 * pre * (1.0 + gelu_tanh(pre))).astype(BF16)

    tiles(half // TILE, convolve)
    copy.wait()


def encode(ids, near, far, rows, stem, weight, ahead):
    half = weight.shape[2]
    feats = stem.shape[1]
    return pl.pallas_call(
        encode_kernel,
        in_specs=[SM] + [VM] * 5 + [HBM],
        out_specs=[VM, VM],
        out_shape=[shape((2 * ROWS, half), BF16), pltpu.VMEM(ahead.shape, BF16)],
        scratch_shapes=[
            pltpu.VMEM((2 * ROWS, feats), BF16),
            pltpu.VMEM((2 * (ROWS - OWN), feats), BF16),
            pltpu.SemaphoreType.DMA(()),
        ],
        compiler_params=params(12),
        cost_estimate=cost(4 * OWN * weight.size, weight.size * 4),
        name="encode",
    )(
        ids,
        near,
        far,
        near_memory(rows),
        near_memory(stem),
        near_memory(weight),
        far_memory(ahead),
    )


def unpacked(both):
    both = both.astype(BF16).astype(F32)
    turned = pltpu.roll(both, 2 * HEAD - 64, 1)
    return (both[:, :128], both[:, 128:256]), (turned[:, 128:256], turned[:, 256:384])


def project_keys_kernel(
    ids, mine, theirs, gain, weight, normed, k0, k1, k2, k3, packed
):
    half = mine.shape[1]
    near = lanes(ids[0] * half, half)
    far = lanes((1 - ids[0]) * half, half)
    rings = [ref[...].astype(F32) for ref in (mine, theirs)]
    binned = [(ring[:ROWS] + ring[ROWS:]) * 0.5 for ring in rings]
    total = sum(jnp.sum(part * part, axis=1, keepdims=True) for part in binned)
    inverse = lax.rsqrt(total * (1.0 / (2 * half)) + EPS)
    here = (binned[0] * inverse * gain[:, near]).astype(BF16)
    there = (binned[1] * inverse * gain[:, far]).astype(BF16)
    normed[0] = here
    normed[1] = there
    low = lax.broadcasted_iota(jnp.int32, (ROWS, 128), 1) < 64
    for pair in range(2):
        at = slice(pair * 2 * HEAD, (pair + 1) * 2 * HEAD)
        keys, values = (
            unpacked(dot(here, weight[kind, near, at]) + dot(there, weight[kind, far, at]))
            for kind in (1, 2)
        )
        for side in range(2):
            head = 2 * pair + side
            key, value = keys[side], values[side]
            packed[head, :, :128] = key[0].astype(BF16)
            packed[head, :, 128:256] = value[0].astype(BF16)
            tail = jnp.where(low, key[1], pltpu.roll(value[1], 64, 1))
            packed[head, :, 256:] = tail.astype(BF16)
    for distance, out in enumerate((k0, k1, k2, k3)):
        out[...] = packed[lax.rem(ids[1] + distance, 4), :OWN, :]


def project_keys(ids, mine, theirs, gain, weight):
    half = mine.shape[1]
    return pl.pallas_call(
        project_keys_kernel,
        in_specs=[SM] + [VM] * 4,
        out_specs=[VM] * 5,
        out_shape=[shape((2, ROWS, half), BF16)] + [shape((OWN, 384), BF16)] * 4,
        scratch_shapes=[pltpu.VMEM((4, ROWS, 384), BF16)],
        compiler_params=params(12),
        cost_estimate=cost(2 * ROWS * weight.size * 2 // 3, weight.size * 2),
        name="project_keys",
    )(ids, mine, theirs, gain, weight)


def project_queries_kernel(ids, normed, weight, q0, q1, q2, q3, packed):
    half = normed.shape[2]
    near = lanes(ids[0] * half, half)
    far = lanes((1 - ids[0]) * half, half)
    low = lax.broadcasted_iota(jnp.int32, (ROWS, 128), 1) < 64
    for pair in range(2):
        at = slice(pair * 2 * HEAD, (pair + 1) * 2 * HEAD)
        both = dot(normed[0], weight[0, near, at]) + dot(normed[1], weight[0, far, at])
        for side, query in enumerate(unpacked(both)):
            packed[2 * pair + side, :, :128] = query[0].astype(BF16)
            packed[2 * pair + side, :, 128:] = jnp.where(low, query[1], 0.0).astype(BF16)
    for distance, out in enumerate((q0, q1, q2, q3)):
        out[...] = packed[lax.rem(ids[1] + distance, 4)]


def project_queries(ids, normed, weight):
    return pl.pallas_call(
        project_queries_kernel,
        in_specs=[SM, VM, VM],
        out_specs=[VM] * 4,
        out_shape=[shape((ROWS, 256), BF16)] * 4,
        scratch_shapes=[pltpu.VMEM((4, ROWS, 256), BF16)],
        compiler_params=params(10),
        cost_estimate=cost(2 * ROWS * weight.size // 3, weight.size),
        name="project_queries",
    )(ids, normed, near_memory(weight))


BLOCK = 4 * ROWS
LOG2E = 1.4426950408889634


def attend_kernel(count, known, resumed, final, ids, scale, queries, *refs):
    pieces, refs = refs[:count], refs[count:]
    inverses, refs = refs[:known], refs[known:]
    if resumed:
        (old_mixed, old_stats), refs = refs[:2], refs[2:]
    sizes = [ref.shape[0] for ref in pieces]
    starts = [sum(sizes[:i]) for i in range(count)]

    def keys(ref):
        return jnp.concatenate([ref[:, :128], ref[:, 256:]], axis=1)

    total_known = sum(ref.shape[1] for ref in inverses)
    if total_known < sum(sizes):
        outs, inverse = refs[:-1], refs[-1]
        lane = lax.broadcasted_iota(jnp.int32, (8, 256), 1)
        ones = (lane < HEAD).astype(F32).astype(BF16)
        for at, size, ref in zip(starts, sizes, pieces):
            if at < total_known:
                continue
            key = keys(ref).astype(F32)
            square = key * key
            high = square.astype(BF16)
            rest = (square - high.astype(F32)).astype(BF16)
            total = dot_t(ones, high) + dot_t(ones, rest)
            at -= total_known
            inverse[:, at : at + size] = lax.rsqrt(total * (1.0 / HEAD) + EPS)
        inverses = (*inverses, inverse)
    else:
        outs = refs

    def inverse_of(at, size):
        for ref in inverses:
            if at < ref.shape[1]:
                return ref[0:1, at : at + size]
            at -= ref.shape[1]

    limit = 1024
    groups, room = [], 0
    for triple in zip(starts, sizes, pieces):
        if room < triple[1]:
            groups.append([])
            room = limit
        groups[-1].append(triple)
        room -= triple[1]

    def unit(query, factor, group):
        scores, peak = [], None
        for at, size, ref in group:
            part = dot_t(query, keys(ref)) * inverse_of(at, size)
            top = jnp.max(part, axis=1, keepdims=True)
            peak = top if peak is None else jnp.maximum(peak, top)
            scores.append(part)
        total, mixed = None, None
        for part, (_, _, ref) in zip(scores, group):
            exps = jnp.exp2((part - peak) * factor)
            sums = jnp.sum(exps, axis=1, keepdims=True)
            values = jnp.concatenate([ref[:, 128:256], ref[:, 256:]], axis=1)
            term = dot(exps.astype(BF16), values)
            total = sums if total is None else total + sums
            mixed = term if mixed is None else mixed + term
        return peak, total, mixed

    for begin in range(0, queries.shape[0], BLOCK):
        rows = slice(begin, begin + BLOCK)
        query = queries[rows, :]
        wide = query.astype(F32)
        own = lax.rsqrt(jnp.sum(wide * wide, axis=1, keepdims=True) * (1.0 / HEAD) + EPS)
        factor = own * (scale[ids[1]] * (LOG2E / HEAD))
        states = [unit(query, factor, group) for group in groups]
        if resumed:
            states.append((old_stats[rows, 0:1], old_stats[rows, 64:65], old_mixed[rows, :]))
        peak = functools.reduce(jnp.maximum, [state[0] for state in states])
        if len(states) > 1:
            shrink = [jnp.exp2((state[0] - peak) * factor) for state in states]
            total = sum(state[1] * part for state, part in zip(states, shrink))
            mixed = sum(state[2] * part for state, part in zip(states, shrink))
        else:
            _, total, mixed = states[0]
        if not final:
            outs[0][rows, :] = mixed
            half = lax.broadcasted_iota(jnp.int32, (BLOCK, 128), 1) < 64
            outs[1][rows, :] = jnp.where(half, peak, total)
            continue
        mixed = mixed / total
        weight = peak * factor + jnp.log(total) * LOG2E
        high = weight.astype(BF16).astype(F32)
        rest = weight - high
        mid = rest.astype(BF16).astype(F32)
        place = lax.broadcasted_iota(jnp.int32, mixed.shape, 1)
        mixed = jnp.where(place == 128, high, mixed)
        mixed = jnp.where(place == 129, mid, mixed)
        mixed = jnp.where(place == 130, rest - mid, mixed)
        outs[0][rows, :] = mixed.astype(BF16)


def attend(ids, scale, queries, pieces, inverses=(), state=(), final=True):
    rows = queries.shape[0]
    keys = sum(piece.shape[0] for piece in pieces)
    if final:
        outs = [shape((rows, 256), BF16)]
    else:
        outs = [shape((rows, 256), F32), shape((rows, 128), F32)]
    known = sum(inverse.shape[1] for inverse in inverses)
    if known < keys:
        outs.append(shape((8, keys - known), F32))
    return pl.pallas_call(
        functools.partial(attend_kernel, len(pieces), len(inverses), bool(state), final),
        in_specs=[SM, SM] + [VM] * (1 + len(pieces) + len(inverses) + len(state)),
        out_specs=[VM] * len(outs),
        out_shape=outs,
        compiler_params=params(28),
        cost_estimate=cost(4 * rows * keys * 256, 8 * rows * 1024),
        name="attend",
    )(ids, scale, near_memory(queries), *pieces, *inverses, *state)


def merge_kernel(a0, a1, *outs):
    parts = [ref[...].astype(F32) for ref in (a0, a1)]
    logs = [p[:, 128:129] + p[:, 129:130] + p[:, 130:131] for p in parts]
    peak = functools.reduce(jnp.maximum, logs)
    shares = [jnp.exp2(log - peak) for log in logs]
    total = sum(shares)
    mixed = sum(p * (share / total) for p, share in zip(parts, shares))
    mixed = jnp.concatenate([mixed[:, :128], pltpu.roll(mixed[:, 128:], 64, 1)], axis=1)
    for block in range(4):
        outs[block][...] = mixed[block * ROWS : (block + 1) * ROWS].astype(BF16)


def merge(parts):
    return pl.pallas_call(
        merge_kernel,
        in_specs=[VM] * 2,
        out_specs=[VM] * 4,
        out_shape=[shape((ROWS, 256), BF16)] * 4,
        compiler_params=params(8),
        cost_estimate=cost(20 * parts[0].size, 10 * parts[0].size),
        name="merge",
    )(*parts)


def output_kernel(mine, ids, a0, a1, a2, a3, weight, out):
    half = out.shape[1]
    side = ids[0] if mine else 1 - ids[0]

    def tile(i):
        at = lanes(side * half + i * TILE, TILE)
        total = None
        for distance, ref in enumerate((a0, a1, a2, a3)):
            head = lax.rem(ids[1] + distance, 4)
            rows = weight[pl.ds(pl.multiple_of(head * HEAD, HEAD), HEAD), at]
            term = dot(ref[:, :HEAD], rows)
            total = term if total is None else total + term
        out[:, lanes(i * TILE, TILE)] = total.astype(out.dtype)

    tiles(half // TILE, tile)


def output(ids, heads, weight, mine, dtype):
    half = weight.shape[1] // 2
    return pl.pallas_call(
        functools.partial(output_kernel, mine),
        in_specs=[SM] + [VM] * 5,
        out_specs=VM,
        out_shape=shape((ROWS, half), dtype),
        compiler_params=params(6),
        cost_estimate=cost(2 * ROWS * weight.size // 2, weight.size),
        name="output",
    )(ids, *heads, weight)


def decode_first_kernel(ids, own, other, encoded, weight, inputs, out):
    half = weight.shape[1]

    def mix(i):
        at = lanes(i * TILE, TILE)
        enc = encoded[:, at].astype(F32)
        even, odd = enc[:ROWS], enc[ROWS:]
        binned = (even + odd) * 0.5
        block = (binned + (own[:, at] + other[:, at].astype(F32))).astype(BF16).astype(F32)
        row = lax.broadcasted_iota(jnp.int32, block.shape, 0)
        outside = ((ids[2] == 0) & (row == ROWS - 1)) | ((ids[2] == 63) & (row == OWN))
        even = jnp.where(outside, 0.0, block + even)
        odd = jnp.where(outside, 0.0, block + odd)
        inputs[:, at] = jnp.concatenate([even, odd], axis=0).astype(BF16)

    tiles(half // TILE, mix)
    decode_tiles(inputs, weight, out, (1 - ids[0]) * half)


def decode_tiles(inputs, weight, out, begin):
    def tile(i):
        at = lanes(begin + i * TILE, TILE)
        result = conv_taps(inputs[...], lambda t: weight[t, :, at], ROWS)
        out[:, lanes(i * TILE, TILE)] = result.astype(out.dtype)

    tiles(out.shape[1] // TILE, tile)


def decode_first(ids, own, other, encoded, weight, width):
    half = weight.shape[1]
    return pl.pallas_call(
        decode_first_kernel,
        in_specs=[SM] + [VM] * 4,
        out_specs=[VM] * 2,
        out_shape=[shape((2 * ROWS, half), BF16), shape((2 * ROWS, width), BF16)],
        compiler_params=params(8),
        cost_estimate=cost(10**6, 10**4),
        name="decode_first",
    )(ids, own, other, encoded, weight)


def decode_kernel(mine, first, ids, inputs, weight, out):
    side = ids[0] if mine else 1 - ids[0]
    decode_tiles(inputs, weight, out, side * weight.shape[1] + first)


def decode(ids, inputs, weight, mine, first, width, dtype):
    half = weight.shape[1]
    return pl.pallas_call(
        functools.partial(decode_kernel, mine, first),
        in_specs=[SM, VM, VM],
        out_specs=VM,
        out_shape=shape((2 * ROWS, width), dtype),
        compiler_params=params(8),
        cost_estimate=cost(10**6, 10**4),
        name="decode",
    )(ids, inputs, weight)


def slope_kernel(first, ids, own, other, inputs, grad, near, far, *refs):
    done, (decoded, slope, paired, wide) = refs[:-4], refs[-4:]
    half = own.shape[1]
    begin = 0
    if done:
        begin = first
        decoded[:, :first] = done[0][...]

    def tile(i):
        at = lanes(i * 128, 128)
        target = lanes(begin + i * 128, 128)
        source = lanes(first + i * 128, 128)
        column = lanes(ids[0] * half + first + i * 128, 128)
        pre = own[:, source] + other[:, at].astype(F32)
        tanh = gelu_tanh(pre)
        result = inputs[:, source].astype(F32) + 0.5 * pre * (1.0 + tanh)
        wide[0, pl.ds(0, OWN, 2), :] = result[:OWN]
        wide[0, pl.ds(1, OWN, 2), :] = result[ROWS : ROWS + OWN]
        decoded[:, target] = wide[0].astype(BF16)
        slant = 0.5 * (1.0 + tanh) + (0.5 * 0.7978845608028654) * pre * (1.0 - tanh * tanh) * (
            1.0 + (3 * 0.044715) * (pre * pre)
        )
        wide[1] = grad[:, column].astype(F32)
        even = wide[1, pl.ds(0, OWN, 2), :]
        odd = wide[1, pl.ds(1, OWN, 2), :]
        paired[:, at] = even + odd
        row = lax.broadcasted_iota(jnp.int32, (ROWS - OWN, 128), 0)
        before, after = sides(ids, near[:, column].astype(F32), far[:, column].astype(F32))
        even_edge = jnp.where(row == 0, after, 0.0)
        odd_edge = jnp.where(row == ROWS - OWN - 1, before, 0.0)
        cotangent = jnp.concatenate([even, even_edge, odd, odd_edge], axis=0)
        slope[:, at] = (cotangent * slant).astype(BF16)

    tiles(other.shape[1] // 128, tile)


def slopes(ids, own, other, inputs, grad, near, far, first, done=()):
    width = other.shape[1]
    return pl.pallas_call(
        functools.partial(slope_kernel, first),
        in_specs=[SM] + [VM] * (6 + len(done)),
        out_specs=[VM] * 3,
        out_shape=[
            shape((2 * OWN, width + (first if done else 0)), BF16),
            shape((2 * ROWS, width), BF16),
            shape((OWN, width), F32),
        ],
        scratch_shapes=[pltpu.VMEM((2, 2 * OWN, 128), F32)],
        compiler_params=params(6),
        cost_estimate=cost(100 * 30 * 1000 * other.size, 14 * other.size),
        name="slopes",
    )(ids, own, other, inputs, grad, near, far, *done)


def backward_kernel(mine, firsts, count, ids, *refs):
    slopes_in, starts, (weight, out) = (
        refs[: len(firsts)],
        refs[len(firsts) : len(firsts) + count],
        refs[len(firsts) + count :],
    )
    half = weight.shape[1]
    side = ids[0] if mine else 1 - ids[0]
    whole = [start for start in starts if start.shape[1] == half]
    chunks = [start for start in starts if start.shape[1] < half]

    def tile(i, chunk, begin):
        inner = lanes(i * TILE, TILE)
        first = mid = last = None
        for offset, slope in zip(firsts, slopes_in):
            at = pl.ds(pl.multiple_of(side * half + offset, TILE), slope.shape[1])
            terms = [dot_t(slope[...], weight[t, inner, at]) for t in range(3)]
            if first is None:
                first, mid, last = terms
            else:
                first, mid, last = first + terms[0], mid + terms[1], last + terms[2]
        total = first[ROWS:] + mid[:ROWS] + mid[ROWS:] + last[:ROWS]
        total = total + below(first[:ROWS], ROWS) + above(last[ROWS:], ROWS)
        total = total[:OWN]
        for start in whole:
            total = total + start[:, inner]
        if chunk is not None:
            total = total + chunk[:, lanes(i * TILE - begin, TILE)]
        out[:, inner] = total.astype(out.dtype)

    if not chunks:
        tiles(half // TILE, lambda i: tile(i, None, 0))
    begin = 0
    for chunk in chunks:
        width = chunk.shape[1]
        tiles(width // TILE, lambda i: tile(i + begin // TILE, chunk, begin))
        begin += width


def backward(ids, parts, starts, weight, mine, dtype):
    half = weight.shape[1]
    size = sum(part.size for _, part in parts)
    return pl.pallas_call(
        functools.partial(backward_kernel, mine, [first for first, _ in parts], len(starts)),
        in_specs=[SM] + [VM] * (len(parts) + len(starts) + 1),
        out_specs=VM,
        out_shape=shape((OWN, half), dtype),
        compiler_params=params(10),
        cost_estimate=cost(100 * 2 * 3 * half * size, 6 * size),
        name="backward",
    )(ids, *[part for _, part in parts], *starts, weight)


def place(at):
    return at // 16, at // 4 % 4, at // 2 % 2, at % 2


def moves(dx=0, dz=0, dy=0, dc=0):
    pairs = []
    for at in range(64):
        x, z, y, c = place(at)
        pairs.append((at, (x + dx) % 4 * 16 + (z + dz) % 4 * 4 + (y ^ dy) * 2 + (c ^ dc)))
    return pairs


def swap(value):
    return lax.ppermute(value, "head", [(0, 1), (1, 0)])


def send(value, **step):
    return lax.ppermute(value, "seq", moves(**step))


def per_device(
    dna_bases,
    stem_weight,
    encoder_weight,
    norm_gain,
    attention_weight,
    logit_scale,
    out_weight,
    decoder_weight,
    grad_out,
):
    at = lax.axis_index("seq")
    x = at // 16
    ids = jnp.stack([lax.axis_index("head"), x, at]).astype(jnp.int32)
    feats = grad_out.shape[1]

    codes, near, far = prepare(ids, dna_bases.reshape(OWN, 128), grad_out)
    near = send(near, dc=1)
    pairs = [(i, i + 1) for i in range(1, 63, 2)]
    far = lax.ppermute(far, "seq", pairs + [(b, a) for a, b in pairs])
    halo = near, far
    rows, stem_weight, encoder_weight = load(codes, stem_weight, encoder_weight)
    encoded, attention_weight = encode(
        ids, *halo, rows, stem_weight, encoder_weight, attention_weight
    )
    gain = norm_gain.reshape(1, feats)
    normed, *keyvals = project_keys(ids, encoded, swap(encoded), gain, attention_weight)

    def spread(blocks):
        return [send(blocks[d], dx=d) for d in (1, 3, 2)]

    def stacked(blocks):
        return jnp.concatenate(lax.optimization_barrier(blocks), axis=0)

    got = spread(keyvals)
    keyvals = stacked([keyvals[0]] + got)
    near = [send(keyvals, dz=1), send(keyvals, dz=3)]
    queries = project_queries(ids, normed, attention_weight)
    *near, got = lax.optimization_barrier((*near, spread(queries)))
    queries = jnp.concatenate([queries[0]] + got, axis=0)
    others = send(queries, dy=1)
    half = keyvals.shape[0] // 2
    far = [send(near[0][:half], dz=1), send(near[1][half:], dz=3)]
    across = [send(piece, dc=1) for piece in (keyvals, *near)]
    *far, across, others = lax.optimization_barrier((*far, across, others))
    far = jnp.concatenate(far, axis=0)
    pieces = [keyvals] + near + across + [far, send(far, dc=1)]
    other, inverse = attend(ids, logit_scale, others, pieces)
    other = send(other, dy=1)
    own = attend(ids, logit_scale, queries, pieces, inverses=[inverse])[0]
    mixed = merge([own, other])
    heads = [mixed[0], send(mixed[1], dx=-1), send(mixed[3], dx=-2), send(mixed[2], dx=-3)]

    sent = swap(output(ids, heads, out_weight, False, BF16))
    kept = output(ids, heads, out_weight, True, F32)
    half = decoder_weight.shape[1]
    split = 2 * TILE
    inputs, early = decode_first(ids, kept, sent, encoded, decoder_weight, split)
    early = swap(early)
    late = decode(ids, inputs, decoder_weight, False, split, half - split, BF16)
    late, inputs = lax.optimization_barrier((late, inputs))
    late = swap(late)
    kept = decode(ids, inputs, decoder_weight, True, 0, half, F32)
    decoded, early, paired = slopes(ids, kept, early, inputs, grad_out, *halo, 0)
    early_back = swap(early)
    decoded, late, rest = slopes(
        ids, kept, late, inputs, grad_out, *halo, split, (decoded,)
    )
    late_back = swap(late)
    total = backward(
        ids, [(0, early), (split, late)], [paired, rest], decoder_weight, True, F32
    )
    total = backward(ids, [(0, early_back)], [total], decoder_weight, False, F32)
    bins_grad = backward(ids, [(split, late_back)], [total], decoder_weight, False, BF16)
    return decoded, bins_grad


def solution(mesh):
    in_specs = (
        P("seq"),
        P(),
        P(None, None, "head"),
        P(),
        P(None, None, "head"),
        P("head"),
        P("head", None),
        P(None, "head", None),
        P("seq", None),
    )
    out_specs = (P("seq", "head"), P("seq", "head"))
    return jax.shard_map(
        per_device, mesh=mesh, in_specs=in_specs, out_specs=out_specs, check_vma=False
    )
```

```python
import functools

import jax
import jax.numpy as jnp
from jax import lax
from jax.experimental import pallas as pl
from jax.experimental.pallas import tpu as pltpu
from jax.sharding import PartitionSpec as P

BF16 = jnp.bfloat16
F32 = jnp.float32
ROWS = 136
OWN = 128
TILE = 256
HEAD = 192
EPS = 1e-06
MIB = 1024 * 1024


def params(mib):
    return pltpu.CompilerParams(vmem_limit_bytes=mib * MIB)


def dot(a, b):
    return jnp.dot(a, b, preferred_element_type=F32)


def dot_t(a, b):
    return lax.dot_general(a, b, (((1,), (1,)), ((), ())), preferred_element_type=F32)


def cost(flops, nbytes):
    return pl.CostEstimate(flops=int(flops), bytes_accessed=int(nbytes), transcendentals=0)


def shape(dims, dtype):
    return jax.ShapeDtypeStruct(dims, dtype)


VM = pl.BlockSpec(memory_space=pltpu.VMEM)
SM = pl.BlockSpec(memory_space=pltpu.SMEM)
HBM = pl.BlockSpec(memory_space=pltpu.HBM)


def above(rows, span):
    parts = [pltpu.roll(rows[i : i + span], 1, 0) for i in range(0, rows.shape[0], span)]
    return jnp.concatenate(parts, axis=0)


def below(rows, span):
    parts = [pltpu.roll(rows[i : i + span], span - 1, 0) for i in range(0, rows.shape[0], span)]
    return jnp.concatenate(parts, axis=0)


def lanes(at, size):
    return pl.ds(at if isinstance(at, int) else pl.multiple_of(at, size), size)


def tiles(count, body):
    for i in range(count):
        body(i)


def gelu_tanh(x):
    return jnp.tanh(0.7978845608028654 * (x + 0.044715 * (x * x * x)))


def conv_taps(rows, weight, span):
    half = rows.shape[0] // 2
    first, mid, last = (dot(rows, weight(t)) for t in range(3))
    even = above(first[half:], span) + mid[:half] + last[half:]
    odd = first[:half] + mid[half:] + below(last[:half], span)
    return jnp.concatenate([even, odd], axis=0)


def sides(ids, near, far):
    odd = lax.rem(ids[2], 2) == 1
    return jnp.where(odd, near, far), jnp.where(odd, far, near)


def prepare_kernel(ids, bases, grad, codes, near, far, code, head, tail, sems):
    rows = grad.shape[0]
    copies = [
        pltpu.make_async_copy(bases, code, sems.at[0]),
        pltpu.make_async_copy(grad.at[pl.ds(0, 16)], head, sems.at[1]),
        pltpu.make_async_copy(grad.at[pl.ds(rows - 16, 16)], tail, sems.at[2]),
    ]
    for copy in copies:
        copy.start()
    for copy in copies:
        copy.wait()
    feats = grad.shape[1]
    letters = (code[...] + 1).astype(F32)
    codes[...] = letters.astype(BF16)
    odd = lax.rem(ids[2], 2) == 1
    last = jnp.concatenate([tail[...].astype(F32)[8:], letters[OWN - 8 :]], axis=1)
    first = jnp.concatenate([head[...].astype(F32)[:8], letters[:8]], axis=1)
    near[...] = jnp.where(odd, first, last).astype(BF16)
    far[...] = jnp.where(odd, last, first).astype(BF16)


def near_memory(value):
    return pltpu.with_memory_space_constraint(value, pltpu.VMEM)


def far_memory(value):
    return pltpu.with_memory_space_constraint(value, pltpu.HBM)


def prepare(ids, bases, grad):
    feats = grad.shape[1]
    return pl.pallas_call(
        prepare_kernel,
        in_specs=[SM, HBM, HBM],
        out_specs=[VM] * 3,
        out_shape=[
            shape((OWN, 128), BF16),
            shape((8, feats + 128), BF16),
            shape((8, feats + 128), BF16),
        ],
        scratch_shapes=[
            pltpu.VMEM(bases.shape, jnp.int32),
            pltpu.VMEM((16, feats), BF16),
            pltpu.VMEM((16, feats), BF16),
            pltpu.SemaphoreType.DMA((3,)),
        ],
        compiler_params=params(4),
        cost_estimate=cost(10**5, 10**5),
        name="prepare",
    )(ids, far_memory(bases), far_memory(grad))


def embed_letters(code, stem, embedded):
    patch = stem.shape[0] // 4
    row = lax.broadcasted_iota(jnp.int32, (2 * patch, 4 * patch), 0)
    col = lax.broadcasted_iota(jnp.int32, (2 * patch, 4 * patch), 1)
    spread = [
        dot(code, (row == col // 4 + offset).astype(F32).astype(BF16)) for offset in (0, patch)
    ]
    spread = jnp.concatenate(spread, axis=0)
    base = lax.broadcasted_iota(jnp.int32, spread.shape, 1) % 4 + 1
    onehot = (spread == base.astype(F32)).astype(F32).astype(BF16)

    def embed(i):
        at = lanes(i * TILE, TILE)
        embedded[:, at] = dot(onehot, stem[:, at]).astype(BF16)

    tiles(stem.shape[1] // TILE, embed)


def load_kernel(codes, stems, weights, embedded, stem, weight, sems):
    copies = [
        pltpu.make_async_copy(stems, stem, sems.at[0]),
        pltpu.make_async_copy(weights, weight, sems.at[1]),
    ]
    for copy in copies:
        copy.start()
    copies[0].wait()
    embed_letters(codes[...], stem, embedded)
    copies[1].wait()


def load(codes, stem, weight):
    return pl.pallas_call(
        load_kernel,
        in_specs=[VM, HBM, HBM],
        out_specs=[VM] * 3,
        out_shape=[
            pltpu.VMEM((2 * OWN, stem.shape[1]), BF16),
            pltpu.VMEM(stem.shape, BF16),
            pltpu.VMEM(weight.shape, BF16),
        ],
        scratch_shapes=[pltpu.SemaphoreType.DMA((2,))],
        compiler_params=params(4),
        cost_estimate=cost(10**5, weight.size * 2),
        name="load",
    )(codes, far_memory(stem), far_memory(weight))


def ring_order(rows):
    half = ROWS - OWN
    return (
        jnp.concatenate([rows[:OWN], rows[2 * OWN : 2 * OWN + half]], axis=0),
        jnp.concatenate([rows[OWN : 2 * OWN], rows[2 * OWN + half :]], axis=0),
    )


def encode_kernel(ids, near, far, rows, stem, weight, ahead, encoded, loaded, embedded, halo, sem):
    copy = pltpu.make_async_copy(ahead, loaded, sem)
    copy.start()
    feats = stem.shape[1]
    half = weight.shape[2]
    place = lax.broadcasted_iota(jnp.int32, (ROWS - OWN, 128), 0)
    before, after = sides(ids, near[:, feats:].astype(F32), far[:, feats:].astype(F32))
    code = jnp.where(place >= 6, before, 0.0)
    code = jnp.where(place < 2, after, code)
    embed_letters(code.astype(BF16), stem, halo)
    embedded[: 2 * OWN, :] = rows[...]
    embedded[2 * OWN :, :] = halo[...]

    def convolve(i):
        at = lanes(i * TILE, TILE)
        parts = [dot(embedded[...], weight[tap, :, at]) for tap in range(3)]
        (first_even, first_odd), (even, odd), (last_even, last_odd) = map(ring_order, parts)
        even = above(first_odd, ROWS) + even + last_odd
        odd = first_even + odd + below(last_even, ROWS)
        pre = jnp.concatenate([even, odd], axis=0)
        mine = embedded[:, lanes(ids[0] * half + i * TILE, TILE)].astype(F32)
        mine = jnp.concatenate(ring_order(mine), axis=0)
        encoded[:, at] = (mine + 0.5 * pre * (1.0 + gelu_tanh(pre))).astype(BF16)

    tiles(half // TILE, convolve)
    copy.wait()


def encode(ids, near, far, rows, stem, weight, ahead):
    half = weight.shape[2]
    feats = stem.shape[1]
    return pl.pallas_call(
        encode_kernel,
        in_specs=[SM] + [VM] * 5 + [HBM],
        out_specs=[VM, VM],
        out_shape=[shape((2 * ROWS, half), BF16), pltpu.VMEM(ahead.shape, BF16)],
        scratch_shapes=[
            pltpu.VMEM((2 * ROWS, feats), BF16),
            pltpu.VMEM((2 * (ROWS - OWN), feats), BF16),
            pltpu.SemaphoreType.DMA(()),
        ],
        compiler_params=params(12),
        cost_estimate=cost(4 * OWN * weight.size, weight.size * 4),
        name="encode",
    )(
        ids,
        near,
        far,
        near_memory(rows),
        near_memory(stem),
        near_memory(weight),
        far_memory(ahead),
    )


def unpacked(both):
    both = both.astype(BF16).astype(F32)
    turned = pltpu.roll(both, 2 * HEAD - 64, 1)
    return (both[:, :128], both[:, 128:256]), (turned[:, 128:256], turned[:, 256:384])


def project_keys_kernel(
    ids, mine, theirs, gain, weight, normed, k0, k1, k2, k3, packed
):
    half = mine.shape[1]
    near = lanes(ids[0] * half, half)
    far = lanes((1 - ids[0]) * half, half)
    rings = [ref[...].astype(F32) for ref in (mine, theirs)]
    binned = [(ring[:ROWS] + ring[ROWS:]) * 0.5 for ring in rings]
    total = sum(jnp.sum(part * part, axis=1, keepdims=True) for part in binned)
    inverse = lax.rsqrt(total * (1.0 / (2 * half)) + EPS)
    here = (binned[0] * inverse * gain[:, near]).astype(BF16)
    there = (binned[1] * inverse * gain[:, far]).astype(BF16)
    normed[0] = here
    normed[1] = there
    low = lax.broadcasted_iota(jnp.int32, (ROWS, 128), 1) < 64
    for pair in range(2):
        at = slice(pair * 2 * HEAD, (pair + 1) * 2 * HEAD)
        keys, values = (
            unpacked(dot(here, weight[kind, near, at]) + dot(there, weight[kind, far, at]))
            for kind in (1, 2)
        )
        for side in range(2):
            head = 2 * pair + side
            key, value = keys[side], values[side]
            packed[head, :, :128] = key[0].astype(BF16)
            packed[head, :, 128:256] = value[0].astype(BF16)
            tail = jnp.where(low, key[1], pltpu.roll(value[1], 64, 1))
            packed[head, :, 256:] = tail.astype(BF16)
    for distance, out in enumerate((k0, k1, k2, k3)):
        out[...] = packed[lax.rem(ids[1] + distance, 4), :OWN, :]


def project_keys(ids, mine, theirs, gain, weight):
    half = mine.shape[1]
    return pl.pallas_call(
        project_keys_kernel,
        in_specs=[SM] + [VM] * 4,
        out_specs=[VM] * 5,
        out_shape=[shape((2, ROWS, half), BF16)] + [shape((OWN, 384), BF16)] * 4,
        scratch_shapes=[pltpu.VMEM((4, ROWS, 384), BF16)],
        compiler_params=params(12),
        cost_estimate=cost(2 * ROWS * weight.size * 2 // 3, weight.size * 2),
        name="project_keys",
    )(ids, mine, theirs, gain, weight)


def project_queries_kernel(ids, normed, weight, q0, q1, q2, q3, packed):
    half = normed.shape[2]
    near = lanes(ids[0] * half, half)
    far = lanes((1 - ids[0]) * half, half)
    low = lax.broadcasted_iota(jnp.int32, (ROWS, 128), 1) < 64
    for pair in range(2):
        at = slice(pair * 2 * HEAD, (pair + 1) * 2 * HEAD)
        both = dot(normed[0], weight[0, near, at]) + dot(normed[1], weight[0, far, at])
        for side, query in enumerate(unpacked(both)):
            packed[2 * pair + side, :, :128] = query[0].astype(BF16)
            packed[2 * pair + side, :, 128:] = jnp.where(low, query[1], 0.0).astype(BF16)
    for distance, out in enumerate((q0, q1, q2, q3)):
        out[...] = packed[lax.rem(ids[1] + distance, 4)]


def project_queries(ids, normed, weight):
    return pl.pallas_call(
        project_queries_kernel,
        in_specs=[SM, VM, VM],
        out_specs=[VM] * 4,
        out_shape=[shape((ROWS, 256), BF16)] * 4,
        scratch_shapes=[pltpu.VMEM((4, ROWS, 256), BF16)],
        compiler_params=params(10),
        cost_estimate=cost(2 * ROWS * weight.size // 3, weight.size),
        name="project_queries",
    )(ids, normed, near_memory(weight))


BLOCK = 4 * ROWS
LOG2E = 1.4426950408889634


def key_columns(ref):
    return jnp.concatenate([ref[:, :128], ref[:, 256:]], axis=1)


def inverse_norms(ref):
    lane = lax.broadcasted_iota(jnp.int32, (8, 256), 1)
    ones = (lane < HEAD).astype(F32).astype(BF16)
    key = key_columns(ref).astype(F32)
    square = key * key
    high = square.astype(BF16)
    rest = (square - high.astype(F32)).astype(BF16)
    total = dot_t(ones, high) + dot_t(ones, rest)
    return lax.rsqrt(total * (1.0 / HEAD) + EPS)


def norms_kernel(*refs):
    pieces, out = refs[:-1], refs[-1]
    at = 0
    for ref in pieces:
        out[:, at : at + ref.shape[0]] = inverse_norms(ref)
        at += ref.shape[0]


def norms(pieces):
    keys = sum(piece.shape[0] for piece in pieces)
    return pl.pallas_call(
        norms_kernel,
        in_specs=[VM] * len(pieces),
        out_specs=VM,
        out_shape=shape((8, keys), F32),
        compiler_params=params(6),
        cost_estimate=cost(10**6, 10**5),
        name="norms",
    )(*pieces)


def attend_kernel(count, known, resumed, final, ids, scale, queries, *refs):
    pieces, refs = refs[:count], refs[count:]
    inverses, refs = refs[:known], refs[known:]
    if resumed:
        (old_mixed, old_stats), refs = refs[:2], refs[2:]
    sizes = [ref.shape[0] for ref in pieces]
    starts = [sum(sizes[:i]) for i in range(count)]

    total_known = sum(ref.shape[1] for ref in inverses)
    if total_known < sum(sizes):
        outs, inverse = refs[:-1], refs[-1]
        for at, size, ref in zip(starts, sizes, pieces):
            if at >= total_known:
                inverse[:, at - total_known : at - total_known + size] = inverse_norms(ref)
        inverses = (*inverses, inverse)
    else:
        outs = refs

    def inverse_of(at, size):
        for ref in inverses:
            if at < ref.shape[1]:
                return ref[0:1, at : at + size]
            at -= ref.shape[1]

    limit = 1024
    groups, room = [], 0
    for triple in zip(starts, sizes, pieces):
        if room < triple[1]:
            groups.append([])
            room = limit
        groups[-1].append(triple)
        room -= triple[1]

    def unit(query, factor, group):
        scores, peak = [], None
        for at, size, ref in group:
            part = dot_t(query, key_columns(ref)) * inverse_of(at, size)
            top = jnp.max(part, axis=1, keepdims=True)
            peak = top if peak is None else jnp.maximum(peak, top)
            scores.append(part)
        total, mixed = None, None
        for part, (_, _, ref) in zip(scores, group):
            exps = jnp.exp2((part - peak) * factor)
            sums = jnp.sum(exps, axis=1, keepdims=True)
            values = jnp.concatenate([ref[:, 128:256], ref[:, 256:]], axis=1)
            term = dot(exps.astype(BF16), values)
            total = sums if total is None else total + sums
            mixed = term if mixed is None else mixed + term
        return peak, total, mixed

    for begin in range(0, queries.shape[0], BLOCK):
        rows = slice(begin, begin + BLOCK)
        query = queries[rows, :]
        wide = query.astype(F32)
        own = lax.rsqrt(jnp.sum(wide * wide, axis=1, keepdims=True) * (1.0 / HEAD) + EPS)
        factor = own * (scale[ids[1]] * (LOG2E / HEAD))
        states = [unit(query, factor, group) for group in groups]
        if resumed:
            states.append((old_stats[rows, 0:1], old_stats[rows, 64:65], old_mixed[rows, :]))
        peak = functools.reduce(jnp.maximum, [state[0] for state in states])
        if len(states) > 1:
            shrink = [jnp.exp2((state[0] - peak) * factor) for state in states]
            total = sum(state[1] * part for state, part in zip(states, shrink))
            mixed = sum(state[2] * part for state, part in zip(states, shrink))
        else:
            _, total, mixed = states[0]
        if not final:
            outs[0][rows, :] = mixed
            half = lax.broadcasted_iota(jnp.int32, (BLOCK, 128), 1) < 64
            outs[1][rows, :] = jnp.where(half, peak, total)
            continue
        mixed = mixed / total
        weight = peak * factor + jnp.log(total) * LOG2E
        high = weight.astype(BF16).astype(F32)
        rest = weight - high
        mid = rest.astype(BF16).astype(F32)
        place = lax.broadcasted_iota(jnp.int32, mixed.shape, 1)
        mixed = jnp.where(place == 128, high, mixed)
        mixed = jnp.where(place == 129, mid, mixed)
        mixed = jnp.where(place == 130, rest - mid, mixed)
        outs[0][rows, :] = mixed.astype(BF16)


def attend(ids, scale, queries, pieces, inverses=(), state=(), final=True):
    rows = queries.shape[0]
    keys = sum(piece.shape[0] for piece in pieces)
    if final:
        outs = [shape((rows, 256), BF16)]
    else:
        outs = [shape((rows, 256), F32), shape((rows, 128), F32)]
    known = sum(inverse.shape[1] for inverse in inverses)
    if known < keys:
        outs.append(shape((8, keys - known), F32))
    return pl.pallas_call(
        functools.partial(attend_kernel, len(pieces), len(inverses), bool(state), final),
        in_specs=[SM, SM] + [VM] * (1 + len(pieces) + len(inverses) + len(state)),
        out_specs=[VM] * len(outs),
        out_shape=outs,
        compiler_params=params(28),
        cost_estimate=cost(4 * rows * keys * 256, 8 * rows * 1024),
        name="attend",
    )(ids, scale, near_memory(queries), *pieces, *inverses, *state)


def merge_kernel(a0, a1, *outs):
    parts = [ref[...].astype(F32) for ref in (a0, a1)]
    logs = [p[:, 128:129] + p[:, 129:130] + p[:, 130:131] for p in parts]
    peak = functools.reduce(jnp.maximum, logs)
    shares = [jnp.exp2(log - peak) for log in logs]
    total = sum(shares)
    mixed = sum(p * (share / total) for p, share in zip(parts, shares))
    mixed = jnp.concatenate([mixed[:, :128], pltpu.roll(mixed[:, 128:], 64, 1)], axis=1)
    for block in range(4):
        outs[block][...] = mixed[block * ROWS : (block + 1) * ROWS].astype(BF16)


def merge(parts):
    return pl.pallas_call(
        merge_kernel,
        in_specs=[VM] * 2,
        out_specs=[VM] * 4,
        out_shape=[shape((ROWS, 256), BF16)] * 4,
        compiler_params=params(8),
        cost_estimate=cost(20 * parts[0].size, 10 * parts[0].size),
        name="merge",
    )(*parts)


def output_kernel(mine, ids, a0, a1, a2, a3, weight, out):
    half = out.shape[1]
    side = ids[0] if mine else 1 - ids[0]

    def tile(i):
        at = lanes(side * half + i * TILE, TILE)
        total = None
        for distance, ref in enumerate((a0, a1, a2, a3)):
            head = lax.rem(ids[1] + distance, 4)
            rows = weight[pl.ds(pl.multiple_of(head * HEAD, HEAD), HEAD), at]
            term = dot(ref[:, :HEAD], rows)
            total = term if total is None else total + term
        out[:, lanes(i * TILE, TILE)] = total.astype(out.dtype)

    tiles(half // TILE, tile)


def output(ids, heads, weight, mine, dtype):
    half = weight.shape[1] // 2
    return pl.pallas_call(
        functools.partial(output_kernel, mine),
        in_specs=[SM] + [VM] * 5,
        out_specs=VM,
        out_shape=shape((ROWS, half), dtype),
        compiler_params=params(6),
        cost_estimate=cost(2 * ROWS * weight.size // 2, weight.size),
        name="output",
    )(ids, *heads, weight)


def decode_first_kernel(ids, own, other, encoded, weight, inputs, out):
    half = weight.shape[1]

    def mix(i):
        at = lanes(i * TILE, TILE)
        enc = encoded[:, at].astype(F32)
        even, odd = enc[:ROWS], enc[ROWS:]
        binned = (even + odd) * 0.5
        block = (binned + (own[:, at] + other[:, at].astype(F32))).astype(BF16).astype(F32)
        row = lax.broadcasted_iota(jnp.int32, block.shape, 0)
        outside = ((ids[2] == 0) & (row == ROWS - 1)) | ((ids[2] == 63) & (row == OWN))
        even = jnp.where(outside, 0.0, block + even)
        odd = jnp.where(outside, 0.0, block + odd)
        inputs[:, at] = jnp.concatenate([even, odd], axis=0).astype(BF16)

    tiles(half // TILE, mix)
    decode_tiles(inputs, weight, out, (1 - ids[0]) * half)


def decode_tiles(inputs, weight, out, begin):
    def tile(i):
        at = lanes(begin + i * TILE, TILE)
        result = conv_taps(inputs[...], lambda t: weight[t, :, at], ROWS)
        out[:, lanes(i * TILE, TILE)] = result.astype(out.dtype)

    tiles(out.shape[1] // TILE, tile)


def decode_first(ids, own, other, encoded, weight, width):
    half = weight.shape[1]
    return pl.pallas_call(
        decode_first_kernel,
        in_specs=[SM] + [VM] * 4,
        out_specs=[VM] * 2,
        out_shape=[shape((2 * ROWS, half), BF16), shape((2 * ROWS, width), BF16)],
        compiler_params=params(8),
        cost_estimate=cost(10**6, 10**4),
        name="decode_first",
    )(ids, own, other, encoded, weight)


def decode_kernel(mine, first, ids, inputs, weight, out):
    side = ids[0] if mine else 1 - ids[0]
    decode_tiles(inputs, weight, out, side * weight.shape[1] + first)


def decode(ids, inputs, weight, mine, first, width, dtype):
    half = weight.shape[1]
    return pl.pallas_call(
        functools.partial(decode_kernel, mine, first),
        in_specs=[SM, VM, VM],
        out_specs=VM,
        out_shape=shape((2 * ROWS, width), dtype),
        compiler_params=params(8),
        cost_estimate=cost(10**6, 10**4),
        name="decode",
    )(ids, inputs, weight)


def slope_kernel(first, ids, own, other, inputs, grad, near, far, *refs):
    done, (decoded, slope, paired, wide) = refs[:-4], refs[-4:]
    half = own.shape[1]
    begin = 0
    if done:
        begin = first
        decoded[:, :first] = done[0][...]

    def tile(i):
        at = lanes(i * 128, 128)
        target = lanes(begin + i * 128, 128)
        source = lanes(first + i * 128, 128)
        column = lanes(ids[0] * half + first + i * 128, 128)
        pre = own[:, source] + other[:, at].astype(F32)
        tanh = gelu_tanh(pre)
        result = inputs[:, source].astype(F32) + 0.5 * pre * (1.0 + tanh)
        wide[2 * i, pl.ds(0, OWN, 2), :] = result[:OWN]
        wide[2 * i, pl.ds(1, OWN, 2), :] = result[ROWS : ROWS + OWN]
        decoded[:, target] = wide[2 * i].astype(BF16)
        slant = 0.5 * (1.0 + tanh) + (0.5 * 0.7978845608028654) * pre * (1.0 - tanh * tanh) * (
            1.0 + (3 * 0.044715) * (pre * pre)
        )
        wide[2 * i + 1] = grad[:, column].astype(F32)
        even = wide[2 * i + 1, pl.ds(0, OWN, 2), :]
        odd = wide[2 * i + 1, pl.ds(1, OWN, 2), :]
        paired[:, at] = even + odd
        row = lax.broadcasted_iota(jnp.int32, (ROWS - OWN, 128), 0)
        before, after = sides(ids, near[:, column].astype(F32), far[:, column].astype(F32))
        even_edge = jnp.where(row == 0, after, 0.0)
        odd_edge = jnp.where(row == ROWS - OWN - 1, before, 0.0)
        cotangent = jnp.concatenate([even, even_edge, odd, odd_edge], axis=0)
        slope[:, at] = (cotangent * slant).astype(BF16)

    tiles(other.shape[1] // 128, tile)


def slopes(ids, own, other, inputs, grad, near, far, first, done=()):
    width = other.shape[1]
    return pl.pallas_call(
        functools.partial(slope_kernel, first),
        in_specs=[SM] + [VM] * (6 + len(done)),
        out_specs=[VM] * 3,
        out_shape=[
            shape((2 * OWN, width + (first if done else 0)), BF16),
            shape((2 * ROWS, width), BF16),
            shape((OWN, width), F32),
        ],
        scratch_shapes=[pltpu.VMEM((width // 64, 2 * OWN, 128), F32)],
        compiler_params=params(8),
        cost_estimate=cost(100 * 30 * 1000 * other.size, 14 * other.size),
        name="slopes",
    )(ids, own, other, inputs, grad, near, far, *done)


def backward_kernel(mine, firsts, count, ids, *refs):
    slopes_in, starts, (weight, out) = (
        refs[: len(firsts)],
        refs[len(firsts) : len(firsts) + count],
        refs[len(firsts) + count :],
    )
    half = weight.shape[1]
    side = ids[0] if mine else 1 - ids[0]
    whole = [start for start in starts if start.shape[1] == half]
    chunks = [start for start in starts if start.shape[1] < half]

    def tile(i, chunk, begin):
        inner = lanes(i * TILE, TILE)
        first = mid = last = None
        for offset, slope in zip(firsts, slopes_in):
            at = pl.ds(pl.multiple_of(side * half + offset, TILE), slope.shape[1])
            terms = [dot_t(slope[...], weight[t, inner, at]) for t in range(3)]
            if first is None:
                first, mid, last = terms
            else:
                first, mid, last = first + terms[0], mid + terms[1], last + terms[2]
        total = first[ROWS:] + mid[:ROWS] + mid[ROWS:] + last[:ROWS]
        total = total + below(first[:ROWS], ROWS) + above(last[ROWS:], ROWS)
        total = total[:OWN]
        for start in whole:
            total = total + start[:, inner]
        if chunk is not None:
            total = total + chunk[:, lanes(i * TILE - begin, TILE)]
        out[:, inner] = total.astype(out.dtype)

    if not chunks:
        tiles(half // TILE, lambda i: tile(i, None, 0))
    begin = 0
    for chunk in chunks:
        width = chunk.shape[1]
        tiles(width // TILE, lambda i: tile(i + begin // TILE, chunk, begin))
        begin += width


def backward(ids, parts, starts, weight, mine, dtype):
    half = weight.shape[1]
    size = sum(part.size for _, part in parts)
    return pl.pallas_call(
        functools.partial(backward_kernel, mine, [first for first, _ in parts], len(starts)),
        in_specs=[SM] + [VM] * (len(parts) + len(starts) + 1),
        out_specs=VM,
        out_shape=shape((OWN, half), dtype),
        compiler_params=params(10),
        cost_estimate=cost(100 * 2 * 3 * half * size, 6 * size),
        name="backward",
    )(ids, *[part for _, part in parts], *starts, weight)


def place(at):
    return at // 16, at // 4 % 4, at // 2 % 2, at % 2


def moves(dx=0, dz=0, dy=0, dc=0):
    pairs = []
    for at in range(64):
        x, z, y, c = place(at)
        pairs.append((at, (x + dx) % 4 * 16 + (z + dz) % 4 * 4 + (y ^ dy) * 2 + (c ^ dc)))
    return pairs


def swap(value):
    return lax.ppermute(value, "head", [(0, 1), (1, 0)])


def send(value, **step):
    return lax.ppermute(value, "seq", moves(**step))


def per_device(
    dna_bases,
    stem_weight,
    encoder_weight,
    norm_gain,
    attention_weight,
    logit_scale,
    out_weight,
    decoder_weight,
    grad_out,
):
    at = lax.axis_index("seq")
    x = at // 16
    ids = jnp.stack([lax.axis_index("head"), x, at]).astype(jnp.int32)
    feats = grad_out.shape[1]

    codes, near, far = prepare(ids, dna_bases.reshape(OWN, 128), grad_out)
    near = send(near, dc=1)
    pairs = [(i, i + 1) for i in range(1, 63, 2)]
    far = lax.ppermute(far, "seq", pairs + [(b, a) for a, b in pairs])
    halo = near, far
    rows, stem_weight, encoder_weight = load(codes, stem_weight, encoder_weight)
    encoded, attention_weight = encode(
        ids, *halo, rows, stem_weight, encoder_weight, attention_weight
    )
    gain = norm_gain.reshape(1, feats)
    normed, *keyvals = project_keys(ids, encoded, swap(encoded), gain, attention_weight)

    def spread(blocks):
        return [send(blocks[d], dx=d) for d in (1, 3, 2)]

    def stacked(blocks):
        return jnp.concatenate(lax.optimization_barrier(blocks), axis=0)

    got = spread(keyvals)
    keyvals = stacked([keyvals[0]] + got)
    near = [send(keyvals, dz=1), send(keyvals, dz=3)]
    queries = project_queries(ids, normed, attention_weight)
    *near, got = lax.optimization_barrier((*near, spread(queries)))
    queries = jnp.concatenate([queries[0]] + got, axis=0)
    others = send(queries, dy=1)
    half = keyvals.shape[0] // 2
    far = [send(near[0][:half], dz=1), send(near[1][half:], dz=3)]
    across = [send(piece, dc=1) for piece in (keyvals, *near)]
    pieces = [keyvals] + near + across
    inverse = norms(pieces)
    *far, inverse, others = lax.optimization_barrier((*far, inverse, others))
    far = jnp.concatenate(far, axis=0)
    pieces += [far, send(far, dc=1)]
    other, later = attend(ids, logit_scale, others, pieces, inverses=[inverse])
    other = send(other, dy=1)
    own = attend(ids, logit_scale, queries, pieces, inverses=[inverse, later])[0]
    mixed = merge([own, other])
    heads = [mixed[0], send(mixed[1], dx=-1), send(mixed[3], dx=-2), send(mixed[2], dx=-3)]

    sent = swap(output(ids, heads, out_weight, False, BF16))
    kept = output(ids, heads, out_weight, True, F32)
    half = decoder_weight.shape[1]
    split = 2 * TILE
    inputs, early = decode_first(ids, kept, sent, encoded, decoder_weight, split)
    early = swap(early)
    late = decode(ids, inputs, decoder_weight, False, split, half - split, BF16)
    late, inputs = lax.optimization_barrier((late, inputs))
    late = swap(late)
    kept = decode(ids, inputs, decoder_weight, True, 0, half, F32)
    decoded, early, paired = slopes(ids, kept, early, inputs, grad_out, *halo, 0)
    early_back = swap(early)
    decoded, late, rest = slopes(
        ids, kept, late, inputs, grad_out, *halo, split, (decoded,)
    )
    late_back = swap(late)
    total = backward(
        ids, [(0, early), (split, late)], [paired, rest], decoder_weight, True, F32
    )
    total = backward(ids, [(0, early_back)], [total], decoder_weight, False, F32)
    bins_grad = backward(ids, [(split, late_back)], [total], decoder_weight, False, BF16)
    return decoded, bins_grad


def solution(mesh):
    in_specs = (
        P("seq"),
        P(),
        P(None, None, "head"),
        P(),
        P(None, None, "head"),
        P("head"),
        P("head", None),
        P(None, "head", None),
        P("seq", None),
    )
    out_specs = (P("seq", "head"), P("seq", "head"))
    return jax.shard_map(
        per_device, mesh=mesh, in_specs=in_specs, out_specs=out_specs, check_vma=False
    )
```

```python
import functools

import jax
import jax.numpy as jnp
from jax import lax
from jax.experimental import pallas as pl
from jax.experimental.pallas import tpu as pltpu
from jax.sharding import PartitionSpec as P

BF16 = jnp.bfloat16
F32 = jnp.float32
ROWS = 136
OWN = 128
TILE = 256
HEAD = 192
EPS = 1e-06
MIB = 1024 * 1024


def params(mib):
    return pltpu.CompilerParams(vmem_limit_bytes=mib * MIB)


def dot(a, b):
    return jnp.dot(a, b, preferred_element_type=F32)


def dot_t(a, b):
    return lax.dot_general(a, b, (((1,), (1,)), ((), ())), preferred_element_type=F32)


def cost(flops, nbytes):
    return pl.CostEstimate(flops=int(flops), bytes_accessed=int(nbytes), transcendentals=0)


def shape(dims, dtype):
    return jax.ShapeDtypeStruct(dims, dtype)


VM = pl.BlockSpec(memory_space=pltpu.VMEM)
HBM = pl.BlockSpec(memory_space=pltpu.HBM)


def above(rows, span):
    parts = [pltpu.roll(rows[i : i + span], 1, 0) for i in range(0, rows.shape[0], span)]
    return jnp.concatenate(parts, axis=0)


def below(rows, span):
    parts = [pltpu.roll(rows[i : i + span], span - 1, 0) for i in range(0, rows.shape[0], span)]
    return jnp.concatenate(parts, axis=0)


def lanes(at, size):
    return pl.ds(at if isinstance(at, int) else pl.multiple_of(at, size), size)


def tiles(count, body):
    for i in range(count):
        body(i)


def gelu_tanh(x):
    return jnp.tanh(0.7978845608028654 * (x + 0.044715 * (x * x * x)))


def conv_taps(rows, weight, span):
    half = rows.shape[0] // 2
    first, mid, last = (dot(rows, weight(t)) for t in range(3))
    even = above(first[half:], span) + mid[:half] + last[half:]
    odd = first[:half] + mid[half:] + below(last[:half], span)
    return jnp.concatenate([even, odd], axis=0)


def position():
    at = lax.axis_index("seq")
    return lax.axis_index("head"), at // 16, at


def sides(odd, near, far):
    return jnp.where(odd, near, far), jnp.where(odd, far, near)


def prepare_kernel(bases, grad, codes, near, far, code, head, tail, sems):
    ids = position()
    rows = grad.shape[0]
    copies = [
        pltpu.make_async_copy(bases, code, sems.at[0]),
        pltpu.make_async_copy(grad.at[pl.ds(0, 16)], head, sems.at[1]),
        pltpu.make_async_copy(grad.at[pl.ds(rows - 16, 16)], tail, sems.at[2]),
    ]
    for copy in copies:
        copy.start()
    for copy in copies:
        copy.wait()
    feats = grad.shape[1]
    letters = (code[...] + 1).astype(F32)
    codes[...] = letters.astype(BF16)
    odd = lax.rem(ids[2], 2) == 1
    last = jnp.concatenate([tail[...].astype(F32)[8:], letters[OWN - 8 :]], axis=1)
    first = jnp.concatenate([head[...].astype(F32)[:8], letters[:8]], axis=1)
    near[...] = jnp.where(odd, first, last).astype(BF16)
    far[...] = jnp.where(odd, last, first).astype(BF16)


def near_memory(value):
    return pltpu.with_memory_space_constraint(value, pltpu.VMEM)


def far_memory(value):
    return pltpu.with_memory_space_constraint(value, pltpu.HBM)


def prepare(bases, grad):
    feats = grad.shape[1]
    return pl.pallas_call(
        prepare_kernel,
        in_specs=[HBM, HBM],
        out_specs=[VM] * 3,
        out_shape=[
            shape((OWN, 128), BF16),
            shape((8, feats + 128), BF16),
            shape((8, feats + 128), BF16),
        ],
        scratch_shapes=[
            pltpu.VMEM(bases.shape, jnp.int32),
            pltpu.VMEM((16, feats), BF16),
            pltpu.VMEM((16, feats), BF16),
            pltpu.SemaphoreType.DMA((3,)),
        ],
        compiler_params=params(4),
        cost_estimate=cost(10**5, 10**5),
        name="prepare",
    )(far_memory(bases), far_memory(grad))


def embed_letters(code, stem, embedded):
    patch = stem.shape[0] // 4
    row = lax.broadcasted_iota(jnp.int32, (2 * patch, 4 * patch), 0)
    col = lax.broadcasted_iota(jnp.int32, (2 * patch, 4 * patch), 1)
    spread = [
        dot(code, (row == col // 4 + offset).astype(F32).astype(BF16)) for offset in (0, patch)
    ]
    spread = jnp.concatenate(spread, axis=0)
    base = lax.broadcasted_iota(jnp.int32, spread.shape, 1) % 4 + 1
    onehot = (spread == base.astype(F32)).astype(F32).astype(BF16)

    def embed(i):
        at = lanes(i * TILE, TILE)
        embedded[:, at] = dot(onehot, stem[:, at]).astype(BF16)

    tiles(stem.shape[1] // TILE, embed)


def load_kernel(codes, stems, weights, embedded, stem, weight, sems):
    copies = [
        pltpu.make_async_copy(stems, stem, sems.at[0]),
        pltpu.make_async_copy(weights, weight, sems.at[1]),
    ]
    for copy in copies:
        copy.start()
    copies[0].wait()
    embed_letters(codes[...], stem, embedded)
    copies[1].wait()


def load(codes, stem, weight):
    return pl.pallas_call(
        load_kernel,
        in_specs=[VM, HBM, HBM],
        out_specs=[VM] * 3,
        out_shape=[
            pltpu.VMEM((2 * OWN, stem.shape[1]), BF16),
            pltpu.VMEM(stem.shape, BF16),
            pltpu.VMEM(weight.shape, BF16),
        ],
        scratch_shapes=[pltpu.SemaphoreType.DMA((2,))],
        compiler_params=params(4),
        cost_estimate=cost(10**5, weight.size * 2),
        name="load",
    )(codes, far_memory(stem), far_memory(weight))


def ring_order(rows):
    half = ROWS - OWN
    return (
        jnp.concatenate([rows[:OWN], rows[2 * OWN : 2 * OWN + half]], axis=0),
        jnp.concatenate([rows[OWN : 2 * OWN], rows[2 * OWN + half :]], axis=0),
    )


def encode_kernel(near, far, rows, stem, weight, ahead, encoded, loaded, embedded, halo, sem):
    ids = position()
    copy = pltpu.make_async_copy(ahead, loaded, sem)
    copy.start()
    feats = stem.shape[1]
    half = weight.shape[2]
    place = lax.broadcasted_iota(jnp.int32, (ROWS - OWN, 128), 0)
    before, after = sides(lax.rem(ids[2], 2) == 1, near[:, feats:].astype(F32), far[:, feats:].astype(F32))
    code = jnp.where(place >= 6, before, 0.0)
    code = jnp.where(place < 2, after, code)
    embed_letters(code.astype(BF16), stem, halo)
    embedded[: 2 * OWN, :] = rows[...]
    embedded[2 * OWN :, :] = halo[...]

    def convolve(i):
        at = lanes(i * TILE, TILE)
        parts = [dot(embedded[...], weight[tap, :, at]) for tap in range(3)]
        (first_even, first_odd), (even, odd), (last_even, last_odd) = map(ring_order, parts)
        even = above(first_odd, ROWS) + even + last_odd
        odd = first_even + odd + below(last_even, ROWS)
        pre = jnp.concatenate([even, odd], axis=0)
        mine = embedded[:, lanes(ids[0] * half + i * TILE, TILE)].astype(F32)
        mine = jnp.concatenate(ring_order(mine), axis=0)
        encoded[:, at] = (mine + 0.5 * pre * (1.0 + gelu_tanh(pre))).astype(BF16)

    tiles(half // TILE, convolve)
    copy.wait()


def encode(near, far, rows, stem, weight, ahead):
    half = weight.shape[2]
    feats = stem.shape[1]
    return pl.pallas_call(
        encode_kernel,
        in_specs=[VM] * 5 + [HBM],
        out_specs=[VM, VM],
        out_shape=[shape((2 * ROWS, half), BF16), pltpu.VMEM(ahead.shape, BF16)],
        scratch_shapes=[
            pltpu.VMEM((2 * ROWS, feats), BF16),
            pltpu.VMEM((2 * (ROWS - OWN), feats), BF16),
            pltpu.SemaphoreType.DMA(()),
        ],
        compiler_params=params(12),
        cost_estimate=cost(4 * OWN * weight.size, weight.size * 4),
        name="encode",
    )(
        near,
        far,
        near_memory(rows),
        near_memory(stem),
        near_memory(weight),
        far_memory(ahead),
    )


def unpacked(both):
    both = both.astype(BF16).astype(F32)
    turned = pltpu.roll(both, 2 * HEAD - 64, 1)
    return (both[:, :128], both[:, 128:256]), (turned[:, 128:256], turned[:, 256:384])


def project_keys_kernel(
    mine, theirs, gain, weight, normed, k0, k1, k2, k3, packed
):
    ids = position()
    half = mine.shape[1]
    near = lanes(ids[0] * half, half)
    far = lanes((1 - ids[0]) * half, half)
    rings = [ref[...].astype(F32) for ref in (mine, theirs)]
    binned = [(ring[:ROWS] + ring[ROWS:]) * 0.5 for ring in rings]
    total = sum(jnp.sum(part * part, axis=1, keepdims=True) for part in binned)
    inverse = lax.rsqrt(total * (1.0 / (2 * half)) + EPS)
    here = (binned[0] * inverse * gain[:, near]).astype(BF16)
    there = (binned[1] * inverse * gain[:, far]).astype(BF16)
    normed[0] = here
    normed[1] = there
    low = lax.broadcasted_iota(jnp.int32, (ROWS, 128), 1) < 64
    for pair in range(2):
        at = slice(pair * 2 * HEAD, (pair + 1) * 2 * HEAD)
        keys, values = (
            unpacked(dot(here, weight[kind, near, at]) + dot(there, weight[kind, far, at]))
            for kind in (1, 2)
        )
        for side in range(2):
            head = 2 * pair + side
            key, value = keys[side], values[side]
            packed[head, :, :128] = key[0].astype(BF16)
            packed[head, :, 128:256] = value[0].astype(BF16)
            tail = jnp.where(low, key[1], pltpu.roll(value[1], 64, 1))
            packed[head, :, 256:] = tail.astype(BF16)
    for distance, out in enumerate((k0, k1, k2, k3)):
        out[...] = packed[lax.rem(ids[1] + distance, 4), :OWN, :]


def project_keys(mine, theirs, gain, weight):
    half = mine.shape[1]
    return pl.pallas_call(
        project_keys_kernel,
        in_specs=[VM] * 4,
        out_specs=[VM] * 5,
        out_shape=[shape((2, ROWS, half), BF16)] + [shape((OWN, 384), BF16)] * 4,
        scratch_shapes=[pltpu.VMEM((4, ROWS, 384), BF16)],
        compiler_params=params(12),
        cost_estimate=cost(2 * ROWS * weight.size * 2 // 3, weight.size * 2),
        name="project_keys",
    )(mine, theirs, gain, weight)


def project_queries_kernel(normed, weight, q0, q1, q2, q3, packed):
    ids = position()
    half = normed.shape[2]
    near = lanes(ids[0] * half, half)
    far = lanes((1 - ids[0]) * half, half)
    low = lax.broadcasted_iota(jnp.int32, (ROWS, 128), 1) < 64
    for pair in range(2):
        at = slice(pair * 2 * HEAD, (pair + 1) * 2 * HEAD)
        both = dot(normed[0], weight[0, near, at]) + dot(normed[1], weight[0, far, at])
        for side, query in enumerate(unpacked(both)):
            packed[2 * pair + side, :, :128] = query[0].astype(BF16)
            packed[2 * pair + side, :, 128:] = jnp.where(low, query[1], 0.0).astype(BF16)
    for distance, out in enumerate((q0, q1, q2, q3)):
        out[...] = packed[lax.rem(ids[1] + distance, 4)]


def project_queries(normed, weight):
    return pl.pallas_call(
        project_queries_kernel,
        in_specs=[VM, VM],
        out_specs=[VM] * 4,
        out_shape=[shape((ROWS, 256), BF16)] * 4,
        scratch_shapes=[pltpu.VMEM((4, ROWS, 256), BF16)],
        compiler_params=params(10),
        cost_estimate=cost(2 * ROWS * weight.size // 3, weight.size),
        name="project_queries",
    )(normed, near_memory(weight))


BLOCK = 4 * ROWS
LOG2E = 1.4426950408889634


def key_columns(ref):
    return jnp.concatenate([ref[:, :128], ref[:, 256:]], axis=1)


def inverse_norms(ref):
    lane = lax.broadcasted_iota(jnp.int32, (8, 256), 1)
    ones = (lane < HEAD).astype(F32).astype(BF16)
    key = key_columns(ref).astype(F32)
    square = key * key
    high = square.astype(BF16)
    rest = (square - high.astype(F32)).astype(BF16)
    total = dot_t(ones, high) + dot_t(ones, rest)
    return lax.rsqrt(total * (1.0 / HEAD) + EPS)


def norms_kernel(*refs):
    pieces, out = refs[:-1], refs[-1]
    at = 0
    for ref in pieces:
        out[:, at : at + ref.shape[0]] = inverse_norms(ref)
        at += ref.shape[0]


def norms(pieces):
    keys = sum(piece.shape[0] for piece in pieces)
    return pl.pallas_call(
        norms_kernel,
        in_specs=[VM] * len(pieces),
        out_specs=VM,
        out_shape=shape((8, keys), F32),
        compiler_params=params(6),
        cost_estimate=cost(10**6, 10**5),
        name="norms",
    )(*pieces)


def attend_kernel(count, known, resumed, final, scale, queries, *refs):
    heads = lax.broadcasted_iota(jnp.int32, scale.shape, 1)
    gain = jnp.sum(jnp.where(heads == position()[1], scale[...], 0.0), axis=1, keepdims=True)
    gain = gain * (LOG2E / HEAD)
    pieces, refs = refs[:count], refs[count:]
    inverses, refs = refs[:known], refs[known:]
    if resumed:
        (old_mixed, old_stats), refs = refs[:2], refs[2:]
    sizes = [ref.shape[0] for ref in pieces]
    starts = [sum(sizes[:i]) for i in range(count)]

    total_known = sum(ref.shape[1] for ref in inverses)
    if total_known < sum(sizes):
        outs, inverse = refs[:-1], refs[-1]
        for at, size, ref in zip(starts, sizes, pieces):
            if at >= total_known:
                inverse[:, at - total_known : at - total_known + size] = inverse_norms(ref)
        inverses = (*inverses, inverse)
    else:
        outs = refs

    def inverse_of(at, size):
        for ref in inverses:
            if at < ref.shape[1]:
                return ref[0:1, at : at + size]
            at -= ref.shape[1]

    limit = 1024
    groups, room = [], 0
    for triple in zip(starts, sizes, pieces):
        if room < triple[1]:
            groups.append([])
            room = limit
        groups[-1].append(triple)
        room -= triple[1]

    def unit(query, factor, group):
        scores, peak = [], None
        for at, size, ref in group:
            part = dot_t(query, key_columns(ref)) * inverse_of(at, size)
            top = jnp.max(part, axis=1, keepdims=True)
            peak = top if peak is None else jnp.maximum(peak, top)
            scores.append(part)
        total, mixed = None, None
        for part, (_, _, ref) in zip(scores, group):
            exps = jnp.exp2((part - peak) * factor)
            sums = jnp.sum(exps, axis=1, keepdims=True)
            values = jnp.concatenate([ref[:, 128:256], ref[:, 256:]], axis=1)
            term = dot(exps.astype(BF16), values)
            total = sums if total is None else total + sums
            mixed = term if mixed is None else mixed + term
        return peak, total, mixed

    for begin in range(0, queries.shape[0], BLOCK):
        rows = slice(begin, begin + BLOCK)
        query = queries[rows, :]
        wide = query.astype(F32)
        own = lax.rsqrt(jnp.sum(wide * wide, axis=1, keepdims=True) * (1.0 / HEAD) + EPS)
        factor = own * gain
        states = [unit(query, factor, group) for group in groups]
        if resumed:
            states.append((old_stats[rows, 0:1], old_stats[rows, 64:65], old_mixed[rows, :]))
        peak = functools.reduce(jnp.maximum, [state[0] for state in states])
        if len(states) > 1:
            shrink = [jnp.exp2((state[0] - peak) * factor) for state in states]
            total = sum(state[1] * part for state, part in zip(states, shrink))
            mixed = sum(state[2] * part for state, part in zip(states, shrink))
        else:
            _, total, mixed = states[0]
        if not final:
            outs[0][rows, :] = mixed
            half = lax.broadcasted_iota(jnp.int32, (BLOCK, 128), 1) < 64
            outs[1][rows, :] = jnp.where(half, peak, total)
            continue
        mixed = mixed / total
        weight = peak * factor + jnp.log(total) * LOG2E
        high = weight.astype(BF16).astype(F32)
        rest = weight - high
        mid = rest.astype(BF16).astype(F32)
        place = lax.broadcasted_iota(jnp.int32, mixed.shape, 1)
        mixed = jnp.where(place == 128, high, mixed)
        mixed = jnp.where(place == 129, mid, mixed)
        mixed = jnp.where(place == 130, rest - mid, mixed)
        outs[0][rows, :] = mixed.astype(BF16)


def attend(scale, queries, pieces, inverses=(), state=(), final=True):
    rows = queries.shape[0]
    keys = sum(piece.shape[0] for piece in pieces)
    if final:
        outs = [shape((rows, 256), BF16)]
    else:
        outs = [shape((rows, 256), F32), shape((rows, 128), F32)]
    known = sum(inverse.shape[1] for inverse in inverses)
    if known < keys:
        outs.append(shape((8, keys - known), F32))
    return pl.pallas_call(
        functools.partial(attend_kernel, len(pieces), len(inverses), bool(state), final),
        in_specs=[VM] + [VM] * (1 + len(pieces) + len(inverses) + len(state)),
        out_specs=[VM] * len(outs),
        out_shape=outs,
        compiler_params=params(28),
        cost_estimate=cost(4 * rows * keys * 256, 8 * rows * 1024),
        name="attend",
    )(scale, near_memory(queries), *pieces, *inverses, *state)


def merge_kernel(a0, a1, *outs):
    parts = [ref[...].astype(F32) for ref in (a0, a1)]
    logs = [p[:, 128:129] + p[:, 129:130] + p[:, 130:131] for p in parts]
    peak = functools.reduce(jnp.maximum, logs)
    shares = [jnp.exp2(log - peak) for log in logs]
    total = sum(shares)
    mixed = sum(p * (share / total) for p, share in zip(parts, shares))
    mixed = jnp.concatenate([mixed[:, :128], pltpu.roll(mixed[:, 128:], 64, 1)], axis=1)
    for block in range(4):
        outs[block][...] = mixed[block * ROWS : (block + 1) * ROWS].astype(BF16)


def merge(parts):
    return pl.pallas_call(
        merge_kernel,
        in_specs=[VM] * 2,
        out_specs=[VM] * 4,
        out_shape=[shape((ROWS, 256), BF16)] * 4,
        compiler_params=params(8),
        cost_estimate=cost(20 * parts[0].size, 10 * parts[0].size),
        name="merge",
    )(*parts)


def output_kernel(mine, a0, a1, a2, a3, weight, out):
    ids = position()
    half = out.shape[1]
    side = ids[0] if mine else 1 - ids[0]

    def tile(i):
        at = lanes(side * half + i * TILE, TILE)
        total = None
        for distance, ref in enumerate((a0, a1, a2, a3)):
            head = lax.rem(ids[1] + distance, 4)
            rows = weight[pl.ds(pl.multiple_of(head * HEAD, HEAD), HEAD), at]
            term = dot(ref[:, :HEAD], rows)
            total = term if total is None else total + term
        out[:, lanes(i * TILE, TILE)] = total.astype(out.dtype)

    tiles(half // TILE, tile)


def output(heads, weight, mine, dtype):
    half = weight.shape[1] // 2
    return pl.pallas_call(
        functools.partial(output_kernel, mine),
        in_specs=[VM] * 5,
        out_specs=VM,
        out_shape=shape((ROWS, half), dtype),
        compiler_params=params(6),
        cost_estimate=cost(2 * ROWS * weight.size // 2, weight.size),
        name="output",
    )(*heads, weight)


def decode_first_kernel(own, other, encoded, weight, inputs, out):
    ids = position()
    half = weight.shape[1]

    def mix(i):
        at = lanes(i * TILE, TILE)
        enc = encoded[:, at].astype(F32)
        even, odd = enc[:ROWS], enc[ROWS:]
        binned = (even + odd) * 0.5
        block = (binned + (own[:, at] + other[:, at].astype(F32))).astype(BF16).astype(F32)
        row = lax.broadcasted_iota(jnp.int32, block.shape, 0)
        outside = ((ids[2] == 0) & (row == ROWS - 1)) | ((ids[2] == 63) & (row == OWN))
        even = jnp.where(outside, 0.0, block + even)
        odd = jnp.where(outside, 0.0, block + odd)
        inputs[:, at] = jnp.concatenate([even, odd], axis=0).astype(BF16)

    tiles(half // TILE, mix)
    decode_tiles(inputs, weight, out, (1 - ids[0]) * half)


def decode_tiles(inputs, weight, out, begin):
    def tile(i):
        at = lanes(begin + i * TILE, TILE)
        result = conv_taps(inputs[...], lambda t: weight[t, :, at], ROWS)
        out[:, lanes(i * TILE, TILE)] = result.astype(out.dtype)

    tiles(out.shape[1] // TILE, tile)


def decode_first(own, other, encoded, weight, width):
    half = weight.shape[1]
    return pl.pallas_call(
        decode_first_kernel,
        in_specs=[VM] * 4,
        out_specs=[VM] * 2,
        out_shape=[shape((2 * ROWS, half), BF16), shape((2 * ROWS, width), BF16)],
        compiler_params=params(8),
        cost_estimate=cost(10**6, 10**4),
        name="decode_first",
    )(own, other, encoded, weight)


def decode_kernel(mine, first, inputs, weight, out):
    ids = position()
    side = ids[0] if mine else 1 - ids[0]
    decode_tiles(inputs, weight, out, side * weight.shape[1] + first)


def decode(inputs, weight, mine, first, width, dtype):
    half = weight.shape[1]
    return pl.pallas_call(
        functools.partial(decode_kernel, mine, first),
        in_specs=[VM, VM],
        out_specs=VM,
        out_shape=shape((2 * ROWS, width), dtype),
        compiler_params=params(8),
        cost_estimate=cost(10**6, 10**4),
        name="decode",
    )(inputs, weight)


def slope_kernel(first, own, other, inputs, grad, near, far, *refs):
    ids = position()
    done, (decoded, slope, paired, wide) = refs[:-4], refs[-4:]
    half = own.shape[1]
    begin = 0
    if done:
        begin = first
        decoded[:, :first] = done[0][...]

    def tile(i):
        at = lanes(i * 128, 128)
        target = lanes(begin + i * 128, 128)
        source = lanes(first + i * 128, 128)
        column = lanes(ids[0] * half + first + i * 128, 128)
        pre = own[:, source] + other[:, at].astype(F32)
        tanh = gelu_tanh(pre)
        result = inputs[:, source].astype(F32) + 0.5 * pre * (1.0 + tanh)
        wide[2 * i, pl.ds(0, OWN, 2), :] = result[:OWN]
        wide[2 * i, pl.ds(1, OWN, 2), :] = result[ROWS : ROWS + OWN]
        decoded[:, target] = wide[2 * i].astype(BF16)
        slant = 0.5 * (1.0 + tanh) + (0.5 * 0.7978845608028654) * pre * (1.0 - tanh * tanh) * (
            1.0 + (3 * 0.044715) * (pre * pre)
        )
        wide[2 * i + 1] = grad[:, column].astype(F32)
        even = wide[2 * i + 1, pl.ds(0, OWN, 2), :]
        odd = wide[2 * i + 1, pl.ds(1, OWN, 2), :]
        paired[:, at] = even + odd
        row = lax.broadcasted_iota(jnp.int32, (ROWS - OWN, 128), 0)
        before, after = sides(lax.rem(ids[2], 2) == 1, near[:, column].astype(F32), far[:, column].astype(F32))
        even_edge = jnp.where(row == 0, after, 0.0)
        odd_edge = jnp.where(row == ROWS - OWN - 1, before, 0.0)
        cotangent = jnp.concatenate([even, even_edge, odd, odd_edge], axis=0)
        slope[:, at] = (cotangent * slant).astype(BF16)

    tiles(other.shape[1] // 128, tile)


def slopes(own, other, inputs, grad, near, far, first, done=()):
    width = other.shape[1]
    return pl.pallas_call(
        functools.partial(slope_kernel, first),
        in_specs=[VM] * (6 + len(done)),
        out_specs=[VM] * 3,
        out_shape=[
            shape((2 * OWN, width + (first if done else 0)), BF16),
            shape((2 * ROWS, width), BF16),
            shape((OWN, width), F32),
        ],
        scratch_shapes=[pltpu.VMEM((width // 64, 2 * OWN, 128), F32)],
        compiler_params=params(8),
        cost_estimate=cost(100 * 30 * 1000 * other.size, 14 * other.size),
        name="slopes",
    )(own, other, inputs, grad, near, far, *done)


def backward_kernel(mine, firsts, count, *refs):
    ids = position()
    slopes_in, starts, (weight, out) = (
        refs[: len(firsts)],
        refs[len(firsts) : len(firsts) + count],
        refs[len(firsts) + count :],
    )
    half = weight.shape[1]
    side = ids[0] if mine else 1 - ids[0]
    whole = [start for start in starts if start.shape[1] == half]
    chunks = [start for start in starts if start.shape[1] < half]

    def tile(i, chunk, begin):
        inner = lanes(i * TILE, TILE)
        first = mid = last = None
        for offset, slope in zip(firsts, slopes_in):
            at = pl.ds(pl.multiple_of(side * half + offset, TILE), slope.shape[1])
            terms = [dot_t(slope[...], weight[t, inner, at]) for t in range(3)]
            if first is None:
                first, mid, last = terms
            else:
                first, mid, last = first + terms[0], mid + terms[1], last + terms[2]
        total = first[ROWS:] + mid[:ROWS] + mid[ROWS:] + last[:ROWS]
        total = total + below(first[:ROWS], ROWS) + above(last[ROWS:], ROWS)
        total = total[:OWN]
        for start in whole:
            total = total + start[:, inner]
        if chunk is not None:
            total = total + chunk[:, lanes(i * TILE - begin, TILE)]
        out[:, inner] = total.astype(out.dtype)

    if not chunks:
        tiles(half // TILE, lambda i: tile(i, None, 0))
    begin = 0
    for chunk in chunks:
        width = chunk.shape[1]
        tiles(width // TILE, lambda i: tile(i + begin // TILE, chunk, begin))
        begin += width


def backward(parts, starts, weight, mine, dtype):
    half = weight.shape[1]
    size = sum(part.size for _, part in parts)
    return pl.pallas_call(
        functools.partial(backward_kernel, mine, [first for first, _ in parts], len(starts)),
        in_specs=[VM] * (len(parts) + len(starts) + 1),
        out_specs=VM,
        out_shape=shape((OWN, half), dtype),
        compiler_params=params(10),
        cost_estimate=cost(100 * 2 * 3 * half * size, 6 * size),
        name="backward",
    )(*[part for _, part in parts], *starts, weight)


def place(at):
    return at // 16, at // 4 % 4, at // 2 % 2, at % 2


def moves(dx=0, dz=0, dy=0, dc=0):
    pairs = []
    for at in range(64):
        x, z, y, c = place(at)
        pairs.append((at, (x + dx) % 4 * 16 + (z + dz) % 4 * 4 + (y ^ dy) * 2 + (c ^ dc)))
    return pairs


def swap(value):
    return lax.ppermute(value, "head", [(0, 1), (1, 0)])


def send(value, **step):
    return lax.ppermute(value, "seq", moves(**step))


def per_device(
    dna_bases,
    stem_weight,
    encoder_weight,
    norm_gain,
    attention_weight,
    logit_scale,
    out_weight,
    decoder_weight,
    grad_out,
):
    at = lax.axis_index("seq")
    x = at // 16
    feats = grad_out.shape[1]

    codes, near, far = prepare(dna_bases.reshape(OWN, 128), grad_out)
    near = send(near, dc=1)
    pairs = [(i, i + 1) for i in range(1, 63, 2)]
    far = lax.ppermute(far, "seq", pairs + [(b, a) for a, b in pairs])
    halo = near, far
    rows, stem_weight, encoder_weight = load(codes, stem_weight, encoder_weight)
    encoded, attention_weight = encode(
        *halo, rows, stem_weight, encoder_weight, attention_weight
    )
    gain = norm_gain.reshape(1, feats)
    normed, *keyvals = project_keys(encoded, swap(encoded), gain, attention_weight)

    def spread(blocks):
        return [send(blocks[d], dx=d) for d in (1, 3, 2)]

    def stacked(blocks):
        return jnp.concatenate(lax.optimization_barrier(blocks), axis=0)

    got = spread(keyvals)
    keyvals = stacked([keyvals[0]] + got)
    near = [send(keyvals, dz=1), send(keyvals, dz=3)]
    queries = project_queries(normed, attention_weight)
    *near, got = lax.optimization_barrier((*near, spread(queries)))
    queries = jnp.concatenate([queries[0]] + got, axis=0)
    others = send(queries, dy=1)
    half = keyvals.shape[0] // 2
    far = [send(near[0][:half], dz=1), send(near[1][half:], dz=3)]
    across = [send(piece, dc=1) for piece in (keyvals, *near)]
    pieces = [keyvals] + near + across
    inverse = norms(pieces)
    *far, inverse, others = lax.optimization_barrier((*far, inverse, others))
    far = jnp.concatenate(far, axis=0)
    pieces += [far, send(far, dc=1)]
    scale = logit_scale.reshape(1, 4)
    other, later = attend(scale, others, pieces, inverses=[inverse])
    other = send(other, dy=1)
    own = attend(scale, queries, pieces, inverses=[inverse, later])[0]
    mixed = merge([own, other])
    heads = [mixed[0], send(mixed[1], dx=-1), send(mixed[3], dx=-2), send(mixed[2], dx=-3)]

    sent = swap(output(heads, out_weight, False, BF16))
    kept = output(heads, out_weight, True, F32)
    half = decoder_weight.shape[1]
    split = 2 * TILE
    inputs, early = decode_first(kept, sent, encoded, decoder_weight, split)
    early = swap(early)
    late = decode(inputs, decoder_weight, False, split, half - split, BF16)
    late, inputs = lax.optimization_barrier((late, inputs))
    late = swap(late)
    kept = decode(inputs, decoder_weight, True, 0, half, F32)
    decoded, early, paired = slopes(kept, early, inputs, grad_out, *halo, 0)
    early_back = swap(early)
    decoded, late, rest = slopes(
        kept, late, inputs, grad_out, *halo, split, (decoded,)
    )
    late_back = swap(late)
    total = backward(
        [(0, early), (split, late)], [paired, rest], decoder_weight, True, F32
    )
    total = backward([(0, early_back)], [total], decoder_weight, False, F32)
    bins_grad = backward([(split, late_back)], [total], decoder_weight, False, BF16)
    return decoded, bins_grad


def solution(mesh):
    in_specs = (
        P("seq"),
        P(),
        P(None, None, "head"),
        P(),
        P(None, None, "head"),
        P("head"),
        P("head", None),
        P(None, "head", None),
        P("seq", None),
    )
    out_specs = (P("seq", "head"), P("seq", "head"))
    return jax.shard_map(
        per_device, mesh=mesh, in_specs=in_specs, out_specs=out_specs, check_vma=False
    )
```

```python
import functools

import jax
import jax.numpy as jnp
from jax import lax
from jax.experimental import pallas as pl
from jax.experimental.pallas import tpu as pltpu
from jax.sharding import PartitionSpec as P

BF16 = jnp.bfloat16
F32 = jnp.float32
ROWS = 136
OWN = 128
TILE = 256
HEAD = 192
EPS = 1e-06
MIB = 1024 * 1024


def params(mib):
    return pltpu.CompilerParams(vmem_limit_bytes=mib * MIB)


def dot(a, b):
    return jnp.dot(a, b, preferred_element_type=F32)


def dot_t(a, b):
    return lax.dot_general(a, b, (((1,), (1,)), ((), ())), preferred_element_type=F32)


def cost(flops, nbytes):
    return pl.CostEstimate(flops=int(flops), bytes_accessed=int(nbytes), transcendentals=0)


def shape(dims, dtype):
    return jax.ShapeDtypeStruct(dims, dtype)


VM = pl.BlockSpec(memory_space=pltpu.VMEM)
HBM = pl.BlockSpec(memory_space=pltpu.HBM)


def above(rows, span):
    parts = [pltpu.roll(rows[i : i + span], 1, 0) for i in range(0, rows.shape[0], span)]
    return jnp.concatenate(parts, axis=0)


def below(rows, span):
    parts = [pltpu.roll(rows[i : i + span], span - 1, 0) for i in range(0, rows.shape[0], span)]
    return jnp.concatenate(parts, axis=0)


def lanes(at, size):
    return pl.ds(at if isinstance(at, int) else pl.multiple_of(at, size), size)


def tiles(count, body):
    for i in range(count):
        body(i)


def gelu_tanh(x):
    return jnp.tanh(0.7978845608028654 * (x + 0.044715 * (x * x * x)))


def conv_taps(rows, weight, span):
    half = rows.shape[0] // 2
    first, mid, last = (dot(rows, weight(t)) for t in range(3))
    even = above(first[half:], span) + mid[:half] + last[half:]
    odd = first[:half] + mid[half:] + below(last[:half], span)
    return jnp.concatenate([even, odd], axis=0)


def position():
    at = lax.axis_index("seq")
    return lax.axis_index("head"), at // 16, at


def sides(odd, near, far):
    return jnp.where(odd, near, far), jnp.where(odd, far, near)


def prepare_kernel(bases, grad, codes, near, far, code, head, tail, sems):
    ids = position()
    rows = grad.shape[0]
    copies = [
        pltpu.make_async_copy(bases, code, sems.at[0]),
        pltpu.make_async_copy(grad.at[pl.ds(0, 16)], head, sems.at[1]),
        pltpu.make_async_copy(grad.at[pl.ds(rows - 16, 16)], tail, sems.at[2]),
    ]
    for copy in copies:
        copy.start()
    for copy in copies:
        copy.wait()
    feats = grad.shape[1]
    letters = (code[...] + 1).astype(F32)
    codes[...] = letters.astype(BF16)
    odd = lax.rem(ids[2], 2) == 1
    last = jnp.concatenate([tail[...].astype(F32)[8:], letters[OWN - 8 :]], axis=1)
    first = jnp.concatenate([head[...].astype(F32)[:8], letters[:8]], axis=1)
    near[...] = jnp.where(odd, first, last).astype(BF16)
    far[...] = jnp.where(odd, last, first).astype(BF16)


def near_memory(value):
    return pltpu.with_memory_space_constraint(value, pltpu.VMEM)


def far_memory(value):
    return pltpu.with_memory_space_constraint(value, pltpu.HBM)


def prepare(bases, grad):
    feats = grad.shape[1]
    return pl.pallas_call(
        prepare_kernel,
        in_specs=[HBM, HBM],
        out_specs=[VM] * 3,
        out_shape=[
            shape((OWN, 128), BF16),
            shape((8, feats + 128), BF16),
            shape((8, feats + 128), BF16),
        ],
        scratch_shapes=[
            pltpu.VMEM(bases.shape, jnp.int32),
            pltpu.VMEM((16, feats), BF16),
            pltpu.VMEM((16, feats), BF16),
            pltpu.SemaphoreType.DMA((3,)),
        ],
        compiler_params=params(4),
        cost_estimate=cost(10**5, 10**5),
        name="prepare",
    )(far_memory(bases), far_memory(grad))


def embed_letters(code, stem, embedded):
    patch = stem.shape[0] // 4
    row = lax.broadcasted_iota(jnp.int32, (2 * patch, 4 * patch), 0)
    col = lax.broadcasted_iota(jnp.int32, (2 * patch, 4 * patch), 1)
    spread = [
        dot(code, (row == col // 4 + offset).astype(F32).astype(BF16)) for offset in (0, patch)
    ]
    spread = jnp.concatenate(spread, axis=0)
    base = lax.broadcasted_iota(jnp.int32, spread.shape, 1) % 4 + 1
    onehot = (spread == base.astype(F32)).astype(F32).astype(BF16)

    def embed(i):
        at = lanes(i * TILE, TILE)
        embedded[:, at] = dot(onehot, stem[:, at]).astype(BF16)

    tiles(stem.shape[1] // TILE, embed)


def load_kernel(codes, stems, weights, embedded, stem, weight, sems):
    copies = [
        pltpu.make_async_copy(stems, stem, sems.at[0]),
        pltpu.make_async_copy(weights, weight, sems.at[1]),
    ]
    for copy in copies:
        copy.start()
    copies[0].wait()
    embed_letters(codes[...], stem, embedded)
    copies[1].wait()


def load(codes, stem, weight):
    return pl.pallas_call(
        load_kernel,
        in_specs=[VM, HBM, HBM],
        out_specs=[VM] * 3,
        out_shape=[
            pltpu.VMEM((2 * OWN, stem.shape[1]), BF16),
            pltpu.VMEM(stem.shape, BF16),
            pltpu.VMEM(weight.shape, BF16),
        ],
        scratch_shapes=[pltpu.SemaphoreType.DMA((2,))],
        compiler_params=params(4),
        cost_estimate=cost(10**5, weight.size * 2),
        name="load",
    )(codes, far_memory(stem), far_memory(weight))


def ring_order(rows):
    half = ROWS - OWN
    return (
        jnp.concatenate([rows[:OWN], rows[2 * OWN : 2 * OWN + half]], axis=0),
        jnp.concatenate([rows[OWN : 2 * OWN], rows[2 * OWN + half :]], axis=0),
    )


def encode_kernel(near, far, rows, stem, weight, encoded, embedded, halo):
    ids = position()
    feats = stem.shape[1]
    half = weight.shape[2]
    place = lax.broadcasted_iota(jnp.int32, (ROWS - OWN, 128), 0)
    before, after = sides(lax.rem(ids[2], 2) == 1, near[:, feats:].astype(F32), far[:, feats:].astype(F32))
    code = jnp.where(place >= 6, before, 0.0)
    code = jnp.where(place < 2, after, code)
    embed_letters(code.astype(BF16), stem, halo)
    embedded[: 2 * OWN, :] = rows[...]
    embedded[2 * OWN :, :] = halo[...]

    def convolve(i):
        at = lanes(i * TILE, TILE)
        parts = [dot(embedded[...], weight[tap, :, at]) for tap in range(3)]
        (first_even, first_odd), (even, odd), (last_even, last_odd) = map(ring_order, parts)
        even = above(first_odd, ROWS) + even + last_odd
        odd = first_even + odd + below(last_even, ROWS)
        pre = jnp.concatenate([even, odd], axis=0)
        mine = embedded[:, lanes(ids[0] * half + i * TILE, TILE)].astype(F32)
        mine = jnp.concatenate(ring_order(mine), axis=0)
        encoded[:, at] = (mine + 0.5 * pre * (1.0 + gelu_tanh(pre))).astype(BF16)

    tiles(half // TILE, convolve)


def encode(near, far, rows, stem, weight):
    half = weight.shape[2]
    feats = stem.shape[1]
    return pl.pallas_call(
        encode_kernel,
        in_specs=[VM] * 5,
        out_specs=VM,
        out_shape=shape((2 * ROWS, half), BF16),
        scratch_shapes=[
            pltpu.VMEM((2 * ROWS, feats), BF16),
            pltpu.VMEM((2 * (ROWS - OWN), feats), BF16),
        ],
        compiler_params=params(12),
        cost_estimate=cost(4 * OWN * weight.size, weight.size * 4),
        name="encode",
    )(near, far, near_memory(rows), near_memory(stem), near_memory(weight))


def fetch_kernel(source, target, sem):
    copy = pltpu.make_async_copy(source, target, sem)
    copy.start()
    copy.wait()


def fetch(value):
    return pl.pallas_call(
        fetch_kernel,
        in_specs=[HBM],
        out_specs=VM,
        out_shape=pltpu.VMEM(value.shape, value.dtype),
        scratch_shapes=[pltpu.SemaphoreType.DMA(())],
        compiler_params=params(2),
        cost_estimate=cost(10**5, value.size * 2),
        name="fetch",
    )(far_memory(value))


def unpacked(both):
    both = both.astype(BF16).astype(F32)
    turned = pltpu.roll(both, 2 * HEAD - 64, 1)
    return (both[:, :128], both[:, 128:256]), (turned[:, 128:256], turned[:, 256:384])


def project_keys_kernel(
    mine, theirs, gain, weight, normed, k0, k1, k2, k3, packed
):
    ids = position()
    half = mine.shape[1]
    near = lanes(ids[0] * half, half)
    far = lanes((1 - ids[0]) * half, half)
    rings = [ref[...].astype(F32) for ref in (mine, theirs)]
    binned = [(ring[:ROWS] + ring[ROWS:]) * 0.5 for ring in rings]
    total = sum(jnp.sum(part * part, axis=1, keepdims=True) for part in binned)
    inverse = lax.rsqrt(total * (1.0 / (2 * half)) + EPS)
    here = (binned[0] * inverse * gain[:, near]).astype(BF16)
    there = (binned[1] * inverse * gain[:, far]).astype(BF16)
    normed[0] = here
    normed[1] = there
    low = lax.broadcasted_iota(jnp.int32, (ROWS, 128), 1) < 64
    for pair in range(2):
        at = slice(pair * 2 * HEAD, (pair + 1) * 2 * HEAD)
        keys, values = (
            unpacked(dot(here, weight[kind, near, at]) + dot(there, weight[kind, far, at]))
            for kind in (1, 2)
        )
        for side in range(2):
            head = 2 * pair + side
            key, value = keys[side], values[side]
            packed[head, :, :128] = key[0].astype(BF16)
            packed[head, :, 128:256] = value[0].astype(BF16)
            tail = jnp.where(low, key[1], pltpu.roll(value[1], 64, 1))
            packed[head, :, 256:] = tail.astype(BF16)
    for distance, out in enumerate((k0, k1, k2, k3)):
        out[...] = packed[lax.rem(ids[1] + distance, 4), :OWN, :]


def project_keys(mine, theirs, gain, weight):
    half = mine.shape[1]
    return pl.pallas_call(
        project_keys_kernel,
        in_specs=[VM] * 4,
        out_specs=[VM] * 5,
        out_shape=[shape((2, ROWS, half), BF16)] + [shape((OWN, 384), BF16)] * 4,
        scratch_shapes=[pltpu.VMEM((4, ROWS, 384), BF16)],
        compiler_params=params(12),
        cost_estimate=cost(2 * ROWS * weight.size * 2 // 3, weight.size * 2),
        name="project_keys",
    )(mine, theirs, gain, near_memory(weight))


def project_queries_kernel(normed, weight, q0, q1, q2, q3, packed):
    ids = position()
    half = normed.shape[2]
    near = lanes(ids[0] * half, half)
    far = lanes((1 - ids[0]) * half, half)
    low = lax.broadcasted_iota(jnp.int32, (ROWS, 128), 1) < 64
    for pair in range(2):
        at = slice(pair * 2 * HEAD, (pair + 1) * 2 * HEAD)
        both = dot(normed[0], weight[0, near, at]) + dot(normed[1], weight[0, far, at])
        for side, query in enumerate(unpacked(both)):
            packed[2 * pair + side, :, :128] = query[0].astype(BF16)
            packed[2 * pair + side, :, 128:] = jnp.where(low, query[1], 0.0).astype(BF16)
    for distance, out in enumerate((q0, q1, q2, q3)):
        out[...] = packed[lax.rem(ids[1] + distance, 4)]


def project_queries(normed, weight):
    return pl.pallas_call(
        project_queries_kernel,
        in_specs=[VM, VM],
        out_specs=[VM] * 4,
        out_shape=[shape((ROWS, 256), BF16)] * 4,
        scratch_shapes=[pltpu.VMEM((4, ROWS, 256), BF16)],
        compiler_params=params(10),
        cost_estimate=cost(2 * ROWS * weight.size // 3, weight.size),
        name="project_queries",
    )(normed, near_memory(weight))


BLOCK = 4 * ROWS
LOG2E = 1.4426950408889634


def key_columns(ref):
    return jnp.concatenate([ref[:, :128], ref[:, 256:]], axis=1)


def inverse_norms(ref):
    lane = lax.broadcasted_iota(jnp.int32, (8, 256), 1)
    ones = (lane < HEAD).astype(F32).astype(BF16)
    key = key_columns(ref).astype(F32)
    square = key * key
    high = square.astype(BF16)
    rest = (square - high.astype(F32)).astype(BF16)
    total = dot_t(ones, high) + dot_t(ones, rest)
    return lax.rsqrt(total * (1.0 / HEAD) + EPS)


def norms_kernel(*refs):
    pieces, out = refs[:-1], refs[-1]
    at = 0
    for ref in pieces:
        out[:, at : at + ref.shape[0]] = inverse_norms(ref)
        at += ref.shape[0]


def norms(pieces):
    keys = sum(piece.shape[0] for piece in pieces)
    return pl.pallas_call(
        norms_kernel,
        in_specs=[VM] * len(pieces),
        out_specs=VM,
        out_shape=shape((8, keys), F32),
        compiler_params=params(6),
        cost_estimate=cost(10**6, 10**5),
        name="norms",
    )(*pieces)


def attend_kernel(count, known, resumed, final, scale, queries, *refs):
    heads = lax.broadcasted_iota(jnp.int32, scale.shape, 1)
    gain = jnp.sum(jnp.where(heads == position()[1], scale[...], 0.0), axis=1, keepdims=True)
    gain = gain * (LOG2E / HEAD)
    pieces, refs = refs[:count], refs[count:]
    inverses, refs = refs[:known], refs[known:]
    if resumed:
        (old_mixed, old_stats), refs = refs[:2], refs[2:]
    sizes = [ref.shape[0] for ref in pieces]
    starts = [sum(sizes[:i]) for i in range(count)]

    total_known = sum(ref.shape[1] for ref in inverses)
    if total_known < sum(sizes):
        outs, inverse = refs[:-1], refs[-1]
        for at, size, ref in zip(starts, sizes, pieces):
            if at >= total_known:
                inverse[:, at - total_known : at - total_known + size] = inverse_norms(ref)
        inverses = (*inverses, inverse)
    else:
        outs = refs

    def inverse_of(at, size):
        for ref in inverses:
            if at < ref.shape[1]:
                return ref[0:1, at : at + size]
            at -= ref.shape[1]

    limit = 1024
    groups, room = [], 0
    for triple in zip(starts, sizes, pieces):
        if room < triple[1]:
            groups.append([])
            room = limit
        groups[-1].append(triple)
        room -= triple[1]

    def unit(query, factor, group):
        scores, peak = [], None
        for at, size, ref in group:
            part = dot_t(query, key_columns(ref)) * inverse_of(at, size)
            top = jnp.max(part, axis=1, keepdims=True)
            peak = top if peak is None else jnp.maximum(peak, top)
            scores.append(part)
        total, mixed = None, None
        for part, (_, _, ref) in zip(scores, group):
            exps = jnp.exp2((part - peak) * factor)
            sums = jnp.sum(exps, axis=1, keepdims=True)
            values = jnp.concatenate([ref[:, 128:256], ref[:, 256:]], axis=1)
            term = dot(exps.astype(BF16), values)
            total = sums if total is None else total + sums
            mixed = term if mixed is None else mixed + term
        return peak, total, mixed

    for begin in range(0, queries.shape[0], BLOCK):
        rows = slice(begin, begin + BLOCK)
        query = queries[rows, :]
        wide = query.astype(F32)
        own = lax.rsqrt(jnp.sum(wide * wide, axis=1, keepdims=True) * (1.0 / HEAD) + EPS)
        factor = own * gain
        states = [unit(query, factor, group) for group in groups]
        if resumed:
            states.append((old_stats[rows, 0:1], old_stats[rows, 64:65], old_mixed[rows, :]))
        peak = functools.reduce(jnp.maximum, [state[0] for state in states])
        if len(states) > 1:
            shrink = [jnp.exp2((state[0] - peak) * factor) for state in states]
            total = sum(state[1] * part for state, part in zip(states, shrink))
            mixed = sum(state[2] * part for state, part in zip(states, shrink))
        else:
            _, total, mixed = states[0]
        if not final:
            outs[0][rows, :] = mixed
            half = lax.broadcasted_iota(jnp.int32, (BLOCK, 128), 1) < 64
            outs[1][rows, :] = jnp.where(half, peak, total)
            continue
        mixed = mixed / total
        weight = peak * factor + jnp.log(total) * LOG2E
        high = weight.astype(BF16).astype(F32)
        rest = weight - high
        mid = rest.astype(BF16).astype(F32)
        place = lax.broadcasted_iota(jnp.int32, mixed.shape, 1)
        mixed = jnp.where(place == 128, high, mixed)
        mixed = jnp.where(place == 129, mid, mixed)
        mixed = jnp.where(place == 130, rest - mid, mixed)
        outs[0][rows, :] = mixed.astype(BF16)


def attend(scale, queries, pieces, inverses=(), state=(), final=True):
    rows = queries.shape[0]
    keys = sum(piece.shape[0] for piece in pieces)
    if final:
        outs = [shape((rows, 256), BF16)]
    else:
        outs = [shape((rows, 256), F32), shape((rows, 128), F32)]
    known = sum(inverse.shape[1] for inverse in inverses)
    if known < keys:
        outs.append(shape((8, keys - known), F32))
    return pl.pallas_call(
        functools.partial(attend_kernel, len(pieces), len(inverses), bool(state), final),
        in_specs=[VM] + [VM] * (1 + len(pieces) + len(inverses) + len(state)),
        out_specs=[VM] * len(outs),
        out_shape=outs,
        compiler_params=params(28),
        cost_estimate=cost(4 * rows * keys * 256, 8 * rows * 1024),
        name="attend",
    )(scale, near_memory(queries), *pieces, *inverses, *state)


def merge_kernel(a0, a1, *outs):
    parts = [ref[...].astype(F32) for ref in (a0, a1)]
    logs = [p[:, 128:129] + p[:, 129:130] + p[:, 130:131] for p in parts]
    peak = functools.reduce(jnp.maximum, logs)
    shares = [jnp.exp2(log - peak) for log in logs]
    total = sum(shares)
    mixed = sum(p * (share / total) for p, share in zip(parts, shares))
    mixed = jnp.concatenate([mixed[:, :128], pltpu.roll(mixed[:, 128:], 64, 1)], axis=1)
    for block in range(4):
        outs[block][...] = mixed[block * ROWS : (block + 1) * ROWS].astype(BF16)


def merge(parts):
    return pl.pallas_call(
        merge_kernel,
        in_specs=[VM] * 2,
        out_specs=[VM] * 4,
        out_shape=[shape((ROWS, 256), BF16)] * 4,
        compiler_params=params(8),
        cost_estimate=cost(20 * parts[0].size, 10 * parts[0].size),
        name="merge",
    )(*parts)


def output_kernel(mine, a0, a1, a2, a3, weight, out):
    ids = position()
    half = out.shape[1]
    side = ids[0] if mine else 1 - ids[0]

    def tile(i):
        at = lanes(side * half + i * TILE, TILE)
        total = None
        for distance, ref in enumerate((a0, a1, a2, a3)):
            head = lax.rem(ids[1] + distance, 4)
            rows = weight[pl.ds(pl.multiple_of(head * HEAD, HEAD), HEAD), at]
            term = dot(ref[:, :HEAD], rows)
            total = term if total is None else total + term
        out[:, lanes(i * TILE, TILE)] = total.astype(out.dtype)

    tiles(half // TILE, tile)


def output(heads, weight, mine, dtype):
    half = weight.shape[1] // 2
    return pl.pallas_call(
        functools.partial(output_kernel, mine),
        in_specs=[VM] * 5,
        out_specs=VM,
        out_shape=shape((ROWS, half), dtype),
        compiler_params=params(6),
        cost_estimate=cost(2 * ROWS * weight.size // 2, weight.size),
        name="output",
    )(*heads, weight)


def decode_first_kernel(own, other, encoded, weight, inputs, out):
    ids = position()
    half = weight.shape[1]

    def mix(i):
        at = lanes(i * TILE, TILE)
        enc = encoded[:, at].astype(F32)
        even, odd = enc[:ROWS], enc[ROWS:]
        binned = (even + odd) * 0.5
        block = (binned + (own[:, at] + other[:, at].astype(F32))).astype(BF16).astype(F32)
        row = lax.broadcasted_iota(jnp.int32, block.shape, 0)
        outside = ((ids[2] == 0) & (row == ROWS - 1)) | ((ids[2] == 63) & (row == OWN))
        even = jnp.where(outside, 0.0, block + even)
        odd = jnp.where(outside, 0.0, block + odd)
        inputs[:, at] = jnp.concatenate([even, odd], axis=0).astype(BF16)

    tiles(half // TILE, mix)
    decode_tiles(inputs, weight, out, (1 - ids[0]) * half)


def decode_tiles(inputs, weight, out, begin):
    def tile(i):
        at = lanes(begin + i * TILE, TILE)
        result = conv_taps(inputs[...], lambda t: weight[t, :, at], ROWS)
        out[:, lanes(i * TILE, TILE)] = result.astype(out.dtype)

    tiles(out.shape[1] // TILE, tile)


def decode_first(own, other, encoded, weight, width):
    half = weight.shape[1]
    return pl.pallas_call(
        decode_first_kernel,
        in_specs=[VM] * 4,
        out_specs=[VM] * 2,
        out_shape=[shape((2 * ROWS, half), BF16), shape((2 * ROWS, width), BF16)],
        compiler_params=params(8),
        cost_estimate=cost(10**6, 10**4),
        name="decode_first",
    )(own, other, encoded, weight)


def decode_kernel(mine, first, inputs, weight, out):
    ids = position()
    side = ids[0] if mine else 1 - ids[0]
    decode_tiles(inputs, weight, out, side * weight.shape[1] + first)


def decode(inputs, weight, mine, first, width, dtype):
    half = weight.shape[1]
    return pl.pallas_call(
        functools.partial(decode_kernel, mine, first),
        in_specs=[VM, VM],
        out_specs=VM,
        out_shape=shape((2 * ROWS, width), dtype),
        compiler_params=params(8),
        cost_estimate=cost(10**6, 10**4),
        name="decode",
    )(inputs, weight)


def slope_kernel(first, own, other, inputs, grad, near, far, *refs):
    ids = position()
    done, (decoded, slope, paired, wide) = refs[:-4], refs[-4:]
    half = own.shape[1]
    begin = 0
    if done:
        begin = first
        decoded[:, :first] = done[0][...]

    def tile(i):
        at = lanes(i * 128, 128)
        target = lanes(begin + i * 128, 128)
        source = lanes(first + i * 128, 128)
        column = lanes(ids[0] * half + first + i * 128, 128)
        pre = own[:, source] + other[:, at].astype(F32)
        tanh = gelu_tanh(pre)
        result = inputs[:, source].astype(F32) + 0.5 * pre * (1.0 + tanh)
        wide[2 * i, pl.ds(0, OWN, 2), :] = result[:OWN]
        wide[2 * i, pl.ds(1, OWN, 2), :] = result[ROWS : ROWS + OWN]
        decoded[:, target] = wide[2 * i].astype(BF16)
        slant = 0.5 * (1.0 + tanh) + (0.5 * 0.7978845608028654) * pre * (1.0 - tanh * tanh) * (
            1.0 + (3 * 0.044715) * (pre * pre)
        )
        wide[2 * i + 1] = grad[:, column].astype(F32)
        even = wide[2 * i + 1, pl.ds(0, OWN, 2), :]
        odd = wide[2 * i + 1, pl.ds(1, OWN, 2), :]
        paired[:, at] = even + odd
        row = lax.broadcasted_iota(jnp.int32, (ROWS - OWN, 128), 0)
        before, after = sides(lax.rem(ids[2], 2) == 1, near[:, column].astype(F32), far[:, column].astype(F32))
        even_edge = jnp.where(row == 0, after, 0.0)
        odd_edge = jnp.where(row == ROWS - OWN - 1, before, 0.0)
        cotangent = jnp.concatenate([even, even_edge, odd, odd_edge], axis=0)
        slope[:, at] = (cotangent * slant).astype(BF16)

    tiles(other.shape[1] // 128, tile)


def slopes(own, other, inputs, grad, near, far, first, done=()):
    width = other.shape[1]
    return pl.pallas_call(
        functools.partial(slope_kernel, first),
        in_specs=[VM] * (6 + len(done)),
        out_specs=[VM] * 3,
        out_shape=[
            shape((2 * OWN, width + (first if done else 0)), BF16),
            shape((2 * ROWS, width), BF16),
            shape((OWN, width), F32),
        ],
        scratch_shapes=[pltpu.VMEM((width // 64, 2 * OWN, 128), F32)],
        compiler_params=params(8),
        cost_estimate=cost(100 * 30 * 1000 * other.size, 14 * other.size),
        name="slopes",
    )(own, other, inputs, grad, near, far, *done)


def backward_kernel(mine, firsts, count, *refs):
    ids = position()
    slopes_in, starts, (weight, out) = (
        refs[: len(firsts)],
        refs[len(firsts) : len(firsts) + count],
        refs[len(firsts) + count :],
    )
    half = weight.shape[1]
    side = ids[0] if mine else 1 - ids[0]
    whole = [start for start in starts if start.shape[1] == half]
    chunks = [start for start in starts if start.shape[1] < half]

    def tile(i, chunk, begin):
        inner = lanes(i * TILE, TILE)
        first = mid = last = None
        for offset, slope in zip(firsts, slopes_in):
            at = pl.ds(pl.multiple_of(side * half + offset, TILE), slope.shape[1])
            terms = [dot_t(slope[...], weight[t, inner, at]) for t in range(3)]
            if first is None:
                first, mid, last = terms
            else:
                first, mid, last = first + terms[0], mid + terms[1], last + terms[2]
        total = first[ROWS:] + mid[:ROWS] + mid[ROWS:] + last[:ROWS]
        total = total + below(first[:ROWS], ROWS) + above(last[ROWS:], ROWS)
        total = total[:OWN]
        for start in whole:
            total = total + start[:, inner]
        if chunk is not None:
            total = total + chunk[:, lanes(i * TILE - begin, TILE)]
        out[:, inner] = total.astype(out.dtype)

    if not chunks:
        tiles(half // TILE, lambda i: tile(i, None, 0))
    begin = 0
    for chunk in chunks:
        width = chunk.shape[1]
        tiles(width // TILE, lambda i: tile(i + begin // TILE, chunk, begin))
        begin += width


def backward(parts, starts, weight, mine, dtype):
    half = weight.shape[1]
    size = sum(part.size for _, part in parts)
    return pl.pallas_call(
        functools.partial(backward_kernel, mine, [first for first, _ in parts], len(starts)),
        in_specs=[VM] * (len(parts) + len(starts) + 1),
        out_specs=VM,
        out_shape=shape((OWN, half), dtype),
        compiler_params=params(10),
        cost_estimate=cost(100 * 2 * 3 * half * size, 6 * size),
        name="backward",
    )(*[part for _, part in parts], *starts, weight)


def place(at):
    return at // 16, at // 4 % 4, at // 2 % 2, at % 2


def moves(dx=0, dz=0, dy=0, dc=0):
    pairs = []
    for at in range(64):
        x, z, y, c = place(at)
        pairs.append((at, (x + dx) % 4 * 16 + (z + dz) % 4 * 4 + (y ^ dy) * 2 + (c ^ dc)))
    return pairs


def swap(value):
    return lax.ppermute(value, "head", [(0, 1), (1, 0)])


def send(value, **step):
    return lax.ppermute(value, "seq", moves(**step))


def per_device(
    dna_bases,
    stem_weight,
    encoder_weight,
    norm_gain,
    attention_weight,
    logit_scale,
    out_weight,
    decoder_weight,
    grad_out,
):
    at = lax.axis_index("seq")
    x = at // 16
    feats = grad_out.shape[1]

    codes, near, far = prepare(dna_bases.reshape(OWN, 128), grad_out)
    near = send(near, dc=1)
    pairs = [(i, i + 1) for i in range(1, 63, 2)]
    far = lax.ppermute(far, "seq", pairs + [(b, a) for a, b in pairs])
    halo = near, far
    rows, stem_weight, encoder_weight = load(codes, stem_weight, encoder_weight)
    encoded = encode(*halo, rows, stem_weight, encoder_weight)
    encoded, attention_weight = lax.optimization_barrier((encoded, attention_weight))
    attention_weight = fetch(attention_weight)
    gain = norm_gain.reshape(1, feats)
    normed, *keyvals = project_keys(encoded, swap(encoded), gain, attention_weight)

    def spread(blocks):
        return [send(blocks[d], dx=d) for d in (1, 3, 2)]

    def stacked(blocks):
        return jnp.concatenate(lax.optimization_barrier(blocks), axis=0)

    got = spread(keyvals)
    keyvals = stacked([keyvals[0]] + got)
    near = [send(keyvals, dz=1), send(keyvals, dz=3)]
    queries = project_queries(normed, attention_weight)
    *near, got = lax.optimization_barrier((*near, spread(queries)))
    queries = jnp.concatenate([queries[0]] + got, axis=0)
    others = send(queries, dy=1)
    half = keyvals.shape[0] // 2
    far = [send(near[0][:half], dz=1), send(near[1][half:], dz=3)]
    across = [send(piece, dc=1) for piece in (keyvals, *near)]
    pieces = [keyvals] + near + across
    inverse = norms(pieces)
    *far, inverse, others = lax.optimization_barrier((*far, inverse, others))
    far = jnp.concatenate(far, axis=0)
    pieces += [far, send(far, dc=1)]
    scale = logit_scale.reshape(1, 4)
    other, later = attend(scale, others, pieces, inverses=[inverse])
    other = send(other, dy=1)
    own = attend(scale, queries, pieces, inverses=[inverse, later])[0]
    mixed = merge([own, other])
    heads = [mixed[0], send(mixed[1], dx=-1), send(mixed[3], dx=-2), send(mixed[2], dx=-3)]

    sent = swap(output(heads, out_weight, False, BF16))
    kept = output(heads, out_weight, True, F32)
    half = decoder_weight.shape[1]
    split = 2 * TILE
    inputs, early = decode_first(kept, sent, encoded, decoder_weight, split)
    early = swap(early)
    late = decode(inputs, decoder_weight, False, split, half - split, BF16)
    late, inputs = lax.optimization_barrier((late, inputs))
    late = swap(late)
    kept = decode(inputs, decoder_weight, True, 0, half, F32)
    decoded, early, paired = slopes(kept, early, inputs, grad_out, *halo, 0)
    early_back = swap(early)
    decoded, late, rest = slopes(
        kept, late, inputs, grad_out, *halo, split, (decoded,)
    )
    late_back = swap(late)
    total = backward(
        [(0, early), (split, late)], [paired, rest], decoder_weight, True, F32
    )
    total = backward([(0, early_back)], [total], decoder_weight, False, F32)
    bins_grad = backward([(split, late_back)], [total], decoder_weight, False, BF16)
    return decoded, bins_grad


def solution(mesh):
    in_specs = (
        P("seq"),
        P(),
        P(None, None, "head"),
        P(),
        P(None, None, "head"),
        P("head"),
        P("head", None),
        P(None, "head", None),
        P("seq", None),
    )
    out_specs = (P("seq", "head"), P("seq", "head"))
    return jax.shard_map(
        per_device, mesh=mesh, in_specs=in_specs, out_specs=out_specs, check_vma=False
    )
```

```python
import functools

import jax
import jax.numpy as jnp
from jax import lax
from jax.experimental import pallas as pl
from jax.experimental.pallas import tpu as pltpu
from jax.sharding import PartitionSpec as P

BF16 = jnp.bfloat16
F32 = jnp.float32
ROWS = 136
OWN = 128
TILE = 256
HEAD = 192
EPS = 1e-06
MIB = 1024 * 1024


def params(mib):
    return pltpu.CompilerParams(vmem_limit_bytes=mib * MIB)


def dot(a, b):
    return jnp.dot(a, b, preferred_element_type=F32)


def dot_t(a, b):
    return lax.dot_general(a, b, (((1,), (1,)), ((), ())), preferred_element_type=F32)


def cost(flops, nbytes):
    return pl.CostEstimate(flops=int(flops), bytes_accessed=int(nbytes), transcendentals=0)


def shape(dims, dtype):
    return jax.ShapeDtypeStruct(dims, dtype)


VM = pl.BlockSpec(memory_space=pltpu.VMEM)
HBM = pl.BlockSpec(memory_space=pltpu.HBM)


def above(rows, span):
    parts = [pltpu.roll(rows[i : i + span], 1, 0) for i in range(0, rows.shape[0], span)]
    return jnp.concatenate(parts, axis=0)


def below(rows, span):
    parts = [pltpu.roll(rows[i : i + span], span - 1, 0) for i in range(0, rows.shape[0], span)]
    return jnp.concatenate(parts, axis=0)


def lanes(at, size):
    return pl.ds(at if isinstance(at, int) else pl.multiple_of(at, size), size)


def tiles(count, body):
    for i in range(count):
        body(i)


def gelu_tanh(x):
    return jnp.tanh(0.7978845608028654 * (x + 0.044715 * (x * x * x)))


def conv_taps(rows, weight, span):
    half = rows.shape[0] // 2
    first, mid, last = (dot(rows, weight(t)) for t in range(3))
    even = above(first[half:], span) + mid[:half] + last[half:]
    odd = first[:half] + mid[half:] + below(last[:half], span)
    return jnp.concatenate([even, odd], axis=0)


def position():
    at = lax.axis_index("seq")
    return lax.axis_index("head"), at // 16, at


def sides(odd, near, far):
    return jnp.where(odd, near, far), jnp.where(odd, far, near)


def prepare_kernel(bases, grad, codes, near, far, code, head, tail, sems):
    ids = position()
    rows = grad.shape[0]
    copies = [
        pltpu.make_async_copy(bases, code, sems.at[0]),
        pltpu.make_async_copy(grad.at[pl.ds(0, 16)], head, sems.at[1]),
        pltpu.make_async_copy(grad.at[pl.ds(rows - 16, 16)], tail, sems.at[2]),
    ]
    for copy in copies:
        copy.start()
    for copy in copies:
        copy.wait()
    feats = grad.shape[1]
    letters = (code[...] + 1).astype(F32)
    codes[...] = letters.astype(BF16)
    odd = lax.rem(ids[2], 2) == 1
    last = jnp.concatenate([tail[...].astype(F32)[8:], letters[OWN - 8 :]], axis=1)
    first = jnp.concatenate([head[...].astype(F32)[:8], letters[:8]], axis=1)
    near[...] = jnp.where(odd, first, last).astype(BF16)
    far[...] = jnp.where(odd, last, first).astype(BF16)


def near_memory(value):
    return pltpu.with_memory_space_constraint(value, pltpu.VMEM)


def far_memory(value):
    return pltpu.with_memory_space_constraint(value, pltpu.HBM)


def prepare(bases, grad):
    feats = grad.shape[1]
    return pl.pallas_call(
        prepare_kernel,
        in_specs=[HBM, HBM],
        out_specs=[VM] * 3,
        out_shape=[
            shape((OWN, 128), BF16),
            shape((8, feats + 128), BF16),
            shape((8, feats + 128), BF16),
        ],
        scratch_shapes=[
            pltpu.VMEM(bases.shape, jnp.int32),
            pltpu.VMEM((16, feats), BF16),
            pltpu.VMEM((16, feats), BF16),
            pltpu.SemaphoreType.DMA((3,)),
        ],
        compiler_params=params(4),
        cost_estimate=cost(10**5, 10**5),
        name="prepare",
    )(far_memory(bases), far_memory(grad))


def embed_letters(code, stem, embedded):
    patch = stem.shape[0] // 4
    row = lax.broadcasted_iota(jnp.int32, (2 * patch, 4 * patch), 0)
    col = lax.broadcasted_iota(jnp.int32, (2 * patch, 4 * patch), 1)
    spread = [
        dot(code, (row == col // 4 + offset).astype(F32).astype(BF16)) for offset in (0, patch)
    ]
    spread = jnp.concatenate(spread, axis=0)
    base = lax.broadcasted_iota(jnp.int32, spread.shape, 1) % 4 + 1
    onehot = (spread == base.astype(F32)).astype(F32).astype(BF16)

    def embed(i):
        at = lanes(i * TILE, TILE)
        embedded[:, at] = dot(onehot, stem[:, at]).astype(BF16)

    tiles(stem.shape[1] // TILE, embed)


def load_kernel(codes, stems, weights, embedded, stem, weight, sems):
    copies = [
        pltpu.make_async_copy(stems, stem, sems.at[0]),
        pltpu.make_async_copy(weights, weight, sems.at[1]),
    ]
    for copy in copies:
        copy.start()
    copies[0].wait()
    embed_letters(codes[...], stem, embedded)
    copies[1].wait()


def load(codes, stem, weight):
    return pl.pallas_call(
        load_kernel,
        in_specs=[VM, HBM, HBM],
        out_specs=[VM] * 3,
        out_shape=[
            pltpu.VMEM((2 * OWN, stem.shape[1]), BF16),
            pltpu.VMEM(stem.shape, BF16),
            pltpu.VMEM(weight.shape, BF16),
        ],
        scratch_shapes=[pltpu.SemaphoreType.DMA((2,))],
        compiler_params=params(4),
        cost_estimate=cost(10**5, weight.size * 2),
        name="load",
    )(codes, far_memory(stem), far_memory(weight))


def ring_order(rows):
    half = ROWS - OWN
    return (
        jnp.concatenate([rows[:OWN], rows[2 * OWN : 2 * OWN + half]], axis=0),
        jnp.concatenate([rows[OWN : 2 * OWN], rows[2 * OWN + half :]], axis=0),
    )


def encode_kernel(near, far, rows, stem, weight, encoded, embedded, halo):
    ids = position()
    feats = stem.shape[1]
    half = weight.shape[2]
    place = lax.broadcasted_iota(jnp.int32, (ROWS - OWN, 128), 0)
    before, after = sides(lax.rem(ids[2], 2) == 1, near[:, feats:].astype(F32), far[:, feats:].astype(F32))
    code = jnp.where(place >= 6, before, 0.0)
    code = jnp.where(place < 2, after, code)
    embed_letters(code.astype(BF16), stem, halo)
    embedded[: 2 * OWN, :] = rows[...]
    embedded[2 * OWN :, :] = halo[...]

    def convolve(i):
        at = lanes(i * TILE, TILE)
        parts = [dot(embedded[...], weight[tap, :, at]) for tap in range(3)]
        (first_even, first_odd), (even, odd), (last_even, last_odd) = map(ring_order, parts)
        even = above(first_odd, ROWS) + even + last_odd
        odd = first_even + odd + below(last_even, ROWS)
        pre = jnp.concatenate([even, odd], axis=0)
        mine = embedded[:, lanes(ids[0] * half + i * TILE, TILE)].astype(F32)
        mine = jnp.concatenate(ring_order(mine), axis=0)
        encoded[:, at] = (mine + 0.5 * pre * (1.0 + gelu_tanh(pre))).astype(BF16)

    tiles(half // TILE, convolve)


def encode(near, far, rows, stem, weight):
    half = weight.shape[2]
    feats = stem.shape[1]
    return pl.pallas_call(
        encode_kernel,
        in_specs=[VM] * 5,
        out_specs=VM,
        out_shape=shape((2 * ROWS, half), BF16),
        scratch_shapes=[
            pltpu.VMEM((2 * ROWS, feats), BF16),
            pltpu.VMEM((2 * (ROWS - OWN), feats), BF16),
        ],
        compiler_params=params(12),
        cost_estimate=cost(4 * OWN * weight.size, weight.size * 4),
        name="encode",
    )(near, far, near_memory(rows), near_memory(stem), near_memory(weight))


def fetch_kernel(source, target, sem):
    copy = pltpu.make_async_copy(source, target, sem)
    copy.start()
    copy.wait()


def fetch(value):
    return pl.pallas_call(
        fetch_kernel,
        in_specs=[HBM],
        out_specs=VM,
        out_shape=pltpu.VMEM(value.shape, value.dtype),
        scratch_shapes=[pltpu.SemaphoreType.DMA(())],
        compiler_params=params(2),
        cost_estimate=cost(10**5, value.size * 2),
        name="fetch",
    )(far_memory(value))


def unpacked(both):
    both = both.astype(BF16).astype(F32)
    turned = pltpu.roll(both, 2 * HEAD - 64, 1)
    return (both[:, :128], both[:, 128:256]), (turned[:, 128:256], turned[:, 256:384])


def project_keys_kernel(
    mine, theirs, gain, weight, normed, k0, k1, k2, k3, packed
):
    ids = position()
    half = mine.shape[1]
    near = lanes(ids[0] * half, half)
    far = lanes((1 - ids[0]) * half, half)
    rings = [ref[...].astype(F32) for ref in (mine, theirs)]
    binned = [(ring[:ROWS] + ring[ROWS:]) * 0.5 for ring in rings]
    total = sum(jnp.sum(part * part, axis=1, keepdims=True) for part in binned)
    inverse = lax.rsqrt(total * (1.0 / (2 * half)) + EPS)
    here = (binned[0] * inverse * gain[:, near]).astype(BF16)
    there = (binned[1] * inverse * gain[:, far]).astype(BF16)
    normed[0] = here
    normed[1] = there
    low = lax.broadcasted_iota(jnp.int32, (ROWS, 128), 1) < 64
    for pair in range(2):
        at = slice(pair * 2 * HEAD, (pair + 1) * 2 * HEAD)
        keys, values = (
            unpacked(dot(here, weight[kind, near, at]) + dot(there, weight[kind, far, at]))
            for kind in (1, 2)
        )
        for side in range(2):
            head = 2 * pair + side
            key, value = keys[side], values[side]
            packed[head, :, :128] = key[0].astype(BF16)
            packed[head, :, 128:256] = value[0].astype(BF16)
            tail = jnp.where(low, key[1], pltpu.roll(value[1], 64, 1))
            packed[head, :, 256:] = tail.astype(BF16)
    for distance, out in enumerate((k0, k1, k2, k3)):
        out[...] = packed[lax.rem(ids[1] + distance, 4), :OWN, :]


def project_keys(mine, theirs, gain, weight):
    half = mine.shape[1]
    return pl.pallas_call(
        project_keys_kernel,
        in_specs=[VM] * 4,
        out_specs=[VM] * 5,
        out_shape=[shape((2, ROWS, half), BF16)] + [shape((OWN, 384), BF16)] * 4,
        scratch_shapes=[pltpu.VMEM((4, ROWS, 384), BF16)],
        compiler_params=params(12),
        cost_estimate=cost(2 * ROWS * weight.size * 2 // 3, weight.size * 2),
        name="project_keys",
    )(mine, theirs, gain, near_memory(weight))


def project_queries_kernel(normed, weight, q0, q1, q2, q3, packed):
    ids = position()
    half = normed.shape[2]
    near = lanes(ids[0] * half, half)
    far = lanes((1 - ids[0]) * half, half)
    low = lax.broadcasted_iota(jnp.int32, (ROWS, 128), 1) < 64
    for pair in range(2):
        at = slice(pair * 2 * HEAD, (pair + 1) * 2 * HEAD)
        both = dot(normed[0], weight[0, near, at]) + dot(normed[1], weight[0, far, at])
        for side, query in enumerate(unpacked(both)):
            packed[2 * pair + side, :, :128] = query[0].astype(BF16)
            packed[2 * pair + side, :, 128:] = jnp.where(low, query[1], 0.0).astype(BF16)
    for distance, out in enumerate((q0, q1, q2, q3)):
        out[...] = packed[lax.rem(ids[1] + distance, 4)]


def project_queries(normed, weight):
    return pl.pallas_call(
        project_queries_kernel,
        in_specs=[VM, VM],
        out_specs=[VM] * 4,
        out_shape=[shape((ROWS, 256), BF16)] * 4,
        scratch_shapes=[pltpu.VMEM((4, ROWS, 256), BF16)],
        compiler_params=params(10),
        cost_estimate=cost(2 * ROWS * weight.size // 3, weight.size),
        name="project_queries",
    )(normed, near_memory(weight))


BLOCK = 4 * ROWS
LOG2E = 1.4426950408889634


def key_columns(ref):
    return jnp.concatenate([ref[:, :128], ref[:, 256:]], axis=1)


def inverse_norms(ref):
    lane = lax.broadcasted_iota(jnp.int32, (8, 256), 1)
    ones = (lane < HEAD).astype(F32).astype(BF16)
    key = key_columns(ref).astype(F32)
    square = key * key
    high = square.astype(BF16)
    rest = (square - high.astype(F32)).astype(BF16)
    total = dot_t(ones, high) + dot_t(ones, rest)
    return lax.rsqrt(total * (1.0 / HEAD) + EPS)


def norms_kernel(*refs):
    pieces, out = refs[:-1], refs[-1]
    at = 0
    for ref in pieces:
        out[:, at : at + ref.shape[0]] = inverse_norms(ref)
        at += ref.shape[0]


def norms(pieces):
    keys = sum(piece.shape[0] for piece in pieces)
    return pl.pallas_call(
        norms_kernel,
        in_specs=[VM] * len(pieces),
        out_specs=VM,
        out_shape=shape((8, keys), F32),
        compiler_params=params(6),
        cost_estimate=cost(10**6, 10**5),
        name="norms",
    )(*pieces)


def attend_kernel(count, known, resumed, final, scale, queries, *refs):
    heads = lax.broadcasted_iota(jnp.int32, scale.shape, 1)
    gain = jnp.sum(jnp.where(heads == position()[1], scale[...], 0.0), axis=1, keepdims=True)
    gain = gain * (LOG2E / HEAD)
    pieces, refs = refs[:count], refs[count:]
    inverses, refs = refs[:known], refs[known:]
    if resumed:
        (old_mixed, old_stats), refs = refs[:2], refs[2:]
    sizes = [ref.shape[0] for ref in pieces]
    starts = [sum(sizes[:i]) for i in range(count)]

    total_known = sum(ref.shape[1] for ref in inverses)
    if total_known < sum(sizes):
        outs, inverse = refs[:-1], refs[-1]
        for at, size, ref in zip(starts, sizes, pieces):
            if at >= total_known:
                inverse[:, at - total_known : at - total_known + size] = inverse_norms(ref)
        inverses = (*inverses, inverse)
    else:
        outs = refs

    def inverse_of(at, size):
        for ref in inverses:
            if at < ref.shape[1]:
                return ref[0:1, at : at + size]
            at -= ref.shape[1]

    limit = 1024
    groups, room = [], 0
    for triple in zip(starts, sizes, pieces):
        if room < triple[1]:
            groups.append([])
            room = limit
        groups[-1].append(triple)
        room -= triple[1]

    def unit(query, factor, group):
        scores, peak = [], None
        for at, size, ref in group:
            part = dot_t(query, key_columns(ref)) * inverse_of(at, size)
            top = jnp.max(part, axis=1, keepdims=True)
            peak = top if peak is None else jnp.maximum(peak, top)
            scores.append(part)
        total, mixed = None, None
        for part, (_, _, ref) in zip(scores, group):
            exps = jnp.exp2((part - peak) * factor)
            sums = jnp.sum(exps, axis=1, keepdims=True)
            values = jnp.concatenate([ref[:, 128:256], ref[:, 256:]], axis=1)
            term = dot(exps.astype(BF16), values)
            total = sums if total is None else total + sums
            mixed = term if mixed is None else mixed + term
        return peak, total, mixed

    for begin in range(0, queries.shape[0], BLOCK):
        rows = slice(begin, begin + BLOCK)
        query = queries[rows, :]
        wide = query.astype(F32)
        own = lax.rsqrt(jnp.sum(wide * wide, axis=1, keepdims=True) * (1.0 / HEAD) + EPS)
        factor = own * gain
        states = [unit(query, factor, group) for group in groups]
        if resumed:
            states.append((old_stats[rows, 0:1], old_stats[rows, 64:65], old_mixed[rows, :]))
        peak = functools.reduce(jnp.maximum, [state[0] for state in states])
        if len(states) > 1:
            shrink = [jnp.exp2((state[0] - peak) * factor) for state in states]
            total = sum(state[1] * part for state, part in zip(states, shrink))
            mixed = sum(state[2] * part for state, part in zip(states, shrink))
        else:
            _, total, mixed = states[0]
        if not final:
            outs[0][rows, :] = mixed
            half = lax.broadcasted_iota(jnp.int32, (BLOCK, 128), 1) < 64
            outs[1][rows, :] = jnp.where(half, peak, total)
            continue
        mixed = mixed / total
        weight = peak * factor + jnp.log(total) * LOG2E
        high = weight.astype(BF16).astype(F32)
        rest = weight - high
        mid = rest.astype(BF16).astype(F32)
        place = lax.broadcasted_iota(jnp.int32, mixed.shape, 1)
        mixed = jnp.where(place == 128, high, mixed)
        mixed = jnp.where(place == 129, mid, mixed)
        mixed = jnp.where(place == 130, rest - mid, mixed)
        outs[0][rows, :] = mixed.astype(BF16)


def attend(scale, queries, pieces, inverses=(), state=(), final=True):
    rows = queries.shape[0]
    keys = sum(piece.shape[0] for piece in pieces)
    if final:
        outs = [shape((rows, 256), BF16)]
    else:
        outs = [shape((rows, 256), F32), shape((rows, 128), F32)]
    known = sum(inverse.shape[1] for inverse in inverses)
    if known < keys:
        outs.append(shape((8, keys - known), F32))
    return pl.pallas_call(
        functools.partial(attend_kernel, len(pieces), len(inverses), bool(state), final),
        in_specs=[VM] + [VM] * (1 + len(pieces) + len(inverses) + len(state)),
        out_specs=[VM] * len(outs),
        out_shape=outs,
        compiler_params=params(28),
        cost_estimate=cost(4 * rows * keys * 256, 8 * rows * 1024),
        name="attend",
    )(scale, near_memory(queries), *pieces, *inverses, *state)


def merge_kernel(a0, a1, *outs):
    parts = [ref[...].astype(F32) for ref in (a0, a1)]
    logs = [p[:, 128:129] + p[:, 129:130] + p[:, 130:131] for p in parts]
    peak = functools.reduce(jnp.maximum, logs)
    shares = [jnp.exp2(log - peak) for log in logs]
    total = sum(shares)
    mixed = sum(p * (share / total) for p, share in zip(parts, shares))
    mixed = jnp.concatenate([mixed[:, :128], pltpu.roll(mixed[:, 128:], 64, 1)], axis=1)
    for block in range(4):
        outs[block][...] = mixed[block * ROWS : (block + 1) * ROWS].astype(BF16)


def merge(parts):
    return pl.pallas_call(
        merge_kernel,
        in_specs=[VM] * 2,
        out_specs=[VM] * 4,
        out_shape=[shape((ROWS, 256), BF16)] * 4,
        compiler_params=params(8),
        cost_estimate=cost(20 * parts[0].size, 10 * parts[0].size),
        name="merge",
    )(*parts)


def output_kernel(mine, a0, a1, a2, a3, weight, out):
    ids = position()
    half = out.shape[1]
    side = ids[0] if mine else 1 - ids[0]

    def tile(i):
        at = lanes(side * half + i * TILE, TILE)
        total = None
        for distance, ref in enumerate((a0, a1, a2, a3)):
            head = lax.rem(ids[1] + distance, 4)
            rows = weight[pl.ds(pl.multiple_of(head * HEAD, HEAD), HEAD), at]
            term = dot(ref[:, :HEAD], rows)
            total = term if total is None else total + term
        out[:, lanes(i * TILE, TILE)] = total.astype(out.dtype)

    tiles(half // TILE, tile)


def output(heads, weight, mine, dtype):
    half = weight.shape[1] // 2
    return pl.pallas_call(
        functools.partial(output_kernel, mine),
        in_specs=[VM] * 5,
        out_specs=VM,
        out_shape=shape((ROWS, half), dtype),
        compiler_params=params(6),
        cost_estimate=cost(2 * ROWS * weight.size // 2, weight.size),
        name="output",
    )(*heads, weight)


def decode_first_kernel(own, other, encoded, weight, inputs, out):
    ids = position()
    half = weight.shape[1]

    def mix(i):
        at = lanes(i * TILE, TILE)
        enc = encoded[:, at].astype(F32)
        even, odd = enc[:ROWS], enc[ROWS:]
        binned = (even + odd) * 0.5
        block = (binned + (own[:, at] + other[:, at].astype(F32))).astype(BF16).astype(F32)
        row = lax.broadcasted_iota(jnp.int32, block.shape, 0)
        outside = ((ids[2] == 0) & (row == ROWS - 1)) | ((ids[2] == 63) & (row == OWN))
        even = jnp.where(outside, 0.0, block + even)
        odd = jnp.where(outside, 0.0, block + odd)
        inputs[:, at] = jnp.concatenate([even, odd], axis=0).astype(BF16)

    tiles(half // TILE, mix)
    decode_tiles(inputs, weight, out, (1 - ids[0]) * half)


def decode_tiles(inputs, weight, out, begin):
    def tile(i):
        at = lanes(begin + i * TILE, TILE)
        result = conv_taps(inputs[...], lambda t: weight[t, :, at], ROWS)
        out[:, lanes(i * TILE, TILE)] = result.astype(out.dtype)

    tiles(out.shape[1] // TILE, tile)


def decode_first(own, other, encoded, weight, width):
    half = weight.shape[1]
    return pl.pallas_call(
        decode_first_kernel,
        in_specs=[VM] * 4,
        out_specs=[VM] * 2,
        out_shape=[shape((2 * ROWS, half), BF16), pltpu.VMEM((2 * ROWS, width), BF16)],
        compiler_params=params(8),
        cost_estimate=cost(10**6, 10**4),
        name="decode_first",
    )(own, other, encoded, weight)


def decode_kernel(mine, first, inputs, weight, out):
    ids = position()
    side = ids[0] if mine else 1 - ids[0]
    decode_tiles(inputs, weight, out, side * weight.shape[1] + first)


def decode(inputs, weight, mine, first, width, dtype):
    half = weight.shape[1]
    return pl.pallas_call(
        functools.partial(decode_kernel, mine, first),
        in_specs=[VM, VM],
        out_specs=VM,
        out_shape=pltpu.VMEM((2 * ROWS, width), dtype),
        compiler_params=params(8),
        cost_estimate=cost(10**6, 10**4),
        name="decode",
    )(inputs, weight)


def slope_kernel(first, own, other, inputs, grad, near, far, *refs):
    ids = position()
    done, (decoded, slope, paired, wide) = refs[:-4], refs[-4:]
    half = own.shape[1]
    begin = 0
    if done:
        begin = first
        decoded[:, :first] = done[0][...]

    def tile(i):
        at = lanes(i * 128, 128)
        target = lanes(begin + i * 128, 128)
        source = lanes(first + i * 128, 128)
        column = lanes(ids[0] * half + first + i * 128, 128)
        pre = own[:, source] + other[:, at].astype(F32)
        tanh = gelu_tanh(pre)
        result = inputs[:, source].astype(F32) + 0.5 * pre * (1.0 + tanh)
        wide[2 * i, pl.ds(0, OWN, 2), :] = result[:OWN]
        wide[2 * i, pl.ds(1, OWN, 2), :] = result[ROWS : ROWS + OWN]
        decoded[:, target] = wide[2 * i].astype(BF16)
        slant = 0.5 * (1.0 + tanh) + (0.5 * 0.7978845608028654) * pre * (1.0 - tanh * tanh) * (
            1.0 + (3 * 0.044715) * (pre * pre)
        )
        wide[2 * i + 1] = grad[:, column].astype(F32)
        even = wide[2 * i + 1, pl.ds(0, OWN, 2), :]
        odd = wide[2 * i + 1, pl.ds(1, OWN, 2), :]
        paired[:, at] = even + odd
        row = lax.broadcasted_iota(jnp.int32, (ROWS - OWN, 128), 0)
        before, after = sides(lax.rem(ids[2], 2) == 1, near[:, column].astype(F32), far[:, column].astype(F32))
        even_edge = jnp.where(row == 0, after, 0.0)
        odd_edge = jnp.where(row == ROWS - OWN - 1, before, 0.0)
        cotangent = jnp.concatenate([even, even_edge, odd, odd_edge], axis=0)
        slope[:, at] = (cotangent * slant).astype(BF16)

    tiles(other.shape[1] // 128, tile)


def slopes(own, other, inputs, grad, near, far, first, done=()):
    width = other.shape[1]
    return pl.pallas_call(
        functools.partial(slope_kernel, first),
        in_specs=[VM] * (6 + len(done)),
        out_specs=[VM] * 3,
        out_shape=[
            shape((2 * OWN, width + (first if done else 0)), BF16),
            pltpu.VMEM((2 * ROWS, width), BF16),
            shape((OWN, width), F32),
        ],
        scratch_shapes=[pltpu.VMEM((width // 64, 2 * OWN, 128), F32)],
        compiler_params=params(8),
        cost_estimate=cost(100 * 30 * 1000 * other.size, 14 * other.size),
        name="slopes",
    )(own, near_memory(other), inputs, near_memory(grad), near, far, *done)


def backward_kernel(mine, firsts, count, *refs):
    ids = position()
    slopes_in, starts, (weight, out) = (
        refs[: len(firsts)],
        refs[len(firsts) : len(firsts) + count],
        refs[len(firsts) + count :],
    )
    half = weight.shape[1]
    side = ids[0] if mine else 1 - ids[0]
    whole = [start for start in starts if start.shape[1] == half]
    chunks = [start for start in starts if start.shape[1] < half]

    def tile(i, chunk, begin):
        inner = lanes(i * TILE, TILE)
        first = mid = last = None
        for offset, slope in zip(firsts, slopes_in):
            at = pl.ds(pl.multiple_of(side * half + offset, TILE), slope.shape[1])
            terms = [dot_t(slope[...], weight[t, inner, at]) for t in range(3)]
            if first is None:
                first, mid, last = terms
            else:
                first, mid, last = first + terms[0], mid + terms[1], last + terms[2]
        total = first[ROWS:] + mid[:ROWS] + mid[ROWS:] + last[:ROWS]
        total = total + below(first[:ROWS], ROWS) + above(last[ROWS:], ROWS)
        total = total[:OWN]
        for start in whole:
            total = total + start[:, inner]
        if chunk is not None:
            total = total + chunk[:, lanes(i * TILE - begin, TILE)]
        out[:, inner] = total.astype(out.dtype)

    if not chunks:
        tiles(half // TILE, lambda i: tile(i, None, 0))
    begin = 0
    for chunk in chunks:
        width = chunk.shape[1]
        tiles(width // TILE, lambda i: tile(i + begin // TILE, chunk, begin))
        begin += width


def backward(parts, starts, weight, mine, dtype):
    half = weight.shape[1]
    size = sum(part.size for _, part in parts)
    return pl.pallas_call(
        functools.partial(backward_kernel, mine, [first for first, _ in parts], len(starts)),
        in_specs=[VM] * (len(parts) + len(starts) + 1),
        out_specs=VM,
        out_shape=shape((OWN, half), dtype),
        compiler_params=params(10),
        cost_estimate=cost(1 * 2 * 3 * half * size, 6 * size),
        name="backward",
    )(*[near_memory(part) for _, part in parts], *starts, weight)


def place(at):
    return at // 16, at // 4 % 4, at // 2 % 2, at % 2


def moves(dx=0, dz=0, dy=0, dc=0):
    pairs = []
    for at in range(64):
        x, z, y, c = place(at)
        pairs.append((at, (x + dx) % 4 * 16 + (z + dz) % 4 * 4 + (y ^ dy) * 2 + (c ^ dc)))
    return pairs


def swap(value):
    return lax.ppermute(value, "head", [(0, 1), (1, 0)])


def send(value, **step):
    return lax.ppermute(value, "seq", moves(**step))


def per_device(
    dna_bases,
    stem_weight,
    encoder_weight,
    norm_gain,
    attention_weight,
    logit_scale,
    out_weight,
    decoder_weight,
    grad_out,
):
    at = lax.axis_index("seq")
    x = at // 16
    feats = grad_out.shape[1]

    codes, near, far = prepare(dna_bases.reshape(OWN, 128), grad_out)
    near = send(near, dc=1)
    pairs = [(i, i + 1) for i in range(1, 63, 2)]
    far = lax.ppermute(far, "seq", pairs + [(b, a) for a, b in pairs])
    halo = near, far
    rows, stem_weight, encoder_weight = load(codes, stem_weight, encoder_weight)
    encoded = encode(*halo, rows, stem_weight, encoder_weight)
    encoded, attention_weight = lax.optimization_barrier((encoded, attention_weight))
    attention_weight = fetch(attention_weight)
    gain = norm_gain.reshape(1, feats)
    normed, *keyvals = project_keys(encoded, swap(encoded), gain, attention_weight)

    def spread(blocks):
        return [send(blocks[d], dx=d) for d in (1, 3, 2)]

    def stacked(blocks):
        return jnp.concatenate(lax.optimization_barrier(blocks), axis=0)

    got = spread(keyvals)
    keyvals = stacked([keyvals[0]] + got)
    near = [send(keyvals, dz=1), send(keyvals, dz=3)]
    queries = project_queries(normed, attention_weight)
    *near, got = lax.optimization_barrier((*near, spread(queries)))
    queries = jnp.concatenate([queries[0]] + got, axis=0)
    others = send(queries, dy=1)
    half = keyvals.shape[0] // 2
    far = [send(near[0][:half], dz=1), send(near[1][half:], dz=3)]
    across = [send(piece, dc=1) for piece in (keyvals, *near)]
    pieces = [keyvals] + near + across
    inverse = norms(pieces)
    *far, inverse, others = lax.optimization_barrier((*far, inverse, others))
    far = jnp.concatenate(far, axis=0)
    pieces += [far, send(far, dc=1)]
    scale = logit_scale.reshape(1, 4)
    other, later = attend(scale, others, pieces, inverses=[inverse])
    other = send(other, dy=1)
    own = attend(scale, queries, pieces, inverses=[inverse, later])[0]
    mixed = merge([own, other])
    heads = [mixed[0], send(mixed[1], dx=-1), send(mixed[3], dx=-2), send(mixed[2], dx=-3)]

    sent = swap(output(heads, out_weight, False, BF16))
    kept = output(heads, out_weight, True, F32)
    half = decoder_weight.shape[1]
    split = 2 * TILE
    inputs, early = decode_first(kept, sent, encoded, decoder_weight, split)
    early = swap(early)
    late = decode(inputs, decoder_weight, False, split, half - split, BF16)
    late, inputs = lax.optimization_barrier((late, inputs))
    late = swap(late)
    kept = decode(inputs, decoder_weight, True, 0, half, F32)
    decoded, early, paired = slopes(kept, early, inputs, grad_out, *halo, 0)
    early_back = swap(early)
    decoded, late, rest = slopes(
        kept, late, inputs, grad_out, *halo, split, (decoded,)
    )
    late_back = swap(late)
    total = backward(
        [(0, early), (split, late)], [paired, rest], decoder_weight, True, F32
    )
    total = backward([(0, early_back)], [total], decoder_weight, False, F32)
    bins_grad = backward([(split, late_back)], [total], decoder_weight, False, BF16)
    return decoded, bins_grad


def solution(mesh):
    in_specs = (
        P("seq"),
        P(),
        P(None, None, "head"),
        P(),
        P(None, None, "head"),
        P("head"),
        P("head", None),
        P(None, "head", None),
        P("seq", None),
    )
    out_specs = (P("seq", "head"), P("seq", "head"))
    return jax.shard_map(
        per_device, mesh=mesh, in_specs=in_specs, out_specs=out_specs, check_vma=False
    )
```

```python
import functools

import jax
import jax.numpy as jnp
from jax import lax
from jax.experimental import pallas as pl
from jax.experimental.pallas import tpu as pltpu
from jax.sharding import PartitionSpec as P

BF16 = jnp.bfloat16
F32 = jnp.float32
ROWS = 136
OWN = 128
TILE = 256
HEAD = 192
EPS = 1e-06
MIB = 1024 * 1024


def params(mib):
    return pltpu.CompilerParams(vmem_limit_bytes=mib * MIB)


def dot(a, b):
    return jnp.dot(a, b, preferred_element_type=F32)


def dot_t(a, b):
    return lax.dot_general(a, b, (((1,), (1,)), ((), ())), preferred_element_type=F32)


def cost(flops, nbytes):
    return pl.CostEstimate(flops=int(flops), bytes_accessed=int(nbytes), transcendentals=0)


def shape(dims, dtype):
    return jax.ShapeDtypeStruct(dims, dtype)


VM = pl.BlockSpec(memory_space=pltpu.VMEM)
HBM = pl.BlockSpec(memory_space=pltpu.HBM)


def above(rows, span):
    parts = [pltpu.roll(rows[i : i + span], 1, 0) for i in range(0, rows.shape[0], span)]
    return jnp.concatenate(parts, axis=0)


def below(rows, span):
    parts = [pltpu.roll(rows[i : i + span], span - 1, 0) for i in range(0, rows.shape[0], span)]
    return jnp.concatenate(parts, axis=0)


def lanes(at, size):
    return pl.ds(at if isinstance(at, int) else pl.multiple_of(at, size), size)


def tiles(count, body):
    for i in range(count):
        body(i)


def gelu_tanh(x):
    return jnp.tanh(0.7978845608028654 * (x + 0.044715 * (x * x * x)))


def conv_taps(rows, weight, span):
    half = rows.shape[0] // 2
    first, mid, last = (dot(rows, weight(t)) for t in range(3))
    even = above(first[half:], span) + mid[:half] + last[half:]
    odd = first[:half] + mid[half:] + below(last[:half], span)
    return jnp.concatenate([even, odd], axis=0)


def position():
    at = lax.axis_index("seq")
    return lax.axis_index("head"), at // 16, at


def sides(odd, near, far):
    return jnp.where(odd, near, far), jnp.where(odd, far, near)


def prepare_kernel(bases, grad, codes, near, far, code, head, tail, sems):
    ids = position()
    rows = grad.shape[0]
    copies = [
        pltpu.make_async_copy(bases, code, sems.at[0]),
        pltpu.make_async_copy(grad.at[pl.ds(0, 16)], head, sems.at[1]),
        pltpu.make_async_copy(grad.at[pl.ds(rows - 16, 16)], tail, sems.at[2]),
    ]
    for copy in copies:
        copy.start()
    for copy in copies:
        copy.wait()
    feats = grad.shape[1]
    letters = (code[...] + 1).astype(F32)
    codes[...] = letters.astype(BF16)
    odd = lax.rem(ids[2], 2) == 1
    last = jnp.concatenate([tail[...].astype(F32)[8:], letters[OWN - 8 :]], axis=1)
    first = jnp.concatenate([head[...].astype(F32)[:8], letters[:8]], axis=1)
    near[...] = jnp.where(odd, first, last).astype(BF16)
    far[...] = jnp.where(odd, last, first).astype(BF16)


def near_memory(value):
    return pltpu.with_memory_space_constraint(value, pltpu.VMEM)


def far_memory(value):
    return pltpu.with_memory_space_constraint(value, pltpu.HBM)


def prepare(bases, grad):
    feats = grad.shape[1]
    return pl.pallas_call(
        prepare_kernel,
        in_specs=[HBM, HBM],
        out_specs=[VM] * 3,
        out_shape=[
            shape((OWN, 128), BF16),
            shape((8, feats + 128), BF16),
            shape((8, feats + 128), BF16),
        ],
        scratch_shapes=[
            pltpu.VMEM(bases.shape, jnp.int32),
            pltpu.VMEM((16, feats), BF16),
            pltpu.VMEM((16, feats), BF16),
            pltpu.SemaphoreType.DMA((3,)),
        ],
        compiler_params=params(4),
        cost_estimate=cost(10**5, 10**5),
        name="prepare",
    )(far_memory(bases), far_memory(grad))


def embed_letters(code, stem, embedded):
    patch = stem.shape[0] // 4
    row = lax.broadcasted_iota(jnp.int32, (2 * patch, 4 * patch), 0)
    col = lax.broadcasted_iota(jnp.int32, (2 * patch, 4 * patch), 1)
    spread = [
        dot(code, (row == col // 4 + offset).astype(F32).astype(BF16)) for offset in (0, patch)
    ]
    spread = jnp.concatenate(spread, axis=0)
    base = lax.broadcasted_iota(jnp.int32, spread.shape, 1) % 4 + 1
    onehot = (spread == base.astype(F32)).astype(F32).astype(BF16)

    def embed(i):
        at = lanes(i * TILE, TILE)
        embedded[:, at] = dot(onehot, stem[:, at]).astype(BF16)

    tiles(stem.shape[1] // TILE, embed)


def load_kernel(codes, stems, weights, embedded, stem, weight, sems):
    copies = [
        pltpu.make_async_copy(stems, stem, sems.at[0]),
        pltpu.make_async_copy(weights, weight, sems.at[1]),
    ]
    for copy in copies:
        copy.start()
    copies[0].wait()
    embed_letters(codes[...], stem, embedded)
    copies[1].wait()


def load(codes, stem, weight):
    return pl.pallas_call(
        load_kernel,
        in_specs=[VM, HBM, HBM],
        out_specs=[VM] * 3,
        out_shape=[
            pltpu.VMEM((2 * OWN, stem.shape[1]), BF16),
            pltpu.VMEM(stem.shape, BF16),
            pltpu.VMEM(weight.shape, BF16),
        ],
        scratch_shapes=[pltpu.SemaphoreType.DMA((2,))],
        compiler_params=params(4),
        cost_estimate=cost(10**5, weight.size * 2),
        name="load",
    )(codes, far_memory(stem), far_memory(weight))


def ring_order(rows):
    half = ROWS - OWN
    return (
        jnp.concatenate([rows[:OWN], rows[2 * OWN : 2 * OWN + half]], axis=0),
        jnp.concatenate([rows[OWN : 2 * OWN], rows[2 * OWN + half :]], axis=0),
    )


def encode_kernel(near, far, rows, stem, weight, encoded, embedded, halo):
    ids = position()
    feats = stem.shape[1]
    half = weight.shape[2]
    place = lax.broadcasted_iota(jnp.int32, (ROWS - OWN, 128), 0)
    before, after = sides(lax.rem(ids[2], 2) == 1, near[:, feats:].astype(F32), far[:, feats:].astype(F32))
    code = jnp.where(place >= 6, before, 0.0)
    code = jnp.where(place < 2, after, code)
    embed_letters(code.astype(BF16), stem, halo)
    embedded[: 2 * OWN, :] = rows[...]
    embedded[2 * OWN :, :] = halo[...]

    def convolve(i):
        at = lanes(i * TILE, TILE)
        parts = [dot(embedded[...], weight[tap, :, at]) for tap in range(3)]
        (first_even, first_odd), (even, odd), (last_even, last_odd) = map(ring_order, parts)
        even = above(first_odd, ROWS) + even + last_odd
        odd = first_even + odd + below(last_even, ROWS)
        pre = jnp.concatenate([even, odd], axis=0)
        mine = embedded[:, lanes(ids[0] * half + i * TILE, TILE)].astype(F32)
        mine = jnp.concatenate(ring_order(mine), axis=0)
        encoded[:, at] = (mine + 0.5 * pre * (1.0 + gelu_tanh(pre))).astype(BF16)

    tiles(half // TILE, convolve)


def encode(near, far, rows, stem, weight):
    half = weight.shape[2]
    feats = stem.shape[1]
    return pl.pallas_call(
        encode_kernel,
        in_specs=[VM] * 5,
        out_specs=VM,
        out_shape=shape((2 * ROWS, half), BF16),
        scratch_shapes=[
            pltpu.VMEM((2 * ROWS, feats), BF16),
            pltpu.VMEM((2 * (ROWS - OWN), feats), BF16),
        ],
        compiler_params=params(12),
        cost_estimate=cost(4 * OWN * weight.size, weight.size * 4),
        name="encode",
    )(near, far, near_memory(rows), near_memory(stem), near_memory(weight))


def fetch_kernel(source, target, sem):
    copy = pltpu.make_async_copy(source, target, sem)
    copy.start()
    copy.wait()


def fetch(value):
    return pl.pallas_call(
        fetch_kernel,
        in_specs=[HBM],
        out_specs=VM,
        out_shape=pltpu.VMEM(value.shape, value.dtype),
        scratch_shapes=[pltpu.SemaphoreType.DMA(())],
        compiler_params=params(2),
        cost_estimate=cost(10**5, value.size * 2),
        name="fetch",
    )(far_memory(value))


def unpacked(both):
    both = both.astype(BF16).astype(F32)
    turned = pltpu.roll(both, 2 * HEAD - 64, 1)
    return (both[:, :128], both[:, 128:256]), (turned[:, 128:256], turned[:, 256:384])


def project_keys_kernel(
    mine, theirs, gain, weight, normed, k0, k1, k2, k3, packed
):
    ids = position()
    half = mine.shape[1]
    near = lanes(ids[0] * half, half)
    far = lanes((1 - ids[0]) * half, half)
    rings = [ref[...].astype(F32) for ref in (mine, theirs)]
    binned = [(ring[:ROWS] + ring[ROWS:]) * 0.5 for ring in rings]
    total = sum(jnp.sum(part * part, axis=1, keepdims=True) for part in binned)
    inverse = lax.rsqrt(total * (1.0 / (2 * half)) + EPS)
    here = (binned[0] * inverse * gain[:, near]).astype(BF16)
    there = (binned[1] * inverse * gain[:, far]).astype(BF16)
    normed[0] = here
    normed[1] = there
    low = lax.broadcasted_iota(jnp.int32, (ROWS, 128), 1) < 64
    for pair in range(2):
        at = slice(pair * 2 * HEAD, (pair + 1) * 2 * HEAD)
        keys, values = (
            unpacked(dot(here, weight[kind, near, at]) + dot(there, weight[kind, far, at]))
            for kind in (1, 2)
        )
        for side in range(2):
            head = 2 * pair + side
            key, value = keys[side], values[side]
            packed[head, :, :128] = key[0].astype(BF16)
            packed[head, :, 128:256] = value[0].astype(BF16)
            tail = jnp.where(low, key[1], pltpu.roll(value[1], 64, 1))
            packed[head, :, 256:] = tail.astype(BF16)
    for distance, out in enumerate((k0, k1, k2, k3)):
        out[...] = packed[lax.rem(ids[1] + distance, 4), :OWN, :]


def project_keys(mine, theirs, gain, weight):
    half = mine.shape[1]
    return pl.pallas_call(
        project_keys_kernel,
        in_specs=[VM] * 4,
        out_specs=[VM] * 5,
        out_shape=[shape((2, ROWS, half), BF16)] + [shape((OWN, 384), BF16)] * 4,
        scratch_shapes=[pltpu.VMEM((4, ROWS, 384), BF16)],
        compiler_params=params(12),
        cost_estimate=cost(2 * ROWS * weight.size * 2 // 3, weight.size * 2),
        name="project_keys",
    )(mine, theirs, gain, near_memory(weight))


def project_queries_kernel(normed, weight, q0, q1, q2, q3, packed):
    ids = position()
    half = normed.shape[2]
    near = lanes(ids[0] * half, half)
    far = lanes((1 - ids[0]) * half, half)
    low = lax.broadcasted_iota(jnp.int32, (ROWS, 128), 1) < 64
    for pair in range(2):
        at = slice(pair * 2 * HEAD, (pair + 1) * 2 * HEAD)
        both = dot(normed[0], weight[0, near, at]) + dot(normed[1], weight[0, far, at])
        for side, query in enumerate(unpacked(both)):
            packed[2 * pair + side, :, :128] = query[0].astype(BF16)
            packed[2 * pair + side, :, 128:] = jnp.where(low, query[1], 0.0).astype(BF16)
    for distance, out in enumerate((q0, q1, q2, q3)):
        out[...] = packed[lax.rem(ids[1] + distance, 4)]


def project_queries(normed, weight):
    return pl.pallas_call(
        project_queries_kernel,
        in_specs=[VM, VM],
        out_specs=[VM] * 4,
        out_shape=[shape((ROWS, 256), BF16)] * 4,
        scratch_shapes=[pltpu.VMEM((4, ROWS, 256), BF16)],
        compiler_params=params(10),
        cost_estimate=cost(2 * ROWS * weight.size // 3, weight.size),
        name="project_queries",
    )(normed, near_memory(weight))


BLOCK = 4 * ROWS
LOG2E = 1.4426950408889634


def key_columns(ref):
    return jnp.concatenate([ref[:, :128], ref[:, 256:]], axis=1)


def inverse_norms(ref):
    lane = lax.broadcasted_iota(jnp.int32, (8, 256), 1)
    ones = (lane < HEAD).astype(F32).astype(BF16)
    key = key_columns(ref).astype(F32)
    square = key * key
    high = square.astype(BF16)
    rest = (square - high.astype(F32)).astype(BF16)
    total = dot_t(ones, high) + dot_t(ones, rest)
    return lax.rsqrt(total * (1.0 / HEAD) + EPS)


def norms_kernel(*refs):
    pieces, out = refs[:-1], refs[-1]
    at = 0
    for ref in pieces:
        out[:, at : at + ref.shape[0]] = inverse_norms(ref)
        at += ref.shape[0]


def norms(pieces):
    keys = sum(piece.shape[0] for piece in pieces)
    return pl.pallas_call(
        norms_kernel,
        in_specs=[VM] * len(pieces),
        out_specs=VM,
        out_shape=shape((8, keys), F32),
        compiler_params=params(6),
        cost_estimate=cost(10**6, 10**5),
        name="norms",
    )(*pieces)


def attend_kernel(count, known, resumed, final, scale, queries, *refs):
    heads = lax.broadcasted_iota(jnp.int32, scale.shape, 1)
    gain = jnp.sum(jnp.where(heads == position()[1], scale[...], 0.0), axis=1, keepdims=True)
    gain = gain * (LOG2E / HEAD)
    pieces, refs = refs[:count], refs[count:]
    inverses, refs = refs[:known], refs[known:]
    if resumed:
        (old_mixed, old_stats), refs = refs[:2], refs[2:]
    sizes = [ref.shape[0] for ref in pieces]
    starts = [sum(sizes[:i]) for i in range(count)]

    total_known = sum(ref.shape[1] for ref in inverses)
    if total_known < sum(sizes):
        outs, inverse = refs[:-1], refs[-1]
        for at, size, ref in zip(starts, sizes, pieces):
            if at >= total_known:
                inverse[:, at - total_known : at - total_known + size] = inverse_norms(ref)
        inverses = (*inverses, inverse)
    else:
        outs = refs

    def inverse_of(at, size):
        for ref in inverses:
            if at < ref.shape[1]:
                return ref[0:1, at : at + size]
            at -= ref.shape[1]

    limit = 1024
    groups, room = [], 0
    for triple in zip(starts, sizes, pieces):
        if room < triple[1]:
            groups.append([])
            room = limit
        groups[-1].append(triple)
        room -= triple[1]

    def unit(query, factor, group):
        scores, peak = [], None
        for at, size, ref in group:
            part = dot_t(query, key_columns(ref)) * inverse_of(at, size)
            top = jnp.max(part, axis=1, keepdims=True)
            peak = top if peak is None else jnp.maximum(peak, top)
            scores.append(part)
        total, mixed = None, None
        for part, (_, _, ref) in zip(scores, group):
            exps = jnp.exp2((part - peak) * factor)
            sums = jnp.sum(exps, axis=1, keepdims=True)
            values = jnp.concatenate([ref[:, 128:256], ref[:, 256:]], axis=1)
            term = dot(exps.astype(BF16), values)
            total = sums if total is None else total + sums
            mixed = term if mixed is None else mixed + term
        return peak, total, mixed

    for begin in range(0, queries.shape[0], BLOCK):
        rows = slice(begin, begin + BLOCK)
        query = queries[rows, :]
        wide = query.astype(F32)
        own = lax.rsqrt(jnp.sum(wide * wide, axis=1, keepdims=True) * (1.0 / HEAD) + EPS)
        factor = own * gain
        states = [unit(query, factor, group) for group in groups]
        if resumed:
            states.append((old_stats[rows, 0:1], old_stats[rows, 64:65], old_mixed[rows, :]))
        peak = functools.reduce(jnp.maximum, [state[0] for state in states])
        if len(states) > 1:
            shrink = [jnp.exp2((state[0] - peak) * factor) for state in states]
            total = sum(state[1] * part for state, part in zip(states, shrink))
            mixed = sum(state[2] * part for state, part in zip(states, shrink))
        else:
            _, total, mixed = states[0]
        if not final:
            outs[0][rows, :] = mixed
            half = lax.broadcasted_iota(jnp.int32, (BLOCK, 128), 1) < 64
            outs[1][rows, :] = jnp.where(half, peak, total)
            continue
        mixed = mixed / total
        weight = peak * factor + jnp.log(total) * LOG2E
        high = weight.astype(BF16).astype(F32)
        rest = weight - high
        mid = rest.astype(BF16).astype(F32)
        place = lax.broadcasted_iota(jnp.int32, mixed.shape, 1)
        mixed = jnp.where(place == 128, high, mixed)
        mixed = jnp.where(place == 129, mid, mixed)
        mixed = jnp.where(place == 130, rest - mid, mixed)
        outs[0][rows, :] = mixed.astype(BF16)


def attend(scale, queries, pieces, inverses=(), state=(), final=True):
    rows = queries.shape[0]
    keys = sum(piece.shape[0] for piece in pieces)
    if final:
        outs = [shape((rows, 256), BF16)]
    else:
        outs = [shape((rows, 256), F32), shape((rows, 128), F32)]
    known = sum(inverse.shape[1] for inverse in inverses)
    if known < keys:
        outs.append(shape((8, keys - known), F32))
    return pl.pallas_call(
        functools.partial(attend_kernel, len(pieces), len(inverses), bool(state), final),
        in_specs=[VM] + [VM] * (1 + len(pieces) + len(inverses) + len(state)),
        out_specs=[VM] * len(outs),
        out_shape=outs,
        compiler_params=params(28),
        cost_estimate=cost(4 * rows * keys * 256, 8 * rows * 1024),
        name="attend",
    )(scale, near_memory(queries), *pieces, *inverses, *state)


def merge_kernel(a0, a1, *outs):
    parts = [ref[...].astype(F32) for ref in (a0, a1)]
    logs = [p[:, 128:129] + p[:, 129:130] + p[:, 130:131] for p in parts]
    peak = functools.reduce(jnp.maximum, logs)
    shares = [jnp.exp2(log - peak) for log in logs]
    total = sum(shares)
    mixed = sum(p * (share / total) for p, share in zip(parts, shares))
    mixed = jnp.concatenate([mixed[:, :128], pltpu.roll(mixed[:, 128:], 64, 1)], axis=1)
    for block in range(4):
        outs[block][...] = mixed[block * ROWS : (block + 1) * ROWS].astype(BF16)


def merge(parts):
    return pl.pallas_call(
        merge_kernel,
        in_specs=[VM] * 2,
        out_specs=[VM] * 4,
        out_shape=[shape((ROWS, 256), BF16)] * 4,
        compiler_params=params(8),
        cost_estimate=cost(20 * parts[0].size, 10 * parts[0].size),
        name="merge",
    )(*parts)


def output_kernel(mine, a0, a1, a2, a3, weight, out):
    ids = position()
    half = out.shape[1]
    side = ids[0] if mine else 1 - ids[0]

    def tile(i):
        at = lanes(side * half + i * TILE, TILE)
        total = None
        for distance, ref in zip((0, 2, 1, 3), (a0, a1, a2, a3)):
            head = lax.rem(ids[1] + distance, 4)
            rows = weight[pl.ds(pl.multiple_of(head * HEAD, HEAD), HEAD), at]
            term = dot(ref[:, :HEAD], rows)
            total = term if total is None else total + term
        out[:, lanes(i * TILE, TILE)] = total.astype(out.dtype)

    tiles(half // TILE, tile)


def output(heads, weight, mine, dtype):
    half = weight.shape[1] // 2
    return pl.pallas_call(
        functools.partial(output_kernel, mine),
        in_specs=[VM] * 5,
        out_specs=VM,
        out_shape=shape((ROWS, half), dtype),
        compiler_params=params(6),
        cost_estimate=cost(2 * ROWS * weight.size // 2, weight.size),
        name="output",
    )(*heads, weight)


def decode_first_kernel(own, other, encoded, weight, inputs, out):
    ids = position()
    half = weight.shape[1]

    def mix(i):
        at = lanes(i * TILE, TILE)
        enc = encoded[:, at].astype(F32)
        even, odd = enc[:ROWS], enc[ROWS:]
        binned = (even + odd) * 0.5
        block = (binned + (own[:, at] + other[:, at].astype(F32))).astype(BF16).astype(F32)
        row = lax.broadcasted_iota(jnp.int32, block.shape, 0)
        outside = ((ids[2] == 0) & (row == ROWS - 1)) | ((ids[2] == 63) & (row == OWN))
        even = jnp.where(outside, 0.0, block + even)
        odd = jnp.where(outside, 0.0, block + odd)
        inputs[:, at] = jnp.concatenate([even, odd], axis=0).astype(BF16)

    tiles(half // TILE, mix)
    decode_tiles(inputs, weight, out, (1 - ids[0]) * half)


def decode_tiles(inputs, weight, out, begin):
    def tile(i):
        at = lanes(begin + i * TILE, TILE)
        result = conv_taps(inputs[...], lambda t: weight[t, :, at], ROWS)
        out[:, lanes(i * TILE, TILE)] = result.astype(out.dtype)

    tiles(out.shape[1] // TILE, tile)


def decode_first(own, other, encoded, weight, width):
    half = weight.shape[1]
    return pl.pallas_call(
        decode_first_kernel,
        in_specs=[VM] * 4,
        out_specs=[VM] * 2,
        out_shape=[shape((2 * ROWS, half), BF16), pltpu.VMEM((2 * ROWS, width), BF16)],
        compiler_params=params(8),
        cost_estimate=cost(10**6, 10**4),
        name="decode_first",
    )(own, other, encoded, weight)


def decode_kernel(mine, first, inputs, weight, out):
    ids = position()
    side = ids[0] if mine else 1 - ids[0]
    decode_tiles(inputs, weight, out, side * weight.shape[1] + first)


def decode(inputs, weight, mine, first, width, dtype):
    half = weight.shape[1]
    return pl.pallas_call(
        functools.partial(decode_kernel, mine, first),
        in_specs=[VM, VM],
        out_specs=VM,
        out_shape=pltpu.VMEM((2 * ROWS, width), dtype),
        compiler_params=params(8),
        cost_estimate=cost(10**6, 10**4),
        name="decode",
    )(inputs, weight)


def slope_kernel(first, own, other, inputs, grad, near, far, *refs):
    ids = position()
    done, (decoded, slope, paired, wide) = refs[:-4], refs[-4:]
    half = own.shape[1]
    begin = 0
    if done:
        begin = first
        decoded[:, :first] = done[0][...]

    def tile(i):
        at = lanes(i * 128, 128)
        target = lanes(begin + i * 128, 128)
        source = lanes(first + i * 128, 128)
        column = lanes(ids[0] * half + first + i * 128, 128)
        pre = own[:, source] + other[:, at].astype(F32)
        tanh = gelu_tanh(pre)
        result = inputs[:, source].astype(F32) + 0.5 * pre * (1.0 + tanh)
        wide[2 * i, pl.ds(0, OWN, 2), :] = result[:OWN]
        wide[2 * i, pl.ds(1, OWN, 2), :] = result[ROWS : ROWS + OWN]
        decoded[:, target] = wide[2 * i].astype(BF16)
        slant = 0.5 * (1.0 + tanh) + (0.5 * 0.7978845608028654) * pre * (1.0 - tanh * tanh) * (
            1.0 + (3 * 0.044715) * (pre * pre)
        )
        wide[2 * i + 1] = grad[:, column].astype(F32)
        even = wide[2 * i + 1, pl.ds(0, OWN, 2), :]
        odd = wide[2 * i + 1, pl.ds(1, OWN, 2), :]
        paired[:, at] = even + odd
        row = lax.broadcasted_iota(jnp.int32, (ROWS - OWN, 128), 0)
        before, after = sides(lax.rem(ids[2], 2) == 1, near[:, column].astype(F32), far[:, column].astype(F32))
        even_edge = jnp.where(row == 0, after, 0.0)
        odd_edge = jnp.where(row == ROWS - OWN - 1, before, 0.0)
        cotangent = jnp.concatenate([even, even_edge, odd, odd_edge], axis=0)
        slope[:, at] = (cotangent * slant).astype(BF16)

    tiles(other.shape[1] // 128, tile)


def slopes(own, other, inputs, grad, near, far, first, done=()):
    width = other.shape[1]
    return pl.pallas_call(
        functools.partial(slope_kernel, first),
        in_specs=[VM] * (6 + len(done)),
        out_specs=[VM] * 3,
        out_shape=[
            shape((2 * OWN, width + (first if done else 0)), BF16),
            pltpu.VMEM((2 * ROWS, width), BF16),
            shape((OWN, width), F32),
        ],
        scratch_shapes=[pltpu.VMEM((width // 64, 2 * OWN, 128), F32)],
        compiler_params=params(8),
        cost_estimate=cost(100 * 30 * 1000 * other.size, 14 * other.size),
        name="slopes",
    )(own, near_memory(other), inputs, near_memory(grad), near, far, *done)


def backward_kernel(mine, firsts, count, *refs):
    ids = position()
    slopes_in, starts, (weight, out) = (
        refs[: len(firsts)],
        refs[len(firsts) : len(firsts) + count],
        refs[len(firsts) + count :],
    )
    half = weight.shape[1]
    side = ids[0] if mine else 1 - ids[0]
    whole = [start for start in starts if start.shape[1] == half]
    chunks = [start for start in starts if start.shape[1] < half]

    def tile(i, chunk, begin):
        inner = lanes(i * TILE, TILE)
        first = mid = last = None
        for offset, slope in zip(firsts, slopes_in):
            at = pl.ds(pl.multiple_of(side * half + offset, TILE), slope.shape[1])
            terms = [dot_t(slope[...], weight[t, inner, at]) for t in range(3)]
            if first is None:
                first, mid, last = terms
            else:
                first, mid, last = first + terms[0], mid + terms[1], last + terms[2]
        total = first[ROWS:] + mid[:ROWS] + mid[ROWS:] + last[:ROWS]
        total = total + below(first[:ROWS], ROWS) + above(last[ROWS:], ROWS)
        total = total[:OWN]
        for start in whole:
            total = total + start[:, inner]
        if chunk is not None:
            total = total + chunk[:, lanes(i * TILE - begin, TILE)]
        out[:, inner] = total.astype(out.dtype)

    if not chunks:
        tiles(half // TILE, lambda i: tile(i, None, 0))
    begin = 0
    for chunk in chunks:
        width = chunk.shape[1]
        tiles(width // TILE, lambda i: tile(i + begin // TILE, chunk, begin))
        begin += width


def backward(parts, starts, weight, mine, dtype):
    half = weight.shape[1]
    size = sum(part.size for _, part in parts)
    return pl.pallas_call(
        functools.partial(backward_kernel, mine, [first for first, _ in parts], len(starts)),
        in_specs=[VM] * (len(parts) + len(starts) + 1),
        out_specs=VM,
        out_shape=shape((OWN, half), dtype),
        compiler_params=params(10),
        cost_estimate=cost(1 * 2 * 3 * half * size, 6 * size),
        name="backward",
    )(*[near_memory(part) for _, part in parts], *starts, weight)


def place(at):
    return at // 16, at // 4 % 4, at // 2 % 2, at % 2


def moves(dx=0, dz=0, dy=0, dc=0):
    pairs = []
    for at in range(64):
        x, z, y, c = place(at)
        pairs.append((at, (x + dx) % 4 * 16 + (z + dz) % 4 * 4 + (y ^ dy) * 2 + (c ^ dc)))
    return pairs


def swap(value):
    return lax.ppermute(value, "head", [(0, 1), (1, 0)])


def send(value, **step):
    return lax.ppermute(value, "seq", moves(**step))


def per_device(
    dna_bases,
    stem_weight,
    encoder_weight,
    norm_gain,
    attention_weight,
    logit_scale,
    out_weight,
    decoder_weight,
    grad_out,
):
    at = lax.axis_index("seq")
    x = at // 16
    feats = grad_out.shape[1]

    codes, near, far = prepare(dna_bases.reshape(OWN, 128), grad_out)
    near = send(near, dc=1)
    pairs = [(i, i + 1) for i in range(1, 63, 2)]
    far = lax.ppermute(far, "seq", pairs + [(b, a) for a, b in pairs])
    halo = near, far
    rows, stem_weight, encoder_weight = load(codes, stem_weight, encoder_weight)
    encoded = encode(*halo, rows, stem_weight, encoder_weight)
    encoded, attention_weight = lax.optimization_barrier((encoded, attention_weight))
    attention_weight = fetch(attention_weight)
    gain = norm_gain.reshape(1, feats)
    normed, *keyvals = project_keys(encoded, swap(encoded), gain, attention_weight)

    def spread(blocks):
        return [send(blocks[d], dx=d) for d in (2, 1, 3)]

    def stacked(blocks):
        return jnp.concatenate(lax.optimization_barrier(blocks), axis=0)

    got = spread(keyvals)
    keyvals = stacked([keyvals[0]] + got)
    near = [send(keyvals, dz=1), send(keyvals, dz=3)]
    queries = project_queries(normed, attention_weight)
    *near, got = lax.optimization_barrier((*near, spread(queries)))
    queries = jnp.concatenate([queries[0]] + got, axis=0)
    others = send(queries, dy=1)
    half = keyvals.shape[0] // 2
    far = [send(near[0][:half], dz=1), send(near[1][half:], dz=3)]
    across = [send(piece, dc=1) for piece in (keyvals, *near)]
    pieces = [keyvals] + near + across
    inverse = norms(pieces)
    *far, inverse, others = lax.optimization_barrier((*far, inverse, others))
    far = jnp.concatenate(far, axis=0)
    pieces += [far, send(far, dc=1)]
    scale = logit_scale.reshape(1, 4)
    other, later = attend(scale, others, pieces, inverses=[inverse])
    other = send(other, dy=1)
    own = attend(scale, queries, pieces, inverses=[inverse, later])[0]
    mixed = merge([own, other])
    heads = [mixed[0], send(mixed[1], dx=-2), send(mixed[2], dx=-1), send(mixed[3], dx=-3)]

    sent = swap(output(heads, out_weight, False, BF16))
    kept = output(heads, out_weight, True, F32)
    half = decoder_weight.shape[1]
    split = 2 * TILE
    inputs, early = decode_first(kept, sent, encoded, decoder_weight, split)
    early = swap(early)
    late = decode(inputs, decoder_weight, False, split, half - split, BF16)
    late, inputs = lax.optimization_barrier((late, inputs))
    late = swap(late)
    kept = decode(inputs, decoder_weight, True, 0, half, F32)
    decoded, early, paired = slopes(kept, early, inputs, grad_out, *halo, 0)
    early_back = swap(early)
    decoded, late, rest = slopes(
        kept, late, inputs, grad_out, *halo, split, (decoded,)
    )
    late_back = swap(late)
    total = backward(
        [(0, early), (split, late)], [paired, rest], decoder_weight, True, F32
    )
    total = backward([(0, early_back)], [total], decoder_weight, False, F32)
    bins_grad = backward([(split, late_back)], [total], decoder_weight, False, BF16)
    return decoded, bins_grad


def solution(mesh):
    in_specs = (
        P("seq"),
        P(),
        P(None, None, "head"),
        P(),
        P(None, None, "head"),
        P("head"),
        P("head", None),
        P(None, "head", None),
        P("seq", None),
    )
    out_specs = (P("seq", "head"), P("seq", "head"))
    return jax.shard_map(
        per_device, mesh=mesh, in_specs=in_specs, out_specs=out_specs, check_vma=False
    )
```
